32 devices in a mesh: cols: 32 (over z, y, x, core).
Axes of the slice: x: 2, y: 2, z: 4, core: 2. Of those that a mesh axis runs over, the one named last changes fastest.
Arguments:
- suction_initial: float32 [128, 16384], P(None, 'cols'), may hold values from -6 to 6
- warmth_initial: float32 [128, 16384], P(None, 'cols'), may hold values from -5 to 5
- soil_class: int32 [128, 16384], P(None, 'cols'), may hold values from 0 to 7
- top_boundary_warmth: float32 [16384], P('cols'), may hold values from -6 to 6
- neighbour_couplings: int32 [2, 128], replicated, may hold values from 0 to 1
- k_sat: float32 [8], replicated, may hold values from 0.1 to 1
- heat_cond: float32 [8], replicated, may hold values from 0.5 to 2
Outputs:
- suction_iterated: float32 [128, 16384], P(None, 'cols')
- warmth_iterated: float32 [128, 16384], P(None, 'cols')
The draws below stay inside these ranges and needn't reach their ends.
All inputs are finite; a program needn't handle non-finite values.
Results may differ from the reference program's by a relative error of at most 0.000066.
Values sent between devices are 32-bit elements; how exact they have to be, the bound alone decides.
No kernel may reach another device: no remote copies, remote signals or barrier semaphores. Data moves between devices by JAX's collectives and lax.ppermute only.
A program may use at most 128 MiB of HBM per device.

```python
import jax
import jax.numpy as jnp
from jax import lax

SOIL_SLABS = 128
UNIT_SPAN = 256
BLK_DEV = 2
PER_STEP = 1
CLASSES = 8
ITERS = 2
PAIR_DEV = 4
COLS = 16384
PAIRS = 128
N_COLS = 32


def chosen_blocks(key):
    number_of_blocks = COLS // UNIT_SPAN
    picks = jax.random.randint(jax.random.fold_in(key, 7), (number_of_blocks,), 0, 8)
    extra = jax.random.randint(jax.random.fold_in(key, 8), (), 0, number_of_blocks)
    positions = jnp.arange(number_of_blocks, dtype=jnp.int32)
    marked = jnp.logical_or(picks == 0, positions == extra)
    return jnp.repeat(marked, UNIT_SPAN)[None, :]


def draw_suction_initial(key, part):
    marked = chosen_blocks(key)
    value_key = jax.random.fold_in(key, 11)
    wet_key = jax.random.fold_in(key, 12)
    spread = jnp.clip(1.5 * jax.random.normal(value_key, (SOIL_SLABS, COLS), jnp.float32), -6.0, 6.0)
    wet = jax.random.uniform(wet_key, (SOIL_SLABS, COLS), jnp.float32, 5.5, 6.0)
    return jnp.where(marked, wet, spread)


def draw_warmth_initial(key, part):
    marked = chosen_blocks(key)
    value_key = jax.random.fold_in(key, 21)
    warm_key = jax.random.fold_in(key, 22)
    spread = jnp.clip(jax.random.normal(value_key, (SOIL_SLABS, COLS), jnp.float32), -5.0, 5.0)
    warm = jax.random.uniform(warm_key, (SOIL_SLABS, COLS), jnp.float32, 2.0, 5.0)
    return jnp.where(marked, warm, spread)


def draw_k_sat(key, part):
    value_key = jax.random.fold_in(key, 31)
    exponent = jax.random.uniform(value_key, (CLASSES,), jnp.float32, -2.302585, 0.0)
    return jnp.exp(exponent)


def set_ends(values, key, least, largest):
    place = [jax.random.randint(jax.random.fold_in(key, axis), (), 0, length) for axis, length in enumerate(values.shape)]
    main_axis = values.shape.index(max(values.shape))
    next_to = place[:main_axis] + [(place[main_axis] + 1) % values.shape[main_axis]] + place[main_axis + 1:]
    return values.at[tuple(place)].set(least).at[tuple(next_to)].set(largest)


def steps_of(rng, dims, pieces, low, high):
    factor_of = 1.0
    for dim, parts in pieces:
        heights = jax.random.uniform(jax.random.fold_in(jax.random.fold_in(rng, 6), dim), (parts,), jnp.float32, low / len(pieces), high / len(pieces))
        factor_of = factor_of * jnp.repeat(jnp.exp(heights), dims[dim] // parts).reshape((-1,) + (1,) * (len(dims) - 1 - dim))
    return factor_of


def centred(key, dims, scale, most, pieces=(), kind=jnp.bfloat16):
    entries = scale * jax.random.normal(key, dims, jnp.float32)
    if pieces:
        entries = entries * steps_of(key, dims, pieces, -0.22, 0.18)
    return jnp.clip(entries, -most, most).astype(kind)


def setup_inputs(seed: int = 0) -> dict:
    seeds = jax.random.split(jax.random.key(seed), 8)
    return {
        "suction_initial": draw_suction_initial(jax.random.fold_in(seeds[7], 71), 0),
        "warmth_initial": draw_warmth_initial(jax.random.fold_in(seeds[7], 71), 0),
        "soil_class": set_ends(jax.random.randint(seeds[2], (SOIL_SLABS, COLS), 0, CLASSES), jax.random.fold_in(seeds[2], 1), 0, CLASSES - 1).astype(jnp.int32),
        "top_boundary_warmth": centred(seeds[3], (COLS,), 1.5, 6.0, ((0, 32),), jnp.float32),
        "neighbour_couplings": set_ends(jax.random.randint(seeds[4], (2, PAIRS), 0, BLK_DEV), jax.random.fold_in(seeds[4], 1), 0, BLK_DEV - 1).astype(jnp.int32),
        "k_sat": draw_k_sat(jax.random.fold_in(seeds[7], 71), 0),
        "heat_cond": jnp.clip(jax.random.uniform(seeds[6], (CLASSES,), jnp.float32, 0.5, 2.0), 0.5, 2.0),
    }


TIME_STEP = 0.5
MELTING_SPECIFIC = 2.0
LATERAL = 0.5
SLOPE = 0.5
CARRY = 2.0


def moisture_of(suction_iterated):
    return 0.05 + 0.4 * jax.nn.sigmoid(suction_iterated)


def passage_coefficient(suction_iterated, warmth_iterated, permeability_profile):
    saturation = jax.nn.sigmoid(suction_iterated)
    melted_portion = jax.nn.sigmoid(2.0 * warmth_iterated)
    return permeability_profile * (melted_portion * saturation * saturation + 0.02)


def below_pad(face):
    return jnp.concatenate([face, jnp.zeros_like(face[:1])], axis=0)


def above_pad(face):
    return jnp.concatenate([jnp.zeros_like(face[:1]), face], axis=0)


def thomas(left_coef, main_coef, right_coef, source):
    zero_row = jnp.zeros_like(main_coef[0])

    def forward(carry, row):
        prev_ratio, prev_value = carry
        left_row, main_row, right_row, source_row = row
        pivot = main_row - left_row * prev_ratio
        ratio_new = right_row / pivot
        value_new = (source_row - left_row * prev_value) / pivot
        return (ratio_new, value_new), (ratio_new, value_new)

    _, (ratios, values) = lax.scan(forward, (zero_row, zero_row), (left_coef, main_coef, right_coef, source))

    def backward(later, row):
        ratio_row, value_row = row
        result = value_row - ratio_row * later
        return result, result

    _, solved = lax.scan(backward, zero_row, (ratios, values), reverse=True)
    return solved


def water_update(suction_iterated, suction_initial, passing_coefficient, side_seepage_inflow):
    saturation = jax.nn.sigmoid(suction_iterated)
    storage_now = 0.05 + 0.4 * saturation
    storage_old = moisture_of(suction_initial)
    boundary_coefficient = 0.5 * (passing_coefficient[:-1] + passing_coefficient[1:])
    descending_motion = -boundary_coefficient * (suction_iterated[1:] - suction_iterated[:-1] - 1.0)
    residual = (storage_now - storage_old) / TIME_STEP + below_pad(descending_motion) - above_pad(descending_motion) - side_seepage_inflow
    capacity = 0.4 * saturation * (1.0 - saturation) + 0.01
    face_above = above_pad(boundary_coefficient)
    face_below = below_pad(boundary_coefficient)
    main_coef = capacity / TIME_STEP + face_above + face_below
    difference_amount = thomas(-face_above, main_coef, -face_below, -residual)
    return suction_iterated + difference_amount


def internal_warmth_step(warmth_iterated, suction_after, warmth_initial, suction_initial, warmth_passing_profile, top_boundary_warmth, side_warmth_inflow):
    dampness_after = moisture_of(suction_after)
    moisture_old = moisture_of(suction_initial)
    melted_portion = jax.nn.sigmoid(2.0 * warmth_iterated)
    liquid_old = jax.nn.sigmoid(2.0 * warmth_initial)
    internal_warmth_new = (1.0 + 2.0 * dampness_after) * warmth_iterated + MELTING_SPECIFIC * dampness_after * melted_portion
    energy_old = (1.0 + 2.0 * moisture_old) * warmth_initial + MELTING_SPECIFIC * moisture_old * liquid_old
    warmth_related = warmth_passing_profile * (1.5 - 0.5 * melted_portion)
    boundary_coefficient = 0.5 * (warmth_related[:-1] + warmth_related[1:])
    descending_motion = -boundary_coefficient * (warmth_iterated[1:] - warmth_iterated[:-1])
    top_boundary_inflow = 2.0 * warmth_related[0] * (top_boundary_warmth - warmth_iterated[0])
    inflow = jnp.concatenate([top_boundary_inflow[None], descending_motion], axis=0)
    residual = (internal_warmth_new - energy_old) / TIME_STEP + below_pad(descending_motion) - inflow - side_warmth_inflow
    apparent = 1.0 + 2.0 * dampness_after + MELTING_SPECIFIC * dampness_after * 2.0 * melted_portion * (1.0 - melted_portion)
    surface_row = jnp.concatenate([2.0 * warmth_related[:1], jnp.zeros_like(warmth_related[1:])], axis=0)
    face_above = above_pad(boundary_coefficient)
    face_below = below_pad(boundary_coefficient)
    main_coef = apparent / TIME_STEP + face_above + face_below + surface_row
    difference_amount = thomas(-face_above, main_coef, -face_below, -residual)
    return warmth_iterated + difference_amount


def pair_flux(upper_prof, lower_prof):
    mean_cond = 0.5 * LATERAL * (upper_prof[2] + lower_prof[2])
    flow = mean_cond * (upper_prof[0] - lower_prof[0] + SLOPE)
    carried = CARRY * (jnp.maximum(flow, 0.0) * upper_prof[1] + jnp.minimum(flow, 0.0) * lower_prof[1])
    return flow, carried


def side_inflow_terms(suction_iterated, warmth_iterated, passing_coefficient, neighbour_couplings):
    number_of_tiles = BLK_DEV * N_COLS
    profile_variables = jnp.stack([suction_iterated, warmth_iterated, passing_coefficient]).reshape(3, SOIL_SLABS, number_of_tiles, UNIT_SPAN)
    water = jnp.zeros((SOIL_SLABS, number_of_tiles, UNIT_SPAN), jnp.float32)
    heat = jnp.zeros((SOIL_SLABS, number_of_tiles, UNIT_SPAN), jnp.float32)
    processor_units = jnp.arange(N_COLS, dtype=jnp.int32)
    for index in range(PAIR_DEV):
        distance = index // PER_STEP + 1
        valid = (processor_units + distance < N_COLS).astype(jnp.float32)[None, :, None]
        upper_blocks = processor_units * BLK_DEV + neighbour_couplings[0, processor_units * PAIR_DEV + index]
        lower_dev = jnp.minimum(processor_units + distance, N_COLS - 1)
        lower_blocks = lower_dev * BLK_DEV + neighbour_couplings[1, processor_units * PAIR_DEV + index]
        flow, carried = pair_flux(profile_variables[:, :, upper_blocks], profile_variables[:, :, lower_blocks])
        flow = flow * valid
        carried = carried * valid
        water = water.at[:, upper_blocks].add(-flow).at[:, lower_blocks].add(flow)
        heat = heat.at[:, upper_blocks].add(-carried).at[:, lower_blocks].add(carried)
    return water.reshape(SOIL_SLABS, number_of_tiles * UNIT_SPAN), heat.reshape(SOIL_SLABS, number_of_tiles * UNIT_SPAN)


def reference(suction_initial, warmth_initial, soil_class, top_boundary_warmth, neighbour_couplings, k_sat, heat_cond):
    permeability_profile = k_sat[soil_class]
    warmth_passing_profile = heat_cond[soil_class]
    suction_iterated = suction_initial
    warmth_iterated = warmth_initial
    for iteration in range(ITERS):
        passing_coefficient = passage_coefficient(suction_iterated, warmth_iterated, permeability_profile)
        side_seepage_inflow, side_warmth_inflow = side_inflow_terms(suction_iterated, warmth_iterated, passing_coefficient, neighbour_couplings)
        suction_after = water_update(suction_iterated, suction_initial, passing_coefficient, side_seepage_inflow)
        warmth_iterated = internal_warmth_step(warmth_iterated, suction_after, warmth_initial, suction_initial, warmth_passing_profile, top_boundary_warmth, side_warmth_inflow)
        suction_iterated = suction_after
    return suction_iterated, warmth_iterated
```

```python
import functools

import jax
import jax.numpy as jnp
from jax import lax
from jax.experimental import pallas as pl
from jax.experimental.pallas import tpu as pltpu
from jax.sharding import PartitionSpec as P

SPAN = 256
ITERS = 2
PAIR_DEV = 4
LANES = 128
PARTS = 8
VMEM_LIMIT = 48 * 1024 * 1024


def shift_down(value, steps):
    return pltpu.roll(value, steps, axis=0)


def shift_up(value, steps):
    return pltpu.roll(value, PARTS - steps, axis=0)


def pack_kernel(suction, warmth, classes, top, out):
    n, _, w, cells = out.shape
    fields = (suction[...], warmth[...], classes[...].astype(jnp.float32))
    for f, field in enumerate(fields):
        turned = field.T
        for b in range(2):
            out[:, 2 * f + b] = turned[b * SPAN : (b + 1) * SPAN].reshape(n, w, cells)
    surface = jnp.concatenate(
        [top[0:1, :SPAN], top[0:1, SPAN:], jnp.zeros((cells - 2, SPAN), jnp.float32)], axis=0
    )
    out[:, 6] = surface.T.reshape(n, w, cells)


def unpack_kernel(got, suction, warmth):
    n, _, w, cells = got.shape
    for f, out in enumerate((suction, warmth)):
        for b in range(2):
            out[:, b * SPAN : (b + 1) * SPAN] = got[:, 2 * f + b].reshape(n * w, cells).T


def solve(rows, steps, matrix, ratio, lead, value, update):
    c_prev = a_prev = d_prev = None
    for j in range(steps):
        above, main, below, source = matrix(j)
        if j == 0:
            r = 1.0 / main
            a_prev = above * r
            d_prev = source * r
        else:
            r = 1.0 / (main - above * c_prev)
            over = above * r
            a_prev = a_prev * over
            d_prev = source * r + d_prev * over
        c_prev = below * r
        ratio[j] = c_prev
        lead[j] = a_prev
        value[j] = d_prev
    last_c, last_a, last_d = c_prev, a_prev, d_prev
    p_first, a_first, d_first = ratio[steps - 2], lead[steps - 2], value[steps - 2]
    for j in range(steps - 3, -1, -1):
        c = ratio[j]
        p_first = c * p_first
        a_first = lead[j] + c * a_first
        d_first = value[j] + c * d_first
    g = 1.0 / (1.0 - last_c * shift_up(a_first, 1))
    up = last_c * shift_up(p_first, 1) * g
    down = last_a * g
    own = (last_d + last_c * shift_up(d_first, 1)) * g
    step = 1
    while step < PARTS:
        g = 1.0 / (1.0 - up * shift_up(down, step) - down * shift_down(up, step))
        own = (own + up * shift_up(own, step) + down * shift_down(own, step)) * g
        up = up * shift_up(up, step) * g
        down = down * shift_down(down, step) * g
        step *= 2
    over = shift_down(own, 1)
    x = own
    update(steps - 1, x)
    for j in range(steps - 2, -1, -1):
        x = ratio[j] * x + (lead[j] * over + value[j])
        update(j, x)


def step_kernel(
    n, w, got, couplings, k_sat, heat_cond, out,
    head, warm, perm, conduct, stored, energy, wet, melt, cond, water, heat, ratio, lead, value, load,
):
    kn, _, kw, cells = got.shape
    half = n * w
    width = 2 * half
    steps = cells // PARTS

    def take(field, target, change):
        for b in range(2):
            turned = got[:, 2 * field + b].reshape(half, cells).T
            for q in range(half // LANES):
                load[2 * b + q] = turned[:, q * LANES : (q + 1) * LANES]
        for j in range(steps):
            for q in range(width // LANES):
                change(j, slice(q * LANES, (q + 1) * LANES), load[q, pl.ds(j, PARTS, stride=steps), :])

    def take_head(j, lanes, v):
        head[j, :, lanes] = v

    def take_warm(j, lanes, v):
        warm[j, :, lanes] = v

    def take_class(j, lanes, v):
        k = jnp.full_like(v, k_sat[0])
        lam = jnp.full_like(v, heat_cond[0])
        for c in range(1, k_sat.shape[0]):
            here = v >= c
            k = jnp.where(here, k_sat[c], k)
            lam = jnp.where(here, heat_cond[c], lam)
        perm[j, :, lanes] = k
        conduct[j, :, lanes] = lam

    take(0, head, take_head)
    take(1, warm, take_warm)
    take(2, perm, take_class)
    surface = got[:, 6].reshape(half, cells).T[0:2]
    top = jnp.concatenate([surface[0:1], surface[1:2]], axis=1)

    pair_rows = couplings[...].astype(jnp.float32)
    lane_dev = lax.broadcasted_iota(jnp.int32, (couplings.shape[1], half), 1) // w
    pair_id = lax.broadcasted_iota(jnp.int32, (couplings.shape[1], half), 0)
    dev = lax.broadcasted_iota(jnp.int32, (PARTS, half), 1) // w
    chosen = []
    for s in range(1, PAIR_DEV + 1):
        upper_at = (pair_id == lane_dev * PAIR_DEV + s - 1).astype(jnp.float32)
        lower_at = (pair_id == (lane_dev - s) * PAIR_DEV + s - 1).astype(jnp.float32)
        upper = jnp.dot(pair_rows, upper_at, preferred_element_type=jnp.float32)[0:1]
        lower = jnp.dot(pair_rows, lower_at, preferred_element_type=jnp.float32)[1:2]
        upper = jnp.broadcast_to(upper, (PARTS, half)) > 0.5
        lower = jnp.broadcast_to(lower, (PARTS, half)) > 0.5
        scale = jnp.where(dev + s < n, 0.25, 0.0)
        chosen.append((upper, lower, scale))

    first_part = lax.broadcasted_iota(jnp.int32, (PARTS, width), 0) == 0
    last_part = lax.broadcasted_iota(jnp.int32, (PARTS, width), 0) == PARTS - 1

    for j in range(steps):
        h, t = head[j], warm[j]
        s0 = jax.nn.sigmoid(h)
        f0 = jax.nn.sigmoid(2.0 * t)
        m0 = 0.05 + 0.4 * s0
        wet[j] = s0
        stored[j] = s0
        energy[j] = (1.0 + 2.0 * m0) * t + 2.0 * m0 * f0

    def lateral(j, _):
        h, t, c = head[j], warm[j], cond[j]
        h0, h1 = h[:, :half], h[:, half:]
        t0, t1 = t[:, :half], t[:, half:]
        c0, c1 = c[:, :half], c[:, half:]
        zero = jnp.zeros((PARTS, half), jnp.float32)
        w0, w1, q0, q1 = zero, zero, zero, zero
        for s in range(1, PAIR_DEV + 1):
            upper, lower, scale = chosen[s - 1]
            back = half - s * w
            h_low = pltpu.roll(jnp.where(lower, h1, h0), back, axis=1)
            t_low = pltpu.roll(jnp.where(lower, t1, t0), back, axis=1)
            c_low = pltpu.roll(jnp.where(lower, c1, c0), back, axis=1)
            flow = (
                scale
                * (jnp.where(upper, c1, c0) + c_low)
                * (jnp.where(upper, h1, h0) - h_low + 0.5)
            )
            carried = flow * jnp.where(flow > 0.0, jnp.where(upper, t1, t0), t_low)
            flow_in = pltpu.roll(flow, s * w, axis=1)
            carried_in = pltpu.roll(carried, s * w, axis=1)
            w0 = w0 - jnp.where(upper, 0.0, flow) + jnp.where(lower, 0.0, flow_in)
            w1 = w1 - jnp.where(upper, flow, 0.0) + jnp.where(lower, flow_in, 0.0)
            q0 = q0 - jnp.where(upper, 0.0, carried) + jnp.where(lower, 0.0, carried_in)
            q1 = q1 - jnp.where(upper, carried, 0.0) + jnp.where(lower, carried_in, 0.0)
        water[j, :, :half] = w0
        water[j, :, half:] = w1
        heat[j, :, :half] = 2.0 * q0
        heat[j, :, half:] = 2.0 * q1
        return 0

    def iteration(_, carry):
        for j in range(steps):
            s, f = wet[j], jax.nn.sigmoid(2.0 * warm[j])
            melt[j] = f
            cond[j] = perm[j] * (f * s * s + 0.02)
        lax.fori_loop(0, steps, lateral, 0)

        def faces(field, potential):
            face_of, flux_of = [], []
            for j in range(steps):
                if j + 1 < steps:
                    c_next, h_next = field(j + 1), potential(j + 1)
                    face = 0.5 * (field(j) + c_next)
                else:
                    c_next, h_next = shift_up(field(0), 1), shift_up(potential(0), 1)
                    face = jnp.where(last_part, 0.0, 0.5 * (field(j) + c_next))
                face_of.append(face)
                flux_of.append(h_next - potential(j))
            return face_of, flux_of

        k_face, rise = faces(lambda j: cond[j], lambda j: head[j])
        k_top = jnp.where(first_part, 0.0, shift_down(k_face[-1], 1))
        q_face = [k * (1.0 - d) for k, d in zip(k_face, rise)]
        q_top = jnp.where(first_part, 0.0, shift_down(q_face[-1], 1))

        def water_matrix(j):
            above = k_top if j == 0 else k_face[j - 1]
            into = q_top if j == 0 else q_face[j - 1]
            s = wet[j]
            main = 0.8 * s * (1.0 - s) + 0.02 + above + k_face[j]
            source = water[j] + into - q_face[j] - 2.0 * (0.4 * (s - stored[j]))
            return above, main, k_face[j], source

        def water_done(j, x):
            h = head[j] + x
            head[j] = h
            wet[j] = jax.nn.sigmoid(h)

        solve(cells, steps, water_matrix, ratio, lead, value, water_done)

        l_face, drop = faces(lambda j: conduct[j] * (1.5 - 0.5 * melt[j]), lambda j: warm[j])
        l_top = jnp.where(first_part, 0.0, shift_down(l_face[-1], 1))
        g_face = [-l * d for l, d in zip(l_face, drop)]
        g_top = jnp.where(first_part, 0.0, shift_down(g_face[-1], 1))
        surface_lam = jnp.where(first_part, 2.0 * conduct[0] * (1.5 - 0.5 * melt[0]), 0.0)

        def heat_matrix(j):
            above = l_top if j == 0 else l_face[j - 1]
            into = g_top if j == 0 else g_face[j - 1]
            t, f = warm[j], melt[j]
            m = 0.05 + 0.4 * wet[j]
            now = (1.0 + 2.0 * m) * t + 2.0 * m * f
            main = 2.0 * (1.0 + 2.0 * m + 4.0 * m * f * (1.0 - f)) + above + l_face[j]
            source = heat[j] + into - g_face[j] - 2.0 * (now - energy[j])
            if j == 0:
                main = main + surface_lam
                source = source + surface_lam * (top - t)
            return above, main, l_face[j], source

        def heat_done(j, x):
            warm[j] = warm[j] + x

        solve(cells, steps, heat_matrix, ratio, lead, value, heat_done)
        return carry

    lax.fori_loop(0, ITERS, iteration, 0)

    for f, field in enumerate((head, warm)):
        for j in range(steps):
            for q in range(width // LANES):
                load[q, pl.ds(j, PARTS, stride=steps), :] = field[j, :, q * LANES : (q + 1) * LANES]
        for b in range(2):
            turned = jnp.concatenate([load[2 * b + q] for q in range(half // LANES)], axis=1).T
            out[:, 2 * f + b] = turned.reshape(kn, kw, cells)


def whole(memory=pltpu.VMEM):
    return pl.BlockSpec(memory_space=memory)


def exchange(chunks):
    return lax.all_to_all(chunks, "cols", split_axis=0, concat_axis=0, tiled=True)


def on_device(suction, warmth, classes, top, couplings, k_sat, heat_cond):
    n = lax.axis_size("cols")
    cells, width = suction.shape
    w = SPAN // n
    steps = cells // PARTS
    params = pltpu.CompilerParams(vmem_limit_bytes=VMEM_LIMIT)
    f32 = jnp.float32

    fit = w % 8 == 0
    kn, kw = (n, w) if fit else (SPAN // 8, 8)

    def to_chunks(a):
        if fit:
            return a
        fields = a.shape[1]
        return jnp.moveaxis(jnp.moveaxis(a, 1, 0).reshape(fields, n, w, cells), 0, 1)

    def from_chunks(a):
        if fit:
            return a
        fields = a.shape[1]
        return jnp.moveaxis(jnp.moveaxis(a, 1, 0).reshape(fields, kn, kw, cells), 0, 1)

    packed = pl.pallas_call(
        pack_kernel,
        out_shape=jax.ShapeDtypeStruct((kn, 7, kw, cells), f32),
        in_specs=[whole()] * 4,
        out_specs=whole(),
        compiler_params=params,
        name="pack",
    )(suction, warmth, classes, top.reshape(1, width))
    got = from_chunks(exchange(to_chunks(packed)))

    padded = jnp.zeros((8, couplings.shape[1]), couplings.dtype).at[:2].set(couplings)
    column = pltpu.VMEM((steps, PARTS, width), f32)
    solved = pl.pallas_call(
        functools.partial(step_kernel, n, w),
        out_shape=jax.ShapeDtypeStruct((kn, 4, kw, cells), f32),
        in_specs=[whole(), whole(), whole(pltpu.SMEM), whole(pltpu.SMEM)],
        out_specs=whole(),
        scratch_shapes=[column] * 14 + [pltpu.VMEM((width // LANES, cells, LANES), f32)],
        compiler_params=params,
        name="steps",
    )(got, padded, k_sat, heat_cond)
    back = from_chunks(exchange(to_chunks(solved)))
    return pl.pallas_call(
        unpack_kernel,
        out_shape=(jax.ShapeDtypeStruct((cells, width), f32),) * 2,
        in_specs=[whole()],
        out_specs=(whole(), whole()),
        compiler_params=params,
        name="unpack",
    )(back)


def solution(mesh):
    placed = (P(None, "cols"), P(None, "cols"), P(None, "cols"), P("cols"), P(), P(), P())
    return jax.shard_map(
        on_device,
        mesh=mesh,
        in_specs=placed,
        out_specs=(P(None, "cols"), P(None, "cols")),
        check_vma=False,
    )
```

```python
import functools

import jax
import jax.numpy as jnp
from jax import lax
from jax.experimental import pallas as pl
from jax.experimental.pallas import tpu as pltpu
from jax.sharding import PartitionSpec as P

SPAN = 256
ITERS = 2
PAIR_DEV = 4
LANES = 128
CHUNKS = SPAN // LANES
SUB = 8
ROWS = SUB // 2
TILES = LANES // ROWS
GROUPS = 2
WIDTH = 2 * LANES
VMEM_LIMIT = 48 * 1024 * 1024


def regroup(first, second):
    upper = lax.broadcasted_iota(jnp.int32, first.shape, 1) < ROWS
    return (
        jnp.where(upper, first, pltpu.roll(second, ROWS, axis=1)),
        jnp.where(upper, pltpu.roll(first, ROWS, axis=1), second),
    )


def pack_kernel(chunk, suction, warmth, classes, out, room, class_room, sems):
    cells = suction.shape[0]
    copies = []
    for f, field in enumerate((suction, warmth, classes)):
        for b in range(2):
            here = pl.ds(b * SPAN + chunk * LANES, LANES)
            target = class_room.at[b] if f == 2 else room.at[f, b]
            copy = pltpu.make_async_copy(field.at[:, here], target, sems.at[f, b])
            copy.start()
            copies.append(copy)
    for f in range(3):
        turned = []
        for b in range(2):
            copies[2 * f + b].wait()
            value = class_room[b].astype(jnp.float32) if f == 2 else room[f, b]
            turned.append(value.T.reshape(TILES // 2, SUB, cells))
        even, odd = regroup(*turned)
        for m in range(TILES // 2):
            out[2 * m, f] = even[m]
            out[2 * m + 1, f] = odd[m]


def columns_of(tiles, field, cells):
    even = jnp.stack([tiles[2 * m, field] for m in range(TILES // 2)])
    odd = jnp.stack([tiles[2 * m + 1, field] for m in range(TILES // 2)])
    return [v.reshape(LANES, cells).T for v in regroup(even, odd)]


def unpack_kernel(*refs):
    chunks, (suction, warmth) = refs[:CHUNKS], refs[CHUNKS:]
    cells = suction.shape[0]
    for f, out in enumerate((suction, warmth)):
        for c, chunk in enumerate(chunks):
            for b, value in enumerate(columns_of(chunk, f, cells)):
                out[:, b * SPAN + c * LANES : b * SPAN + (c + 1) * LANES] = value


def reciprocal(x):
    r = pl.reciprocal(x, approx=True)
    return r * (2.0 - x * r)


def sigmoid(x):
    return 0.5 + 0.5 * jnp.tanh(0.5 * x)


def following(value):
    first, second = value[:, :WIDTH], value[:, WIDTH:]
    return jnp.concatenate([second, pltpu.roll(first, SUB - 1, axis=0)], axis=1)


def preceding(value):
    first, second = value[:, :WIDTH], value[:, WIDTH:]
    return jnp.concatenate([pltpu.roll(second, 1, axis=0), first], axis=1)


def solve(steps, matrix, ratio, lead, value, update):
    c_prev = a_prev = d_prev = None
    for j in range(steps):
        above, main, below, source = matrix(j)
        if j == 0:
            r = reciprocal(main)
            a_prev = above * r
            d_prev = source * r
        else:
            r = reciprocal(main - above * c_prev)
            over = above * r
            a_prev = a_prev * over
            d_prev = source * r + d_prev * over
        c_prev = below * r
        ratio[j] = c_prev
        lead[j] = a_prev
        value[j] = d_prev
    last_c, last_a, last_d = c_prev, a_prev, d_prev
    p_first, a_first, d_first = ratio[steps - 2], lead[steps - 2], value[steps - 2]
    for j in range(steps - 3, -1, -1):
        c = ratio[j]
        p_first = c * p_first
        a_first = lead[j] + c * a_first
        d_first = value[j] + c * d_first
    g = reciprocal(1.0 - last_c * following(a_first))
    up = last_c * following(p_first) * g
    down = last_a * g
    own = (last_d + last_c * following(d_first)) * g
    step = 0
    while step < SUB:
        if step == 0:
            after, before = following, preceding
        else:
            after = functools.partial(pltpu.roll, shift=SUB - step, axis=0)
            before = functools.partial(pltpu.roll, shift=step, axis=0)
        g = reciprocal(1.0 - up * after(down) - down * before(up))
        own = (own + up * after(own) + down * before(own)) * g
        up = up * after(up) * g
        down = down * before(down) * g
        step = max(1, 2 * step)
    over = preceding(own)
    x = own
    update(steps - 1, x)
    for j in range(steps - 2, -1, -1):
        x = ratio[j] * x + (lead[j] * over + value[j])
        update(j, x)


def step_kernel(
    n, w, chunk, got, surface, couplings, k_sat, heat_cond, out,
    head, warm, perm, conduct, stored, energy, wet, melt, cond, water, heat, ratio, lead, value, load,
):
    cells = got.shape[-1]
    steps = cells // (SUB * GROUPS)
    stride = steps * GROUPS

    def lanes_of(g, b):
        return slice((g * 2 + b) * LANES, (g * 2 + b + 1) * LANES)

    def take(field, change):
        for b, turned in enumerate(columns_of(got, field, cells)):
            load[b] = turned
            for j in range(steps):
                for g in range(GROUPS):
                    change(j, lanes_of(g, b), load[b, pl.ds(g * steps + j, SUB, stride=stride), :])

    def take_head(j, lanes, v):
        head[j, :, lanes] = v

    def take_warm(j, lanes, v):
        warm[j, :, lanes] = v

    def take_class(j, lanes, v):
        k = jnp.full_like(v, k_sat[0])
        lam = jnp.full_like(v, heat_cond[0])
        for c in range(1, k_sat.shape[0]):
            here = v >= c
            k = jnp.where(here, k_sat[c], k)
            lam = jnp.where(here, heat_cond[c], lam)
        perm[j, :, lanes] = k
        conduct[j, :, lanes] = lam

    take(0, take_head)
    take(1, take_warm)
    take(2, take_class)

    me = lax.axis_index("cols")
    lane_dev = lax.broadcasted_iota(jnp.int32, (n, LANES), 1) // w
    row_dev = lax.broadcasted_iota(jnp.int32, (n, LANES), 0)
    tops = []
    for b in range(2):
        rows = surface[:, b * SPAN + chunk * LANES : b * SPAN + (chunk + 1) * LANES]
        rows = jnp.where(lane_dev == me, rows, 0.0)
        reach = w
        while reach < LANES:
            rows = rows + pltpu.roll(rows, reach, axis=1)
            reach *= 2
        tops.append(jnp.sum(jnp.where(row_dev == lane_dev, rows, 0.0), axis=0, keepdims=True))
    top = jnp.concatenate(tops * GROUPS, axis=1)

    pair_rows = couplings[...].astype(jnp.float32)
    pairs = couplings.shape[1]
    pair_dev = lax.broadcasted_iota(jnp.int32, (pairs, LANES), 1) // w
    pair_id = lax.broadcasted_iota(jnp.int32, (pairs, LANES), 0)
    dev = lax.broadcasted_iota(jnp.int32, (SUB, LANES), 1) // w
    chosen = []
    for s in range(1, PAIR_DEV + 1):
        upper_at = (pair_id == pair_dev * PAIR_DEV + s - 1).astype(jnp.float32)
        lower_at = (pair_id == (pair_dev - s) * PAIR_DEV + s - 1).astype(jnp.float32)
        upper = jnp.dot(pair_rows, upper_at, preferred_element_type=jnp.float32)[0:1]
        lower = jnp.dot(pair_rows, lower_at, preferred_element_type=jnp.float32)[1:2]
        upper = jnp.broadcast_to(upper, (SUB, LANES)) > 0.5
        lower = jnp.broadcast_to(lower, (SUB, LANES)) > 0.5
        scale = jnp.where(dev + s < n, 0.25, 0.0)
        chosen.append((upper, lower, scale))

    part = lax.broadcasted_iota(jnp.int32, (SUB, GROUPS * WIDTH), 0)
    group = lax.broadcasted_iota(jnp.int32, (SUB, GROUPS * WIDTH), 1) // WIDTH
    first_part = jnp.logical_and(part == 0, group == 0)
    last_part = jnp.logical_and(part == SUB - 1, group == GROUPS - 1)

    for j in range(steps):
        h, t = head[j], warm[j]
        s0 = sigmoid(h)
        f0 = sigmoid(2.0 * t)
        m0 = 0.05 + 0.4 * s0
        wet[j] = s0
        stored[j] = s0
        energy[j] = (1.0 + 2.0 * m0) * t + 2.0 * m0 * f0

    def lateral(j, _):
        for g in range(GROUPS):
            l0, l1 = lanes_of(g, 0), lanes_of(g, 1)
            h0, h1 = head[j, :, l0], head[j, :, l1]
            t0, t1 = warm[j, :, l0], warm[j, :, l1]
            c0, c1 = cond[j, :, l0], cond[j, :, l1]
            zero = jnp.zeros((SUB, LANES), jnp.float32)
            w0, w1, q0, q1 = zero, zero, zero, zero
            for s in range(1, PAIR_DEV + 1):
                upper, lower, scale = chosen[s - 1]
                back = LANES - s * w
                h_low = pltpu.roll(jnp.where(lower, h1, h0), back, axis=1)
                t_low = pltpu.roll(jnp.where(lower, t1, t0), back, axis=1)
                c_low = pltpu.roll(jnp.where(lower, c1, c0), back, axis=1)
                flow = (
                    scale
                    * (jnp.where(upper, c1, c0) + c_low)
                    * (jnp.where(upper, h1, h0) - h_low + 0.5)
                )
                carried = flow * jnp.where(flow > 0.0, jnp.where(upper, t1, t0), t_low)
                flow_in = pltpu.roll(flow, s * w, axis=1)
                carried_in = pltpu.roll(carried, s * w, axis=1)
                w0 = w0 - jnp.where(upper, 0.0, flow) + jnp.where(lower, 0.0, flow_in)
                w1 = w1 - jnp.where(upper, flow, 0.0) + jnp.where(lower, flow_in, 0.0)
                q0 = q0 - jnp.where(upper, 0.0, carried) + jnp.where(lower, 0.0, carried_in)
                q1 = q1 - jnp.where(upper, carried, 0.0) + jnp.where(lower, carried_in, 0.0)
            water[j, :, l0] = w0
            water[j, :, l1] = w1
            heat[j, :, l0] = 2.0 * q0
            heat[j, :, l1] = 2.0 * q1
        return 0

    def faces(field, potential):
        face_of, rise_of = [], []
        for j in range(steps):
            if j + 1 < steps:
                c_next, v_next = field(j + 1), potential(j + 1)
                face = 0.5 * (field(j) + c_next)
            else:
                c_next, v_next = following(field(0)), following(potential(0))
                face = jnp.where(last_part, 0.0, 0.5 * (field(j) + c_next))
            face_of.append(face)
            rise_of.append(v_next - potential(j))
        return face_of, rise_of

    def iteration(_, carry):
        for j in range(steps):
            s, f = wet[j], sigmoid(2.0 * warm[j])
            melt[j] = f
            cond[j] = perm[j] * (f * s * s + 0.02)
        lax.fori_loop(0, steps, lateral, 0)

        k_face, rise = faces(lambda j: cond[j], lambda j: head[j])
        k_top = jnp.where(first_part, 0.0, preceding(k_face[-1]))
        q_face = [k * (1.0 - d) for k, d in zip(k_face, rise)]
        q_top = jnp.where(first_part, 0.0, preceding(q_face[-1]))

        def water_matrix(j):
            above = k_top if j == 0 else k_face[j - 1]
            into = q_top if j == 0 else q_face[j - 1]
            s = wet[j]
            main = 0.8 * s * (1.0 - s) + 0.02 + above + k_face[j]
            source = water[j] + into - q_face[j] - 0.8 * (s - stored[j])
            return above, main, k_face[j], source

        def water_done(j, x):
            h = head[j] + x
            head[j] = h
            wet[j] = sigmoid(h)

        solve(steps, water_matrix, ratio, lead, value, water_done)

        l_face, rise = faces(lambda j: conduct[j] * (1.5 - 0.5 * melt[j]), lambda j: warm[j])
        l_top = jnp.where(first_part, 0.0, preceding(l_face[-1]))
        g_face = [-l * d for l, d in zip(l_face, rise)]
        g_top = jnp.where(first_part, 0.0, preceding(g_face[-1]))
        surface_lam = jnp.where(first_part, 2.0 * conduct[0] * (1.5 - 0.5 * melt[0]), 0.0)

        def heat_matrix(j):
            above = l_top if j == 0 else l_face[j - 1]
            into = g_top if j == 0 else g_face[j - 1]
            t, f = warm[j], melt[j]
            m = 0.05 + 0.4 * wet[j]
            now = (1.0 + 2.0 * m) * t + 2.0 * m * f
            main = 2.0 * (1.0 + 2.0 * m + 4.0 * m * f * (1.0 - f)) + above + l_face[j]
            source = heat[j] + into - g_face[j] - 2.0 * (now - energy[j])
            if j == 0:
                main = main + surface_lam
                source = source + surface_lam * (top - t)
            return above, main, l_face[j], source

        def heat_done(j, x):
            warm[j] = warm[j] + x

        solve(steps, heat_matrix, ratio, lead, value, heat_done)
        return carry

    lax.fori_loop(0, ITERS, iteration, 0)

    for f, field in enumerate((head, warm)):
        turned = []
        for b in range(2):
            for j in range(steps):
                for g in range(GROUPS):
                    load[b, pl.ds(g * steps + j, SUB, stride=stride), :] = field[j, :, lanes_of(g, b)]
            turned.append(load[b].T.reshape(TILES // 2, SUB, cells))
        even, odd = regroup(*turned)
        for m in range(TILES // 2):
            out[2 * m, f] = even[m]
            out[2 * m + 1, f] = odd[m]


def whole(memory=pltpu.VMEM):
    return pl.BlockSpec(memory_space=memory)


def exchange(tiles, n):
    w = LANES // n
    _, fields, _, cells = tiles.shape
    if w != ROWS:
        tiles = tiles.reshape(TILES, fields, 2, ROWS, cells).transpose(1, 2, 0, 3, 4)
        tiles = tiles.reshape(fields, 2, n, w, cells).transpose(2, 0, 1, 3, 4)
    tiles = lax.all_to_all(tiles, "cols", split_axis=0, concat_axis=0, tiled=True)
    if w != ROWS:
        tiles = tiles.transpose(1, 2, 0, 3, 4).reshape(fields, 2, TILES, ROWS, cells)
        tiles = tiles.transpose(2, 0, 1, 3, 4).reshape(TILES, fields, SUB, cells)
    return tiles


def on_device(suction, warmth, classes, top, couplings, k_sat, heat_cond):
    n = lax.axis_size("cols")
    cells, width = suction.shape
    w = LANES // n
    steps = cells // (SUB * GROUPS)
    params = pltpu.CompilerParams(vmem_limit_bytes=VMEM_LIMIT)
    f32 = jnp.float32

    surface = lax.all_gather(top, "cols")
    got = []
    for c in range(CHUNKS):
        packed = pl.pallas_call(
            functools.partial(pack_kernel, c),
            out_shape=jax.ShapeDtypeStruct((TILES, 3, SUB, cells), f32),
            in_specs=[whole(pltpu.HBM)] * 3,
            out_specs=whole(),
            scratch_shapes=[
                pltpu.VMEM((2, 2, cells, LANES), f32),
                pltpu.VMEM((2, cells, LANES), classes.dtype),
                pltpu.SemaphoreType.DMA((3, 2)),
            ],
            compiler_params=params,
            name="pack",
        )(suction, warmth, classes)
        got.append(exchange(packed, n))

    column = pltpu.VMEM((steps, SUB, GROUPS * WIDTH), f32)
    back = []
    for c in range(CHUNKS):
        solved = pl.pallas_call(
            functools.partial(step_kernel, n, w, c),
            out_shape=jax.ShapeDtypeStruct((TILES, 2, SUB, cells), f32),
            in_specs=[whole(), whole(), whole(), whole(pltpu.SMEM), whole(pltpu.SMEM)],
            out_specs=whole(),
            scratch_shapes=[column] * 14 + [pltpu.VMEM((2, cells, LANES), f32)],
            compiler_params=params,
            cost_estimate=pl.CostEstimate(flops=100_000_000, bytes_accessed=2_000_000, transcendentals=0),
            name="steps",
        )(got[c], surface, couplings, k_sat, heat_cond)
        back.append(exchange(solved, n))
    return pl.pallas_call(
        unpack_kernel,
        out_shape=(jax.ShapeDtypeStruct((cells, width), f32),) * 2,
        in_specs=[whole()] * CHUNKS,
        out_specs=(whole(), whole()),
        compiler_params=params,
        name="unpack",
    )(*back)


def solution(mesh):
    placed = (P(None, "cols"), P(None, "cols"), P(None, "cols"), P("cols"), P(), P(), P())
    return jax.shard_map(
        on_device,
        mesh=mesh,
        in_specs=placed,
        out_specs=(P(None, "cols"), P(None, "cols")),
        check_vma=False,
    )
```

```python
import functools

import jax
import jax.numpy as jnp
from jax import lax
from jax.experimental import pallas as pl
from jax.experimental.pallas import tpu as pltpu
from jax.sharding import PartitionSpec as P

SPAN = 256
ITERS = 2
PAIR_DEV = 4
LANES = 128
PARTS = 8
VMEM_LIMIT = 32 * 1024 * 1024
PACK_LIMIT = 60 * 1024 * 1024


def reciprocal(x):
    r = pl.reciprocal(x, approx=True)
    return r * (2.0 - x * r)


def sigmoid(x):
    return 0.5 + 0.5 * jnp.tanh(0.5 * x)


def shift_down(value, steps):
    return pltpu.roll(value, steps, axis=0)


def shift_up(value, steps):
    return pltpu.roll(value, PARTS - steps, axis=0)


def pack_kernel(suction, warmth, classes, top, out, room, class_room, sems):
    n, _, w, cells = out.shape
    copies = []
    for f, field in enumerate((suction, warmth, classes)):
        for b in range(2):
            target = class_room.at[b] if f == 2 else room.at[f, b]
            copies.append(
                pltpu.make_async_copy(field.at[:, pl.ds(b * SPAN, SPAN)], target, sems.at[f, b])
            )
            copies[-1].start()
    for f in range(3):
        for b in range(2):
            copies[2 * f + b].wait()
            value = class_room[b].astype(jnp.float32) if f == 2 else room[f, b]
            out[:, 2 * f + b] = value.T.reshape(n, w, cells)
    surface = jnp.concatenate(
        [top[0:1, :SPAN], top[0:1, SPAN:], jnp.zeros((cells - 2, SPAN), jnp.float32)], axis=0
    )
    out[:, 6] = surface.T.reshape(n, w, cells)


def unpack_kernel(got, suction, warmth):
    n, _, w, cells = got.shape
    for f, out in enumerate((suction, warmth)):
        for b in range(2):
            out[:, b * SPAN : (b + 1) * SPAN] = got[:, 2 * f + b].reshape(n * w, cells).T


def solve(rows, steps, matrix, ratio, lead, value, update):
    c_prev = a_prev = d_prev = None
    for j in range(steps):
        above, main, below, source = matrix(j)
        if j == 0:
            r = reciprocal(main)
            a_prev = above * r
            d_prev = source * r
        else:
            r = reciprocal(main - above * c_prev)
            over = above * r
            a_prev = a_prev * over
            d_prev = source * r + d_prev * over
        c_prev = below * r
        ratio[j] = c_prev
        lead[j] = a_prev
        value[j] = d_prev
    last_c, last_a, last_d = c_prev, a_prev, d_prev
    p_first, a_first, d_first = ratio[steps - 2], lead[steps - 2], value[steps - 2]
    for j in range(steps - 3, -1, -1):
        c = ratio[j]
        p_first = c * p_first
        a_first = lead[j] + c * a_first
        d_first = value[j] + c * d_first
    g = reciprocal(1.0 - last_c * shift_up(a_first, 1))
    up = last_c * shift_up(p_first, 1) * g
    down = last_a * g
    own = (last_d + last_c * shift_up(d_first, 1)) * g
    step = 1
    while step < PARTS:
        g = reciprocal(1.0 - up * shift_up(down, step) - down * shift_down(up, step))
        own = (own + up * shift_up(own, step) + down * shift_down(own, step)) * g
        up = up * shift_up(up, step) * g
        down = down * shift_down(down, step) * g
        step *= 2
    over = shift_down(own, 1)
    x = own
    update(steps - 1, x)
    for j in range(steps - 2, -1, -1):
        x = ratio[j] * x + (lead[j] * over + value[j])
        update(j, x)


def step_kernel(
    n, w, got, couplings, k_sat, heat_cond, out,
    head, warm, perm, conduct, stored, energy, wet, melt, cond, water, heat, ratio, lead, value, load,
):
    kn, _, kw, cells = got.shape
    half = n * w
    width = 2 * half
    steps = cells // PARTS

    def take(field, target, change):
        for b in range(2):
            turned = got[:, 2 * field + b].reshape(half, cells).T
            for q in range(half // LANES):
                load[2 * b + q] = turned[:, q * LANES : (q + 1) * LANES]
        for j in range(steps):
            for q in range(width // LANES):
                change(j, slice(q * LANES, (q + 1) * LANES), load[q, pl.ds(j, PARTS, stride=steps), :])

    def take_head(j, lanes, v):
        head[j, :, lanes] = v

    def take_warm(j, lanes, v):
        warm[j, :, lanes] = v

    def take_class(j, lanes, v):
        k = jnp.full_like(v, k_sat[0])
        lam = jnp.full_like(v, heat_cond[0])
        for c in range(1, k_sat.shape[0]):
            here = v >= c
            k = jnp.where(here, k_sat[c], k)
            lam = jnp.where(here, heat_cond[c], lam)
        perm[j, :, lanes] = k
        conduct[j, :, lanes] = lam

    take(0, head, take_head)
    take(1, warm, take_warm)
    take(2, perm, take_class)
    surface = got[:, 6].reshape(half, cells).T[0:2]
    top = jnp.concatenate([surface[0:1], surface[1:2]], axis=1)

    pair_rows = couplings[...].astype(jnp.float32)
    lane_dev = lax.broadcasted_iota(jnp.int32, (couplings.shape[1], half), 1) // w
    pair_id = lax.broadcasted_iota(jnp.int32, (couplings.shape[1], half), 0)
    dev = lax.broadcasted_iota(jnp.int32, (PARTS, half), 1) // w
    chosen = []
    for s in range(1, PAIR_DEV + 1):
        upper_at = (pair_id == lane_dev * PAIR_DEV + s - 1).astype(jnp.float32)
        lower_at = (pair_id == (lane_dev - s) * PAIR_DEV + s - 1).astype(jnp.float32)
        upper = jnp.dot(pair_rows, upper_at, preferred_element_type=jnp.float32)[0:1]
        lower = jnp.dot(pair_rows, lower_at, preferred_element_type=jnp.float32)[1:2]
        upper = jnp.broadcast_to(upper, (PARTS, half)) > 0.5
        lower = jnp.broadcast_to(lower, (PARTS, half)) > 0.5
        scale = jnp.where(dev + s < n, 0.25, 0.0)
        chosen.append((upper, lower, scale))

    first_part = lax.broadcasted_iota(jnp.int32, (PARTS, width), 0) == 0
    last_part = lax.broadcasted_iota(jnp.int32, (PARTS, width), 0) == PARTS - 1

    for j in range(steps):
        h, t = head[j], warm[j]
        s0 = sigmoid(h)
        f0 = sigmoid(2.0 * t)
        m0 = 0.05 + 0.4 * s0
        wet[j] = s0
        stored[j] = s0
        energy[j] = (1.0 + 2.0 * m0) * t + 2.0 * m0 * f0

    def lateral(j, _):
        h, t, c = head[j], warm[j], cond[j]
        h0, h1 = h[:, :half], h[:, half:]
        t0, t1 = t[:, :half], t[:, half:]
        c0, c1 = c[:, :half], c[:, half:]
        zero = jnp.zeros((PARTS, half), jnp.float32)
        w0, w1, q0, q1 = zero, zero, zero, zero
        for s in range(1, PAIR_DEV + 1):
            upper, lower, scale = chosen[s - 1]
            back = half - s * w
            h_low = pltpu.roll(jnp.where(lower, h1, h0), back, axis=1)
            t_low = pltpu.roll(jnp.where(lower, t1, t0), back, axis=1)
            c_low = pltpu.roll(jnp.where(lower, c1, c0), back, axis=1)
            flow = (
                scale
                * (jnp.where(upper, c1, c0) + c_low)
                * (jnp.where(upper, h1, h0) - h_low + 0.5)
            )
            carried = flow * jnp.where(flow > 0.0, jnp.where(upper, t1, t0), t_low)
            flow_in = pltpu.roll(flow, s * w, axis=1)
            carried_in = pltpu.roll(carried, s * w, axis=1)
            w0 = w0 - jnp.where(upper, 0.0, flow) + jnp.where(lower, 0.0, flow_in)
            w1 = w1 - jnp.where(upper, flow, 0.0) + jnp.where(lower, flow_in, 0.0)
            q0 = q0 - jnp.where(upper, 0.0, carried) + jnp.where(lower, 0.0, carried_in)
            q1 = q1 - jnp.where(upper, carried, 0.0) + jnp.where(lower, carried_in, 0.0)
        water[j, :, :half] = w0
        water[j, :, half:] = w1
        heat[j, :, :half] = 2.0 * q0
        heat[j, :, half:] = 2.0 * q1
        return 0

    def iteration(_, carry):
        for j in range(steps):
            s, f = wet[j], sigmoid(2.0 * warm[j])
            melt[j] = f
            cond[j] = perm[j] * (f * s * s + 0.02)
        lax.fori_loop(0, steps, lateral, 0)

        def faces(field, potential):
            face_of, flux_of = [], []
            for j in range(steps):
                if j + 1 < steps:
                    c_next, h_next = field(j + 1), potential(j + 1)
                    face = 0.5 * (field(j) + c_next)
                else:
                    c_next, h_next = shift_up(field(0), 1), shift_up(potential(0), 1)
                    face = jnp.where(last_part, 0.0, 0.5 * (field(j) + c_next))
                face_of.append(face)
                flux_of.append(h_next - potential(j))
            return face_of, flux_of

        k_face, rise = faces(lambda j: cond[j], lambda j: head[j])
        k_top = jnp.where(first_part, 0.0, shift_down(k_face[-1], 1))
        q_face = [k * (1.0 - d) for k, d in zip(k_face, rise)]
        q_top = jnp.where(first_part, 0.0, shift_down(q_face[-1], 1))

        def water_matrix(j):
            above = k_top if j == 0 else k_face[j - 1]
            into = q_top if j == 0 else q_face[j - 1]
            s = wet[j]
            main = 0.8 * s * (1.0 - s) + 0.02 + above + k_face[j]
            source = water[j] + into - q_face[j] - 2.0 * (0.4 * (s - stored[j]))
            return above, main, k_face[j], source

        def water_done(j, x):
            h = head[j] + x
            head[j] = h
            wet[j] = sigmoid(h)

        solve(cells, steps, water_matrix, ratio, lead, value, water_done)

        l_face, drop = faces(lambda j: conduct[j] * (1.5 - 0.5 * melt[j]), lambda j: warm[j])
        l_top = jnp.where(first_part, 0.0, shift_down(l_face[-1], 1))
        g_face = [-l * d for l, d in zip(l_face, drop)]
        g_top = jnp.where(first_part, 0.0, shift_down(g_face[-1], 1))
        surface_lam = jnp.where(first_part, 2.0 * conduct[0] * (1.5 - 0.5 * melt[0]), 0.0)

        def heat_matrix(j):
            above = l_top if j == 0 else l_face[j - 1]
            into = g_top if j == 0 else g_face[j - 1]
            t, f = warm[j], melt[j]
            m = 0.05 + 0.4 * wet[j]
            now = (1.0 + 2.0 * m) * t + 2.0 * m * f
            main = 2.0 * (1.0 + 2.0 * m + 4.0 * m * f * (1.0 - f)) + above + l_face[j]
            source = heat[j] + into - g_face[j] - 2.0 * (now - energy[j])
            if j == 0:
                main = main + surface_lam
                source = source + surface_lam * (top - t)
            return above, main, l_face[j], source

        def heat_done(j, x):
            warm[j] = warm[j] + x

        solve(cells, steps, heat_matrix, ratio, lead, value, heat_done)
        return carry

    lax.fori_loop(0, ITERS, iteration, 0)

    for f, field in enumerate((head, warm)):
        for j in range(steps):
            for q in range(width // LANES):
                load[q, pl.ds(j, PARTS, stride=steps), :] = field[j, :, q * LANES : (q + 1) * LANES]
        for b in range(2):
            turned = jnp.concatenate([load[2 * b + q] for q in range(half // LANES)], axis=1).T
            out[:, 2 * f + b] = turned.reshape(kn, kw, cells)


def whole(memory=pltpu.VMEM):
    return pl.BlockSpec(memory_space=memory)


def exchange(chunks):
    return lax.all_to_all(chunks, "cols", split_axis=0, concat_axis=0, tiled=True)


def on_device(suction, warmth, classes, top, couplings, k_sat, heat_cond):
    n = lax.axis_size("cols")
    cells, width = suction.shape
    w = SPAN // n
    steps = cells // PARTS
    params = pltpu.CompilerParams(vmem_limit_bytes=VMEM_LIMIT)
    f32 = jnp.float32

    fit = w % 8 == 0
    kn, kw = (n, w) if fit else (SPAN // 8, 8)

    def to_chunks(a):
        if fit:
            return a
        fields = a.shape[1]
        return jnp.moveaxis(jnp.moveaxis(a, 1, 0).reshape(fields, n, w, cells), 0, 1)

    def from_chunks(a):
        if fit:
            return a
        fields = a.shape[1]
        return jnp.moveaxis(jnp.moveaxis(a, 1, 0).reshape(fields, kn, kw, cells), 0, 1)

    packed = pl.pallas_call(
        pack_kernel,
        out_shape=jax.ShapeDtypeStruct((kn, 7, kw, cells), f32),
        in_specs=[whole(pltpu.HBM)] * 3 + [whole()],
        out_specs=whole(),
        scratch_shapes=[
            pltpu.VMEM((2, 2, cells, SPAN), f32),
            pltpu.VMEM((2, cells, SPAN), classes.dtype),
            pltpu.SemaphoreType.DMA((3, 2)),
        ],
        compiler_params=pltpu.CompilerParams(vmem_limit_bytes=PACK_LIMIT),
        name="pack",
    )(suction, warmth, classes, top.reshape(1, width))
    got = from_chunks(exchange(to_chunks(packed)))

    padded = jnp.zeros((8, couplings.shape[1]), couplings.dtype).at[:2].set(couplings)
    column = pltpu.VMEM((steps, PARTS, width), f32)
    solved = pl.pallas_call(
        functools.partial(step_kernel, n, w),
        out_shape=jax.ShapeDtypeStruct((kn, 4, kw, cells), f32),
        in_specs=[whole(), whole(), whole(pltpu.SMEM), whole(pltpu.SMEM)],
        out_specs=whole(),
        scratch_shapes=[column] * 14 + [pltpu.VMEM((width // LANES, cells, LANES), f32)],
        compiler_params=params,
        name="steps",
    )(got, padded, k_sat, heat_cond)
    back = from_chunks(exchange(to_chunks(solved)))
    return pl.pallas_call(
        unpack_kernel,
        out_shape=(jax.ShapeDtypeStruct((cells, width), f32),) * 2,
        in_specs=[whole()],
        out_specs=(whole(), whole()),
        compiler_params=params,
        name="unpack",
    )(back)


def solution(mesh):
    placed = (P(None, "cols"), P(None, "cols"), P(None, "cols"), P("cols"), P(), P(), P())
    return jax.shard_map(
        on_device,
        mesh=mesh,
        in_specs=placed,
        out_specs=(P(None, "cols"), P(None, "cols")),
        check_vma=False,
    )
```

```python
import functools

import jax
import jax.numpy as jnp
from jax import lax
from jax.experimental import pallas as pl
from jax.experimental.pallas import tpu as pltpu
from jax.sharding import PartitionSpec as P

SPAN = 256
ITERS = 2
PAIR_DEV = 4
LANES = 128
SUB = 8
GROUPS = 2
WIDTH = 2 * SPAN
VMEM_LIMIT = 32 * 1024 * 1024
PACK_LIMIT = 60 * 1024 * 1024


def pack_kernel(suction, warmth, classes, top, out, room, class_room, turned, in_sems, out_sems):
    n, _, w, cells = turned.shape
    tiles = SPAN // LANES
    part = LANES // w
    into, sent = [], []
    for f, field in enumerate((suction, warmth, classes)):
        for q in range(2 * tiles):
            target = class_room.at[q] if f == 2 else room.at[f, q]
            into.append(
                pltpu.make_async_copy(field.at[:, pl.ds(q * LANES, LANES)], target, in_sems.at[f, q])
            )
            into[-1].start()

    def send(slot):
        sent.append(pltpu.make_async_copy(turned.at[:, slot], out.at[:, slot], out_sems.at[slot]))
        sent[-1].start()

    surface = jnp.concatenate(
        [top[0:1, :SPAN], top[0:1, SPAN:], jnp.zeros((cells - 2, SPAN), jnp.float32)], axis=0
    )
    turned[:, 6] = surface.T.reshape(n, w, cells)
    send(6)
    for f in range(3):
        for b in range(2):
            for i in range(tiles):
                q = b * tiles + i
                into[2 * tiles * f + q].wait()
                value = class_room[q].astype(jnp.float32) if f == 2 else room[f, q]
                turned[i * part : (i + 1) * part, 2 * f + b] = value.T.reshape(part, w, cells)
            send(2 * f + b)
    for copy in sent:
        copy.wait()


def unpack_kernel(got, suction, warmth, room, sems):
    n, _, w, cells = got.shape
    sent = []
    for f, out in enumerate((suction, warmth)):
        for b in range(2):
            here = pl.ds(b * SPAN, SPAN)
            room[f, b] = got[:, 2 * f + b].reshape(n * w, cells).T
            sent.append(pltpu.make_async_copy(room.at[f, b], out.at[:, here], sems.at[f, b]))
            sent[-1].start()
    for copy in sent:
        copy.wait()


def reciprocal(x):
    r = pl.reciprocal(x, approx=True)
    return r * (2.0 - x * r)


def sigmoid(x):
    return 0.5 + 0.5 * jnp.tanh(0.5 * x)


def following(value):
    first, second = value[:, :WIDTH], value[:, WIDTH:]
    return jnp.concatenate([second, pltpu.roll(first, SUB - 1, axis=0)], axis=1)


def preceding(value):
    first, second = value[:, :WIDTH], value[:, WIDTH:]
    return jnp.concatenate([pltpu.roll(second, 1, axis=0), first], axis=1)


def solve(steps, matrix, ratio, lead, value, update):
    c_prev = a_prev = d_prev = None
    for j in range(steps):
        above, main, below, source = matrix(j)
        if j == 0:
            r = reciprocal(main)
            a_prev = above * r
            d_prev = source * r
        else:
            r = reciprocal(main - above * c_prev)
            over = above * r
            a_prev = a_prev * over
            d_prev = source * r + d_prev * over
        c_prev = below * r
        ratio[j] = c_prev
        lead[j] = a_prev
        value[j] = d_prev
    last_c, last_a, last_d = c_prev, a_prev, d_prev
    p_first, a_first, d_first = ratio[steps - 2], lead[steps - 2], value[steps - 2]
    for j in range(steps - 3, -1, -1):
        c = ratio[j]
        p_first = c * p_first
        a_first = lead[j] + c * a_first
        d_first = value[j] + c * d_first
    g = reciprocal(1.0 - last_c * following(a_first))
    up = last_c * following(p_first) * g
    down = last_a * g
    own = (last_d + last_c * following(d_first)) * g
    step = 0
    while step < SUB:
        if step == 0:
            after, before = following, preceding
        else:
            after = functools.partial(pltpu.roll, shift=SUB - step, axis=0)
            before = functools.partial(pltpu.roll, shift=step, axis=0)
        g = reciprocal(1.0 - up * after(down) - down * before(up))
        own = (own + up * after(own) + down * before(own)) * g
        up = up * after(up) * g
        down = down * before(down) * g
        step = max(1, 2 * step)
    over = preceding(own)
    x = own
    update(steps - 1, x)
    for j in range(steps - 2, -1, -1):
        x = ratio[j] * x + (lead[j] * over + value[j])
        update(j, x)


def step_kernel(
    n, w, got, couplings, k_sat, heat_cond, out,
    head, warm, perm, conduct, stored, energy, wet, melt, cond, water, heat, ratio, lead, value, load,
):
    kn, _, kw, cells = got.shape
    steps = cells // (SUB * GROUPS)
    stride = steps * GROUPS

    def lanes_of(g, b):
        return slice((g * 2 + b) * SPAN, (g * 2 + b + 1) * SPAN)

    def take(field, change):
        for b in range(2):
            turned = got[:, 2 * field + b].reshape(SPAN, cells).T
            for q in range(SPAN // LANES):
                load[q] = turned[:, q * LANES : (q + 1) * LANES]
            for j in range(steps):
                for g in range(GROUPS):
                    for q in range(SPAN // LANES):
                        here = (g * 2 + b) * SPAN + q * LANES
                        value = load[q, pl.ds(g * steps + j, SUB, stride=stride), :]
                        change(j, slice(here, here + LANES), value)

    def take_head(j, lanes, v):
        head[j, :, lanes] = v

    def take_warm(j, lanes, v):
        warm[j, :, lanes] = v

    def take_class(j, lanes, v):
        k = jnp.full_like(v, k_sat[0])
        lam = jnp.full_like(v, heat_cond[0])
        for c in range(1, k_sat.shape[0]):
            here = v >= c
            k = jnp.where(here, k_sat[c], k)
            lam = jnp.where(here, heat_cond[c], lam)
        perm[j, :, lanes] = k
        conduct[j, :, lanes] = lam

    take(0, take_head)
    take(1, take_warm)
    take(2, take_class)

    surface = got[:, 6].reshape(SPAN, cells).T[0:2]
    top = jnp.concatenate([surface[0:1], surface[1:2]] * GROUPS, axis=1)

    pair_rows = couplings[...].astype(jnp.float32)
    pairs = couplings.shape[1]
    pair_dev = lax.broadcasted_iota(jnp.int32, (pairs, SPAN), 1) // w
    pair_id = lax.broadcasted_iota(jnp.int32, (pairs, SPAN), 0)
    dev = lax.broadcasted_iota(jnp.int32, (SUB, SPAN), 1) // w
    chosen = []
    for s in range(1, PAIR_DEV + 1):
        upper_at = (pair_id == pair_dev * PAIR_DEV + s - 1).astype(jnp.float32)
        lower_at = (pair_id == (pair_dev - s) * PAIR_DEV + s - 1).astype(jnp.float32)
        upper = jnp.dot(pair_rows, upper_at, preferred_element_type=jnp.float32)[0:1]
        lower = jnp.dot(pair_rows, lower_at, preferred_element_type=jnp.float32)[1:2]
        upper = jnp.broadcast_to(upper, (SUB, SPAN)) > 0.5
        lower = jnp.broadcast_to(lower, (SUB, SPAN)) > 0.5
        scale = jnp.where(dev + s < n, 0.25, 0.0)
        chosen.append((upper, lower, scale))

    part = lax.broadcasted_iota(jnp.int32, (SUB, GROUPS * WIDTH), 0)
    group = lax.broadcasted_iota(jnp.int32, (SUB, GROUPS * WIDTH), 1) // WIDTH
    first_part = jnp.logical_and(part == 0, group == 0)
    last_part = jnp.logical_and(part == SUB - 1, group == GROUPS - 1)

    for j in range(steps):
        h, t = head[j], warm[j]
        s0 = sigmoid(h)
        f0 = sigmoid(2.0 * t)
        m0 = 0.05 + 0.4 * s0
        wet[j] = s0
        stored[j] = s0
        energy[j] = (1.0 + 2.0 * m0) * t + 2.0 * m0 * f0

    def lateral(j):
        for g in range(GROUPS):
            l0, l1 = lanes_of(g, 0), lanes_of(g, 1)
            h0, h1 = head[j, :, l0], head[j, :, l1]
            t0, t1 = warm[j, :, l0], warm[j, :, l1]
            c0, c1 = cond[j, :, l0], cond[j, :, l1]
            water_all = water_1 = heat_all = heat_1 = None
            for s in range(1, PAIR_DEV + 1):
                upper, lower, scale = chosen[s - 1]
                back = SPAN - s * w
                h_low = pltpu.roll(jnp.where(lower, h1, h0), back, axis=1)
                t_low = pltpu.roll(jnp.where(lower, t1, t0), back, axis=1)
                c_low = pltpu.roll(jnp.where(lower, c1, c0), back, axis=1)
                flow = (
                    scale
                    * (jnp.where(upper, c1, c0) + c_low)
                    * (jnp.where(upper, h1, h0) - h_low + 0.5)
                )
                carried = flow * jnp.where(flow > 0.0, jnp.where(upper, t1, t0), t_low)
                flow_in = pltpu.roll(flow, s * w, axis=1)
                carried_in = pltpu.roll(carried, s * w, axis=1)
                net = flow_in - flow
                net_1 = jnp.where(lower, flow_in, 0.0) - jnp.where(upper, flow, 0.0)
                brought = carried_in - carried
                brought_1 = jnp.where(lower, carried_in, 0.0) - jnp.where(upper, carried, 0.0)
                if s == 1:
                    water_all, water_1, heat_all, heat_1 = net, net_1, brought, brought_1
                else:
                    water_all, water_1 = water_all + net, water_1 + net_1
                    heat_all, heat_1 = heat_all + brought, heat_1 + brought_1
            water[j, :, l0] = water_all - water_1
            water[j, :, l1] = water_1
            heat[j, :, l0] = 2.0 * (heat_all - heat_1)
            heat[j, :, l1] = 2.0 * heat_1

    def faces(field, potential):
        face_of, rise_of = [], []
        for j in range(steps):
            if j + 1 < steps:
                c_next, v_next = field(j + 1), potential(j + 1)
                face = 0.5 * (field(j) + c_next)
            else:
                c_next, v_next = following(field(0)), following(potential(0))
                face = jnp.where(last_part, 0.0, 0.5 * (field(j) + c_next))
            face_of.append(face)
            rise_of.append(v_next - potential(j))
        return face_of, rise_of

    def iteration(_, carry):
        for j in range(steps):
            s, f = wet[j], sigmoid(2.0 * warm[j])
            melt[j] = f
            cond[j] = perm[j] * (f * s * s + 0.02)
        for j in range(steps):
            lateral(j)

        k_face, rise = faces(lambda j: cond[j], lambda j: head[j])
        k_top = jnp.where(first_part, 0.0, preceding(k_face[-1]))
        q_face = [k * (1.0 - d) for k, d in zip(k_face, rise)]
        q_top = jnp.where(first_part, 0.0, preceding(q_face[-1]))

        def water_matrix(j):
            above = k_top if j == 0 else k_face[j - 1]
            into = q_top if j == 0 else q_face[j - 1]
            s = wet[j]
            main = 0.8 * s * (1.0 - s) + 0.02 + above + k_face[j]
            source = water[j] + into - q_face[j] - 0.8 * (s - stored[j])
            return above, main, k_face[j], source

        def water_done(j, x):
            h = head[j] + x
            head[j] = h
            wet[j] = sigmoid(h)

        solve(steps, water_matrix, ratio, lead, value, water_done)

        l_face, rise = faces(lambda j: conduct[j] * (1.5 - 0.5 * melt[j]), lambda j: warm[j])
        l_top = jnp.where(first_part, 0.0, preceding(l_face[-1]))
        g_face = [-l * d for l, d in zip(l_face, rise)]
        g_top = jnp.where(first_part, 0.0, preceding(g_face[-1]))
        surface_lam = jnp.where(first_part, 2.0 * conduct[0] * (1.5 - 0.5 * melt[0]), 0.0)

        def heat_matrix(j):
            above = l_top if j == 0 else l_face[j - 1]
            into = g_top if j == 0 else g_face[j - 1]
            t, f = warm[j], melt[j]
            m = 0.05 + 0.4 * wet[j]
            now = (1.0 + 2.0 * m) * t + 2.0 * m * f
            main = 2.0 * (1.0 + 2.0 * m + 4.0 * m * f * (1.0 - f)) + above + l_face[j]
            source = heat[j] + into - g_face[j] - 2.0 * (now - energy[j])
            if j == 0:
                main = main + surface_lam
                source = source + surface_lam * (top - t)
            return above, main, l_face[j], source

        def heat_done(j, x):
            warm[j] = warm[j] + x

        solve(steps, heat_matrix, ratio, lead, value, heat_done)
        return carry

    lax.fori_loop(0, ITERS, iteration, 0)

    for f, field in enumerate((head, warm)):
        for b in range(2):
            for j in range(steps):
                for g in range(GROUPS):
                    for q in range(SPAN // LANES):
                        here = (g * 2 + b) * SPAN + q * LANES
                        load[q, pl.ds(g * steps + j, SUB, stride=stride), :] = field[j, :, here : here + LANES]
            turned = jnp.concatenate([load[q] for q in range(SPAN // LANES)], axis=1).T
            out[:, 2 * f + b] = turned.reshape(kn, kw, cells)


def whole(memory=pltpu.VMEM):
    return pl.BlockSpec(memory_space=memory)


def exchange(chunks):
    return lax.all_to_all(chunks, "cols", split_axis=0, concat_axis=0, tiled=True)


def on_device(suction, warmth, classes, top, couplings, k_sat, heat_cond):
    n = lax.axis_size("cols")
    cells, width = suction.shape
    w = SPAN // n
    steps = cells // (SUB * GROUPS)
    params = pltpu.CompilerParams(vmem_limit_bytes=VMEM_LIMIT)
    f32 = jnp.float32

    fit = w % 8 == 0
    kn, kw = (n, w) if fit else (SPAN // 8, 8)

    def to_chunks(a):
        if fit:
            return a
        fields = a.shape[1]
        return jnp.moveaxis(jnp.moveaxis(a, 1, 0).reshape(fields, n, w, cells), 0, 1)

    def from_chunks(a):
        if fit:
            return a
        fields = a.shape[1]
        return jnp.moveaxis(jnp.moveaxis(a, 1, 0).reshape(fields, kn, kw, cells), 0, 1)

    packed = pl.pallas_call(
        pack_kernel,
        out_shape=jax.ShapeDtypeStruct((kn, 7, kw, cells), f32),
        in_specs=[whole(pltpu.HBM)] * 3 + [whole()],
        out_specs=whole(pltpu.HBM),
        scratch_shapes=[
            pltpu.VMEM((2, width // LANES, cells, LANES), f32),
            pltpu.VMEM((width // LANES, cells, LANES), classes.dtype),
            pltpu.VMEM((kn, 7, kw, cells), f32),
            pltpu.SemaphoreType.DMA((3, width // LANES)),
            pltpu.SemaphoreType.DMA((7,)),
        ],
        compiler_params=pltpu.CompilerParams(vmem_limit_bytes=PACK_LIMIT),
        name="pack",
    )(suction, warmth, classes, top.reshape(1, width))
    got = from_chunks(exchange(to_chunks(packed)))

    column = pltpu.VMEM((steps, SUB, GROUPS * width), f32)
    solved = pl.pallas_call(
        functools.partial(step_kernel, n, w),
        out_shape=jax.ShapeDtypeStruct((kn, 4, kw, cells), f32),
        in_specs=[whole(), whole(), whole(pltpu.SMEM), whole(pltpu.SMEM)],
        out_specs=whole(),
        scratch_shapes=[column] * 14 + [pltpu.VMEM((SPAN // LANES, cells, LANES), f32)],
        compiler_params=params,
        name="steps",
    )(got, couplings, k_sat, heat_cond)
    back = from_chunks(exchange(to_chunks(solved)))
    return pl.pallas_call(
        unpack_kernel,
        out_shape=(jax.ShapeDtypeStruct((cells, width), f32),) * 2,
        in_specs=[whole()],
        out_specs=(whole(pltpu.HBM), whole(pltpu.HBM)),
        scratch_shapes=[pltpu.VMEM((2, 2, cells, SPAN), f32), pltpu.SemaphoreType.DMA((2, 2))],
        compiler_params=params,
        name="unpack",
    )(back)


def solution(mesh):
    placed = (P(None, "cols"), P(None, "cols"), P(None, "cols"), P("cols"), P(), P(), P())
    return jax.shard_map(
        on_device,
        mesh=mesh,
        in_specs=placed,
        out_specs=(P(None, "cols"), P(None, "cols")),
        check_vma=False,
    )
```

```python
import functools

import jax
import jax.numpy as jnp
from jax import lax
from jax.experimental import pallas as pl
from jax.experimental.pallas import tpu as pltpu
from jax.sharding import PartitionSpec as P

SPAN = 256
PAIR_DEV = 4
LANES = 128
CHUNKS = SPAN // LANES
TEAM = 16
OWN = LANES // TEAM
SUB = 8
GROUPS = 2
WIDTH = 2 * LANES
ALL = GROUPS * WIDTH
EDGE = PAIR_DEV * OWN
VMEM_LIMIT = 32 * 1024 * 1024
PACK_LIMIT = 60 * 1024 * 1024
DISTANCES = range(1, PAIR_DEV + 1)
F32 = jnp.float32


def cut_count(n):
    return min(n // TEAM - 1, 2)


def place(cut):
    team = lax.axis_index("cols") // TEAM
    return team, lax.rem(team, 2) == cut


def sign_of(cut):
    return jnp.where(place(cut)[1], 1.0, -1.0).astype(F32)


def reciprocal(x):
    r = pl.reciprocal(x, approx=True)
    return r * (2.0 - x * r)


def sigmoid(x):
    return 0.5 + 0.5 * jnp.tanh(0.5 * x)


def passage(h, t, k):
    s = sigmoid(h)
    return k * (sigmoid(2.0 * t) * s * s + 0.02)


def lanes_of(g, b):
    return slice((g * 2 + b) * LANES, (g * 2 + b + 1) * LANES)


def following(value):
    first, second = value[:, :WIDTH], value[:, WIDTH:]
    return jnp.concatenate([second, pltpu.roll(first, SUB - 1, axis=0)], axis=1)


def preceding(value):
    first, second = value[:, :WIDTH], value[:, WIDTH:]
    return jnp.concatenate([pltpu.roll(second, 1, axis=0), first], axis=1)


def solve(steps, matrix, ratio, lead, value, update):
    c_prev = a_prev = d_prev = None
    for j in range(steps):
        above, main, below, source = matrix(j)
        if j == 0:
            r = reciprocal(main)
            a_prev = above * r
            d_prev = source * r
        else:
            r = reciprocal(main - above * c_prev)
            over = above * r
            a_prev = a_prev * over
            d_prev = source * r + d_prev * over
        c_prev = below * r
        ratio[j] = c_prev
        lead[j] = a_prev
        value[j] = d_prev
    last_c, last_a, last_d = c_prev, a_prev, d_prev
    p_first, a_first, d_first = ratio[steps - 2], lead[steps - 2], value[steps - 2]
    for j in range(steps - 3, -1, -1):
        c = ratio[j]
        p_first = c * p_first
        a_first = lead[j] + c * a_first
        d_first = value[j] + c * d_first
    g = reciprocal(1.0 - last_c * following(a_first))
    up = last_c * following(p_first) * g
    down = last_a * g
    own = (last_d + last_c * following(d_first)) * g
    step = 0
    while step < SUB:
        if step == 0:
            after, before = following, preceding
        else:
            after = functools.partial(pltpu.roll, shift=SUB - step, axis=0)
            before = functools.partial(pltpu.roll, shift=step, axis=0)
        g = reciprocal(1.0 - up * after(down) - down * before(up))
        own = (own + up * after(own) + down * before(own)) * g
        up = up * after(up) * g
        down = down * before(down) * g
        step = max(1, 2 * step)
    over = preceding(own)
    x = own
    update(steps - 1, x)
    for j in range(steps - 2, -1, -1):
        x = ratio[j] * x + (lead[j] * over + value[j])
        update(j, x)


def pack_kernel(suction, warmth, classes, top, out, room, class_room, turned, in_sems, out_sems):
    cells = turned.shape[-1]
    quarters = 2 * CHUNKS
    into, sent = [], []
    for f, field in enumerate((suction, warmth, classes)):
        for q in range(quarters):
            target = class_room.at[q] if f == 2 else room.at[f, q]
            into.append(
                pltpu.make_async_copy(field.at[:, pl.ds(q * LANES, LANES)], target, in_sems.at[f, q])
            )
            into[-1].start()

    def send(slot, value):
        turned[:, slot] = value.T.reshape(TEAM, OWN, cells)
        sent.append(pltpu.make_async_copy(turned.at[:, slot], out.at[:, slot], out_sems.at[slot]))
        sent[-1].start()

    rows = [top[0:1, q * LANES : (q + 1) * LANES] for q in range(quarters)]
    send(3 * quarters, jnp.concatenate(rows + [jnp.zeros((cells - quarters, LANES), F32)], axis=0))
    for f in range(3):
        for q in range(quarters):
            into[f * quarters + q].wait()
            send(f * quarters + q, class_room[q].astype(F32) if f == 2 else room[f, q])
    for copy in sent:
        copy.wait()


def unpack_kernel(got, suction, warmth, room, sems):
    cells = got.shape[-1]
    sent = []
    for f, out in enumerate((suction, warmth)):
        for q in range(2 * CHUNKS):
            room[f, q] = got[:, f * 2 * CHUNKS + q].reshape(LANES, cells).T
            here = out.at[:, pl.ds(q * LANES, LANES)]
            sent.append(pltpu.make_async_copy(room.at[f, q], here, sems.at[f, q]))
            sent[-1].start()
    for copy in sent:
        copy.wait()


def mask_rows(cuts):
    return 3 * PAIR_DEV + cuts * (2 * PAIR_DEV + 1)


def cut_row(cut):
    return 3 * PAIR_DEV + cut * (2 * PAIR_DEV + 1)


def mask_kernel(n, couplings, out):
    pair_rows = couplings[...].astype(F32)
    pairs = couplings.shape[1]
    pair_id = lax.broadcasted_iota(jnp.int32, (pairs, LANES), 0)
    lane = lax.broadcasted_iota(jnp.int32, (pairs, LANES), 1)
    lane_1 = lax.broadcasted_iota(jnp.int32, (SUB, LANES), 1)

    def chosen(dev, s):
        at = (pair_id == dev * PAIR_DEV + s - 1).astype(F32)
        found = jnp.dot(pair_rows, at, preferred_element_type=F32)
        return found[0:1], found[1:2]

    def put(row, value):
        out[row] = jnp.broadcast_to(value, (SUB, LANES))

    team = lax.axis_index("cols") // TEAM
    dev = team * TEAM + lane // OWN
    for s in DISTANCES:
        put(s - 1, chosen(dev, s)[0])
        put(PAIR_DEV + s - 1, chosen(dev - s, s)[1])
        put(2 * PAIR_DEV + s - 1, jnp.where(lane_1 // OWN + s < TEAM, 0.25, 0.0))
    block = lax.rem(lane_1 // EDGE, 2)
    edge = lax.rem(lane, EDGE) // OWN
    edge_1 = lax.rem(lane_1, EDGE) // OWN
    for cut in range(cut_count(n)):
        _, above = place(cut)
        row = cut_row(cut)
        partner = jnp.where(above, team + 1, team - 1)
        there = jnp.logical_and(partner >= 0, partner < n // TEAM)
        factor = jnp.where(there, 0.25, 0.0) * sign_of(cut)
        for s in DISTANCES:
            start = team * TEAM + jnp.where(above, TEAM - PAIR_DEV, -s)
            up, down = chosen(start + edge, s)
            mine = jnp.where(above, up, down)
            inward = jnp.where(above, edge_1, PAIR_DEV - 1 - edge_1)
            active = jnp.logical_and(inward >= PAIR_DEV - s, jnp.abs(mine - block.astype(F32)) < 0.5)
            put(row + s - 1, jnp.where(active, factor, 0.0))
            apart = jnp.where(above, PAIR_DEV - s, s - PAIR_DEV)
            up, down = chosen(start + edge + apart, s)
            theirs = jnp.where(above, down, up)
            put(row + PAIR_DEV + s - 1, jnp.where(jnp.abs(theirs - block.astype(F32)) < 0.5, 1.0, 0.0))
        outward = jnp.where(above, LANES - 1 - lane_1, lane_1)
        put(row + 2 * PAIR_DEV, jnp.where(outward < EDGE, 1.0, 0.0))


def edge_shift(cut, m):
    return lax.rem(EDGE * m + jnp.where(place(cut)[1], EDGE, 0), LANES)


def halo_of(cut, value):
    part = lax.broadcasted_iota(jnp.int32, (SUB, LANES), 1) // EDGE
    packed = None
    for m in range(2 * GROUPS):
        moved = pltpu.roll(value[:, m * LANES : (m + 1) * LANES], edge_shift(cut, m), axis=1)
        packed = moved if m == 0 else jnp.where(part == m, moved, packed)
    return packed


def first_kernel(chunk, cuts, *refs):
    got, k_sat, heat_cond = refs[:3]
    head, warm, perm, conduct, wet, melt, cond, energy, top = refs[3:12]
    halos, load = refs[12 : 12 + cuts], refs[-1]
    cells = got.shape[-1]
    steps = head.shape[0]
    stride = steps * GROUPS

    def take(field, change):
        for b in range(2):
            load[b] = got[:, (field * 2 + b) * CHUNKS + chunk].reshape(LANES, cells).T
            for j in range(steps):
                for g in range(GROUPS):
                    change(j, lanes_of(g, b), load[b, pl.ds(g * steps + j, SUB, stride=stride), :])

    def take_head(j, lanes, v):
        head[j, :, lanes] = v

    def take_warm(j, lanes, v):
        warm[j, :, lanes] = v

    def take_class(j, lanes, v):
        k = jnp.full_like(v, k_sat[0])
        lam = jnp.full_like(v, heat_cond[0])
        for c in range(1, k_sat.shape[0]):
            here = v >= c
            k = jnp.where(here, k_sat[c], k)
            lam = jnp.where(here, heat_cond[c], lam)
        perm[j, :, lanes] = k
        conduct[j, :, lanes] = lam

    take(0, take_head)
    take(1, take_warm)
    take(2, take_class)
    surface = got[:, 6 * CHUNKS].reshape(LANES, cells).T[0:SUB]
    rows = [surface[b * CHUNKS + chunk : b * CHUNKS + chunk + 1] for b in range(2)]
    top[...] = jnp.concatenate(rows * GROUPS, axis=1)
    for j in range(steps):
        h, t, k = head[j], warm[j], perm[j]
        s, f = sigmoid(h), sigmoid(2.0 * t)
        m = 0.05 + 0.4 * s
        wet[j] = s
        melt[j] = f
        cond[j] = k * (f * s * s + 0.02)
        energy[j] = (1.0 + 2.0 * m) * t + 2.0 * m * f
        for cut in range(cuts):
            for i, v in enumerate((h, t, k)):
                halos[cut][i, j] = halo_of(cut, v)


def team_kernel(masks, head, warm, cond, water, heat):
    steps = head.shape[0]
    upper = [masks[s - 1] > 0.5 for s in DISTANCES]
    lower = [masks[PAIR_DEV + s - 1] > 0.5 for s in DISTANCES]
    for j in range(steps):
        for g in range(GROUPS):
            l0, l1 = lanes_of(g, 0), lanes_of(g, 1)
            h0, h1 = head[j, :, l0], head[j, :, l1]
            t0, t1 = warm[j, :, l0], warm[j, :, l1]
            c0, c1 = cond[j, :, l0], cond[j, :, l1]
            total = None
            for s in DISTANCES:
                up, low = upper[s - 1], lower[s - 1]
                back = LANES - s * OWN
                h_low = pltpu.roll(jnp.where(low, h1, h0), back, axis=1)
                t_low = pltpu.roll(jnp.where(low, t1, t0), back, axis=1)
                c_low = pltpu.roll(jnp.where(low, c1, c0), back, axis=1)
                flow = (
                    masks[2 * PAIR_DEV + s - 1]
                    * (jnp.where(up, c1, c0) + c_low)
                    * (jnp.where(up, h1, h0) - h_low + 0.5)
                )
                carried = flow * jnp.where(flow > 0.0, jnp.where(up, t1, t0), t_low)
                flow_in = pltpu.roll(flow, s * OWN, axis=1)
                carried_in = pltpu.roll(carried, s * OWN, axis=1)
                part = (
                    flow_in - flow,
                    jnp.where(low, flow_in, 0.0) - jnp.where(up, flow, 0.0),
                    carried_in - carried,
                    jnp.where(low, carried_in, 0.0) - jnp.where(up, carried, 0.0),
                )
                total = part if total is None else [a + b for a, b in zip(total, part)]
            water[j, :, l0] = total[0] - total[1]
            water[j, :, l1] = total[1]
            heat[j, :, l0] = 2.0 * (total[2] - total[3])
            heat[j, :, l1] = 2.0 * total[3]


def cross_flows(cut, masks, mine, theirs):
    row = cut_row(cut)
    sign = sign_of(cut)
    above = place(cut)[1]
    lane = lax.broadcasted_iota(jnp.int32, (SUB, LANES), 1)
    first_block = lax.rem(lane, 2 * EDGE) < EDGE
    h, t, k = mine
    c = passage(h, t, k)
    far = [theirs[0], theirs[1], passage(*theirs)]
    other = [
        jnp.where(first_block, pltpu.roll(v, LANES - EDGE, axis=1), pltpu.roll(v, EDGE, axis=1)) for v in far
    ]
    water = heat = jnp.zeros((SUB, LANES), F32)
    for s in DISTANCES:
        same = masks[row + PAIR_DEV + s - 1] > 0.5
        picked = [jnp.where(same, a, b) for a, b in zip(far, other)]
        apart = (PAIR_DEV - s) * OWN
        if apart:
            shift = jnp.where(above, apart, LANES - apart)
            picked = [pltpu.roll(v, shift, axis=1) for v in picked]
        h_far, t_far, c_far = picked
        flow = masks[row + s - 1] * (c + c_far) * (sign * (h - h_far) + 0.5)
        water = water - flow
        heat = heat - flow * jnp.where(flow > 0.0, t, t_far)
    return water, heat


def advance(steps, cuts, masks, head, warm, conduct, stored, energy, wet, melt, cond, water, heat, top,
            mine, theirs, new_head, new_warm, new_wet, inflow, warm_inflow, ratio, lead, value, finish):
    for j in range(steps):
        w_parts = [water[j, :, m * LANES : (m + 1) * LANES] for m in range(2 * GROUPS)]
        q_parts = [heat[j, :, m * LANES : (m + 1) * LANES] for m in range(2 * GROUPS)]
        for cut in range(cuts):
            beside = masks[cut_row(cut) + 2 * PAIR_DEV]
            w_far, q_far = cross_flows(cut, masks, mine(cut, j), theirs(cut, j))
            for m in range(2 * GROUPS):
                shift = lax.rem(LANES - edge_shift(cut, m), LANES)
                w_parts[m] = w_parts[m] + beside * pltpu.roll(w_far, shift, axis=1)
                q_parts[m] = q_parts[m] + 2.0 * beside * pltpu.roll(q_far, shift, axis=1)
        for m in range(2 * GROUPS):
            inflow[j, :, m * LANES : (m + 1) * LANES] = w_parts[m]
            warm_inflow[j, :, m * LANES : (m + 1) * LANES] = q_parts[m]

    part = lax.broadcasted_iota(jnp.int32, (SUB, ALL), 0)
    group = lax.broadcasted_iota(jnp.int32, (SUB, ALL), 1) // WIDTH
    first_part = jnp.logical_and(part == 0, group == 0)
    last_part = jnp.logical_and(part == SUB - 1, group == GROUPS - 1)

    def faces(fields, potential):
        face_of, rise_of = [], []
        for j in range(steps):
            if j + 1 < steps:
                c_next, v_next = fields[j + 1], potential[j + 1]
                face = 0.5 * (fields[j] + c_next)
            else:
                c_next, v_next = following(fields[0]), following(potential[0])
                face = jnp.where(last_part, 0.0, 0.5 * (fields[j] + c_next))
            face_of.append(face)
            rise_of.append(v_next - potential[j])
        return face_of, rise_of

    k_face, rise = faces([cond[j] for j in range(steps)], head)
    k_top = jnp.where(first_part, 0.0, preceding(k_face[-1]))
    q_face = [k * (1.0 - d) for k, d in zip(k_face, rise)]
    q_top = jnp.where(first_part, 0.0, preceding(q_face[-1]))

    def water_matrix(j):
        above = k_top if j == 0 else k_face[j - 1]
        into = q_top if j == 0 else q_face[j - 1]
        s = wet[j]
        main = 0.8 * s * (1.0 - s) + 0.02 + above + k_face[j]
        source = inflow[j] + into - q_face[j] - 0.8 * (s - stored[j])
        return above, main, k_face[j], source

    def water_done(j, x):
        h = head[j] + x
        new_head[j] = h
        new_wet[j] = sigmoid(h)

    solve(steps, water_matrix, ratio, lead, value, water_done)

    l_cell = [conduct[j] * (1.5 - 0.5 * melt[j]) for j in range(steps)]
    l_face, rise = faces(l_cell, warm)
    l_top = jnp.where(first_part, 0.0, preceding(l_face[-1]))
    g_face = [l * d for l, d in zip(l_face, rise)]
    g_top = jnp.where(first_part, 0.0, preceding(g_face[-1]))
    surface_lam = jnp.where(first_part, 2.0 * l_cell[0], 0.0)

    def heat_matrix(j):
        above = l_top if j == 0 else l_face[j - 1]
        out_of = g_top if j == 0 else g_face[j - 1]
        t, f = warm[j], melt[j]
        m2 = 0.1 + 0.8 * new_wet[j]
        now = (1.0 + m2) * t + m2 * f
        main = 2.0 + 2.0 * m2 * (1.0 + 2.0 * f * (1.0 - f)) + above + l_face[j]
        source = warm_inflow[j] - out_of + g_face[j] - 2.0 * (now - energy[j])
        if j == 0:
            main = main + surface_lam
            source = source + surface_lam * (top[...] - t)
        return above, main, l_face[j], source

    def heat_done(j, x):
        t = warm[j] + x
        new_warm[j] = t
        finish(j, t)

    solve(steps, heat_matrix, ratio, lead, value, heat_done)


def middle_kernel(cuts, *refs):
    masks, head, warm, perm, conduct, wet, melt, cond, energy, top, water, heat = refs[:12]
    own, far = refs[12 : 12 + cuts], refs[12 + cuts : 12 + 2 * cuts]
    new_head, new_warm, new_wet, new_melt, new_cond = refs[12 + 2 * cuts : 17 + 2 * cuts]
    halos = refs[17 + 2 * cuts : 17 + 3 * cuts]
    inflow, warm_inflow, ratio, lead, value = refs[17 + 3 * cuts :]

    def finish(j, t):
        s, f = new_wet[j], sigmoid(2.0 * t)
        new_melt[j] = f
        new_cond[j] = perm[j] * (f * s * s + 0.02)
        for cut in range(cuts):
            halos[cut][0, j] = halo_of(cut, new_head[j])
            halos[cut][1, j] = halo_of(cut, t)

    advance(
        head.shape[0], cuts, masks, head, warm, conduct, wet, energy, wet, melt, cond, water, heat, top,
        lambda cut, j: [own[cut][i, j] for i in range(3)],
        lambda cut, j: [far[cut][i, j] for i in range(3)],
        new_head, new_warm, new_wet, inflow, warm_inflow, ratio, lead, value, finish,
    )


def last_kernel(chunk, cuts, *refs):
    masks, head, warm, conduct, stored, wet, melt, cond, energy, top, water, heat = refs[:12]
    own, far = refs[12 : 12 + cuts], refs[12 + cuts : 12 + 2 * cuts]
    own_k, far_k = refs[12 + 2 * cuts : 12 + 3 * cuts], refs[12 + 3 * cuts : 12 + 4 * cuts]
    others = refs[12 + 4 * cuts : -10]
    out, new_head, new_warm, new_wet, inflow, warm_inflow, ratio, lead, value, load = refs[-10:]
    steps = head.shape[0]
    cells = steps * GROUPS * SUB
    stride = steps * GROUPS
    advance(
        steps, cuts, masks, head, warm, conduct, stored, energy, wet, melt, cond, water, heat, top,
        lambda cut, j: [own[cut][0, j], own[cut][1, j], own_k[cut][2, j]],
        lambda cut, j: [far[cut][0, j], far[cut][1, j], far_k[cut][2, j]],
        new_head, new_warm, new_wet, inflow, warm_inflow, ratio, lead, value, lambda j, t: None,
    )
    final = chunk == CHUNKS - 1
    for f, field in enumerate((new_head, new_warm)):
        for b in range(2):
            slot = f * 2 + b
            for j in range(steps):
                for g in range(GROUPS):
                    load[slot, pl.ds(g * steps + j, SUB, stride=stride), :] = field[j, :, lanes_of(g, b)]
            turned = load[slot].T.reshape(TEAM, OWN, cells)
            if final:
                out[:, slot * CHUNKS + chunk] = turned
                for c, other in enumerate(others):
                    out[:, slot * CHUNKS + c] = other[:, slot]
            else:
                out[:, slot] = turned


def whole(memory=pltpu.VMEM):
    return pl.BlockSpec(memory_space=memory)


def call(kernel, name, args, outs, scratch=(), specs=None, out_specs=None, limit=VMEM_LIMIT, work=2_000_000):
    return pl.pallas_call(
        kernel,
        out_shape=[jax.ShapeDtypeStruct(shape, F32) for shape in outs],
        in_specs=specs or [whole()] * len(args),
        out_specs=out_specs or [whole()] * len(outs),
        scratch_shapes=scratch,
        compiler_params=pltpu.CompilerParams(vmem_limit_bytes=limit),
        cost_estimate=pl.CostEstimate(flops=work, bytes_accessed=work, transcendentals=0),
        name=name,
    )(*args)


def exchange(tiles, n):
    teams = [list(range(start, start + TEAM)) for start in range(0, n, TEAM)]
    return lax.all_to_all(
        tiles, "cols", split_axis=0, concat_axis=0, tiled=True, axis_index_groups=teams
    )


def swap(cut, n, value):
    pairs = []
    for team in range(cut, n // TEAM - 1, 2):
        for i in range(team * TEAM, (team + 1) * TEAM):
            pairs += [(i, i + TEAM), (i + TEAM, i)]
    return lax.ppermute(value, "cols", pairs)


def on_device(suction, warmth, classes, top, couplings, k_sat, heat_cond):
    n = lax.axis_size("cols")
    cells, width = suction.shape
    steps = cells // (SUB * GROUPS)
    quarters = width // LANES
    cuts = cut_count(n)
    column = (steps, SUB, ALL)
    halo = (steps, SUB, LANES)
    room = pltpu.VMEM(column, F32)
    smem = whole(pltpu.SMEM)
    hbm = whole(pltpu.HBM)

    masks = call(
        functools.partial(mask_kernel, n), "masks", (couplings,), [(mask_rows(cuts), SUB, LANES)]
    )[0]
    packed = call(
        pack_kernel,
        "pack",
        (suction, warmth, classes, top.reshape(1, width)),
        [(TEAM, 3 * quarters + 1, OWN, cells)],
        scratch=[
            pltpu.VMEM((2, quarters, cells, LANES), F32),
            pltpu.VMEM((quarters, cells, LANES), classes.dtype),
            pltpu.VMEM((TEAM, 3 * quarters + 1, OWN, cells), F32),
            pltpu.SemaphoreType.DMA((3, quarters)),
            pltpu.SemaphoreType.DMA((3 * quarters + 1,)),
        ],
        specs=[hbm, hbm, hbm, whole()],
        out_specs=[hbm],
        limit=PACK_LIMIT,
    )[0]
    got = exchange(packed, n)

    first, sides = [], []
    for c in range(CHUNKS):
        values = call(
            functools.partial(first_kernel, c, cuts),
            "first",
            (got, k_sat, heat_cond),
            [column] * 8 + [(1, ALL)] + [(3,) + halo] * cuts,
            scratch=[pltpu.VMEM((2, cells, LANES), F32)],
            specs=[whole(), smem, smem],
        )
        first.append(values[:9])
        mine = values[9:]
        sides.append((mine, [swap(cut, n, v) for cut, v in enumerate(mine)]))

    second, later = [], []
    for c in range(CHUNKS):
        head, warm, perm, conduct, wet, melt, cond, energy, surface = first[c]
        water, heat = call(team_kernel, "team", (masks, head, warm, cond), [column] * 2)
        mine, theirs = sides[c]
        values = call(
            functools.partial(middle_kernel, cuts),
            "middle",
            (masks, head, warm, perm, conduct, wet, melt, cond, energy, surface, water, heat, *mine, *theirs),
            [column] * 5 + [(2,) + halo] * cuts,
            scratch=[room] * 5,
        )
        second.append(values[:5])
        mine = values[5:]
        later.append((mine, [swap(cut, n, v) for cut, v in enumerate(mine)]))

    done = []
    for c in range(CHUNKS):
        conduct, stored, energy, surface = first[c][3], first[c][4], first[c][7], first[c][8]
        head, warm, wet, melt, cond = second[c]
        water, heat = call(team_kernel, "team", (masks, head, warm, cond), [column] * 2)
        mine, theirs = later[c]
        mine_k, theirs_k = sides[c]
        final = c == CHUNKS - 1
        done += call(
            functools.partial(last_kernel, c, cuts),
            "last",
            (
                masks, head, warm, conduct, stored, wet, melt, cond, energy, surface, water, heat,
                *mine, *theirs, *mine_k, *theirs_k, *(done if final else ()),
            ),
            [(TEAM, 2 * quarters if final else 4, OWN, cells)],
            scratch=[room] * 8 + [pltpu.VMEM((4, cells, LANES), F32)],
        )
    back = exchange(done[-1], n)
    return tuple(
        call(
            unpack_kernel,
            "unpack",
            (back,),
            [(cells, width)] * 2,
            scratch=[
                pltpu.VMEM((2, quarters, cells, LANES), F32),
                pltpu.SemaphoreType.DMA((2, quarters)),
            ],
            out_specs=[hbm, hbm],
        )
    )


def solution(mesh):
    placed = (P(None, "cols"), P(None, "cols"), P(None, "cols"), P("cols"), P(), P(), P())
    return jax.shard_map(
        on_device,
        mesh=mesh,
        in_specs=placed,
        out_specs=(P(None, "cols"), P(None, "cols")),
        check_vma=False,
    )
```

```python
import functools

import jax
import jax.numpy as jnp
from jax import lax
from jax.experimental import pallas as pl
from jax.experimental.pallas import tpu as pltpu
from jax.sharding import PartitionSpec as P

SPAN = 256
PAIR_DEV = 4
LANES = 128
CHUNKS = SPAN // LANES
TEAM = 16
OWN = LANES // TEAM
SUB = 8
GROUPS = 2
WIDTH = 2 * LANES
ALL = GROUPS * WIDTH
EDGE = PAIR_DEV * OWN
VMEM_LIMIT = 32 * 1024 * 1024
PACK_LIMIT = 60 * 1024 * 1024
DISTANCES = range(1, PAIR_DEV + 1)
F32 = jnp.float32


def cut_count(n):
    return min(n // TEAM - 1, 2)


def place(cut):
    team = lax.axis_index("cols") // TEAM
    return team, lax.rem(team, 2) == cut


def sign_of(cut):
    return jnp.where(place(cut)[1], 1.0, -1.0).astype(F32)


def reciprocal(x):
    r = pl.reciprocal(x, approx=True)
    return r * (2.0 - x * r)


def sigmoid(x):
    return 0.5 + 0.5 * jnp.tanh(0.5 * x)


def passage(h, t, k):
    s = sigmoid(h)
    return k * (sigmoid(2.0 * t) * s * s + 0.02)


def lanes_of(g, b):
    return slice((g * 2 + b) * LANES, (g * 2 + b + 1) * LANES)


def following(value):
    first, second = value[:, :WIDTH], value[:, WIDTH:]
    return jnp.concatenate([second, pltpu.roll(first, SUB - 1, axis=0)], axis=1)


def preceding(value):
    first, second = value[:, :WIDTH], value[:, WIDTH:]
    return jnp.concatenate([pltpu.roll(second, 1, axis=0), first], axis=1)


def solve(steps, matrix, ratio, lead, value, update):
    c_prev = a_prev = d_prev = None
    for j in range(steps):
        above, main, below, source = matrix(j)
        if j == 0:
            r = reciprocal(main)
            a_prev = above * r
            d_prev = source * r
        else:
            r = reciprocal(main - above * c_prev)
            over = above * r
            a_prev = a_prev * over
            d_prev = source * r + d_prev * over
        c_prev = below * r
        ratio[j] = c_prev
        lead[j] = a_prev
        value[j] = d_prev
    last_c, last_a, last_d = c_prev, a_prev, d_prev
    p_first, a_first, d_first = ratio[steps - 2], lead[steps - 2], value[steps - 2]
    for j in range(steps - 3, -1, -1):
        c = ratio[j]
        p_first = c * p_first
        a_first = lead[j] + c * a_first
        d_first = value[j] + c * d_first
    g = reciprocal(1.0 - last_c * following(a_first))
    up = last_c * following(p_first) * g
    down = last_a * g
    own = (last_d + last_c * following(d_first)) * g
    step = 0
    while step < SUB:
        if step == 0:
            after, before = following, preceding
        else:
            after = functools.partial(pltpu.roll, shift=SUB - step, axis=0)
            before = functools.partial(pltpu.roll, shift=step, axis=0)
        g = reciprocal(1.0 - up * after(down) - down * before(up))
        own = (own + up * after(own) + down * before(own)) * g
        up = up * after(up) * g
        down = down * before(down) * g
        step = max(1, 2 * step)
    over = preceding(own)
    x = own
    update(steps - 1, x)
    for j in range(steps - 2, -1, -1):
        x = ratio[j] * x + (lead[j] * over + value[j])
        update(j, x)


def pack_kernel(suction, warmth, classes, top, out, room, class_room, turned, in_sems, out_sems):
    cells = turned.shape[-1]
    quarters = 2 * CHUNKS
    into, sent = [], []
    for f, field in enumerate((suction, warmth, classes)):
        for q in range(quarters):
            target = class_room.at[q] if f == 2 else room.at[f, q]
            into.append(
                pltpu.make_async_copy(field.at[:, pl.ds(q * LANES, LANES)], target, in_sems.at[f, q])
            )
            into[-1].start()

    def send(slot, value):
        turned[:, slot] = value.T.reshape(TEAM, OWN, cells)
        sent.append(pltpu.make_async_copy(turned.at[:, slot], out.at[:, slot], out_sems.at[slot]))
        sent[-1].start()

    rows = [top[0:1, q * LANES : (q + 1) * LANES] for q in range(quarters)]
    send(3 * quarters, jnp.concatenate(rows + [jnp.zeros((cells - quarters, LANES), F32)], axis=0))
    for f in range(3):
        for q in range(quarters):
            into[f * quarters + q].wait()
            send(f * quarters + q, class_room[q].astype(F32) if f == 2 else room[f, q])
    for copy in sent:
        copy.wait()


def unpack_kernel(got, suction, warmth, room, sems):
    cells = got.shape[-1]
    sent = []
    for f, out in enumerate((suction, warmth)):
        for q in range(2 * CHUNKS):
            room[f, q] = got[:, f * 2 * CHUNKS + q].reshape(LANES, cells).T
            here = out.at[:, pl.ds(q * LANES, LANES)]
            sent.append(pltpu.make_async_copy(room.at[f, q], here, sems.at[f, q]))
            sent[-1].start()
    for copy in sent:
        copy.wait()


def mask_rows(cuts):
    return 3 * PAIR_DEV + cuts * (2 * PAIR_DEV + 1)


def cut_row(cut):
    return 3 * PAIR_DEV + cut * (2 * PAIR_DEV + 1)


def mask_kernel(n, couplings, out):
    pair_rows = couplings[...].astype(F32)
    pairs = couplings.shape[1]
    pair_id = lax.broadcasted_iota(jnp.int32, (pairs, LANES), 0)
    lane = lax.broadcasted_iota(jnp.int32, (pairs, LANES), 1)
    lane_1 = lax.broadcasted_iota(jnp.int32, (SUB, LANES), 1)

    def chosen(dev, s):
        at = (pair_id == dev * PAIR_DEV + s - 1).astype(F32)
        found = jnp.dot(pair_rows, at, preferred_element_type=F32)
        return found[0:1], found[1:2]

    def put(row, value):
        out[row] = jnp.broadcast_to(value, (SUB, LANES))

    team = lax.axis_index("cols") // TEAM
    dev = team * TEAM + lane // OWN
    for s in DISTANCES:
        put(s - 1, chosen(dev, s)[0])
        put(PAIR_DEV + s - 1, chosen(dev - s, s)[1])
        put(2 * PAIR_DEV + s - 1, jnp.where(lane_1 // OWN + s < TEAM, 0.25, 0.0))
    block = lax.rem(lane_1 // EDGE, 2)
    edge = lax.rem(lane, EDGE) // OWN
    edge_1 = lax.rem(lane_1, EDGE) // OWN
    for cut in range(cut_count(n)):
        _, above = place(cut)
        row = cut_row(cut)
        partner = jnp.where(above, team + 1, team - 1)
        there = jnp.logical_and(partner >= 0, partner < n // TEAM)
        factor = jnp.where(there, 0.25, 0.0) * sign_of(cut)
        for s in DISTANCES:
            start = team * TEAM + jnp.where(above, TEAM - PAIR_DEV, -s)
            up, down = chosen(start + edge, s)
            mine = jnp.where(above, up, down)
            inward = jnp.where(above, edge_1, PAIR_DEV - 1 - edge_1)
            active = jnp.logical_and(inward >= PAIR_DEV - s, jnp.abs(mine - block.astype(F32)) < 0.5)
            put(row + s - 1, jnp.where(active, factor, 0.0))
            apart = jnp.where(above, PAIR_DEV - s, s - PAIR_DEV)
            up, down = chosen(start + edge + apart, s)
            theirs = jnp.where(above, down, up)
            put(row + PAIR_DEV + s - 1, jnp.where(jnp.abs(theirs - block.astype(F32)) < 0.5, 1.0, 0.0))
        outward = jnp.where(above, LANES - 1 - lane_1, lane_1)
        put(row + 2 * PAIR_DEV, jnp.where(outward < EDGE, 1.0, 0.0))


def edge_shift(cut, m):
    return lax.rem(EDGE * m + jnp.where(place(cut)[1], EDGE, 0), LANES)


def halo_of(cut, value):
    part = lax.broadcasted_iota(jnp.int32, (SUB, LANES), 1) // EDGE
    packed = None
    for m in range(2 * GROUPS):
        moved = pltpu.roll(value[:, m * LANES : (m + 1) * LANES], edge_shift(cut, m), axis=1)
        packed = moved if m == 0 else jnp.where(part == m, moved, packed)
    return packed


def first_kernel(chunk, cuts, *refs):
    got, k_sat, heat_cond = refs[:3]
    head, warm, perm, conduct, wet, melt, cond, energy, top = refs[3:12]
    halos, load = refs[12 : 12 + cuts], refs[-1]
    cells = got.shape[-1]
    steps = head.shape[0]
    stride = steps * GROUPS

    for field in range(3):
        for b in range(2):
            load[field * 2 + b] = got[:, (field * 2 + b) * CHUNKS + chunk].reshape(LANES, cells).T
    surface = got[:, 6 * CHUNKS].reshape(LANES, cells).T[0:SUB]
    rows = [surface[b * CHUNKS + chunk : b * CHUNKS + chunk + 1] for b in range(2)]
    top[...] = jnp.concatenate(rows * GROUPS, axis=1)

    def fetch(field, j):
        parts = [
            load[field * 2 + b, pl.ds(g * steps + j, SUB, stride=stride), :]
            for g in range(GROUPS)
            for b in range(2)
        ]
        return jnp.concatenate(parts, axis=1)

    for j in range(steps):
        h, t, v = [fetch(field, j) for field in range(3)]
        k = jnp.full_like(v, k_sat[0])
        lam = jnp.full_like(v, heat_cond[0])
        for c in range(1, k_sat.shape[0]):
            here = v >= c
            k = jnp.where(here, k_sat[c], k)
            lam = jnp.where(here, heat_cond[c], lam)
        s, f = sigmoid(h), sigmoid(2.0 * t)
        m = 0.05 + 0.4 * s
        head[j], warm[j], perm[j], conduct[j] = h, t, k, lam
        wet[j] = s
        melt[j] = f
        cond[j] = k * (f * s * s + 0.02)
        energy[j] = (1.0 + 2.0 * m) * t + 2.0 * m * f
        for cut in range(cuts):
            for i, v in enumerate((h, t, k)):
                halos[cut][i, j] = halo_of(cut, v)


def team_kernel(masks, head, warm, cond, water_out, heat_out, water, heat):
    steps = head.shape[0]
    upper = [masks[s - 1] > 0.5 for s in DISTANCES]
    lower = [masks[PAIR_DEV + s - 1] > 0.5 for s in DISTANCES]
    for j in range(steps):
        for g in range(GROUPS):
            l0, l1 = lanes_of(g, 0), lanes_of(g, 1)
            h0, h1 = head[j, :, l0], head[j, :, l1]
            t0, t1 = warm[j, :, l0], warm[j, :, l1]
            c0, c1 = cond[j, :, l0], cond[j, :, l1]
            total = None
            for s in DISTANCES:
                up, low = upper[s - 1], lower[s - 1]
                back = LANES - s * OWN
                h_low = pltpu.roll(jnp.where(low, h1, h0), back, axis=1)
                t_low = pltpu.roll(jnp.where(low, t1, t0), back, axis=1)
                c_low = pltpu.roll(jnp.where(low, c1, c0), back, axis=1)
                flow = (
                    masks[2 * PAIR_DEV + s - 1]
                    * (jnp.where(up, c1, c0) + c_low)
                    * (jnp.where(up, h1, h0) - h_low + 0.5)
                )
                carried = flow * jnp.where(flow > 0.0, jnp.where(up, t1, t0), t_low)
                flow_in = pltpu.roll(flow, s * OWN, axis=1)
                carried_in = pltpu.roll(carried, s * OWN, axis=1)
                part = (
                    flow_in - flow,
                    jnp.where(low, flow_in, 0.0) - jnp.where(up, flow, 0.0),
                    carried_in - carried,
                    jnp.where(low, carried_in, 0.0) - jnp.where(up, carried, 0.0),
                )
                total = part if total is None else [a + b for a, b in zip(total, part)]
            water[j, :, l0] = total[0] - total[1]
            water[j, :, l1] = total[1]
            heat[j, :, l0] = 2.0 * (total[2] - total[3])
            heat[j, :, l1] = 2.0 * total[3]
    water_out[...] = water[...]
    heat_out[...] = heat[...]


def cross_flows(cut, masks, mine, theirs):
    row = cut_row(cut)
    sign = sign_of(cut)
    above = place(cut)[1]
    lane = lax.broadcasted_iota(jnp.int32, (SUB, LANES), 1)
    first_block = lax.rem(lane, 2 * EDGE) < EDGE
    h, t, k = mine
    c = passage(h, t, k)
    far = [theirs[0], theirs[1], passage(*theirs)]
    other = [
        jnp.where(first_block, pltpu.roll(v, LANES - EDGE, axis=1), pltpu.roll(v, EDGE, axis=1)) for v in far
    ]
    water = heat = jnp.zeros((SUB, LANES), F32)
    for s in DISTANCES:
        same = masks[row + PAIR_DEV + s - 1] > 0.5
        picked = [jnp.where(same, a, b) for a, b in zip(far, other)]
        apart = (PAIR_DEV - s) * OWN
        if apart:
            shift = jnp.where(above, apart, LANES - apart)
            picked = [pltpu.roll(v, shift, axis=1) for v in picked]
        h_far, t_far, c_far = picked
        flow = masks[row + s - 1] * (c + c_far) * (sign * (h - h_far) + 0.5)
        water = water - flow
        heat = heat - flow * jnp.where(flow > 0.0, t, t_far)
    return water, heat


def advance(steps, cuts, masks, head, warm, conduct, stored, energy, wet, melt, cond, water, heat, top,
            mine, theirs, new_head, new_warm, new_wet, inflow, warm_inflow, ratio, lead, value, finish):
    for j in range(steps):
        w_parts = [water[j, :, m * LANES : (m + 1) * LANES] for m in range(2 * GROUPS)]
        q_parts = [heat[j, :, m * LANES : (m + 1) * LANES] for m in range(2 * GROUPS)]
        for cut in range(cuts):
            beside = masks[cut_row(cut) + 2 * PAIR_DEV]
            w_far, q_far = cross_flows(cut, masks, mine(cut, j), theirs(cut, j))
            for m in range(2 * GROUPS):
                shift = lax.rem(LANES - edge_shift(cut, m), LANES)
                w_parts[m] = w_parts[m] + beside * pltpu.roll(w_far, shift, axis=1)
                q_parts[m] = q_parts[m] + 2.0 * beside * pltpu.roll(q_far, shift, axis=1)
        for m in range(2 * GROUPS):
            inflow[j, :, m * LANES : (m + 1) * LANES] = w_parts[m]
            warm_inflow[j, :, m * LANES : (m + 1) * LANES] = q_parts[m]

    part = lax.broadcasted_iota(jnp.int32, (SUB, ALL), 0)
    group = lax.broadcasted_iota(jnp.int32, (SUB, ALL), 1) // WIDTH
    first_part = jnp.logical_and(part == 0, group == 0)
    last_part = jnp.logical_and(part == SUB - 1, group == GROUPS - 1)

    def faces(fields, potential):
        face_of, rise_of = [], []
        for j in range(steps):
            if j + 1 < steps:
                c_next, v_next = fields[j + 1], potential[j + 1]
                face = 0.5 * (fields[j] + c_next)
            else:
                c_next, v_next = following(fields[0]), following(potential[0])
                face = jnp.where(last_part, 0.0, 0.5 * (fields[j] + c_next))
            face_of.append(face)
            rise_of.append(v_next - potential[j])
        return face_of, rise_of

    k_face, rise = faces([cond[j] for j in range(steps)], head)
    k_top = jnp.where(first_part, 0.0, preceding(k_face[-1]))
    q_face = [k * (1.0 - d) for k, d in zip(k_face, rise)]
    q_top = jnp.where(first_part, 0.0, preceding(q_face[-1]))

    def water_matrix(j):
        above = k_top if j == 0 else k_face[j - 1]
        into = q_top if j == 0 else q_face[j - 1]
        s = wet[j]
        main = 0.8 * s * (1.0 - s) + 0.02 + above + k_face[j]
        source = inflow[j] + into - q_face[j] - 0.8 * (s - stored[j])
        return above, main, k_face[j], source

    def water_done(j, x):
        h = head[j] + x
        new_head[j] = h
        new_wet[j] = sigmoid(h)

    solve(steps, water_matrix, ratio, lead, value, water_done)

    l_cell = [conduct[j] * (1.5 - 0.5 * melt[j]) for j in range(steps)]
    l_face, rise = faces(l_cell, warm)
    l_top = jnp.where(first_part, 0.0, preceding(l_face[-1]))
    g_face = [l * d for l, d in zip(l_face, rise)]
    g_top = jnp.where(first_part, 0.0, preceding(g_face[-1]))
    surface_lam = jnp.where(first_part, 2.0 * l_cell[0], 0.0)

    def heat_matrix(j):
        above = l_top if j == 0 else l_face[j - 1]
        out_of = g_top if j == 0 else g_face[j - 1]
        t, f = warm[j], melt[j]
        m2 = 0.1 + 0.8 * new_wet[j]
        now = (1.0 + m2) * t + m2 * f
        main = 2.0 + 2.0 * m2 * (1.0 + 2.0 * f * (1.0 - f)) + above + l_face[j]
        source = warm_inflow[j] - out_of + g_face[j] - 2.0 * (now - energy[j])
        if j == 0:
            main = main + surface_lam
            source = source + surface_lam * (top[...] - t)
        return above, main, l_face[j], source

    def heat_done(j, x):
        t = warm[j] + x
        new_warm[j] = t
        finish(j, t)

    solve(steps, heat_matrix, ratio, lead, value, heat_done)


def middle_kernel(cuts, *refs):
    masks, head, warm, perm, conduct, wet, melt, cond, energy, top, water, heat = refs[:12]
    own, far = refs[12 : 12 + cuts], refs[12 + cuts : 12 + 2 * cuts]
    new_head, new_warm, new_wet, new_melt, new_cond = refs[12 + 2 * cuts : 17 + 2 * cuts]
    halos = refs[17 + 2 * cuts : 17 + 3 * cuts]
    inflow, warm_inflow, ratio, lead, value = refs[17 + 3 * cuts :]

    def finish(j, t):
        s, f = new_wet[j], sigmoid(2.0 * t)
        new_melt[j] = f
        new_cond[j] = perm[j] * (f * s * s + 0.02)
        for cut in range(cuts):
            halos[cut][0, j] = halo_of(cut, new_head[j])
            halos[cut][1, j] = halo_of(cut, t)

    advance(
        head.shape[0], cuts, masks, head, warm, conduct, wet, energy, wet, melt, cond, water, heat, top,
        lambda cut, j: [own[cut][i, j] for i in range(3)],
        lambda cut, j: [far[cut][i, j] for i in range(3)],
        new_head, new_warm, new_wet, inflow, warm_inflow, ratio, lead, value, finish,
    )


def last_kernel(chunk, cuts, *refs):
    masks, head, warm, conduct, stored, wet, melt, cond, energy, top, water, heat = refs[:12]
    own, far = refs[12 : 12 + cuts], refs[12 + cuts : 12 + 2 * cuts]
    own_k, far_k = refs[12 + 2 * cuts : 12 + 3 * cuts], refs[12 + 3 * cuts : 12 + 4 * cuts]
    others = refs[12 + 4 * cuts : -10]
    out, new_head, new_warm, new_wet, inflow, warm_inflow, ratio, lead, value, load = refs[-10:]
    steps = head.shape[0]
    cells = steps * GROUPS * SUB
    stride = steps * GROUPS
    advance(
        steps, cuts, masks, head, warm, conduct, stored, energy, wet, melt, cond, water, heat, top,
        lambda cut, j: [own[cut][0, j], own[cut][1, j], own_k[cut][2, j]],
        lambda cut, j: [far[cut][0, j], far[cut][1, j], far_k[cut][2, j]],
        new_head, new_warm, new_wet, inflow, warm_inflow, ratio, lead, value, lambda j, t: None,
    )
    final = chunk == CHUNKS - 1
    for f, field in enumerate((new_head, new_warm)):
        for b in range(2):
            slot = f * 2 + b
            for j in range(steps):
                for g in range(GROUPS):
                    load[slot, pl.ds(g * steps + j, SUB, stride=stride), :] = field[j, :, lanes_of(g, b)]
            turned = load[slot].T.reshape(TEAM, OWN, cells)
            if final:
                out[:, slot * CHUNKS + chunk] = turned
                for c, other in enumerate(others):
                    out[:, slot * CHUNKS + c] = other[:, slot]
            else:
                out[:, slot] = turned


def whole(memory=pltpu.VMEM):
    return pl.BlockSpec(memory_space=memory)


def call(kernel, name, args, outs, scratch=(), specs=None, out_specs=None, limit=VMEM_LIMIT, work=2_000_000):
    return pl.pallas_call(
        kernel,
        out_shape=[jax.ShapeDtypeStruct(shape, F32) for shape in outs],
        in_specs=specs or [whole()] * len(args),
        out_specs=out_specs or [whole()] * len(outs),
        scratch_shapes=scratch,
        compiler_params=pltpu.CompilerParams(vmem_limit_bytes=limit),
        cost_estimate=pl.CostEstimate(flops=work, bytes_accessed=work, transcendentals=0),
        name=name,
    )(*args)


def exchange(tiles, n):
    teams = [list(range(start, start + TEAM)) for start in range(0, n, TEAM)]
    return lax.all_to_all(
        tiles, "cols", split_axis=0, concat_axis=0, tiled=True, axis_index_groups=teams
    )


def swap(cut, n, value):
    pairs = []
    for team in range(cut, n // TEAM - 1, 2):
        for i in range(team * TEAM, (team + 1) * TEAM):
            pairs += [(i, i + TEAM), (i + TEAM, i)]
    return lax.ppermute(value, "cols", pairs)


def on_device(suction, warmth, classes, top, couplings, k_sat, heat_cond):
    n = lax.axis_size("cols")
    cells, width = suction.shape
    steps = cells // (SUB * GROUPS)
    quarters = width // LANES
    cuts = cut_count(n)
    column = (steps, SUB, ALL)
    halo = (steps, SUB, LANES)
    room = pltpu.VMEM(column, F32)
    smem = whole(pltpu.SMEM)
    hbm = whole(pltpu.HBM)

    masks = call(
        functools.partial(mask_kernel, n), "masks", (couplings,), [(mask_rows(cuts), SUB, LANES)]
    )[0]
    packed = call(
        pack_kernel,
        "pack",
        (suction, warmth, classes, top.reshape(1, width)),
        [(TEAM, 3 * quarters + 1, OWN, cells)],
        scratch=[
            pltpu.VMEM((2, quarters, cells, LANES), F32),
            pltpu.VMEM((quarters, cells, LANES), classes.dtype),
            pltpu.VMEM((TEAM, 3 * quarters + 1, OWN, cells), F32),
            pltpu.SemaphoreType.DMA((3, quarters)),
            pltpu.SemaphoreType.DMA((3 * quarters + 1,)),
        ],
        specs=[hbm, hbm, hbm, whole()],
        out_specs=[hbm],
        limit=PACK_LIMIT,
    )[0]
    got = exchange(packed, n)

    first, sides = [], []
    for c in range(CHUNKS):
        values = call(
            functools.partial(first_kernel, c, cuts),
            "first",
            (got, k_sat, heat_cond),
            [column] * 8 + [(1, ALL)] + [(3,) + halo] * cuts,
            scratch=[pltpu.VMEM((6, cells, LANES), F32)],
            specs=[whole(), smem, smem],
        )
        first.append(values[:9])
        mine = values[9:]
        sides.append((mine, [swap(cut, n, v) for cut, v in enumerate(mine)]))

    second, later = [], []
    for c in range(CHUNKS):
        head, warm, perm, conduct, wet, melt, cond, energy, surface = first[c]
        water, heat = call(team_kernel, "team", (masks, head, warm, cond), [column] * 2, scratch=[room] * 2)
        mine, theirs = sides[c]
        values = call(
            functools.partial(middle_kernel, cuts),
            "middle",
            (masks, head, warm, perm, conduct, wet, melt, cond, energy, surface, water, heat, *mine, *theirs),
            [column] * 5 + [(2,) + halo] * cuts,
            scratch=[room] * 5,
        )
        second.append(values[:5])
        mine = values[5:]
        later.append((mine, [swap(cut, n, v) for cut, v in enumerate(mine)]))

    done = []
    for c in range(CHUNKS):
        conduct, stored, energy, surface = first[c][3], first[c][4], first[c][7], first[c][8]
        head, warm, wet, melt, cond = second[c]
        water, heat = call(team_kernel, "team", (masks, head, warm, cond), [column] * 2, scratch=[room] * 2)
        mine, theirs = later[c]
        mine_k, theirs_k = sides[c]
        final = c == CHUNKS - 1
        done += call(
            functools.partial(last_kernel, c, cuts),
            "last",
            (
                masks, head, warm, conduct, stored, wet, melt, cond, energy, surface, water, heat,
                *mine, *theirs, *mine_k, *theirs_k, *(done if final else ()),
            ),
            [(TEAM, 2 * quarters if final else 4, OWN, cells)],
            scratch=[room] * 8 + [pltpu.VMEM((4, cells, LANES), F32)],
        )
    back = exchange(done[-1], n)
    return tuple(
        call(
            unpack_kernel,
            "unpack",
            (back,),
            [(cells, width)] * 2,
            scratch=[
                pltpu.VMEM((2, quarters, cells, LANES), F32),
                pltpu.SemaphoreType.DMA((2, quarters)),
            ],
            out_specs=[hbm, hbm],
        )
    )


def solution(mesh):
    placed = (P(None, "cols"), P(None, "cols"), P(None, "cols"), P("cols"), P(), P(), P())
    return jax.shard_map(
        on_device,
        mesh=mesh,
        in_specs=placed,
        out_specs=(P(None, "cols"), P(None, "cols")),
        check_vma=False,
    )
```

```python
import functools

import jax
import jax.numpy as jnp
from jax import lax
from jax.experimental import pallas as pl
from jax.experimental.pallas import tpu as pltpu
from jax.sharding import PartitionSpec as P

SPAN = 256
PAIR_DEV = 4
LANES = 128
CHUNKS = SPAN // LANES
TEAM = 16
OWN = LANES // TEAM
SUB = 8
GROUPS = 2
WIDTH = 2 * LANES
ALL = GROUPS * WIDTH
EDGE = PAIR_DEV * OWN
VMEM_LIMIT = 32 * 1024 * 1024
PACK_LIMIT = 60 * 1024 * 1024
DISTANCES = range(1, PAIR_DEV + 1)
F32 = jnp.float32


def cut_count(n):
    return min(n // TEAM - 1, 2)


def place(cut):
    team = lax.axis_index("cols") // TEAM
    return team, lax.rem(team, 2) == cut


def sign_of(cut):
    return jnp.where(place(cut)[1], 1.0, -1.0).astype(F32)


def reciprocal(x):
    r = pl.reciprocal(x, approx=True)
    return r * (2.0 - x * r)


def sigmoid(x):
    return 0.5 + 0.5 * jnp.tanh(0.5 * x)


def passage(h, t, k):
    s = sigmoid(h)
    return k * (sigmoid(2.0 * t) * s * s + 0.02)


def lanes_of(g, b):
    return slice((g * 2 + b) * LANES, (g * 2 + b + 1) * LANES)


def following(value):
    first, second = value[:, :WIDTH], value[:, WIDTH:]
    return jnp.concatenate([second, pltpu.roll(first, SUB - 1, axis=0)], axis=1)


def preceding(value):
    first, second = value[:, :WIDTH], value[:, WIDTH:]
    return jnp.concatenate([pltpu.roll(second, 1, axis=0), first], axis=1)


def solve(steps, matrix, ratio, lead, value, update):
    c_prev = a_prev = d_prev = None
    for j in range(steps):
        above, main, below, source = matrix(j)
        if j == 0:
            r = reciprocal(main)
            a_prev = above * r
            d_prev = source * r
        else:
            r = reciprocal(main - above * c_prev)
            over = above * r
            a_prev = a_prev * over
            d_prev = source * r + d_prev * over
        c_prev = below * r
        ratio[j] = c_prev
        lead[j] = a_prev
        value[j] = d_prev
    last_c, last_a, last_d = c_prev, a_prev, d_prev
    p_first, a_first, d_first = ratio[steps - 2], lead[steps - 2], value[steps - 2]
    for j in range(steps - 3, -1, -1):
        c = ratio[j]
        p_first = c * p_first
        a_first = lead[j] + c * a_first
        d_first = value[j] + c * d_first
    g = reciprocal(1.0 - last_c * following(a_first))
    up = last_c * following(p_first) * g
    down = last_a * g
    own = (last_d + last_c * following(d_first)) * g
    step = 0
    while step < SUB:
        if step == 0:
            after, before = following, preceding
        else:
            after = functools.partial(pltpu.roll, shift=SUB - step, axis=0)
            before = functools.partial(pltpu.roll, shift=step, axis=0)
        g = reciprocal(1.0 - up * after(down) - down * before(up))
        own = (own + up * after(own) + down * before(own)) * g
        up = up * after(up) * g
        down = down * before(down) * g
        step = max(1, 2 * step)
    over = preceding(own)
    x = own
    update(steps - 1, x)
    for j in range(steps - 2, -1, -1):
        x = ratio[j] * x + (lead[j] * over + value[j])
        update(j, x)


def mask_rows(cuts):
    return 3 * PAIR_DEV + cuts * (2 * PAIR_DEV + 1)


def cut_row(cut):
    return 3 * PAIR_DEV + cut * (2 * PAIR_DEV + 1)


def fill_masks(n, couplings, out):
    pair_rows = couplings[...].astype(F32)
    pairs = couplings.shape[1]
    pair_id = lax.broadcasted_iota(jnp.int32, (pairs, LANES), 0)
    lane = lax.broadcasted_iota(jnp.int32, (pairs, LANES), 1)
    lane_1 = lax.broadcasted_iota(jnp.int32, (SUB, LANES), 1)

    def chosen(dev, s):
        at = (pair_id == dev * PAIR_DEV + s - 1).astype(F32)
        found = jnp.dot(pair_rows, at, preferred_element_type=F32)
        return found[0:1], found[1:2]

    def put(row, value):
        out[row] = jnp.broadcast_to(value, (SUB, LANES))

    team = lax.axis_index("cols") // TEAM
    dev = team * TEAM + lane // OWN
    for s in DISTANCES:
        put(s - 1, chosen(dev, s)[0])
        put(PAIR_DEV + s - 1, chosen(dev - s, s)[1])
        put(2 * PAIR_DEV + s - 1, jnp.where(lane_1 // OWN + s < TEAM, 0.25, 0.0))
    block = lax.rem(lane_1 // EDGE, 2)
    edge = lax.rem(lane, EDGE) // OWN
    edge_1 = lax.rem(lane_1, EDGE) // OWN
    for cut in range(cut_count(n)):
        _, above = place(cut)
        row = cut_row(cut)
        partner = jnp.where(above, team + 1, team - 1)
        there = jnp.logical_and(partner >= 0, partner < n // TEAM)
        factor = jnp.where(there, 0.25, 0.0) * sign_of(cut)
        for s in DISTANCES:
            start = team * TEAM + jnp.where(above, TEAM - PAIR_DEV, -s)
            up, down = chosen(start + edge, s)
            mine = jnp.where(above, up, down)
            inward = jnp.where(above, edge_1, PAIR_DEV - 1 - edge_1)
            active = jnp.logical_and(inward >= PAIR_DEV - s, jnp.abs(mine - block.astype(F32)) < 0.5)
            put(row + s - 1, jnp.where(active, factor, 0.0))
            apart = jnp.where(above, PAIR_DEV - s, s - PAIR_DEV)
            up, down = chosen(start + edge + apart, s)
            theirs = jnp.where(above, down, up)
            put(row + PAIR_DEV + s - 1, jnp.where(jnp.abs(theirs - block.astype(F32)) < 0.5, 1.0, 0.0))
        outward = jnp.where(above, LANES - 1 - lane_1, lane_1)
        put(row + 2 * PAIR_DEV, jnp.where(outward < EDGE, 1.0, 0.0))


def pack_kernel(
    n, suction, warmth, classes, top, couplings, out, masks, room, class_room, turned, pairs, in_sems, out_sems, pair_sem
):
    cells = turned.shape[-1]
    pair_copy = pltpu.make_async_copy(couplings, pairs, pair_sem)
    pair_copy.start()
    quarters = 2 * CHUNKS
    into, sent = [], []
    for f, field in enumerate((suction, warmth, classes)):
        for q in range(quarters):
            target = class_room.at[q] if f == 2 else room.at[f, q]
            into.append(
                pltpu.make_async_copy(field.at[:, pl.ds(q * LANES, LANES)], target, in_sems.at[f, q])
            )
            into[-1].start()

    def send(slot, value):
        turned[:, slot] = value.T.reshape(TEAM, OWN, cells)
        sent.append(pltpu.make_async_copy(turned.at[:, slot], out.at[:, slot], out_sems.at[slot]))
        sent[-1].start()

    rows = [top[0:1, q * LANES : (q + 1) * LANES] for q in range(quarters)]
    send(3 * quarters, jnp.concatenate(rows + [jnp.zeros((cells - quarters, LANES), F32)], axis=0))
    pair_copy.wait()
    fill_masks(n, pairs, masks)
    for f in range(3):
        for q in range(quarters):
            into[f * quarters + q].wait()
            send(f * quarters + q, class_room[q].astype(F32) if f == 2 else room[f, q])
    for copy in sent:
        copy.wait()


def unpack_kernel(got, suction, warmth, room, sems):
    cells = got.shape[-1]
    sent = []
    for f, out in enumerate((suction, warmth)):
        for q in range(2 * CHUNKS):
            room[f, q] = got[:, f * 2 * CHUNKS + q].reshape(LANES, cells).T
            here = out.at[:, pl.ds(q * LANES, LANES)]
            sent.append(pltpu.make_async_copy(room.at[f, q], here, sems.at[f, q]))
            sent[-1].start()
    for copy in sent:
        copy.wait()


def edge_shift(cut, m):
    return lax.rem(EDGE * m + jnp.where(place(cut)[1], EDGE, 0), LANES)


def halo_of(cut, value):
    part = lax.broadcasted_iota(jnp.int32, (SUB, LANES), 1) // EDGE
    packed = None
    for m in range(2 * GROUPS):
        moved = pltpu.roll(value[:, m * LANES : (m + 1) * LANES], edge_shift(cut, m), axis=1)
        packed = moved if m == 0 else jnp.where(part == m, moved, packed)
    return packed


def first_kernel(chunk, cuts, *refs):
    got, k_sat, heat_cond = refs[:3]
    head, warm, perm, conduct, wet, melt, cond, energy, top = refs[3:12]
    halos, load = refs[12 : 12 + cuts], refs[-1]
    cells = got.shape[-1]
    steps = head.shape[0]
    stride = steps * GROUPS

    for field in range(3):
        for b in range(2):
            load[field * 2 + b] = got[:, (field * 2 + b) * CHUNKS + chunk].reshape(LANES, cells).T
    surface = got[:, 6 * CHUNKS].reshape(LANES, cells).T[0:SUB]
    rows = [surface[b * CHUNKS + chunk : b * CHUNKS + chunk + 1] for b in range(2)]
    top[...] = jnp.concatenate(rows * GROUPS, axis=1)

    def fetch(field, j):
        parts = [
            load[field * 2 + b, pl.ds(g * steps + j, SUB, stride=stride), :]
            for g in range(GROUPS)
            for b in range(2)
        ]
        return jnp.concatenate(parts, axis=1)

    for j in range(steps):
        h, t, v = [fetch(field, j) for field in range(3)]
        k = jnp.full_like(v, k_sat[0])
        lam = jnp.full_like(v, heat_cond[0])
        for c in range(1, k_sat.shape[0]):
            here = v >= c
            k = jnp.where(here, k_sat[c], k)
            lam = jnp.where(here, heat_cond[c], lam)
        s, f = sigmoid(h), sigmoid(2.0 * t)
        m = 0.05 + 0.4 * s
        head[j], warm[j], perm[j], conduct[j] = h, t, k, lam
        wet[j] = s
        melt[j] = f
        cond[j] = k * (f * s * s + 0.02)
        energy[j] = (1.0 + 2.0 * m) * t + 2.0 * m * f
        for cut in range(cuts):
            for i, v in enumerate((h, t, k)):
                halos[cut][i, j] = halo_of(cut, v)


def team_kernel(masks, head, warm, cond, water, heat):
    steps = head.shape[0]
    upper = [masks[s - 1] > 0.5 for s in DISTANCES]
    lower = [masks[PAIR_DEV + s - 1] > 0.5 for s in DISTANCES]

    def step(j, _):
        for g in range(GROUPS):
            l0, l1 = lanes_of(g, 0), lanes_of(g, 1)
            h0, h1 = head[j, :, l0], head[j, :, l1]
            t0, t1 = warm[j, :, l0], warm[j, :, l1]
            c0, c1 = cond[j, :, l0], cond[j, :, l1]
            total = None
            for s in DISTANCES:
                up, low = upper[s - 1], lower[s - 1]
                back = LANES - s * OWN
                h_low = pltpu.roll(jnp.where(low, h1, h0), back, axis=1)
                t_low = pltpu.roll(jnp.where(low, t1, t0), back, axis=1)
                c_low = pltpu.roll(jnp.where(low, c1, c0), back, axis=1)
                flow = (
                    masks[2 * PAIR_DEV + s - 1]
                    * (jnp.where(up, c1, c0) + c_low)
                    * (jnp.where(up, h1, h0) - h_low + 0.5)
                )
                carried = flow * jnp.where(flow > 0.0, jnp.where(up, t1, t0), t_low)
                flow_in = pltpu.roll(flow, s * OWN, axis=1)
                carried_in = pltpu.roll(carried, s * OWN, axis=1)
                part = (
                    flow_in - flow,
                    jnp.where(low, flow_in, 0.0) - jnp.where(up, flow, 0.0),
                    carried_in - carried,
                    jnp.where(low, carried_in, 0.0) - jnp.where(up, carried, 0.0),
                )
                total = part if total is None else [a + b for a, b in zip(total, part)]
            water[j, :, l0] = total[0] - total[1]
            water[j, :, l1] = total[1]
            heat[j, :, l0] = 2.0 * (total[2] - total[3])
            heat[j, :, l1] = 2.0 * total[3]

    lax.fori_loop(0, steps, step, None)


def cross_flows(cut, masks, mine, theirs):
    row = cut_row(cut)
    sign = sign_of(cut)
    above = place(cut)[1]
    lane = lax.broadcasted_iota(jnp.int32, (SUB, LANES), 1)
    first_block = lax.rem(lane, 2 * EDGE) < EDGE
    h, t, k = mine
    c = passage(h, t, k)
    far = [theirs[0], theirs[1], passage(*theirs)]
    other = [
        jnp.where(first_block, pltpu.roll(v, LANES - EDGE, axis=1), pltpu.roll(v, EDGE, axis=1)) for v in far
    ]
    water = heat = jnp.zeros((SUB, LANES), F32)
    for s in DISTANCES:
        same = masks[row + PAIR_DEV + s - 1] > 0.5
        picked = [jnp.where(same, a, b) for a, b in zip(far, other)]
        apart = (PAIR_DEV - s) * OWN
        if apart:
            shift = jnp.where(above, apart, LANES - apart)
            picked = [pltpu.roll(v, shift, axis=1) for v in picked]
        h_far, t_far, c_far = picked
        flow = masks[row + s - 1] * (c + c_far) * (sign * (h - h_far) + 0.5)
        water = water - flow
        heat = heat - flow * jnp.where(flow > 0.0, t, t_far)
    return water, heat


def advance(steps, cuts, masks, head, warm, conduct, stored, energy, wet, melt, cond, water, heat, top,
            mine, theirs, new_head, new_warm, new_wet, inflow, warm_inflow, ratio, lead, value, finish):
    for j in range(steps):
        w_parts = [water[j, :, m * LANES : (m + 1) * LANES] for m in range(2 * GROUPS)]
        q_parts = [heat[j, :, m * LANES : (m + 1) * LANES] for m in range(2 * GROUPS)]
        for cut in range(cuts):
            beside = masks[cut_row(cut) + 2 * PAIR_DEV]
            w_far, q_far = cross_flows(cut, masks, mine(cut, j), theirs(cut, j))
            for m in range(2 * GROUPS):
                shift = lax.rem(LANES - edge_shift(cut, m), LANES)
                w_parts[m] = w_parts[m] + beside * pltpu.roll(w_far, shift, axis=1)
                q_parts[m] = q_parts[m] + 2.0 * beside * pltpu.roll(q_far, shift, axis=1)
        for m in range(2 * GROUPS):
            inflow[j, :, m * LANES : (m + 1) * LANES] = w_parts[m]
            warm_inflow[j, :, m * LANES : (m + 1) * LANES] = q_parts[m]

    part = lax.broadcasted_iota(jnp.int32, (SUB, ALL), 0)
    group = lax.broadcasted_iota(jnp.int32, (SUB, ALL), 1) // WIDTH
    first_part = jnp.logical_and(part == 0, group == 0)
    last_part = jnp.logical_and(part == SUB - 1, group == GROUPS - 1)

    def faces(fields, potential):
        face_of, rise_of = [], []
        for j in range(steps):
            if j + 1 < steps:
                c_next, v_next = fields[j + 1], potential[j + 1]
                face = 0.5 * (fields[j] + c_next)
            else:
                c_next, v_next = following(fields[0]), following(potential[0])
                face = jnp.where(last_part, 0.0, 0.5 * (fields[j] + c_next))
            face_of.append(face)
            rise_of.append(v_next - potential[j])
        return face_of, rise_of

    k_face, rise = faces([cond[j] for j in range(steps)], head)
    k_top = jnp.where(first_part, 0.0, preceding(k_face[-1]))
    q_face = [k * (1.0 - d) for k, d in zip(k_face, rise)]
    q_top = jnp.where(first_part, 0.0, preceding(q_face[-1]))

    def water_matrix(j):
        above = k_top if j == 0 else k_face[j - 1]
        into = q_top if j == 0 else q_face[j - 1]
        s = wet[j]
        main = 0.8 * s * (1.0 - s) + 0.02 + above + k_face[j]
        source = inflow[j] + into - q_face[j] - 0.8 * (s - stored[j])
        return above, main, k_face[j], source

    def water_done(j, x):
        h = head[j] + x
        new_head[j] = h
        new_wet[j] = sigmoid(h)

    solve(steps, water_matrix, ratio, lead, value, water_done)

    l_cell = [conduct[j] * (1.5 - 0.5 * melt[j]) for j in range(steps)]
    l_face, rise = faces(l_cell, warm)
    l_top = jnp.where(first_part, 0.0, preceding(l_face[-1]))
    g_face = [l * d for l, d in zip(l_face, rise)]
    g_top = jnp.where(first_part, 0.0, preceding(g_face[-1]))
    surface_lam = jnp.where(first_part, 2.0 * l_cell[0], 0.0)

    def heat_matrix(j):
        above = l_top if j == 0 else l_face[j - 1]
        out_of = g_top if j == 0 else g_face[j - 1]
        t, f = warm[j], melt[j]
        m2 = 0.1 + 0.8 * new_wet[j]
        now = (1.0 + m2) * t + m2 * f
        main = 2.0 + 2.0 * m2 * (1.0 + 2.0 * f * (1.0 - f)) + above + l_face[j]
        source = warm_inflow[j] - out_of + g_face[j] - 2.0 * (now - energy[j])
        if j == 0:
            main = main + surface_lam
            source = source + surface_lam * (top[...] - t)
        return above, main, l_face[j], source

    def heat_done(j, x):
        t = warm[j] + x
        new_warm[j] = t
        finish(j, t)

    solve(steps, heat_matrix, ratio, lead, value, heat_done)


def middle_kernel(cuts, *refs):
    masks, head, warm, perm, conduct, wet, melt, cond, energy, top, water, heat = refs[:12]
    own, far = refs[12 : 12 + cuts], refs[12 + cuts : 12 + 2 * cuts]
    new_head, new_warm, new_wet, new_melt, new_cond = refs[12 + 2 * cuts : 17 + 2 * cuts]
    halos = refs[17 + 2 * cuts : 17 + 3 * cuts]
    inflow, warm_inflow, ratio, lead, value = refs[17 + 3 * cuts :]

    def finish(j, t):
        s, f = new_wet[j], sigmoid(2.0 * t)
        new_melt[j] = f
        new_cond[j] = perm[j] * (f * s * s + 0.02)
        for cut in range(cuts):
            halos[cut][0, j] = halo_of(cut, new_head[j])
            halos[cut][1, j] = halo_of(cut, t)

    advance(
        head.shape[0], cuts, masks, head, warm, conduct, wet, energy, wet, melt, cond, water, heat, top,
        lambda cut, j: [own[cut][i, j] for i in range(3)],
        lambda cut, j: [far[cut][i, j] for i in range(3)],
        new_head, new_warm, new_wet, inflow, warm_inflow, ratio, lead, value, finish,
    )


def last_kernel(chunk, cuts, *refs):
    masks, head, warm, conduct, stored, wet, melt, cond, energy, top, water, heat = refs[:12]
    own, far = refs[12 : 12 + cuts], refs[12 + cuts : 12 + 2 * cuts]
    own_k, far_k = refs[12 + 2 * cuts : 12 + 3 * cuts], refs[12 + 3 * cuts : 12 + 4 * cuts]
    others = refs[12 + 4 * cuts : -10]
    out, new_head, new_warm, new_wet, inflow, warm_inflow, ratio, lead, value, load = refs[-10:]
    steps = head.shape[0]
    cells = steps * GROUPS * SUB
    stride = steps * GROUPS
    advance(
        steps, cuts, masks, head, warm, conduct, stored, energy, wet, melt, cond, water, heat, top,
        lambda cut, j: [own[cut][0, j], own[cut][1, j], own_k[cut][2, j]],
        lambda cut, j: [far[cut][0, j], far[cut][1, j], far_k[cut][2, j]],
        new_head, new_warm, new_wet, inflow, warm_inflow, ratio, lead, value, lambda j, t: None,
    )
    final = chunk == CHUNKS - 1
    for f, field in enumerate((new_head, new_warm)):
        for b in range(2):
            slot = f * 2 + b
            for j in range(steps):
                for g in range(GROUPS):
                    load[slot, pl.ds(g * steps + j, SUB, stride=stride), :] = field[j, :, lanes_of(g, b)]
            turned = load[slot].T.reshape(TEAM, OWN, cells)
            if final:
                out[:, slot * CHUNKS + chunk] = turned
                for c, other in enumerate(others):
                    out[:, slot * CHUNKS + c] = other[:, slot]
            else:
                out[:, slot] = turned


def whole(memory=pltpu.VMEM):
    return pl.BlockSpec(memory_space=memory)


def call(kernel, name, args, outs, scratch=(), specs=None, out_specs=None, limit=VMEM_LIMIT, work=2_000_000):
    return pl.pallas_call(
        kernel,
        out_shape=[jax.ShapeDtypeStruct(shape, F32) for shape in outs],
        in_specs=specs or [whole()] * len(args),
        out_specs=out_specs or [whole()] * len(outs),
        scratch_shapes=scratch,
        compiler_params=pltpu.CompilerParams(vmem_limit_bytes=limit),
        cost_estimate=pl.CostEstimate(flops=work, bytes_accessed=work, transcendentals=0),
        name=name,
    )(*args)


def exchange(tiles, n):
    teams = [list(range(start, start + TEAM)) for start in range(0, n, TEAM)]
    return lax.all_to_all(
        tiles, "cols", split_axis=0, concat_axis=0, tiled=True, axis_index_groups=teams
    )


def swap(cut, n, value):
    pairs = []
    for team in range(cut, n // TEAM - 1, 2):
        for i in range(team * TEAM, (team + 1) * TEAM):
            pairs += [(i, i + TEAM), (i + TEAM, i)]
    return lax.ppermute(value, "cols", pairs)


def on_device(suction, warmth, classes, top, couplings, k_sat, heat_cond):
    n = lax.axis_size("cols")
    cells, width = suction.shape
    steps = cells // (SUB * GROUPS)
    quarters = width // LANES
    cuts = cut_count(n)
    column = (steps, SUB, ALL)
    halo = (steps, SUB, LANES)
    room = pltpu.VMEM(column, F32)
    smem = whole(pltpu.SMEM)
    hbm = whole(pltpu.HBM)

    packed, masks = call(
        functools.partial(pack_kernel, n),
        "pack",
        (suction, warmth, classes, top.reshape(1, width), couplings),
        [(TEAM, 3 * quarters + 1, OWN, cells), (mask_rows(cuts), SUB, LANES)],
        scratch=[
            pltpu.VMEM((2, quarters, cells, LANES), F32),
            pltpu.VMEM((quarters, cells, LANES), classes.dtype),
            pltpu.VMEM((TEAM, 3 * quarters + 1, OWN, cells), F32),
            pltpu.VMEM(couplings.shape, couplings.dtype),
            pltpu.SemaphoreType.DMA((3, quarters)),
            pltpu.SemaphoreType.DMA((3 * quarters + 1,)),
            pltpu.SemaphoreType.DMA,
        ],
        specs=[hbm, hbm, hbm, whole(), hbm],
        out_specs=[hbm, whole()],
        limit=PACK_LIMIT,
    )
    got = exchange(packed, n)

    first, sides = [], []
    for c in range(CHUNKS):
        values = call(
            functools.partial(first_kernel, c, cuts),
            "first",
            (got, k_sat, heat_cond),
            [column] * 8 + [(1, ALL)] + [(3,) + halo] * cuts,
            scratch=[pltpu.VMEM((6, cells, LANES), F32)],
            specs=[whole(), smem, smem],
        )
        first.append(values[:9])
        mine = values[9:]
        sides.append((mine, [swap(cut, n, v) for cut, v in enumerate(mine)]))

    second, later = [], []
    for c in range(CHUNKS):
        head, warm, perm, conduct, wet, melt, cond, energy, surface = first[c]
        water, heat = call(team_kernel, "team", (masks, head, warm, cond), [column] * 2)
        mine, theirs = sides[c]
        values = call(
            functools.partial(middle_kernel, cuts),
            "middle",
            (masks, head, warm, perm, conduct, wet, melt, cond, energy, surface, water, heat, *mine, *theirs),
            [column] * 5 + [(2,) + halo] * cuts,
            scratch=[room] * 5,
        )
        second.append(values[:5])
        mine = values[5:]
        later.append((mine, [swap(cut, n, v) for cut, v in enumerate(mine)]))

    done = []
    for c in range(CHUNKS):
        conduct, stored, energy, surface = first[c][3], first[c][4], first[c][7], first[c][8]
        head, warm, wet, melt, cond = second[c]
        water, heat = call(team_kernel, "team", (masks, head, warm, cond), [column] * 2)
        mine, theirs = later[c]
        mine_k, theirs_k = sides[c]
        final = c == CHUNKS - 1
        done += call(
            functools.partial(last_kernel, c, cuts),
            "last",
            (
                masks, head, warm, conduct, stored, wet, melt, cond, energy, surface, water, heat,
                *mine, *theirs, *mine_k, *theirs_k, *(done if final else ()),
            ),
            [(TEAM, 2 * quarters if final else 4, OWN, cells)],
            scratch=[room] * 8 + [pltpu.VMEM((4, cells, LANES), F32)],
        )
    back = exchange(done[-1], n)
    return tuple(
        call(
            unpack_kernel,
            "unpack",
            (back,),
            [(cells, width)] * 2,
            scratch=[
                pltpu.VMEM((2, quarters, cells, LANES), F32),
                pltpu.SemaphoreType.DMA((2, quarters)),
            ],
            out_specs=[hbm, hbm],
        )
    )


def solution(mesh):
    placed = (P(None, "cols"), P(None, "cols"), P(None, "cols"), P("cols"), P(), P(), P())
    return jax.shard_map(
        on_device,
        mesh=mesh,
        in_specs=placed,
        out_specs=(P(None, "cols"), P(None, "cols")),
        check_vma=False,
    )
```

```python
import functools

import jax
import jax.numpy as jnp
from jax import lax
from jax.experimental import pallas as pl
from jax.experimental.pallas import tpu as pltpu
from jax.sharding import PartitionSpec as P

SPAN = 256
PAIR_DEV = 4
LANES = 128
CHUNKS = SPAN // LANES
TEAM = 16
OWN = LANES // TEAM
SUB = 8
GROUPS = 2
WIDTH = 2 * LANES
ALL = GROUPS * WIDTH
EDGE = PAIR_DEV * OWN
VMEM_LIMIT = 32 * 1024 * 1024
PACK_LIMIT = 60 * 1024 * 1024
DISTANCES = range(1, PAIR_DEV + 1)
SENDS = 4
F32 = jnp.float32


def cut_count(n):
    return min(n // TEAM - 1, 2)


def place(cut):
    team = lax.axis_index("cols") // TEAM
    return team, lax.rem(team, 2) == cut


def sign_of(cut):
    return jnp.where(place(cut)[1], 1.0, -1.0).astype(F32)


def reciprocal(x):
    r = pl.reciprocal(x, approx=True)
    return r * (2.0 - x * r)


def sigmoid(x):
    return 0.5 + 0.5 * jnp.tanh(0.5 * x)


def passage(h, t, k):
    s = sigmoid(h)
    return k * (sigmoid(2.0 * t) * s * s + 0.02)


def lanes_of(g, b):
    return slice((g * 2 + b) * LANES, (g * 2 + b + 1) * LANES)


def following(value):
    first, second = value[:, :WIDTH], value[:, WIDTH:]
    return jnp.concatenate([second, pltpu.roll(first, SUB - 1, axis=0)], axis=1)


def preceding(value):
    first, second = value[:, :WIDTH], value[:, WIDTH:]
    return jnp.concatenate([pltpu.roll(second, 1, axis=0), first], axis=1)


def solve(steps, matrix, ratio, lead, value, update):
    c_prev = a_prev = d_prev = None
    for j in range(steps):
        above, main, below, source = matrix(j)
        if j == 0:
            r = reciprocal(main)
            a_prev = above * r
            d_prev = source * r
        else:
            r = reciprocal(main - above * c_prev)
            over = above * r
            a_prev = a_prev * over
            d_prev = source * r + d_prev * over
        c_prev = below * r
        ratio[j] = c_prev
        lead[j] = a_prev
        value[j] = d_prev
    last_c, last_a, last_d = c_prev, a_prev, d_prev
    p_first, a_first, d_first = ratio[steps - 2], lead[steps - 2], value[steps - 2]
    for j in range(steps - 3, -1, -1):
        c = ratio[j]
        p_first = c * p_first
        a_first = lead[j] + c * a_first
        d_first = value[j] + c * d_first
    g = reciprocal(1.0 - last_c * following(a_first))
    up = last_c * following(p_first) * g
    down = last_a * g
    own = (last_d + last_c * following(d_first)) * g
    step = 0
    while step < SUB:
        if step == 0:
            after, before = following, preceding
        else:
            after = functools.partial(pltpu.roll, shift=SUB - step, axis=0)
            before = functools.partial(pltpu.roll, shift=step, axis=0)
        g = reciprocal(1.0 - up * after(down) - down * before(up))
        own = (own + up * after(own) + down * before(own)) * g
        up = up * after(up) * g
        down = down * before(down) * g
        step = max(1, 2 * step)
    over = preceding(own)
    x = own
    update(steps - 1, x)
    for j in range(steps - 2, -1, -1):
        x = ratio[j] * x + (lead[j] * over + value[j])
        update(j, x)


def mask_rows(cuts):
    return 3 * PAIR_DEV + cuts * (2 * PAIR_DEV + 1)


def cut_row(cut):
    return 3 * PAIR_DEV + cut * (2 * PAIR_DEV + 1)


def mask_kernel(n, couplings, out):
    pair_rows = couplings[...].astype(F32)
    pairs = couplings.shape[1]
    pair_id = lax.broadcasted_iota(jnp.int32, (pairs, LANES), 0)
    lane = lax.broadcasted_iota(jnp.int32, (pairs, LANES), 1)
    lane_1 = lax.broadcasted_iota(jnp.int32, (SUB, LANES), 1)

    def chosen(dev, s):
        at = (pair_id == dev * PAIR_DEV + s - 1).astype(F32)
        found = jnp.dot(pair_rows, at, preferred_element_type=F32)
        return found[0:1], found[1:2]

    def put(row, value):
        out[row] = jnp.broadcast_to(value, (SUB, LANES))

    team = lax.axis_index("cols") // TEAM
    dev = team * TEAM + lane // OWN
    for s in DISTANCES:
        put(s - 1, chosen(dev, s)[0])
        put(PAIR_DEV + s - 1, chosen(dev - s, s)[1])
        put(2 * PAIR_DEV + s - 1, jnp.where(lane_1 // OWN + s < TEAM, 0.25, 0.0))
    block = lax.rem(lane_1 // EDGE, 2)
    edge = lax.rem(lane, EDGE) // OWN
    edge_1 = lax.rem(lane_1, EDGE) // OWN
    for cut in range(cut_count(n)):
        _, above = place(cut)
        row = cut_row(cut)
        partner = jnp.where(above, team + 1, team - 1)
        there = jnp.logical_and(partner >= 0, partner < n // TEAM)
        factor = jnp.where(there, 0.25, 0.0) * sign_of(cut)
        for s in DISTANCES:
            start = team * TEAM + jnp.where(above, TEAM - PAIR_DEV, -s)
            up, down = chosen(start + edge, s)
            mine = jnp.where(above, up, down)
            inward = jnp.where(above, edge_1, PAIR_DEV - 1 - edge_1)
            active = jnp.logical_and(inward >= PAIR_DEV - s, jnp.abs(mine - block.astype(F32)) < 0.5)
            put(row + s - 1, jnp.where(active, factor, 0.0))
            apart = jnp.where(above, PAIR_DEV - s, s - PAIR_DEV)
            up, down = chosen(start + edge + apart, s)
            theirs = jnp.where(above, down, up)
            put(row + PAIR_DEV + s - 1, jnp.where(jnp.abs(theirs - block.astype(F32)) < 0.5, 1.0, 0.0))
        outward = jnp.where(above, LANES - 1 - lane_1, lane_1)
        put(row + 2 * PAIR_DEV, jnp.where(outward < EDGE, 1.0, 0.0))


def pack_kernel(suction, warmth, classes, top, out, room, class_room, turned, in_sems, out_sems):
    cells = turned.shape[-1]
    quarters = 2 * CHUNKS
    into = []
    for f, field in enumerate((suction, warmth, classes)):
        into.append(pltpu.make_async_copy(field, class_room if f == 2 else room.at[f], in_sems.at[f]))
        into[-1].start()

    def put(slot, value):
        turned[:, slot] = value.T.reshape(TEAM, OWN, cells)

    rows = [top[0:1, q * LANES : (q + 1) * LANES] for q in range(quarters)]
    put(3 * quarters, jnp.concatenate(rows + [jnp.zeros((cells - quarters, LANES), F32)], axis=0))
    for f in range(3):
        into[f].wait()
        for q in range(quarters):
            lanes = slice(q * LANES, (q + 1) * LANES)
            put(f * quarters + q, class_room[:, lanes].astype(F32) if f == 2 else room[f, :, lanes])
    sent = []
    for i in range(SENDS):
        rows = pl.ds(i * (TEAM // SENDS), TEAM // SENDS)
        sent.append(pltpu.make_async_copy(turned.at[rows], out.at[rows], out_sems.at[i]))
        sent[-1].start()
    for copy in sent:
        copy.wait()


def unpack_kernel(got, suction, warmth, room, sems):
    cells = got.shape[-1]
    quarters = 2 * CHUNKS
    sent = []
    for f, out in enumerate((suction, warmth)):
        for q in range(quarters):
            room[f, :, q * LANES : (q + 1) * LANES] = got[:, f * quarters + q].reshape(LANES, cells).T
        sent.append(pltpu.make_async_copy(room.at[f], out, sems.at[f]))
        sent[-1].start()
    for copy in sent:
        copy.wait()


def edge_shift(cut, m):
    return lax.rem(EDGE * m + jnp.where(place(cut)[1], EDGE, 0), LANES)


def halo_of(cut, value):
    part = lax.broadcasted_iota(jnp.int32, (SUB, LANES), 1) // EDGE
    packed = None
    for m in range(2 * GROUPS):
        moved = pltpu.roll(value[:, m * LANES : (m + 1) * LANES], edge_shift(cut, m), axis=1)
        packed = moved if m == 0 else jnp.where(part == m, moved, packed)
    return packed


def first_kernel(chunk, cuts, *refs):
    got, k_sat, heat_cond = refs[:3]
    head, warm, perm, conduct, wet, melt, cond, energy, top = refs[3:12]
    halos, load = refs[12 : 12 + cuts], refs[-1]
    cells = got.shape[-1]
    steps = head.shape[0]
    stride = steps * GROUPS

    for field in range(3):
        for b in range(2):
            load[field * 2 + b] = got[:, (field * 2 + b) * CHUNKS + chunk].reshape(LANES, cells).T
    surface = got[:, 6 * CHUNKS].reshape(LANES, cells).T[0:SUB]
    rows = [surface[b * CHUNKS + chunk : b * CHUNKS + chunk + 1] for b in range(2)]
    top[...] = jnp.concatenate(rows * GROUPS, axis=1)

    def fetch(field, j):
        parts = [
            load[field * 2 + b, pl.ds(g * steps + j, SUB, stride=stride), :]
            for g in range(GROUPS)
            for b in range(2)
        ]
        return jnp.concatenate(parts, axis=1)

    for j in range(steps):
        h, t, v = [fetch(field, j) for field in range(3)]
        k = jnp.full_like(v, k_sat[0])
        lam = jnp.full_like(v, heat_cond[0])
        for c in range(1, k_sat.shape[0]):
            here = v >= c
            k = jnp.where(here, k_sat[c], k)
            lam = jnp.where(here, heat_cond[c], lam)
        s, f = sigmoid(h), sigmoid(2.0 * t)
        m = 0.05 + 0.4 * s
        head[j], warm[j], perm[j], conduct[j] = h, t, k, lam
        wet[j] = s
        melt[j] = f
        cond[j] = k * (f * s * s + 0.02)
        energy[j] = (1.0 + 2.0 * m) * t + 2.0 * m * f
        for cut in range(cuts):
            for i, v in enumerate((h, t, k)):
                halos[cut][i, j] = halo_of(cut, v)


def team_kernel(masks, head, warm, cond, water, heat):
    steps = head.shape[0]
    upper = [masks[s - 1] > 0.5 for s in DISTANCES]
    lower = [masks[PAIR_DEV + s - 1] > 0.5 for s in DISTANCES]

    def step(j, _):
        for g in range(GROUPS):
            l0, l1 = lanes_of(g, 0), lanes_of(g, 1)
            h0, h1 = head[j, :, l0], head[j, :, l1]
            t0, t1 = warm[j, :, l0], warm[j, :, l1]
            c0, c1 = cond[j, :, l0], cond[j, :, l1]
            total = None
            for s in DISTANCES:
                up, low = upper[s - 1], lower[s - 1]
                back = LANES - s * OWN
                h_low = pltpu.roll(jnp.where(low, h1, h0), back, axis=1)
                t_low = pltpu.roll(jnp.where(low, t1, t0), back, axis=1)
                c_low = pltpu.roll(jnp.where(low, c1, c0), back, axis=1)
                flow = (
                    masks[2 * PAIR_DEV + s - 1]
                    * (jnp.where(up, c1, c0) + c_low)
                    * (jnp.where(up, h1, h0) - h_low + 0.5)
                )
                carried = flow * jnp.where(flow > 0.0, jnp.where(up, t1, t0), t_low)
                flow_in = pltpu.roll(flow, s * OWN, axis=1)
                carried_in = pltpu.roll(carried, s * OWN, axis=1)
                part = (
                    flow_in - flow,
                    jnp.where(low, flow_in, 0.0) - jnp.where(up, flow, 0.0),
                    carried_in - carried,
                    jnp.where(low, carried_in, 0.0) - jnp.where(up, carried, 0.0),
                )
                total = part if total is None else [a + b for a, b in zip(total, part)]
            water[j, :, l0] = total[0] - total[1]
            water[j, :, l1] = total[1]
            heat[j, :, l0] = 2.0 * (total[2] - total[3])
            heat[j, :, l1] = 2.0 * total[3]

    lax.fori_loop(0, steps, step, None)


def cross_flows(cut, masks, mine, theirs):
    row = cut_row(cut)
    sign = sign_of(cut)
    above = place(cut)[1]
    lane = lax.broadcasted_iota(jnp.int32, (SUB, LANES), 1)
    first_block = lax.rem(lane, 2 * EDGE) < EDGE
    h, t, k = mine
    c = passage(h, t, k)
    far = [theirs[0], theirs[1], passage(*theirs)]
    other = [
        jnp.where(first_block, pltpu.roll(v, LANES - EDGE, axis=1), pltpu.roll(v, EDGE, axis=1)) for v in far
    ]
    water = heat = jnp.zeros((SUB, LANES), F32)
    for s in DISTANCES:
        same = masks[row + PAIR_DEV + s - 1] > 0.5
        picked = [jnp.where(same, a, b) for a, b in zip(far, other)]
        apart = (PAIR_DEV - s) * OWN
        if apart:
            shift = jnp.where(above, apart, LANES - apart)
            picked = [pltpu.roll(v, shift, axis=1) for v in picked]
        h_far, t_far, c_far = picked
        flow = masks[row + s - 1] * (c + c_far) * (sign * (h - h_far) + 0.5)
        water = water - flow
        heat = heat - flow * jnp.where(flow > 0.0, t, t_far)
    return water, heat


def advance(steps, cuts, masks, head, warm, conduct, stored, energy, wet, melt, cond, water, heat, top,
            mine, theirs, new_head, new_warm, new_wet, inflow, warm_inflow, ratio, lead, value, finish):
    for j in range(steps):
        w_parts = [water[j, :, m * LANES : (m + 1) * LANES] for m in range(2 * GROUPS)]
        q_parts = [heat[j, :, m * LANES : (m + 1) * LANES] for m in range(2 * GROUPS)]
        for cut in range(cuts):
            beside = masks[cut_row(cut) + 2 * PAIR_DEV]
            w_far, q_far = cross_flows(cut, masks, mine(cut, j), theirs(cut, j))
            for m in range(2 * GROUPS):
                shift = lax.rem(LANES - edge_shift(cut, m), LANES)
                w_parts[m] = w_parts[m] + beside * pltpu.roll(w_far, shift, axis=1)
                q_parts[m] = q_parts[m] + 2.0 * beside * pltpu.roll(q_far, shift, axis=1)
        for m in range(2 * GROUPS):
            inflow[j, :, m * LANES : (m + 1) * LANES] = w_parts[m]
            warm_inflow[j, :, m * LANES : (m + 1) * LANES] = q_parts[m]

    part = lax.broadcasted_iota(jnp.int32, (SUB, ALL), 0)
    group = lax.broadcasted_iota(jnp.int32, (SUB, ALL), 1) // WIDTH
    first_part = jnp.logical_and(part == 0, group == 0)
    last_part = jnp.logical_and(part == SUB - 1, group == GROUPS - 1)

    def faces(fields, potential):
        face_of, rise_of = [], []
        for j in range(steps):
            if j + 1 < steps:
                c_next, v_next = fields[j + 1], potential[j + 1]
                face = 0.5 * (fields[j] + c_next)
            else:
                c_next, v_next = following(fields[0]), following(potential[0])
                face = jnp.where(last_part, 0.0, 0.5 * (fields[j] + c_next))
            face_of.append(face)
            rise_of.append(v_next - potential[j])
        return face_of, rise_of

    k_face, rise = faces([cond[j] for j in range(steps)], head)
    k_top = jnp.where(first_part, 0.0, preceding(k_face[-1]))
    q_face = [k * (1.0 - d) for k, d in zip(k_face, rise)]
    q_top = jnp.where(first_part, 0.0, preceding(q_face[-1]))

    def water_matrix(j):
        above = k_top if j == 0 else k_face[j - 1]
        into = q_top if j == 0 else q_face[j - 1]
        s = wet[j]
        main = 0.8 * s * (1.0 - s) + 0.02 + above + k_face[j]
        source = inflow[j] + into - q_face[j] - 0.8 * (s - stored[j])
        return above, main, k_face[j], source

    def water_done(j, x):
        h = head[j] + x
        new_head[j] = h
        new_wet[j] = sigmoid(h)

    solve(steps, water_matrix, ratio, lead, value, water_done)

    l_cell = [conduct[j] * (1.5 - 0.5 * melt[j]) for j in range(steps)]
    l_face, rise = faces(l_cell, warm)
    l_top = jnp.where(first_part, 0.0, preceding(l_face[-1]))
    g_face = [l * d for l, d in zip(l_face, rise)]
    g_top = jnp.where(first_part, 0.0, preceding(g_face[-1]))
    surface_lam = jnp.where(first_part, 2.0 * l_cell[0], 0.0)

    def heat_matrix(j):
        above = l_top if j == 0 else l_face[j - 1]
        out_of = g_top if j == 0 else g_face[j - 1]
        t, f = warm[j], melt[j]
        m2 = 0.1 + 0.8 * new_wet[j]
        now = (1.0 + m2) * t + m2 * f
        main = 2.0 + 2.0 * m2 * (1.0 + 2.0 * f * (1.0 - f)) + above + l_face[j]
        source = warm_inflow[j] - out_of + g_face[j] - 2.0 * (now - energy[j])
        if j == 0:
            main = main + surface_lam
            source = source + surface_lam * (top[...] - t)
        return above, main, l_face[j], source

    def heat_done(j, x):
        t = warm[j] + x
        new_warm[j] = t
        finish(j, t)

    solve(steps, heat_matrix, ratio, lead, value, heat_done)


def middle_kernel(cuts, *refs):
    masks, head, warm, perm, conduct, wet, melt, cond, energy, top, water, heat = refs[:12]
    own, far = refs[12 : 12 + cuts], refs[12 + cuts : 12 + 2 * cuts]
    new_head, new_warm, new_wet, new_melt, new_cond = refs[12 + 2 * cuts : 17 + 2 * cuts]
    halos = refs[17 + 2 * cuts : 17 + 3 * cuts]
    inflow, warm_inflow, ratio, lead, value = refs[17 + 3 * cuts :]

    def finish(j, t):
        s, f = new_wet[j], sigmoid(2.0 * t)
        new_melt[j] = f
        new_cond[j] = perm[j] * (f * s * s + 0.02)
        for cut in range(cuts):
            halos[cut][0, j] = halo_of(cut, new_head[j])
            halos[cut][1, j] = halo_of(cut, t)

    advance(
        head.shape[0], cuts, masks, head, warm, conduct, wet, energy, wet, melt, cond, water, heat, top,
        lambda cut, j: [own[cut][i, j] for i in range(3)],
        lambda cut, j: [far[cut][i, j] for i in range(3)],
        new_head, new_warm, new_wet, inflow, warm_inflow, ratio, lead, value, finish,
    )


def last_kernel(chunk, cuts, *refs):
    masks, head, warm, conduct, stored, wet, melt, cond, energy, top, water, heat = refs[:12]
    own, far = refs[12 : 12 + cuts], refs[12 + cuts : 12 + 2 * cuts]
    own_k, far_k = refs[12 + 2 * cuts : 12 + 3 * cuts], refs[12 + 3 * cuts : 12 + 4 * cuts]
    others = refs[12 + 4 * cuts : -10]
    out, new_head, new_warm, new_wet, inflow, warm_inflow, ratio, lead, value, load = refs[-10:]
    steps = head.shape[0]
    cells = steps * GROUPS * SUB
    stride = steps * GROUPS
    advance(
        steps, cuts, masks, head, warm, conduct, stored, energy, wet, melt, cond, water, heat, top,
        lambda cut, j: [own[cut][0, j], own[cut][1, j], own_k[cut][2, j]],
        lambda cut, j: [far[cut][0, j], far[cut][1, j], far_k[cut][2, j]],
        new_head, new_warm, new_wet, inflow, warm_inflow, ratio, lead, value, lambda j, t: None,
    )
    final = chunk == CHUNKS - 1
    for f, field in enumerate((new_head, new_warm)):
        for b in range(2):
            slot = f * 2 + b
            for j in range(steps):
                for g in range(GROUPS):
                    load[slot, pl.ds(g * steps + j, SUB, stride=stride), :] = field[j, :, lanes_of(g, b)]
            turned = load[slot].T.reshape(TEAM, OWN, cells)
            if final:
                out[:, slot * CHUNKS + chunk] = turned
                for c, other in enumerate(others):
                    out[:, slot * CHUNKS + c] = other[:, slot]
            else:
                out[:, slot] = turned


def whole(memory=pltpu.VMEM):
    return pl.BlockSpec(memory_space=memory)


def call(kernel, name, args, outs, scratch=(), specs=None, out_specs=None, limit=VMEM_LIMIT, work=2_000_000):
    return pl.pallas_call(
        kernel,
        out_shape=[jax.ShapeDtypeStruct(shape, F32) for shape in outs],
        in_specs=specs or [whole()] * len(args),
        out_specs=out_specs or [whole()] * len(outs),
        scratch_shapes=scratch,
        compiler_params=pltpu.CompilerParams(vmem_limit_bytes=limit),
        cost_estimate=pl.CostEstimate(flops=work, bytes_accessed=work, transcendentals=0),
        name=name,
    )(*args)


def exchange(tiles, n):
    teams = [list(range(start, start + TEAM)) for start in range(0, n, TEAM)]
    return lax.all_to_all(
        tiles, "cols", split_axis=0, concat_axis=0, tiled=True, axis_index_groups=teams
    )


def swap(cut, n, value):
    pairs = []
    for team in range(cut, n // TEAM - 1, 2):
        for i in range(team * TEAM, (team + 1) * TEAM):
            pairs += [(i, i + TEAM), (i + TEAM, i)]
    return lax.ppermute(value, "cols", pairs)


def on_device(suction, warmth, classes, top, couplings, k_sat, heat_cond):
    n = lax.axis_size("cols")
    cells, width = suction.shape
    steps = cells // (SUB * GROUPS)
    quarters = width // LANES
    cuts = cut_count(n)
    column = (steps, SUB, ALL)
    halo = (steps, SUB, LANES)
    room = pltpu.VMEM(column, F32)
    smem = whole(pltpu.SMEM)
    hbm = whole(pltpu.HBM)

    masks = call(
        functools.partial(mask_kernel, n), "masks", (couplings,), [(mask_rows(cuts), SUB, LANES)]
    )[0]
    packed = call(
        pack_kernel,
        "pack",
        (suction, warmth, classes, top.reshape(1, width)),
        [(TEAM, 3 * quarters + 1, OWN, cells)],
        scratch=[
            pltpu.VMEM((2, cells, width), F32),
            pltpu.VMEM((cells, width), classes.dtype),
            pltpu.VMEM((TEAM, 3 * quarters + 1, OWN, cells), F32),
            pltpu.SemaphoreType.DMA((3,)),
            pltpu.SemaphoreType.DMA((SENDS,)),
        ],
        specs=[hbm, hbm, hbm, whole()],
        out_specs=[hbm],
        limit=PACK_LIMIT,
    )[0]
    got = exchange(packed, n)

    first, sides = [], []
    for c in range(CHUNKS):
        values = call(
            functools.partial(first_kernel, c, cuts),
            "first",
            (got, k_sat, heat_cond),
            [column] * 8 + [(1, ALL)] + [(3,) + halo] * cuts,
            scratch=[pltpu.VMEM((6, cells, LANES), F32)],
            specs=[whole(), smem, smem],
        )
        first.append(values[:9])
        mine = values[9:]
        sides.append((mine, [swap(cut, n, v) for cut, v in enumerate(mine)]))

    second, later = [], []
    for c in range(CHUNKS):
        head, warm, perm, conduct, wet, melt, cond, energy, surface = first[c]
        water, heat = call(team_kernel, "team", (masks, head, warm, cond), [column] * 2)
        mine, theirs = sides[c]
        values = call(
            functools.partial(middle_kernel, cuts),
            "middle",
            (masks, head, warm, perm, conduct, wet, melt, cond, energy, surface, water, heat, *mine, *theirs),
            [column] * 5 + [(2,) + halo] * cuts,
            scratch=[room] * 5,
        )
        second.append(values[:5])
        mine = values[5:]
        later.append((mine, [swap(cut, n, v) for cut, v in enumerate(mine)]))

    done = []
    for c in range(CHUNKS):
        conduct, stored, energy, surface = first[c][3], first[c][4], first[c][7], first[c][8]
        head, warm, wet, melt, cond = second[c]
        water, heat = call(team_kernel, "team", (masks, head, warm, cond), [column] * 2)
        mine, theirs = later[c]
        mine_k, theirs_k = sides[c]
        final = c == CHUNKS - 1
        done += call(
            functools.partial(last_kernel, c, cuts),
            "last",
            (
                masks, head, warm, conduct, stored, wet, melt, cond, energy, surface, water, heat,
                *mine, *theirs, *mine_k, *theirs_k, *(done if final else ()),
            ),
            [(TEAM, 2 * quarters if final else 4, OWN, cells)],
            scratch=[room] * 8 + [pltpu.VMEM((4, cells, LANES), F32)],
        )
    back = exchange(done[-1], n)
    return tuple(
        call(
            unpack_kernel,
            "unpack",
            (back,),
            [(cells, width)] * 2,
            scratch=[
                pltpu.VMEM((2, cells, width), F32),
                pltpu.SemaphoreType.DMA((2,)),
            ],
            out_specs=[hbm, hbm],
        )
    )


def solution(mesh):
    placed = (P(None, "cols"), P(None, "cols"), P(None, "cols"), P("cols"), P(), P(), P())
    return jax.shard_map(
        on_device,
        mesh=mesh,
        in_specs=placed,
        out_specs=(P(None, "cols"), P(None, "cols")),
        check_vma=False,
    )
```

```python
import functools

import jax
import jax.numpy as jnp
from jax import lax
from jax.experimental import pallas as pl
from jax.experimental.pallas import tpu as pltpu
from jax.sharding import PartitionSpec as P

SPAN = 256
PAIR_DEV = 4
LANES = 128
CHUNKS = SPAN // LANES
TEAM = 16
OWN = LANES // TEAM
SUB = 8
GROUPS = 2
WIDTH = 2 * LANES
ALL = GROUPS * WIDTH
EDGE = PAIR_DEV * OWN
VMEM_LIMIT = 32 * 1024 * 1024
PACK_LIMIT = 60 * 1024 * 1024
DISTANCES = range(1, PAIR_DEV + 1)
SENDS = 4
F32 = jnp.float32


def cut_count(n):
    return min(n // TEAM - 1, 2)


def place(cut):
    team = lax.axis_index("cols") // TEAM
    return team, lax.rem(team, 2) == cut


def sign_of(cut):
    return jnp.where(place(cut)[1], 1.0, -1.0).astype(F32)


def reciprocal(x):
    r = pl.reciprocal(x, approx=True)
    return r * (2.0 - x * r)


def sigmoid(x):
    return 0.5 + 0.5 * jnp.tanh(0.5 * x)


def passage(h, t, k):
    s = sigmoid(h)
    return k * (sigmoid(2.0 * t) * s * s + 0.02)


def lanes_of(g, b):
    return slice((g * 2 + b) * LANES, (g * 2 + b + 1) * LANES)


def following(value):
    first, second = value[:, :WIDTH], value[:, WIDTH:]
    return jnp.concatenate([second, pltpu.roll(first, SUB - 1, axis=0)], axis=1)


def preceding(value):
    first, second = value[:, :WIDTH], value[:, WIDTH:]
    return jnp.concatenate([pltpu.roll(second, 1, axis=0), first], axis=1)


def solve(steps, matrix, ratio, lead, value, update):
    c_prev = a_prev = d_prev = None
    for j in range(steps):
        above, main, below, source = matrix(j)
        if j == 0:
            r = reciprocal(main)
            a_prev = above * r
            d_prev = source * r
        else:
            r = reciprocal(main - above * c_prev)
            over = above * r
            a_prev = a_prev * over
            d_prev = source * r + d_prev * over
        c_prev = below * r
        ratio[j] = c_prev
        lead[j] = a_prev
        value[j] = d_prev
    last_c, last_a, last_d = c_prev, a_prev, d_prev
    p_first, a_first, d_first = ratio[steps - 2], lead[steps - 2], value[steps - 2]
    for j in range(steps - 3, -1, -1):
        c = ratio[j]
        p_first = c * p_first
        a_first = lead[j] + c * a_first
        d_first = value[j] + c * d_first
    g = reciprocal(1.0 - last_c * following(a_first))
    up = last_c * following(p_first) * g
    down = last_a * g
    own = (last_d + last_c * following(d_first)) * g
    step = 0
    while step < SUB:
        if step == 0:
            after, before = following, preceding
        else:
            after = functools.partial(pltpu.roll, shift=SUB - step, axis=0)
            before = functools.partial(pltpu.roll, shift=step, axis=0)
        g = reciprocal(1.0 - up * after(down) - down * before(up))
        own = (own + up * after(own) + down * before(own)) * g
        up = up * after(up) * g
        down = down * before(down) * g
        step = max(1, 2 * step)
    over = preceding(own)
    x = own
    update(steps - 1, x)
    for j in range(steps - 2, -1, -1):
        x = ratio[j] * x + (lead[j] * over + value[j])
        update(j, x)


def mask_rows(cuts):
    return 3 * PAIR_DEV + cuts * (2 * PAIR_DEV + 1)


def cut_row(cut):
    return 3 * PAIR_DEV + cut * (2 * PAIR_DEV + 1)


def mask_kernel(n, couplings, out):
    pair_rows = couplings[...].astype(F32)
    pairs = couplings.shape[1]
    pair_id = lax.broadcasted_iota(jnp.int32, (pairs, LANES), 0)
    lane = lax.broadcasted_iota(jnp.int32, (pairs, LANES), 1)
    lane_1 = lax.broadcasted_iota(jnp.int32, (SUB, LANES), 1)

    def chosen(dev, s):
        at = (pair_id == dev * PAIR_DEV + s - 1).astype(F32)
        found = jnp.dot(pair_rows, at, preferred_element_type=F32)
        return found[0:1], found[1:2]

    def put(row, value):
        out[row] = jnp.broadcast_to(value, (SUB, LANES))

    team = lax.axis_index("cols") // TEAM
    dev = team * TEAM + lane // OWN
    for s in DISTANCES:
        put(s - 1, chosen(dev, s)[0])
        put(PAIR_DEV + s - 1, chosen(dev - s, s)[1])
        put(2 * PAIR_DEV + s - 1, jnp.where(lane_1 // OWN + s < TEAM, 0.25, 0.0))
    block = lax.rem(lane_1 // EDGE, 2)
    edge = lax.rem(lane, EDGE) // OWN
    edge_1 = lax.rem(lane_1, EDGE) // OWN
    for cut in range(cut_count(n)):
        _, above = place(cut)
        row = cut_row(cut)
        partner = jnp.where(above, team + 1, team - 1)
        there = jnp.logical_and(partner >= 0, partner < n // TEAM)
        factor = jnp.where(there, 0.25, 0.0) * sign_of(cut)
        for s in DISTANCES:
            start = team * TEAM + jnp.where(above, TEAM - PAIR_DEV, -s)
            up, down = chosen(start + edge, s)
            mine = jnp.where(above, up, down)
            inward = jnp.where(above, edge_1, PAIR_DEV - 1 - edge_1)
            active = jnp.logical_and(inward >= PAIR_DEV - s, jnp.abs(mine - block.astype(F32)) < 0.5)
            put(row + s - 1, jnp.where(active, factor, 0.0))
            apart = jnp.where(above, PAIR_DEV - s, s - PAIR_DEV)
            up, down = chosen(start + edge + apart, s)
            theirs = jnp.where(above, down, up)
            put(row + PAIR_DEV + s - 1, jnp.where(jnp.abs(theirs - block.astype(F32)) < 0.5, 1.0, 0.0))
        outward = jnp.where(above, LANES - 1 - lane_1, lane_1)
        put(row + 2 * PAIR_DEV, jnp.where(outward < EDGE, 1.0, 0.0))


def pack_kernel(suction, warmth, classes, top, out, room, class_room, turned, in_sems, out_sems):
    cells = turned.shape[-1]
    quarters = 2 * CHUNKS
    into = []
    for f, field in enumerate((suction, warmth, classes)):
        into.append(pltpu.make_async_copy(field, class_room if f == 2 else room.at[f], in_sems.at[f]))
        into[-1].start()

    def put(slot, value):
        turned[:, slot] = value.T.reshape(TEAM, OWN, cells)

    rows = [top[0:1, q * LANES : (q + 1) * LANES] for q in range(quarters)]
    put(3 * quarters, jnp.concatenate(rows + [jnp.zeros((cells - quarters, LANES), F32)], axis=0))
    for f in range(3):
        into[f].wait()
        for q in range(quarters):
            lanes = slice(q * LANES, (q + 1) * LANES)
            put(f * quarters + q, class_room[:, lanes].astype(F32) if f == 2 else room[f, :, lanes])
    sent = []
    for i in range(SENDS):
        rows = pl.ds(i * (TEAM // SENDS), TEAM // SENDS)
        sent.append(pltpu.make_async_copy(turned.at[rows], out.at[rows], out_sems.at[i]))
        sent[-1].start()
    for copy in sent:
        copy.wait()


def unpack_kernel(got, suction, warmth, room, sems):
    cells = got.shape[-1]
    quarters = 2 * CHUNKS
    sent = []
    for f, out in enumerate((suction, warmth)):
        for q in range(quarters):
            room[f, :, q * LANES : (q + 1) * LANES] = got[:, f * quarters + q].reshape(LANES, cells).T
        sent.append(pltpu.make_async_copy(room.at[f], out, sems.at[f]))
        sent[-1].start()
    for copy in sent:
        copy.wait()


def edge_shift(cut, m):
    return lax.rem(EDGE * m + jnp.where(place(cut)[1], EDGE, 0), LANES)


def halo_of(cut, value):
    part = lax.broadcasted_iota(jnp.int32, (SUB, LANES), 1) // EDGE
    packed = None
    for m in range(2 * GROUPS):
        moved = pltpu.roll(value[:, m * LANES : (m + 1) * LANES], edge_shift(cut, m), axis=1)
        packed = moved if m == 0 else jnp.where(part == m, moved, packed)
    return packed


def edge_kernel(cuts, got, k_sat, *refs):
    halos, load = refs[:-1], refs[-1]
    cells = got.shape[-1]
    steps = halos[0].shape[1]
    stride = steps * GROUPS
    second = lax.broadcasted_iota(jnp.int32, (SUB, LANES), 1) >= 2 * EDGE
    for chunk in range(CHUNKS):
        for cut in range(cuts):
            start = jnp.where(place(cut)[1], TEAM - PAIR_DEV, 0)
            for f in range(3):
                rows = [
                    got[pl.ds(start, PAIR_DEV), (f * 2 + b) * CHUNKS + chunk].reshape(EDGE, cells)
                    for b in range(2)
                ]
                slot = (chunk * cuts + cut) * 3 + f
                load[slot] = jnp.concatenate(rows * GROUPS, axis=0).T
    for chunk in range(CHUNKS):
        for cut in range(cuts):
            for f in range(3):
                slot = (chunk * cuts + cut) * 3 + f
                for j in range(steps):
                    v = jnp.where(
                        second,
                        load[slot, pl.ds(steps + j, SUB, stride=stride), :],
                        load[slot, pl.ds(j, SUB, stride=stride), :],
                    )
                    if f == 2:
                        k = jnp.full_like(v, k_sat[0])
                        for c in range(1, k_sat.shape[0]):
                            k = jnp.where(v >= c, k_sat[c], k)
                        v = k
                    halos[chunk * cuts + cut][f, j] = v


def first_kernel(
    chunk, got, k_sat, heat_cond, head, warm, perm, conduct, wet, melt, cond, energy, top, load
):
    cells = got.shape[-1]
    steps = head.shape[0]
    stride = steps * GROUPS

    for field in range(3):
        for b in range(2):
            load[field * 2 + b] = got[:, (field * 2 + b) * CHUNKS + chunk].reshape(LANES, cells).T
    surface = got[:, 6 * CHUNKS].reshape(LANES, cells).T[0:SUB]
    rows = [surface[b * CHUNKS + chunk : b * CHUNKS + chunk + 1] for b in range(2)]
    top[...] = jnp.concatenate(rows * GROUPS, axis=1)

    def fetch(field, j):
        parts = [
            load[field * 2 + b, pl.ds(g * steps + j, SUB, stride=stride), :]
            for g in range(GROUPS)
            for b in range(2)
        ]
        return jnp.concatenate(parts, axis=1)

    for j in range(steps):
        h, t, v = [fetch(field, j) for field in range(3)]
        k = jnp.full_like(v, k_sat[0])
        lam = jnp.full_like(v, heat_cond[0])
        for c in range(1, k_sat.shape[0]):
            here = v >= c
            k = jnp.where(here, k_sat[c], k)
            lam = jnp.where(here, heat_cond[c], lam)
        s, f = sigmoid(h), sigmoid(2.0 * t)
        m = 0.05 + 0.4 * s
        head[j], warm[j], perm[j], conduct[j] = h, t, k, lam
        wet[j] = s
        melt[j] = f
        cond[j] = k * (f * s * s + 0.02)
        energy[j] = (1.0 + 2.0 * m) * t + 2.0 * m * f


def team_kernel(masks, head, warm, cond, water, heat):
    steps = head.shape[0]
    upper = [masks[s - 1] > 0.5 for s in DISTANCES]
    lower = [masks[PAIR_DEV + s - 1] > 0.5 for s in DISTANCES]

    def step(j, _):
        for g in range(GROUPS):
            l0, l1 = lanes_of(g, 0), lanes_of(g, 1)
            h0, h1 = head[j, :, l0], head[j, :, l1]
            t0, t1 = warm[j, :, l0], warm[j, :, l1]
            c0, c1 = cond[j, :, l0], cond[j, :, l1]
            total = None
            for s in DISTANCES:
                up, low = upper[s - 1], lower[s - 1]
                back = LANES - s * OWN
                h_low = pltpu.roll(jnp.where(low, h1, h0), back, axis=1)
                t_low = pltpu.roll(jnp.where(low, t1, t0), back, axis=1)
                c_low = pltpu.roll(jnp.where(low, c1, c0), back, axis=1)
                flow = (
                    masks[2 * PAIR_DEV + s - 1]
                    * (jnp.where(up, c1, c0) + c_low)
                    * (jnp.where(up, h1, h0) - h_low + 0.5)
                )
                carried = flow * jnp.where(flow > 0.0, jnp.where(up, t1, t0), t_low)
                flow_in = pltpu.roll(flow, s * OWN, axis=1)
                carried_in = pltpu.roll(carried, s * OWN, axis=1)
                part = (
                    flow_in - flow,
                    jnp.where(low, flow_in, 0.0) - jnp.where(up, flow, 0.0),
                    carried_in - carried,
                    jnp.where(low, carried_in, 0.0) - jnp.where(up, carried, 0.0),
                )
                total = part if total is None else [a + b for a, b in zip(total, part)]
            water[j, :, l0] = total[0] - total[1]
            water[j, :, l1] = total[1]
            heat[j, :, l0] = 2.0 * (total[2] - total[3])
            heat[j, :, l1] = 2.0 * total[3]

    lax.fori_loop(0, steps, step, None)


def cross_flows(cut, masks, mine, theirs):
    row = cut_row(cut)
    sign = sign_of(cut)
    above = place(cut)[1]
    lane = lax.broadcasted_iota(jnp.int32, (SUB, LANES), 1)
    first_block = lax.rem(lane, 2 * EDGE) < EDGE
    h, t, k = mine
    c = passage(h, t, k)
    far = [theirs[0], theirs[1], passage(*theirs)]
    other = [
        jnp.where(first_block, pltpu.roll(v, LANES - EDGE, axis=1), pltpu.roll(v, EDGE, axis=1)) for v in far
    ]
    water = heat = jnp.zeros((SUB, LANES), F32)
    for s in DISTANCES:
        same = masks[row + PAIR_DEV + s - 1] > 0.5
        picked = [jnp.where(same, a, b) for a, b in zip(far, other)]
        apart = (PAIR_DEV - s) * OWN
        if apart:
            shift = jnp.where(above, apart, LANES - apart)
            picked = [pltpu.roll(v, shift, axis=1) for v in picked]
        h_far, t_far, c_far = picked
        flow = masks[row + s - 1] * (c + c_far) * (sign * (h - h_far) + 0.5)
        water = water - flow
        heat = heat - flow * jnp.where(flow > 0.0, t, t_far)
    return water, heat


def advance(steps, cuts, masks, head, warm, conduct, stored, energy, wet, melt, cond, water, heat, top,
            mine, theirs, new_head, new_warm, new_wet, inflow, warm_inflow, ratio, lead, value, finish):
    for j in range(steps):
        w_parts = [water[j, :, m * LANES : (m + 1) * LANES] for m in range(2 * GROUPS)]
        q_parts = [heat[j, :, m * LANES : (m + 1) * LANES] for m in range(2 * GROUPS)]
        for cut in range(cuts):
            beside = masks[cut_row(cut) + 2 * PAIR_DEV]
            w_far, q_far = cross_flows(cut, masks, mine(cut, j), theirs(cut, j))
            for m in range(2 * GROUPS):
                shift = lax.rem(LANES - edge_shift(cut, m), LANES)
                w_parts[m] = w_parts[m] + beside * pltpu.roll(w_far, shift, axis=1)
                q_parts[m] = q_parts[m] + 2.0 * beside * pltpu.roll(q_far, shift, axis=1)
        for m in range(2 * GROUPS):
            inflow[j, :, m * LANES : (m + 1) * LANES] = w_parts[m]
            warm_inflow[j, :, m * LANES : (m + 1) * LANES] = q_parts[m]

    part = lax.broadcasted_iota(jnp.int32, (SUB, ALL), 0)
    group = lax.broadcasted_iota(jnp.int32, (SUB, ALL), 1) // WIDTH
    first_part = jnp.logical_and(part == 0, group == 0)
    last_part = jnp.logical_and(part == SUB - 1, group == GROUPS - 1)

    def faces(fields, potential):
        face_of, rise_of = [], []
        for j in range(steps):
            if j + 1 < steps:
                c_next, v_next = fields[j + 1], potential[j + 1]
                face = 0.5 * (fields[j] + c_next)
            else:
                c_next, v_next = following(fields[0]), following(potential[0])
                face = jnp.where(last_part, 0.0, 0.5 * (fields[j] + c_next))
            face_of.append(face)
            rise_of.append(v_next - potential[j])
        return face_of, rise_of

    k_face, rise = faces([cond[j] for j in range(steps)], head)
    k_top = jnp.where(first_part, 0.0, preceding(k_face[-1]))
    q_face = [k * (1.0 - d) for k, d in zip(k_face, rise)]
    q_top = jnp.where(first_part, 0.0, preceding(q_face[-1]))

    def water_matrix(j):
        above = k_top if j == 0 else k_face[j - 1]
        into = q_top if j == 0 else q_face[j - 1]
        s = wet[j]
        main = 0.8 * s * (1.0 - s) + 0.02 + above + k_face[j]
        source = inflow[j] + into - q_face[j] - 0.8 * (s - stored[j])
        return above, main, k_face[j], source

    def water_done(j, x):
        h = head[j] + x
        new_head[j] = h
        new_wet[j] = sigmoid(h)

    solve(steps, water_matrix, ratio, lead, value, water_done)

    l_cell = [conduct[j] * (1.5 - 0.5 * melt[j]) for j in range(steps)]
    l_face, rise = faces(l_cell, warm)
    l_top = jnp.where(first_part, 0.0, preceding(l_face[-1]))
    g_face = [l * d for l, d in zip(l_face, rise)]
    g_top = jnp.where(first_part, 0.0, preceding(g_face[-1]))
    surface_lam = jnp.where(first_part, 2.0 * l_cell[0], 0.0)

    def heat_matrix(j):
        above = l_top if j == 0 else l_face[j - 1]
        out_of = g_top if j == 0 else g_face[j - 1]
        t, f = warm[j], melt[j]
        m2 = 0.1 + 0.8 * new_wet[j]
        now = (1.0 + m2) * t + m2 * f
        main = 2.0 + 2.0 * m2 * (1.0 + 2.0 * f * (1.0 - f)) + above + l_face[j]
        source = warm_inflow[j] - out_of + g_face[j] - 2.0 * (now - energy[j])
        if j == 0:
            main = main + surface_lam
            source = source + surface_lam * (top[...] - t)
        return above, main, l_face[j], source

    def heat_done(j, x):
        t = warm[j] + x
        new_warm[j] = t
        finish(j, t)

    solve(steps, heat_matrix, ratio, lead, value, heat_done)


def middle_kernel(cuts, *refs):
    masks, head, warm, perm, conduct, wet, melt, cond, energy, top, water, heat = refs[:12]
    own, far = refs[12 : 12 + cuts], refs[12 + cuts : 12 + 2 * cuts]
    new_head, new_warm, new_wet, new_melt, new_cond = refs[12 + 2 * cuts : 17 + 2 * cuts]
    halos = refs[17 + 2 * cuts : 17 + 3 * cuts]
    inflow, warm_inflow, ratio, lead, value = refs[17 + 3 * cuts :]

    def finish(j, t):
        s, f = new_wet[j], sigmoid(2.0 * t)
        new_melt[j] = f
        new_cond[j] = perm[j] * (f * s * s + 0.02)
        for cut in range(cuts):
            halos[cut][0, j] = halo_of(cut, new_head[j])
            halos[cut][1, j] = halo_of(cut, t)

    advance(
        head.shape[0], cuts, masks, head, warm, conduct, wet, energy, wet, melt, cond, water, heat, top,
        lambda cut, j: [own[cut][i, j] for i in range(3)],
        lambda cut, j: [far[cut][i, j] for i in range(3)],
        new_head, new_warm, new_wet, inflow, warm_inflow, ratio, lead, value, finish,
    )


def last_kernel(chunk, cuts, *refs):
    masks, head, warm, conduct, stored, wet, melt, cond, energy, top, water, heat = refs[:12]
    own, far = refs[12 : 12 + cuts], refs[12 + cuts : 12 + 2 * cuts]
    own_k, far_k = refs[12 + 2 * cuts : 12 + 3 * cuts], refs[12 + 3 * cuts : 12 + 4 * cuts]
    others = refs[12 + 4 * cuts : -10]
    out, new_head, new_warm, new_wet, inflow, warm_inflow, ratio, lead, value, load = refs[-10:]
    steps = head.shape[0]
    cells = steps * GROUPS * SUB
    stride = steps * GROUPS
    advance(
        steps, cuts, masks, head, warm, conduct, stored, energy, wet, melt, cond, water, heat, top,
        lambda cut, j: [own[cut][0, j], own[cut][1, j], own_k[cut][2, j]],
        lambda cut, j: [far[cut][0, j], far[cut][1, j], far_k[cut][2, j]],
        new_head, new_warm, new_wet, inflow, warm_inflow, ratio, lead, value, lambda j, t: None,
    )
    final = chunk == CHUNKS - 1
    for f, field in enumerate((new_head, new_warm)):
        for b in range(2):
            slot = f * 2 + b
            for j in range(steps):
                for g in range(GROUPS):
                    load[slot, pl.ds(g * steps + j, SUB, stride=stride), :] = field[j, :, lanes_of(g, b)]
            turned = load[slot].T.reshape(TEAM, OWN, cells)
            if final:
                out[:, slot * CHUNKS + chunk] = turned
                for c, other in enumerate(others):
                    out[:, slot * CHUNKS + c] = other[:, slot]
            else:
                out[:, slot] = turned


def whole(memory=pltpu.VMEM):
    return pl.BlockSpec(memory_space=memory)


def call(kernel, name, args, outs, scratch=(), specs=None, out_specs=None, limit=VMEM_LIMIT, work=2_000_000):
    return pl.pallas_call(
        kernel,
        out_shape=[jax.ShapeDtypeStruct(shape, F32) for shape in outs],
        in_specs=specs or [whole()] * len(args),
        out_specs=out_specs or [whole()] * len(outs),
        scratch_shapes=scratch,
        compiler_params=pltpu.CompilerParams(vmem_limit_bytes=limit),
        cost_estimate=pl.CostEstimate(flops=work, bytes_accessed=work, transcendentals=0),
        name=name,
    )(*args)


def exchange(tiles, n):
    teams = [list(range(start, start + TEAM)) for start in range(0, n, TEAM)]
    return lax.all_to_all(
        tiles, "cols", split_axis=0, concat_axis=0, tiled=True, axis_index_groups=teams
    )


def swap(cut, n, value):
    pairs = []
    for team in range(cut, n // TEAM - 1, 2):
        for i in range(team * TEAM, (team + 1) * TEAM):
            pairs += [(i, i + TEAM), (i + TEAM, i)]
    return lax.ppermute(value, "cols", pairs)


def on_device(suction, warmth, classes, top, couplings, k_sat, heat_cond):
    n = lax.axis_size("cols")
    cells, width = suction.shape
    steps = cells // (SUB * GROUPS)
    quarters = width // LANES
    cuts = cut_count(n)
    column = (steps, SUB, ALL)
    halo = (steps, SUB, LANES)
    room = pltpu.VMEM(column, F32)
    smem = whole(pltpu.SMEM)
    hbm = whole(pltpu.HBM)

    masks = call(
        functools.partial(mask_kernel, n), "masks", (couplings,), [(mask_rows(cuts), SUB, LANES)]
    )[0]
    packed = call(
        pack_kernel,
        "pack",
        (suction, warmth, classes, top.reshape(1, width)),
        [(TEAM, 3 * quarters + 1, OWN, cells)],
        scratch=[
            pltpu.VMEM((2, cells, width), F32),
            pltpu.VMEM((cells, width), classes.dtype),
            pltpu.VMEM((TEAM, 3 * quarters + 1, OWN, cells), F32),
            pltpu.SemaphoreType.DMA((3,)),
            pltpu.SemaphoreType.DMA((SENDS,)),
        ],
        specs=[hbm, hbm, hbm, whole()],
        out_specs=[hbm],
        limit=PACK_LIMIT,
    )[0]
    got = exchange(packed, n)

    edges = call(
        functools.partial(edge_kernel, cuts),
        "edges",
        (got, k_sat),
        [(3,) + halo] * (CHUNKS * cuts),
        scratch=[pltpu.VMEM((3 * CHUNKS * cuts, cells, LANES), F32)],
        specs=[whole(), smem],
    )
    first = [
        call(
            functools.partial(first_kernel, c),
            "first",
            (got, k_sat, heat_cond),
            [column] * 8 + [(1, ALL)],
            scratch=[pltpu.VMEM((6, cells, LANES), F32)],
            specs=[whole(), smem, smem],
        )
        for c in range(CHUNKS)
    ]
    flows, sides = [], []
    for c in range(CHUNKS):
        mine = tuple(edges[c * cuts : (c + 1) * cuts])
        if c:
            mine, flows[-1] = lax.optimization_barrier((mine, flows[-1]))
        sides.append((mine, [swap(cut, n, v) for cut, v in enumerate(mine)]))
        flows.append(tuple(call(team_kernel, "team", (masks, first[c][0], first[c][1], first[c][6]), [column] * 2)))

    second, later = [], []
    for c in range(CHUNKS):
        head, warm, perm, conduct, wet, melt, cond, energy, surface = first[c]
        water, heat = flows[c]
        mine, theirs = sides[c]
        values = call(
            functools.partial(middle_kernel, cuts),
            "middle",
            (masks, head, warm, perm, conduct, wet, melt, cond, energy, surface, water, heat, *mine, *theirs),
            [column] * 5 + [(2,) + halo] * cuts,
            scratch=[room] * 5,
        )
        second.append(values[:5])
        mine = values[5:]
        later.append((mine, [swap(cut, n, v) for cut, v in enumerate(mine)]))

    done = []
    for c in range(CHUNKS):
        conduct, stored, energy, surface = first[c][3], first[c][4], first[c][7], first[c][8]
        head, warm, wet, melt, cond = second[c]
        water, heat = call(team_kernel, "team", (masks, head, warm, cond), [column] * 2)
        mine, theirs = later[c]
        mine_k, theirs_k = sides[c]
        final = c == CHUNKS - 1
        done += call(
            functools.partial(last_kernel, c, cuts),
            "last",
            (
                masks, head, warm, conduct, stored, wet, melt, cond, energy, surface, water, heat,
                *mine, *theirs, *mine_k, *theirs_k, *(done if final else ()),
            ),
            [(TEAM, 2 * quarters if final else 4, OWN, cells)],
            scratch=[room] * 8 + [pltpu.VMEM((4, cells, LANES), F32)],
        )
    back = exchange(done[-1], n)
    return tuple(
        call(
            unpack_kernel,
            "unpack",
            (back,),
            [(cells, width)] * 2,
            scratch=[
                pltpu.VMEM((2, cells, width), F32),
                pltpu.SemaphoreType.DMA((2,)),
            ],
            out_specs=[hbm, hbm],
        )
    )


def solution(mesh):
    placed = (P(None, "cols"), P(None, "cols"), P(None, "cols"), P("cols"), P(), P(), P())
    return jax.shard_map(
        on_device,
        mesh=mesh,
        in_specs=placed,
        out_specs=(P(None, "cols"), P(None, "cols")),
        check_vma=False,
    )
```

```python
import functools

import jax
import jax.numpy as jnp
from jax import lax
from jax.experimental import pallas as pl
from jax.experimental.pallas import tpu as pltpu
from jax.sharding import PartitionSpec as P

SPAN = 256
PAIR_DEV = 4
LANES = 128
CHUNKS = SPAN // LANES
TEAM = 16
OWN = LANES // TEAM
SUB = 8
GROUPS = 2
WIDTH = 2 * LANES
ALL = GROUPS * WIDTH
EDGE = PAIR_DEV * OWN
VMEM_LIMIT = 32 * 1024 * 1024
PACK_LIMIT = 60 * 1024 * 1024
DISTANCES = range(1, PAIR_DEV + 1)
SENDS = 4
F32 = jnp.float32


def cut_count(n):
    return min(n // TEAM - 1, 2)


def place(cut):
    team = lax.axis_index("cols") // TEAM
    return team, lax.rem(team, 2) == cut


def sign_of(cut):
    return jnp.where(place(cut)[1], 1.0, -1.0).astype(F32)


def reciprocal(x):
    r = pl.reciprocal(x, approx=True)
    return r * (2.0 - x * r)


def sigmoid(x):
    return 0.5 + 0.5 * jnp.tanh(0.5 * x)


def passage(h, t, k):
    s = sigmoid(h)
    return k * (sigmoid(2.0 * t) * s * s + 0.02)


def lanes_of(g, b):
    return slice((g * 2 + b) * LANES, (g * 2 + b + 1) * LANES)


def following(value):
    first, second = value[:, :WIDTH], value[:, WIDTH:]
    return jnp.concatenate([second, pltpu.roll(first, SUB - 1, axis=0)], axis=1)


def preceding(value):
    first, second = value[:, :WIDTH], value[:, WIDTH:]
    return jnp.concatenate([pltpu.roll(second, 1, axis=0), first], axis=1)


def solve(steps, matrix, ratio, lead, value, update):
    c_prev = a_prev = d_prev = None
    for j in range(steps):
        above, main, below, source = matrix(j)
        if j == 0:
            r = reciprocal(main)
            a_prev = above * r
            d_prev = source * r
        else:
            r = reciprocal(main - above * c_prev)
            over = above * r
            a_prev = a_prev * over
            d_prev = source * r + d_prev * over
        c_prev = below * r
        ratio[j] = c_prev
        lead[j] = a_prev
        value[j] = d_prev
    last_c, last_a, last_d = c_prev, a_prev, d_prev
    p_first, a_first, d_first = ratio[steps - 2], lead[steps - 2], value[steps - 2]
    for j in range(steps - 3, -1, -1):
        c = ratio[j]
        p_first = c * p_first
        a_first = lead[j] + c * a_first
        d_first = value[j] + c * d_first
    g = reciprocal(1.0 - last_c * following(a_first))
    up = last_c * following(p_first) * g
    down = last_a * g
    own = (last_d + last_c * following(d_first)) * g
    step = 0
    while step < SUB:
        if step == 0:
            after, before = following, preceding
        else:
            after = functools.partial(pltpu.roll, shift=SUB - step, axis=0)
            before = functools.partial(pltpu.roll, shift=step, axis=0)
        g = reciprocal(1.0 - up * after(down) - down * before(up))
        own = (own + up * after(own) + down * before(own)) * g
        up = up * after(up) * g
        down = down * before(down) * g
        step = max(1, 2 * step)
    over = preceding(own)
    x = own
    update(steps - 1, x)
    for j in range(steps - 2, -1, -1):
        x = ratio[j] * x + (lead[j] * over + value[j])
        update(j, x)


def mask_rows(cuts):
    return 3 * PAIR_DEV + cuts * (2 * PAIR_DEV + 1)


def cut_row(cut):
    return 3 * PAIR_DEV + cut * (2 * PAIR_DEV + 1)


def mask_kernel(n, couplings, out):
    pair_rows = couplings[...].astype(F32)
    pairs = couplings.shape[1]
    pair_id = lax.broadcasted_iota(jnp.int32, (pairs, LANES), 0)
    lane = lax.broadcasted_iota(jnp.int32, (pairs, LANES), 1)
    lane_1 = lax.broadcasted_iota(jnp.int32, (SUB, LANES), 1)

    def chosen(dev, s):
        at = (pair_id == dev * PAIR_DEV + s - 1).astype(F32)
        found = jnp.dot(pair_rows, at, preferred_element_type=F32)
        return found[0:1], found[1:2]

    def put(row, value):
        out[row] = jnp.broadcast_to(value, (SUB, LANES))

    team = lax.axis_index("cols") // TEAM
    dev = team * TEAM + lane // OWN
    for s in DISTANCES:
        put(s - 1, chosen(dev, s)[0])
        put(PAIR_DEV + s - 1, chosen(dev - s, s)[1])
        put(2 * PAIR_DEV + s - 1, jnp.where(lane_1 // OWN + s < TEAM, 0.25, 0.0))
    block = lax.rem(lane_1 // EDGE, 2)
    edge = lax.rem(lane, EDGE) // OWN
    edge_1 = lax.rem(lane_1, EDGE) // OWN
    for cut in range(cut_count(n)):
        _, above = place(cut)
        row = cut_row(cut)
        partner = jnp.where(above, team + 1, team - 1)
        there = jnp.logical_and(partner >= 0, partner < n // TEAM)
        factor = jnp.where(there, 0.25, 0.0) * sign_of(cut)
        for s in DISTANCES:
            start = team * TEAM + jnp.where(above, TEAM - PAIR_DEV, -s)
            up, down = chosen(start + edge, s)
            mine = jnp.where(above, up, down)
            inward = jnp.where(above, edge_1, PAIR_DEV - 1 - edge_1)
            active = jnp.logical_and(inward >= PAIR_DEV - s, jnp.abs(mine - block.astype(F32)) < 0.5)
            put(row + s - 1, jnp.where(active, factor, 0.0))
            apart = jnp.where(above, PAIR_DEV - s, s - PAIR_DEV)
            up, down = chosen(start + edge + apart, s)
            theirs = jnp.where(above, down, up)
            put(row + PAIR_DEV + s - 1, jnp.where(jnp.abs(theirs - block.astype(F32)) < 0.5, 1.0, 0.0))
        outward = jnp.where(above, LANES - 1 - lane_1, lane_1)
        put(row + 2 * PAIR_DEV, jnp.where(outward < EDGE, 1.0, 0.0))


def pack_kernel(suction, warmth, classes, top, out, room, class_room, turned, in_sems, out_sems):
    cells = turned.shape[-1]
    quarters = 2 * CHUNKS
    into = []
    for f, field in enumerate((suction, warmth, classes)):
        into.append(pltpu.make_async_copy(field, class_room if f == 2 else room.at[f], in_sems.at[f]))
        into[-1].start()

    def put(slot, value):
        turned[:, slot] = value.T.reshape(TEAM, OWN, cells)

    rows = [top[0:1, q * LANES : (q + 1) * LANES] for q in range(quarters)]
    put(3 * quarters, jnp.concatenate(rows + [jnp.zeros((cells - quarters, LANES), F32)], axis=0))
    for f in range(3):
        into[f].wait()
        for q in range(quarters):
            lanes = slice(q * LANES, (q + 1) * LANES)
            put(f * quarters + q, class_room[:, lanes].astype(F32) if f == 2 else room[f, :, lanes])
    sent = []
    for i in range(SENDS):
        rows = pl.ds(i * (TEAM // SENDS), TEAM // SENDS)
        sent.append(pltpu.make_async_copy(turned.at[rows], out.at[rows], out_sems.at[i]))
        sent[-1].start()
    for copy in sent:
        copy.wait()


def unpack_kernel(got, suction, warmth, room, sems):
    cells = got.shape[-1]
    quarters = 2 * CHUNKS
    sent = []
    for f, out in enumerate((suction, warmth)):
        for q in range(quarters):
            room[f, :, q * LANES : (q + 1) * LANES] = got[:, f * quarters + q].reshape(LANES, cells).T
        sent.append(pltpu.make_async_copy(room.at[f], out, sems.at[f]))
        sent[-1].start()
    for copy in sent:
        copy.wait()


def edge_shift(cut, m):
    return lax.rem(EDGE * m + jnp.where(place(cut)[1], EDGE, 0), LANES)


def halo_of(cut, value):
    part = lax.broadcasted_iota(jnp.int32, (SUB, LANES), 1) // EDGE
    packed = None
    for m in range(2 * GROUPS):
        moved = pltpu.roll(value[:, m * LANES : (m + 1) * LANES], edge_shift(cut, m), axis=1)
        packed = moved if m == 0 else jnp.where(part == m, moved, packed)
    return packed


def edge_kernel(cuts, got, k_sat, *refs):
    halos, load = refs[:-1], refs[-1]
    cells = got.shape[-1]
    steps = halos[0].shape[0]
    stride = steps * GROUPS
    second = lax.broadcasted_iota(jnp.int32, (SUB, LANES), 1) >= 2 * EDGE
    for chunk in range(CHUNKS):
        for cut in range(cuts):
            start = jnp.where(place(cut)[1], TEAM - PAIR_DEV, 0)
            for f in range(3):
                rows = [
                    got[pl.ds(start, PAIR_DEV), (f * 2 + b) * CHUNKS + chunk].reshape(EDGE, cells)
                    for b in range(2)
                ]
                slot = (chunk * cuts + cut) * 3 + f
                load[slot] = jnp.concatenate(rows * GROUPS, axis=0).T
    for chunk in range(CHUNKS):
        for cut in range(cuts):
            for f in range(3):
                slot = (chunk * cuts + cut) * 3 + f
                for j in range(steps):
                    v = jnp.where(
                        second,
                        load[slot, pl.ds(steps + j, SUB, stride=stride), :],
                        load[slot, pl.ds(j, SUB, stride=stride), :],
                    )
                    if f == 2:
                        k = jnp.full_like(v, k_sat[0])
                        for c in range(1, k_sat.shape[0]):
                            k = jnp.where(v >= c, k_sat[c], k)
                        v = k
                    halos[slot][j] = v


def first_kernel(
    chunk, got, k_sat, heat_cond, head, warm, perm, conduct, wet, melt, cond, energy, top, load
):
    cells = got.shape[-1]
    steps = head.shape[0]
    stride = steps * GROUPS

    for field in range(3):
        for b in range(2):
            load[field * 2 + b] = got[:, (field * 2 + b) * CHUNKS + chunk].reshape(LANES, cells).T
    surface = got[:, 6 * CHUNKS].reshape(LANES, cells).T[0:SUB]
    rows = [surface[b * CHUNKS + chunk : b * CHUNKS + chunk + 1] for b in range(2)]
    top[...] = jnp.concatenate(rows * GROUPS, axis=1)

    def fetch(field, j):
        parts = [
            load[field * 2 + b, pl.ds(g * steps + j, SUB, stride=stride), :]
            for g in range(GROUPS)
            for b in range(2)
        ]
        return jnp.concatenate(parts, axis=1)

    for j in range(steps):
        h, t, v = [fetch(field, j) for field in range(3)]
        k = jnp.full_like(v, k_sat[0])
        lam = jnp.full_like(v, heat_cond[0])
        for c in range(1, k_sat.shape[0]):
            here = v >= c
            k = jnp.where(here, k_sat[c], k)
            lam = jnp.where(here, heat_cond[c], lam)
        s, f = sigmoid(h), sigmoid(2.0 * t)
        m = 0.05 + 0.4 * s
        head[j], warm[j], perm[j], conduct[j] = h, t, k, lam
        wet[j] = s
        melt[j] = f
        cond[j] = k * (f * s * s + 0.02)
        energy[j] = (1.0 + 2.0 * m) * t + 2.0 * m * f


def team_kernel(masks, head, warm, cond, water, heat):
    steps = head.shape[0]
    upper = [masks[s - 1] > 0.5 for s in DISTANCES]
    lower = [masks[PAIR_DEV + s - 1] > 0.5 for s in DISTANCES]

    def step(j, _):
        for g in range(GROUPS):
            l0, l1 = lanes_of(g, 0), lanes_of(g, 1)
            h0, h1 = head[j, :, l0], head[j, :, l1]
            t0, t1 = warm[j, :, l0], warm[j, :, l1]
            c0, c1 = cond[j, :, l0], cond[j, :, l1]
            total = None
            for s in DISTANCES:
                up, low = upper[s - 1], lower[s - 1]
                back = LANES - s * OWN
                h_low = pltpu.roll(jnp.where(low, h1, h0), back, axis=1)
                t_low = pltpu.roll(jnp.where(low, t1, t0), back, axis=1)
                c_low = pltpu.roll(jnp.where(low, c1, c0), back, axis=1)
                flow = (
                    masks[2 * PAIR_DEV + s - 1]
                    * (jnp.where(up, c1, c0) + c_low)
                    * (jnp.where(up, h1, h0) - h_low + 0.5)
                )
                carried = flow * jnp.where(flow > 0.0, jnp.where(up, t1, t0), t_low)
                flow_in = pltpu.roll(flow, s * OWN, axis=1)
                carried_in = pltpu.roll(carried, s * OWN, axis=1)
                part = (
                    flow_in - flow,
                    jnp.where(low, flow_in, 0.0) - jnp.where(up, flow, 0.0),
                    carried_in - carried,
                    jnp.where(low, carried_in, 0.0) - jnp.where(up, carried, 0.0),
                )
                total = part if total is None else [a + b for a, b in zip(total, part)]
            water[j, :, l0] = total[0] - total[1]
            water[j, :, l1] = total[1]
            heat[j, :, l0] = 2.0 * (total[2] - total[3])
            heat[j, :, l1] = 2.0 * total[3]

    lax.fori_loop(0, steps, step, None)


def cross_flows(cut, masks, mine, theirs):
    row = cut_row(cut)
    sign = sign_of(cut)
    above = place(cut)[1]
    lane = lax.broadcasted_iota(jnp.int32, (SUB, LANES), 1)
    first_block = lax.rem(lane, 2 * EDGE) < EDGE
    h, t, k = mine
    c = passage(h, t, k)
    far = [theirs[0], theirs[1], passage(*theirs)]
    other = [
        jnp.where(first_block, pltpu.roll(v, LANES - EDGE, axis=1), pltpu.roll(v, EDGE, axis=1)) for v in far
    ]
    water = heat = jnp.zeros((SUB, LANES), F32)
    for s in DISTANCES:
        same = masks[row + PAIR_DEV + s - 1] > 0.5
        picked = [jnp.where(same, a, b) for a, b in zip(far, other)]
        apart = (PAIR_DEV - s) * OWN
        if apart:
            shift = jnp.where(above, apart, LANES - apart)
            picked = [pltpu.roll(v, shift, axis=1) for v in picked]
        h_far, t_far, c_far = picked
        flow = masks[row + s - 1] * (c + c_far) * (sign * (h - h_far) + 0.5)
        water = water - flow
        heat = heat - flow * jnp.where(flow > 0.0, t, t_far)
    return water, heat


def advance(steps, cuts, masks, head, warm, conduct, stored, energy, wet, melt, cond, water, heat, top,
            mine, theirs, new_head, new_warm, new_wet, inflow, warm_inflow, ratio, lead, value, finish):
    for j in range(steps):
        w_parts = [water[j, :, m * LANES : (m + 1) * LANES] for m in range(2 * GROUPS)]
        q_parts = [heat[j, :, m * LANES : (m + 1) * LANES] for m in range(2 * GROUPS)]
        for cut in range(cuts):
            beside = masks[cut_row(cut) + 2 * PAIR_DEV]
            w_far, q_far = cross_flows(cut, masks, mine(cut, j), theirs(cut, j))
            for m in range(2 * GROUPS):
                shift = lax.rem(LANES - edge_shift(cut, m), LANES)
                w_parts[m] = w_parts[m] + beside * pltpu.roll(w_far, shift, axis=1)
                q_parts[m] = q_parts[m] + 2.0 * beside * pltpu.roll(q_far, shift, axis=1)
        for m in range(2 * GROUPS):
            inflow[j, :, m * LANES : (m + 1) * LANES] = w_parts[m]
            warm_inflow[j, :, m * LANES : (m + 1) * LANES] = q_parts[m]

    part = lax.broadcasted_iota(jnp.int32, (SUB, ALL), 0)
    group = lax.broadcasted_iota(jnp.int32, (SUB, ALL), 1) // WIDTH
    first_part = jnp.logical_and(part == 0, group == 0)
    last_part = jnp.logical_and(part == SUB - 1, group == GROUPS - 1)

    def faces(fields, potential):
        face_of, rise_of = [], []
        for j in range(steps):
            if j + 1 < steps:
                c_next, v_next = fields[j + 1], potential[j + 1]
                face = 0.5 * (fields[j] + c_next)
            else:
                c_next, v_next = following(fields[0]), following(potential[0])
                face = jnp.where(last_part, 0.0, 0.5 * (fields[j] + c_next))
            face_of.append(face)
            rise_of.append(v_next - potential[j])
        return face_of, rise_of

    k_face, rise = faces([cond[j] for j in range(steps)], head)
    k_top = jnp.where(first_part, 0.0, preceding(k_face[-1]))
    q_face = [k * (1.0 - d) for k, d in zip(k_face, rise)]
    q_top = jnp.where(first_part, 0.0, preceding(q_face[-1]))

    def water_matrix(j):
        above = k_top if j == 0 else k_face[j - 1]
        into = q_top if j == 0 else q_face[j - 1]
        s = wet[j]
        main = 0.8 * s * (1.0 - s) + 0.02 + above + k_face[j]
        source = inflow[j] + into - q_face[j] - 0.8 * (s - stored[j])
        return above, main, k_face[j], source

    def water_done(j, x):
        h = head[j] + x
        new_head[j] = h
        new_wet[j] = sigmoid(h)

    solve(steps, water_matrix, ratio, lead, value, water_done)

    l_cell = [conduct[j] * (1.5 - 0.5 * melt[j]) for j in range(steps)]
    l_face, rise = faces(l_cell, warm)
    l_top = jnp.where(first_part, 0.0, preceding(l_face[-1]))
    g_face = [l * d for l, d in zip(l_face, rise)]
    g_top = jnp.where(first_part, 0.0, preceding(g_face[-1]))
    surface_lam = jnp.where(first_part, 2.0 * l_cell[0], 0.0)

    def heat_matrix(j):
        above = l_top if j == 0 else l_face[j - 1]
        out_of = g_top if j == 0 else g_face[j - 1]
        t, f = warm[j], melt[j]
        m2 = 0.1 + 0.8 * new_wet[j]
        now = (1.0 + m2) * t + m2 * f
        main = 2.0 + 2.0 * m2 * (1.0 + 2.0 * f * (1.0 - f)) + above + l_face[j]
        source = warm_inflow[j] - out_of + g_face[j] - 2.0 * (now - energy[j])
        if j == 0:
            main = main + surface_lam
            source = source + surface_lam * (top[...] - t)
        return above, main, l_face[j], source

    def heat_done(j, x):
        t = warm[j] + x
        new_warm[j] = t
        finish(j, t)

    solve(steps, heat_matrix, ratio, lead, value, heat_done)


def middle_kernel(cuts, *refs):
    masks, head, warm, perm, conduct, wet, melt, cond, energy, top, water, heat = refs[:12]
    own, far = refs[12 : 12 + 3 * cuts], refs[12 + 3 * cuts : 12 + 6 * cuts]
    new_head, new_warm, new_wet, new_melt, new_cond = refs[12 + 6 * cuts : 17 + 6 * cuts]
    halos = refs[17 + 6 * cuts : 17 + 8 * cuts]
    inflow, warm_inflow, ratio, lead, value = refs[17 + 8 * cuts :]

    def finish(j, t):
        s, f = new_wet[j], sigmoid(2.0 * t)
        new_melt[j] = f
        new_cond[j] = perm[j] * (f * s * s + 0.02)
        for cut in range(cuts):
            halos[2 * cut][j] = halo_of(cut, new_head[j])
            halos[2 * cut + 1][j] = halo_of(cut, t)

    advance(
        head.shape[0], cuts, masks, head, warm, conduct, wet, energy, wet, melt, cond, water, heat, top,
        lambda cut, j: [own[3 * cut + i][j] for i in range(3)],
        lambda cut, j: [far[3 * cut + i][j] for i in range(3)],
        new_head, new_warm, new_wet, inflow, warm_inflow, ratio, lead, value, finish,
    )


def last_kernel(chunk, cuts, *refs):
    masks, head, warm, conduct, stored, wet, melt, cond, energy, top, water, heat = refs[:12]
    own, far, others = refs[12 : 12 + 3 * cuts], refs[12 + 3 * cuts : 12 + 6 * cuts], refs[12 + 6 * cuts : -10]
    out, new_head, new_warm, new_wet, inflow, warm_inflow, ratio, lead, value, load = refs[-10:]
    steps = head.shape[0]
    cells = steps * GROUPS * SUB
    stride = steps * GROUPS
    advance(
        steps, cuts, masks, head, warm, conduct, stored, energy, wet, melt, cond, water, heat, top,
        lambda cut, j: [own[3 * cut + i][j] for i in range(3)],
        lambda cut, j: [far[3 * cut + i][j] for i in range(3)],
        new_head, new_warm, new_wet, inflow, warm_inflow, ratio, lead, value, lambda j, t: None,
    )
    final = chunk == CHUNKS - 1
    for f, field in enumerate((new_head, new_warm)):
        for b in range(2):
            slot = f * 2 + b
            for j in range(steps):
                for g in range(GROUPS):
                    load[slot, pl.ds(g * steps + j, SUB, stride=stride), :] = field[j, :, lanes_of(g, b)]
            turned = load[slot].T.reshape(TEAM, OWN, cells)
            if final:
                out[:, slot * CHUNKS + chunk] = turned
                for c, other in enumerate(others):
                    out[:, slot * CHUNKS + c] = other[:, slot]
            else:
                out[:, slot] = turned


def whole(memory=pltpu.VMEM):
    return pl.BlockSpec(memory_space=memory)


def call(kernel, name, args, outs, scratch=(), specs=None, out_specs=None, limit=VMEM_LIMIT, work=2_000_000):
    return pl.pallas_call(
        kernel,
        out_shape=[jax.ShapeDtypeStruct(shape, F32) for shape in outs],
        in_specs=specs or [whole()] * len(args),
        out_specs=out_specs or [whole()] * len(outs),
        scratch_shapes=scratch,
        compiler_params=pltpu.CompilerParams(vmem_limit_bytes=limit),
        cost_estimate=pl.CostEstimate(flops=work, bytes_accessed=work, transcendentals=0),
        name=name,
    )(*args)


def exchange(tiles, n):
    teams = [list(range(start, start + TEAM)) for start in range(0, n, TEAM)]
    return lax.all_to_all(
        tiles, "cols", split_axis=0, concat_axis=0, tiled=True, axis_index_groups=teams
    )


def swap(cut, n, value):
    pairs = []
    for team in range(cut, n // TEAM - 1, 2):
        for i in range(team * TEAM, (team + 1) * TEAM):
            pairs += [(i, i + TEAM), (i + TEAM, i)]
    return lax.ppermute(value, "cols", pairs)


def on_device(suction, warmth, classes, top, couplings, k_sat, heat_cond):
    n = lax.axis_size("cols")
    cells, width = suction.shape
    steps = cells // (SUB * GROUPS)
    quarters = width // LANES
    cuts = cut_count(n)
    column = (steps, SUB, ALL)
    halo = (steps, SUB, LANES)
    room = pltpu.VMEM(column, F32)
    smem = whole(pltpu.SMEM)
    hbm = whole(pltpu.HBM)

    masks = call(
        functools.partial(mask_kernel, n), "masks", (couplings,), [(mask_rows(cuts), SUB, LANES)]
    )[0]
    packed = call(
        pack_kernel,
        "pack",
        (suction, warmth, classes, top.reshape(1, width)),
        [(TEAM, 3 * quarters + 1, OWN, cells)],
        scratch=[
            pltpu.VMEM((2, cells, width), F32),
            pltpu.VMEM((cells, width), classes.dtype),
            pltpu.VMEM((TEAM, 3 * quarters + 1, OWN, cells), F32),
            pltpu.SemaphoreType.DMA((3,)),
            pltpu.SemaphoreType.DMA((SENDS,)),
        ],
        specs=[hbm, hbm, hbm, whole()],
        out_specs=[hbm],
        limit=PACK_LIMIT,
    )[0]
    got = exchange(packed, n)

    edges = call(
        functools.partial(edge_kernel, cuts),
        "edges",
        (got, k_sat),
        [halo] * (3 * CHUNKS * cuts),
        scratch=[pltpu.VMEM((3 * CHUNKS * cuts, cells, LANES), F32)],
        specs=[whole(), smem],
    )
    first = [
        call(
            functools.partial(first_kernel, c),
            "first",
            (got, k_sat, heat_cond),
            [column] * 8 + [(1, ALL)],
            scratch=[pltpu.VMEM((6, cells, LANES), F32)],
            specs=[whole(), smem, smem],
        )
        for c in range(CHUNKS)
    ]
    flows, sides = [], []
    for c in range(CHUNKS):
        mine = tuple(edges[3 * c * cuts : 3 * (c + 1) * cuts])
        if c:
            mine, flows[-1] = lax.optimization_barrier((mine, flows[-1]))
        sides.append((mine, [swap(i // 3, n, v) for i, v in enumerate(mine)]))
        flows.append(tuple(call(team_kernel, "team", (masks, first[c][0], first[c][1], first[c][6]), [column] * 2)))

    second, later = [], []
    for c in range(CHUNKS):
        head, warm, perm, conduct, wet, melt, cond, energy, surface = first[c]
        water, heat = flows[c]
        mine, theirs = sides[c]
        values = call(
            functools.partial(middle_kernel, cuts),
            "middle",
            (masks, head, warm, perm, conduct, wet, melt, cond, energy, surface, water, heat, *mine, *theirs),
            [column] * 5 + [halo] * (2 * cuts),
            scratch=[room] * 5,
        )
        second.append(values[:5])
        sent = values[5:]
        came = [swap(i // 2, n, v) for i, v in enumerate(sent)]
        later.append(
            [
                [v for cut in range(cuts) for v in (*new[2 * cut : 2 * cut + 2], old[3 * cut + 2])]
                for new, old in ((sent, mine), (came, theirs))
            ]
        )

    done = []
    for c in range(CHUNKS):
        conduct, stored, energy, surface = first[c][3], first[c][4], first[c][7], first[c][8]
        head, warm, wet, melt, cond = second[c]
        water, heat = call(team_kernel, "team", (masks, head, warm, cond), [column] * 2)
        mine, theirs = later[c]
        final = c == CHUNKS - 1
        done += call(
            functools.partial(last_kernel, c, cuts),
            "last",
            (
                masks, head, warm, conduct, stored, wet, melt, cond, energy, surface, water, heat,
                *mine, *theirs, *(done if final else ()),
            ),
            [(TEAM, 2 * quarters if final else 4, OWN, cells)],
            scratch=[room] * 8 + [pltpu.VMEM((4, cells, LANES), F32)],
        )
    back = exchange(done[-1], n)
    return tuple(
        call(
            unpack_kernel,
            "unpack",
            (back,),
            [(cells, width)] * 2,
            scratch=[
                pltpu.VMEM((2, cells, width), F32),
                pltpu.SemaphoreType.DMA((2,)),
            ],
            out_specs=[hbm, hbm],
        )
    )


def solution(mesh):
    placed = (P(None, "cols"), P(None, "cols"), P(None, "cols"), P("cols"), P(), P(), P())
    return jax.shard_map(
        on_device,
        mesh=mesh,
        in_specs=placed,
        out_specs=(P(None, "cols"), P(None, "cols")),
        check_vma=False,
    )
```

```python
import functools

import jax
import jax.numpy as jnp
from jax import lax
from jax.experimental import pallas as pl
from jax.experimental.pallas import tpu as pltpu
from jax.sharding import PartitionSpec as P

SPAN = 256
PAIR_DEV = 4
LANES = 128
CHUNKS = SPAN // LANES
TEAM = 16
OWN = LANES // TEAM
SUB = 8
GROUPS = 2
WIDTH = 2 * LANES
ALL = GROUPS * WIDTH
EDGE = PAIR_DEV * OWN
VMEM_LIMIT = 32 * 1024 * 1024
DISTANCES = range(1, PAIR_DEV + 1)
F32 = jnp.float32


def cut_count(n):
    return min(n // TEAM - 1, 2)


def place(cut):
    team = lax.axis_index("cols") // TEAM
    return team, lax.rem(team, 2) == cut


def sign_of(cut):
    return jnp.where(place(cut)[1], 1.0, -1.0).astype(F32)


def reciprocal(x):
    r = pl.reciprocal(x, approx=True)
    return r * (2.0 - x * r)


def sigmoid(x):
    return 0.5 + 0.5 * jnp.tanh(0.5 * x)


def passage(h, t, k):
    s = sigmoid(h)
    return k * (sigmoid(2.0 * t) * s * s + 0.02)


def lanes_of(g, b):
    return slice((g * 2 + b) * LANES, (g * 2 + b + 1) * LANES)


def following(value):
    first, second = value[:, :WIDTH], value[:, WIDTH:]
    return jnp.concatenate([second, pltpu.roll(first, SUB - 1, axis=0)], axis=1)


def preceding(value):
    first, second = value[:, :WIDTH], value[:, WIDTH:]
    return jnp.concatenate([pltpu.roll(second, 1, axis=0), first], axis=1)


def solve(steps, matrix, ratio, lead, value, update):
    c_prev = a_prev = d_prev = None
    for j in range(steps):
        above, main, below, source = matrix(j)
        if j == 0:
            r = reciprocal(main)
            a_prev = above * r
            d_prev = source * r
        else:
            r = reciprocal(main - above * c_prev)
            over = above * r
            a_prev = a_prev * over
            d_prev = source * r + d_prev * over
        c_prev = below * r
        ratio[j] = c_prev
        lead[j] = a_prev
        value[j] = d_prev
    last_c, last_a, last_d = c_prev, a_prev, d_prev
    p_first, a_first, d_first = ratio[steps - 2], lead[steps - 2], value[steps - 2]
    for j in range(steps - 3, -1, -1):
        c = ratio[j]
        p_first = c * p_first
        a_first = lead[j] + c * a_first
        d_first = value[j] + c * d_first
    g = reciprocal(1.0 - last_c * following(a_first))
    up = last_c * following(p_first) * g
    down = last_a * g
    own = (last_d + last_c * following(d_first)) * g
    step = 0
    while step < SUB:
        if step == 0:
            after, before = following, preceding
        else:
            after = functools.partial(pltpu.roll, shift=SUB - step, axis=0)
            before = functools.partial(pltpu.roll, shift=step, axis=0)
        g = reciprocal(1.0 - up * after(down) - down * before(up))
        own = (own + up * after(own) + down * before(own)) * g
        up = up * after(up) * g
        down = down * before(down) * g
        step = max(1, 2 * step)
    over = preceding(own)
    x = own
    update(steps - 1, x)
    for j in range(steps - 2, -1, -1):
        x = ratio[j] * x + (lead[j] * over + value[j])
        update(j, x)


def mask_rows(cuts):
    return 3 * PAIR_DEV + cuts * (2 * PAIR_DEV + 1)


def cut_row(cut):
    return 3 * PAIR_DEV + cut * (2 * PAIR_DEV + 1)


def mask_kernel(n, couplings, out):
    pair_rows = couplings[...].astype(F32)
    pairs = couplings.shape[1]
    pair_id = lax.broadcasted_iota(jnp.int32, (pairs, LANES), 0)
    lane = lax.broadcasted_iota(jnp.int32, (pairs, LANES), 1)
    lane_1 = lax.broadcasted_iota(jnp.int32, (SUB, LANES), 1)

    def chosen(dev, s):
        at = (pair_id == dev * PAIR_DEV + s - 1).astype(F32)
        found = jnp.dot(pair_rows, at, preferred_element_type=F32)
        return found[0:1], found[1:2]

    def put(row, value):
        out[row] = jnp.broadcast_to(value, (SUB, LANES))

    team = lax.axis_index("cols") // TEAM
    dev = team * TEAM + lane // OWN
    for s in DISTANCES:
        put(s - 1, chosen(dev, s)[0])
        put(PAIR_DEV + s - 1, chosen(dev - s, s)[1])
        put(2 * PAIR_DEV + s - 1, jnp.where(lane_1 // OWN + s < TEAM, 0.25, 0.0))
    block = lax.rem(lane_1 // EDGE, 2)
    edge = lax.rem(lane, EDGE) // OWN
    edge_1 = lax.rem(lane_1, EDGE) // OWN
    for cut in range(cut_count(n)):
        _, above = place(cut)
        row = cut_row(cut)
        partner = jnp.where(above, team + 1, team - 1)
        there = jnp.logical_and(partner >= 0, partner < n // TEAM)
        factor = jnp.where(there, 0.25, 0.0) * sign_of(cut)
        for s in DISTANCES:
            start = team * TEAM + jnp.where(above, TEAM - PAIR_DEV, -s)
            up, down = chosen(start + edge, s)
            mine = jnp.where(above, up, down)
            inward = jnp.where(above, edge_1, PAIR_DEV - 1 - edge_1)
            active = jnp.logical_and(inward >= PAIR_DEV - s, jnp.abs(mine - block.astype(F32)) < 0.5)
            put(row + s - 1, jnp.where(active, factor, 0.0))
            apart = jnp.where(above, PAIR_DEV - s, s - PAIR_DEV)
            up, down = chosen(start + edge + apart, s)
            theirs = jnp.where(above, down, up)
            put(row + PAIR_DEV + s - 1, jnp.where(jnp.abs(theirs - block.astype(F32)) < 0.5, 1.0, 0.0))
        outward = jnp.where(above, LANES - 1 - lane_1, lane_1)
        put(row + 2 * PAIR_DEV, jnp.where(outward < EDGE, 1.0, 0.0))


def pack_kernel(suction, warmth, classes, surface, out, room, class_room, top, in_sems):
    cells = out.shape[-1]
    quarters = 2 * CHUNKS
    into = []
    for f, field in enumerate((suction, warmth, classes, surface)):
        target = (room.at[0], room.at[1], class_room, top)[f]
        into.append(pltpu.make_async_copy(field, target, in_sems.at[f]))
        into[-1].start()

    def put(slot, value):
        out[:, slot] = value.T.reshape(TEAM, OWN, cells)

    for f in range(3):
        into[f].wait()
        for q in range(quarters):
            lanes = slice(q * LANES, (q + 1) * LANES)
            put(f * quarters + q, class_room[:, lanes].astype(F32) if f == 2 else room[f, :, lanes])
    into[3].wait()
    rows = [top[0:1, q * LANES : (q + 1) * LANES] for q in range(quarters)]
    put(3 * quarters, jnp.concatenate(rows + [jnp.zeros((cells - quarters, LANES), F32)], axis=0))


def unpack_kernel(got, suction, warmth, room, sems):
    cells = got.shape[-1]
    quarters = 2 * CHUNKS
    sent = []
    for f, out in enumerate((suction, warmth)):
        for q in range(quarters):
            room[f, :, q * LANES : (q + 1) * LANES] = got[:, f * quarters + q].reshape(LANES, cells).T
        sent.append(pltpu.make_async_copy(room.at[f], out, sems.at[f]))
        sent[-1].start()
    for copy in sent:
        copy.wait()


def edge_shift(cut, m):
    return lax.rem(EDGE * m + jnp.where(place(cut)[1], EDGE, 0), LANES)


def halo_of(cut, value):
    part = lax.broadcasted_iota(jnp.int32, (SUB, LANES), 1) // EDGE
    packed = None
    for m in range(2 * GROUPS):
        moved = pltpu.roll(value[:, m * LANES : (m + 1) * LANES], edge_shift(cut, m), axis=1)
        packed = moved if m == 0 else jnp.where(part == m, moved, packed)
    return packed


def edge_kernel(cuts, got, k_sat, *refs):
    halos, load = refs[:-1], refs[-1]
    cells = got.shape[-1]
    steps = halos[0].shape[1]
    stride = steps * GROUPS
    second = lax.broadcasted_iota(jnp.int32, (SUB, LANES), 1) >= 2 * EDGE
    for chunk in range(CHUNKS):
        for cut in range(cuts):
            start = jnp.where(place(cut)[1], TEAM - PAIR_DEV, 0)
            for f in range(3):
                rows = [
                    got[pl.ds(start, PAIR_DEV), (f * 2 + b) * CHUNKS + chunk].reshape(EDGE, cells)
                    for b in range(2)
                ]
                slot = (chunk * cuts + cut) * 3 + f
                load[slot] = jnp.concatenate(rows * GROUPS, axis=0).T
    for chunk in range(CHUNKS):
        for cut in range(cuts):
            for f in range(3):
                slot = (chunk * cuts + cut) * 3 + f
                for j in range(steps):
                    v = jnp.where(
                        second,
                        load[slot, pl.ds(steps + j, SUB, stride=stride), :],
                        load[slot, pl.ds(j, SUB, stride=stride), :],
                    )
                    if f == 2:
                        k = jnp.full_like(v, k_sat[0])
                        for c in range(1, k_sat.shape[0]):
                            k = jnp.where(v >= c, k_sat[c], k)
                        v = k
                    halos[chunk * cuts + cut][f, j] = v


def first_kernel(
    chunk, got, k_sat, heat_cond, head, warm, perm, conduct, wet, melt, cond, energy, top, load
):
    cells = got.shape[-1]
    steps = head.shape[0]
    stride = steps * GROUPS

    for field in range(3):
        for b in range(2):
            load[field * 2 + b] = got[:, (field * 2 + b) * CHUNKS + chunk].reshape(LANES, cells).T
    surface = got[:, 6 * CHUNKS].reshape(LANES, cells).T[0:SUB]
    rows = [surface[b * CHUNKS + chunk : b * CHUNKS + chunk + 1] for b in range(2)]
    top[...] = jnp.concatenate(rows * GROUPS, axis=1)

    def fetch(field, j):
        parts = [
            load[field * 2 + b, pl.ds(g * steps + j, SUB, stride=stride), :]
            for g in range(GROUPS)
            for b in range(2)
        ]
        return jnp.concatenate(parts, axis=1)

    for j in range(steps):
        h, t, v = [fetch(field, j) for field in range(3)]
        k = jnp.full_like(v, k_sat[0])
        lam = jnp.full_like(v, heat_cond[0])
        for c in range(1, k_sat.shape[0]):
            here = v >= c
            k = jnp.where(here, k_sat[c], k)
            lam = jnp.where(here, heat_cond[c], lam)
        s, f = sigmoid(h), sigmoid(2.0 * t)
        m = 0.05 + 0.4 * s
        head[j], warm[j], perm[j], conduct[j] = h, t, k, lam
        wet[j] = s
        melt[j] = f
        cond[j] = k * (f * s * s + 0.02)
        energy[j] = (1.0 + 2.0 * m) * t + 2.0 * m * f


def team_kernel(masks, head, warm, cond, water, heat):
    steps = head.shape[0]
    upper = [masks[s - 1] > 0.5 for s in DISTANCES]
    lower = [masks[PAIR_DEV + s - 1] > 0.5 for s in DISTANCES]

    def step(j, _):
        for g in range(GROUPS):
            l0, l1 = lanes_of(g, 0), lanes_of(g, 1)
            h0, h1 = head[j, :, l0], head[j, :, l1]
            t0, t1 = warm[j, :, l0], warm[j, :, l1]
            c0, c1 = cond[j, :, l0], cond[j, :, l1]
            total = None
            for s in DISTANCES:
                up, low = upper[s - 1], lower[s - 1]
                back = LANES - s * OWN
                h_low = pltpu.roll(jnp.where(low, h1, h0), back, axis=1)
                t_low = pltpu.roll(jnp.where(low, t1, t0), back, axis=1)
                c_low = pltpu.roll(jnp.where(low, c1, c0), back, axis=1)
                flow = (
                    masks[2 * PAIR_DEV + s - 1]
                    * (jnp.where(up, c1, c0) + c_low)
                    * (jnp.where(up, h1, h0) - h_low + 0.5)
                )
                carried = flow * jnp.where(flow > 0.0, jnp.where(up, t1, t0), t_low)
                flow_in = pltpu.roll(flow, s * OWN, axis=1)
                carried_in = pltpu.roll(carried, s * OWN, axis=1)
                part = (
                    flow_in - flow,
                    jnp.where(low, flow_in, 0.0) - jnp.where(up, flow, 0.0),
                    carried_in - carried,
                    jnp.where(low, carried_in, 0.0) - jnp.where(up, carried, 0.0),
                )
                total = part if total is None else [a + b for a, b in zip(total, part)]
            water[j, :, l0] = total[0] - total[1]
            water[j, :, l1] = total[1]
            heat[j, :, l0] = 2.0 * (total[2] - total[3])
            heat[j, :, l1] = 2.0 * total[3]

    lax.fori_loop(0, steps, step, None)


def cross_flows(cut, masks, mine, theirs):
    row = cut_row(cut)
    sign = sign_of(cut)
    above = place(cut)[1]
    lane = lax.broadcasted_iota(jnp.int32, (SUB, LANES), 1)
    first_block = lax.rem(lane, 2 * EDGE) < EDGE
    h, t, k = mine
    c = passage(h, t, k)
    far = [theirs[0], theirs[1], passage(*theirs)]
    other = [
        jnp.where(first_block, pltpu.roll(v, LANES - EDGE, axis=1), pltpu.roll(v, EDGE, axis=1)) for v in far
    ]
    water = heat = jnp.zeros((SUB, LANES), F32)
    for s in DISTANCES:
        same = masks[row + PAIR_DEV + s - 1] > 0.5
        picked = [jnp.where(same, a, b) for a, b in zip(far, other)]
        apart = (PAIR_DEV - s) * OWN
        if apart:
            shift = jnp.where(above, apart, LANES - apart)
            picked = [pltpu.roll(v, shift, axis=1) for v in picked]
        h_far, t_far, c_far = picked
        flow = masks[row + s - 1] * (c + c_far) * (sign * (h - h_far) + 0.5)
        water = water - flow
        heat = heat - flow * jnp.where(flow > 0.0, t, t_far)
    return water, heat


def advance(steps, cuts, masks, head, warm, conduct, stored, energy, wet, melt, cond, water, heat, top,
            mine, theirs, new_head, new_warm, new_wet, inflow, warm_inflow, ratio, lead, value, finish):
    for j in range(steps):
        w_parts = [water[j, :, m * LANES : (m + 1) * LANES] for m in range(2 * GROUPS)]
        q_parts = [heat[j, :, m * LANES : (m + 1) * LANES] for m in range(2 * GROUPS)]
        for cut in range(cuts):
            beside = masks[cut_row(cut) + 2 * PAIR_DEV]
            w_far, q_far = cross_flows(cut, masks, mine(cut, j), theirs(cut, j))
            for m in range(2 * GROUPS):
                shift = lax.rem(LANES - edge_shift(cut, m), LANES)
                w_parts[m] = w_parts[m] + beside * pltpu.roll(w_far, shift, axis=1)
                q_parts[m] = q_parts[m] + 2.0 * beside * pltpu.roll(q_far, shift, axis=1)
        for m in range(2 * GROUPS):
            inflow[j, :, m * LANES : (m + 1) * LANES] = w_parts[m]
            warm_inflow[j, :, m * LANES : (m + 1) * LANES] = q_parts[m]

    part = lax.broadcasted_iota(jnp.int32, (SUB, ALL), 0)
    group = lax.broadcasted_iota(jnp.int32, (SUB, ALL), 1) // WIDTH
    first_part = jnp.logical_and(part == 0, group == 0)
    last_part = jnp.logical_and(part == SUB - 1, group == GROUPS - 1)

    def faces(fields, potential):
        face_of, rise_of = [], []
        for j in range(steps):
            if j + 1 < steps:
                c_next, v_next = fields[j + 1], potential[j + 1]
                face = 0.5 * (fields[j] + c_next)
            else:
                c_next, v_next = following(fields[0]), following(potential[0])
                face = jnp.where(last_part, 0.0, 0.5 * (fields[j] + c_next))
            face_of.append(face)
            rise_of.append(v_next - potential[j])
        return face_of, rise_of

    k_face, rise = faces([cond[j] for j in range(steps)], head)
    k_top = jnp.where(first_part, 0.0, preceding(k_face[-1]))
    q_face = [k * (1.0 - d) for k, d in zip(k_face, rise)]
    q_top = jnp.where(first_part, 0.0, preceding(q_face[-1]))

    def water_matrix(j):
        above = k_top if j == 0 else k_face[j - 1]
        into = q_top if j == 0 else q_face[j - 1]
        s = wet[j]
        main = 0.8 * s * (1.0 - s) + 0.02 + above + k_face[j]
        source = inflow[j] + into - q_face[j] - 0.8 * (s - stored[j])
        return above, main, k_face[j], source

    def water_done(j, x):
        h = head[j] + x
        new_head[j] = h
        new_wet[j] = sigmoid(h)

    solve(steps, water_matrix, ratio, lead, value, water_done)

    l_cell = [conduct[j] * (1.5 - 0.5 * melt[j]) for j in range(steps)]
    l_face, rise = faces(l_cell, warm)
    l_top = jnp.where(first_part, 0.0, preceding(l_face[-1]))
    g_face = [l * d for l, d in zip(l_face, rise)]
    g_top = jnp.where(first_part, 0.0, preceding(g_face[-1]))
    surface_lam = jnp.where(first_part, 2.0 * l_cell[0], 0.0)

    def heat_matrix(j):
        above = l_top if j == 0 else l_face[j - 1]
        out_of = g_top if j == 0 else g_face[j - 1]
        t, f = warm[j], melt[j]
        m2 = 0.1 + 0.8 * new_wet[j]
        now = (1.0 + m2) * t + m2 * f
        main = 2.0 + 2.0 * m2 * (1.0 + 2.0 * f * (1.0 - f)) + above + l_face[j]
        source = warm_inflow[j] - out_of + g_face[j] - 2.0 * (now - energy[j])
        if j == 0:
            main = main + surface_lam
            source = source + surface_lam * (top[...] - t)
        return above, main, l_face[j], source

    def heat_done(j, x):
        t = warm[j] + x
        new_warm[j] = t
        finish(j, t)

    solve(steps, heat_matrix, ratio, lead, value, heat_done)


def middle_kernel(cuts, *refs):
    masks, head, warm, perm, conduct, wet, melt, cond, energy, top, water, heat = refs[:12]
    own, far = refs[12 : 12 + cuts], refs[12 + cuts : 12 + 2 * cuts]
    new_head, new_warm, new_wet, new_melt, new_cond = refs[12 + 2 * cuts : 17 + 2 * cuts]
    halos = refs[17 + 2 * cuts : 17 + 3 * cuts]
    inflow, warm_inflow, ratio, lead, value = refs[17 + 3 * cuts :]

    def finish(j, t):
        s, f = new_wet[j], sigmoid(2.0 * t)
        new_melt[j] = f
        new_cond[j] = perm[j] * (f * s * s + 0.02)
        for cut in range(cuts):
            halos[cut][0, j] = halo_of(cut, new_head[j])
            halos[cut][1, j] = halo_of(cut, t)

    advance(
        head.shape[0], cuts, masks, head, warm, conduct, wet, energy, wet, melt, cond, water, heat, top,
        lambda cut, j: [own[cut][i, j] for i in range(3)],
        lambda cut, j: [far[cut][i, j] for i in range(3)],
        new_head, new_warm, new_wet, inflow, warm_inflow, ratio, lead, value, finish,
    )


def last_kernel(chunk, cuts, *refs):
    masks, head, warm, conduct, stored, wet, melt, cond, energy, top, water, heat = refs[:12]
    own, far = refs[12 : 12 + cuts], refs[12 + cuts : 12 + 2 * cuts]
    own_k, far_k = refs[12 + 2 * cuts : 12 + 3 * cuts], refs[12 + 3 * cuts : 12 + 4 * cuts]
    others = refs[12 + 4 * cuts : -10]
    out, new_head, new_warm, new_wet, inflow, warm_inflow, ratio, lead, value, load = refs[-10:]
    steps = head.shape[0]
    cells = steps * GROUPS * SUB
    stride = steps * GROUPS
    advance(
        steps, cuts, masks, head, warm, conduct, stored, energy, wet, melt, cond, water, heat, top,
        lambda cut, j: [own[cut][0, j], own[cut][1, j], own_k[cut][2, j]],
        lambda cut, j: [far[cut][0, j], far[cut][1, j], far_k[cut][2, j]],
        new_head, new_warm, new_wet, inflow, warm_inflow, ratio, lead, value, lambda j, t: None,
    )
    final = chunk == CHUNKS - 1
    for f, field in enumerate((new_head, new_warm)):
        for b in range(2):
            slot = f * 2 + b
            for j in range(steps):
                for g in range(GROUPS):
                    load[slot, pl.ds(g * steps + j, SUB, stride=stride), :] = field[j, :, lanes_of(g, b)]
            turned = load[slot].T.reshape(TEAM, OWN, cells)
            if final:
                out[:, slot * CHUNKS + chunk] = turned
                for c, other in enumerate(others):
                    out[:, slot * CHUNKS + c] = other[:, slot]
            else:
                out[:, slot] = turned


def whole(memory=pltpu.VMEM):
    return pl.BlockSpec(memory_space=memory)


def call(kernel, name, args, outs, scratch=(), specs=None, out_specs=None, limit=VMEM_LIMIT, work=2_000_000):
    return pl.pallas_call(
        kernel,
        out_shape=[jax.ShapeDtypeStruct(shape, F32) for shape in outs],
        in_specs=specs or [whole()] * len(args),
        out_specs=out_specs or [whole()] * len(outs),
        scratch_shapes=scratch,
        compiler_params=pltpu.CompilerParams(vmem_limit_bytes=limit),
        cost_estimate=pl.CostEstimate(flops=work, bytes_accessed=work, transcendentals=0),
        name=name,
    )(*args)


def exchange(tiles, n):
    teams = [list(range(start, start + TEAM)) for start in range(0, n, TEAM)]
    return lax.all_to_all(
        tiles, "cols", split_axis=0, concat_axis=0, tiled=True, axis_index_groups=teams
    )


def swap(cut, n, value):
    pairs = []
    for team in range(cut, n // TEAM - 1, 2):
        for i in range(team * TEAM, (team + 1) * TEAM):
            pairs += [(i, i + TEAM), (i + TEAM, i)]
    return lax.ppermute(value, "cols", pairs)


def on_device(suction, warmth, classes, top, couplings, k_sat, heat_cond):
    n = lax.axis_size("cols")
    cells, width = suction.shape
    steps = cells // (SUB * GROUPS)
    quarters = width // LANES
    cuts = cut_count(n)
    column = (steps, SUB, ALL)
    halo = (steps, SUB, LANES)
    room = pltpu.VMEM(column, F32)
    smem = whole(pltpu.SMEM)
    hbm = whole(pltpu.HBM)

    masks = call(
        functools.partial(mask_kernel, n), "masks", (couplings,), [(mask_rows(cuts), SUB, LANES)]
    )[0]
    packed = call(
        pack_kernel,
        "pack",
        [pltpu.with_memory_space_constraint(v, pltpu.HBM) for v in (suction, warmth, classes, top.reshape(1, width))],
        [(TEAM, 3 * quarters + 1, OWN, cells)],
        scratch=[
            pltpu.VMEM((2, cells, width), F32),
            pltpu.VMEM((cells, width), classes.dtype),
            pltpu.VMEM((1, width), F32),
            pltpu.SemaphoreType.DMA((4,)),
        ],
        specs=[hbm] * 4,
    )[0]
    got = exchange(packed, n)

    edges = call(
        functools.partial(edge_kernel, cuts),
        "edges",
        (got, k_sat),
        [(3,) + halo] * (CHUNKS * cuts),
        scratch=[pltpu.VMEM((3 * CHUNKS * cuts, cells, LANES), F32)],
        specs=[whole(), smem],
    )
    first = [
        call(
            functools.partial(first_kernel, c),
            "first",
            (got, k_sat, heat_cond),
            [column] * 8 + [(1, ALL)],
            scratch=[pltpu.VMEM((6, cells, LANES), F32)],
            specs=[whole(), smem, smem],
        )
        for c in range(CHUNKS)
    ]
    flows, sides = [], []
    for c in range(CHUNKS):
        mine = tuple(edges[c * cuts : (c + 1) * cuts])
        sides.append((mine, [swap(cut, n, v) for cut, v in enumerate(mine)]))
        flows.append(tuple(call(team_kernel, "team", (masks, first[c][0], first[c][1], first[c][6]), [column] * 2)))

    second, later = [], []
    for c in range(CHUNKS):
        head, warm, perm, conduct, wet, melt, cond, energy, surface = first[c]
        water, heat = flows[c]
        mine, theirs = sides[c]
        values = call(
            functools.partial(middle_kernel, cuts),
            "middle",
            (masks, head, warm, perm, conduct, wet, melt, cond, energy, surface, water, heat, *mine, *theirs),
            [column] * 5 + [(2,) + halo] * cuts,
            scratch=[room] * 5,
        )
        second.append(values[:5])
        mine = values[5:]
        later.append((mine, [swap(cut, n, v) for cut, v in enumerate(mine)]))

    done = []
    for c in range(CHUNKS):
        conduct, stored, energy, surface = first[c][3], first[c][4], first[c][7], first[c][8]
        head, warm, wet, melt, cond = second[c]
        water, heat = call(team_kernel, "team", (masks, head, warm, cond), [column] * 2)
        mine, theirs = later[c]
        mine_k, theirs_k = sides[c]
        final = c == CHUNKS - 1
        done += call(
            functools.partial(last_kernel, c, cuts),
            "last",
            (
                masks, head, warm, conduct, stored, wet, melt, cond, energy, surface, water, heat,
                *mine, *theirs, *mine_k, *theirs_k, *(done if final else ()),
            ),
            [(TEAM, 2 * quarters if final else 4, OWN, cells)],
            scratch=[room] * 8 + [pltpu.VMEM((4, cells, LANES), F32)],
        )
    back = exchange(done[-1], n)
    return tuple(
        call(
            unpack_kernel,
            "unpack",
            (back,),
            [(cells, width)] * 2,
            scratch=[
                pltpu.VMEM((2, cells, width), F32),
                pltpu.SemaphoreType.DMA((2,)),
            ],
            out_specs=[hbm, hbm],
        )
    )


def solution(mesh):
    placed = (P(None, "cols"), P(None, "cols"), P(None, "cols"), P("cols"), P(), P(), P())
    return jax.shard_map(
        on_device,
        mesh=mesh,
        in_specs=placed,
        out_specs=(P(None, "cols"), P(None, "cols")),
        check_vma=False,
    )
```

```python
import functools

import jax
import jax.numpy as jnp
from jax import lax
from jax.experimental import pallas as pl
from jax.experimental.pallas import tpu as pltpu
from jax.sharding import PartitionSpec as P

SPAN = 256
PAIR_DEV = 4
LANES = 128
CHUNKS = SPAN // LANES
TEAM = 16
OWN = LANES // TEAM
SUB = 8
GROUPS = 2
WIDTH = 2 * LANES
ALL = GROUPS * WIDTH
EDGE = PAIR_DEV * OWN
VMEM_LIMIT = 32 * 1024 * 1024
DISTANCES = range(1, PAIR_DEV + 1)
F32 = jnp.float32


def cut_count(n):
    return min(n // TEAM - 1, 2)


def place(cut):
    team = lax.axis_index("cols") // TEAM
    return team, lax.rem(team, 2) == cut


def far_edge(above):
    return jnp.where(above, 0, PAIR_DEV - 1)


def sign_of(cut):
    return jnp.where(place(cut)[1], 1.0, -1.0).astype(F32)


def reciprocal(x):
    r = pl.reciprocal(x, approx=True)
    return r * (2.0 - x * r)


def sigmoid(x):
    return 0.5 + 0.5 * jnp.tanh(0.5 * x)


def passage(h, t, k):
    s = sigmoid(h)
    return k * (sigmoid(2.0 * t) * s * s + 0.02)


def lanes_of(g, b):
    return slice((g * 2 + b) * LANES, (g * 2 + b + 1) * LANES)


def following(value):
    first, second = value[:, :WIDTH], value[:, WIDTH:]
    return jnp.concatenate([second, pltpu.roll(first, SUB - 1, axis=0)], axis=1)


def preceding(value):
    first, second = value[:, :WIDTH], value[:, WIDTH:]
    return jnp.concatenate([pltpu.roll(second, 1, axis=0), first], axis=1)


def solve(steps, matrix, ratio, lead, value, update):
    c_prev = a_prev = d_prev = None
    for j in range(steps):
        above, main, below, source = matrix(j)
        if j == 0:
            r = reciprocal(main)
            a_prev = above * r
            d_prev = source * r
        else:
            r = reciprocal(main - above * c_prev)
            over = above * r
            a_prev = a_prev * over
            d_prev = source * r + d_prev * over
        c_prev = below * r
        ratio[j] = c_prev
        lead[j] = a_prev
        value[j] = d_prev
    last_c, last_a, last_d = c_prev, a_prev, d_prev
    p_first, a_first, d_first = ratio[steps - 2], lead[steps - 2], value[steps - 2]
    for j in range(steps - 3, -1, -1):
        c = ratio[j]
        p_first = c * p_first
        a_first = lead[j] + c * a_first
        d_first = value[j] + c * d_first
    g = reciprocal(1.0 - last_c * following(a_first))
    up = last_c * following(p_first) * g
    down = last_a * g
    own = (last_d + last_c * following(d_first)) * g
    step = 0
    while step < SUB:
        if step == 0:
            after, before = following, preceding
        else:
            after = functools.partial(pltpu.roll, shift=SUB - step, axis=0)
            before = functools.partial(pltpu.roll, shift=step, axis=0)
        g = reciprocal(1.0 - up * after(down) - down * before(up))
        own = (own + up * after(own) + down * before(own)) * g
        up = up * after(up) * g
        down = down * before(down) * g
        step = max(1, 2 * step)
    over = preceding(own)
    x = own
    update(steps - 1, x)
    for j in range(steps - 2, -1, -1):
        x = ratio[j] * x + (lead[j] * over + value[j])
        update(j, x)


def mask_rows(cuts):
    return 3 * PAIR_DEV + cuts * (2 * PAIR_DEV + 1)


def cut_row(cut):
    return 3 * PAIR_DEV + cut * (2 * PAIR_DEV + 1)


def mask_kernel(n, couplings, out):
    pair_rows = couplings[...].astype(F32)
    pairs = couplings.shape[1]
    pair_id = lax.broadcasted_iota(jnp.int32, (pairs, LANES), 0)
    lane = lax.broadcasted_iota(jnp.int32, (pairs, LANES), 1)
    lane_1 = lax.broadcasted_iota(jnp.int32, (SUB, LANES), 1)

    def chosen(dev, s):
        at = (pair_id == dev * PAIR_DEV + s - 1).astype(F32)
        found = jnp.dot(pair_rows, at, preferred_element_type=F32)
        return found[0:1], found[1:2]

    def put(row, value):
        out[row] = jnp.broadcast_to(value, (SUB, LANES))

    team = lax.axis_index("cols") // TEAM
    dev = team * TEAM + lane // OWN
    for s in DISTANCES:
        put(s - 1, chosen(dev, s)[0])
        put(PAIR_DEV + s - 1, chosen(dev - s, s)[1])
        put(2 * PAIR_DEV + s - 1, jnp.where(lane_1 // OWN + s < TEAM, 0.25, 0.0))
    block = lax.rem(lane_1 // EDGE, 2)
    edge = lax.rem(lane, EDGE) // OWN
    edge_1 = lax.rem(lane_1, EDGE) // OWN
    for cut in range(cut_count(n)):
        _, above = place(cut)
        row = cut_row(cut)
        partner = jnp.where(above, team + 1, team - 1)
        there = jnp.logical_and(partner >= 0, partner < n // TEAM)
        factor = jnp.where(there, 0.25, 0.0) * sign_of(cut)
        for s in DISTANCES:
            start = team * TEAM + jnp.where(above, TEAM - PAIR_DEV, -s)
            up, down = chosen(start + edge, s)
            mine = jnp.where(above, up, down)
            inward = jnp.where(above, edge_1, PAIR_DEV - 1 - edge_1)
            active = jnp.logical_and(inward >= PAIR_DEV - s, jnp.abs(mine - block.astype(F32)) < 0.5)
            put(row + s - 1, jnp.where(active, factor, 0.0))
            apart = jnp.where(above, PAIR_DEV - s, s - PAIR_DEV)
            up, down = chosen(start + edge + apart, s)
            theirs = jnp.where(edge_1 == far_edge(jnp.logical_not(above)), 0.0, jnp.where(above, down, up))
            put(row + PAIR_DEV + s - 1, jnp.where(jnp.abs(theirs - block.astype(F32)) < 0.5, 1.0, 0.0))
        outward = jnp.where(above, LANES - 1 - lane_1, lane_1)
        put(row + 2 * PAIR_DEV, jnp.where(outward < EDGE, 1.0, 0.0))


def pack_kernel(suction, warmth, classes, surface, out, room, class_room, top, in_sems):
    cells = out.shape[-1]
    quarters = 2 * CHUNKS
    into = []
    for f, field in enumerate((suction, warmth, classes, surface)):
        target = (room.at[0], room.at[1], class_room, top)[f]
        into.append(pltpu.make_async_copy(field, target, in_sems.at[f]))
        into[-1].start()

    def put(slot, value):
        out[:, slot] = value.T.reshape(TEAM, OWN, cells)

    for f in range(3):
        into[f].wait()
        for q in range(quarters):
            lanes = slice(q * LANES, (q + 1) * LANES)
            put(f * quarters + q, class_room[:, lanes].astype(F32) if f == 2 else room[f, :, lanes])
    into[3].wait()
    rows = [top[0:1, q * LANES : (q + 1) * LANES] for q in range(quarters)]
    put(3 * quarters, jnp.concatenate(rows + [jnp.zeros((cells - quarters, LANES), F32)], axis=0))


def unpack_kernel(got, suction, warmth, room, sems):
    cells = got.shape[-1]
    quarters = 2 * CHUNKS
    sent = []
    for f, out in enumerate((suction, warmth)):
        for q in range(quarters):
            room[f, :, q * LANES : (q + 1) * LANES] = got[:, f * quarters + q].reshape(LANES, cells).T
        sent.append(pltpu.make_async_copy(room.at[f], out, sems.at[f]))
        sent[-1].start()
    for copy in sent:
        copy.wait()


def edge_shift(cut, m):
    return lax.rem(EDGE * m + jnp.where(place(cut)[1], EDGE, 0), LANES)


def halo_of(cut, value):
    part = lax.broadcasted_iota(jnp.int32, (SUB, LANES), 1) // EDGE
    packed = None
    for m in range(2 * GROUPS):
        moved = pltpu.roll(value[:, m * LANES : (m + 1) * LANES], edge_shift(cut, m), axis=1)
        packed = moved if m == 0 else jnp.where(part == m, moved, packed)
    return packed


def needed_block(cut, couplings):
    team, above = place(cut)
    pair = (team * TEAM + jnp.where(above, TEAM - PAIR_DEV, -1)) * PAIR_DEV + PAIR_DEV - 1
    return couplings[jnp.where(above, 0, 1), jnp.maximum(pair, 0)]


def pieces(above):
    spare = PAIR_DEV + far_edge(above)
    parts = [j if j < PAIR_DEV else j + jnp.where(above, 1, 0) for j in range(2 * PAIR_DEV - 1)]
    return [(part, lax.rem((spare - part) * OWN + LANES, LANES)) for part in parts]


def halo_parts():
    return lax.rem(lax.broadcasted_iota(jnp.int32, (SUB, LANES), 1) // OWN, 2 * PAIR_DEV)


def squeeze(cut, block, values):
    above = place(cut)[1]
    part = halo_parts()
    single = jnp.where(block == 1, far_edge(above), -1)
    values = [jnp.where(part == single, pltpu.roll(v, LANES - EDGE, axis=1), v) for v in values]
    spare = part == PAIR_DEV + far_edge(above)
    return [
        jnp.where(spare, pltpu.roll(values[-1], shift, axis=1), v)
        for v, (_, shift) in zip(values[:-1], pieces(above))
    ]


def unsqueeze(cut, values):
    part = halo_parts()
    last = values[0]
    for v, (piece, shift) in zip(values, pieces(jnp.logical_not(place(cut)[1]))):
        last = jnp.where(part == piece, pltpu.roll(v, lax.rem(LANES - shift, LANES), axis=1), last)
    return list(values) + [last]


def edge_kernel(cuts, got, couplings, k_sat, *refs):
    halos, sent, load = refs[: CHUNKS * cuts], refs[CHUNKS * cuts : -1], refs[-1]
    cells = got.shape[-1]
    steps = halos[0].shape[1]
    stride = steps * GROUPS
    second = lax.broadcasted_iota(jnp.int32, (SUB, LANES), 1) >= 2 * EDGE
    for chunk in range(CHUNKS):
        for cut in range(cuts):
            start = jnp.where(place(cut)[1], TEAM - PAIR_DEV, 0)
            for f in range(3):
                rows = [
                    got[pl.ds(start, PAIR_DEV), (f * 2 + b) * CHUNKS + chunk].reshape(EDGE, cells)
                    for b in range(2)
                ]
                slot = (chunk * cuts + cut) * 3 + f
                load[slot] = jnp.concatenate(rows * GROUPS, axis=0).T
    for chunk in range(CHUNKS):
        for cut in range(cuts):
            for f in range(3):
                slot = (chunk * cuts + cut) * 3 + f
                values = []
                for j in range(steps):
                    v = jnp.where(
                        second,
                        load[slot, pl.ds(steps + j, SUB, stride=stride), :],
                        load[slot, pl.ds(j, SUB, stride=stride), :],
                    )
                    if f == 2:
                        k = jnp.full_like(v, k_sat[0])
                        for c in range(1, k_sat.shape[0]):
                            k = jnp.where(v >= c, k_sat[c], k)
                        v = k
                    halos[chunk * cuts + cut][f, j] = v
                    values.append(v)
                for j, v in enumerate(squeeze(cut, needed_block(cut, couplings), values)):
                    sent[chunk * cuts + cut][f, j] = v


def first_kernel(
    chunk, got, k_sat, heat_cond, head, warm, perm, conduct, wet, melt, cond, energy, top, load
):
    cells = got.shape[-1]
    steps = head.shape[0]
    stride = steps * GROUPS

    for field in range(3):
        for b in range(2):
            load[field * 2 + b] = got[:, (field * 2 + b) * CHUNKS + chunk].reshape(LANES, cells).T
    surface = got[:, 6 * CHUNKS].reshape(LANES, cells).T[0:SUB]
    rows = [surface[b * CHUNKS + chunk : b * CHUNKS + chunk + 1] for b in range(2)]
    top[...] = jnp.concatenate(rows * GROUPS, axis=1)

    def fetch(field, j):
        parts = [
            load[field * 2 + b, pl.ds(g * steps + j, SUB, stride=stride), :]
            for g in range(GROUPS)
            for b in range(2)
        ]
        return jnp.concatenate(parts, axis=1)

    for j in range(steps):
        h, t, v = [fetch(field, j) for field in range(3)]
        k = jnp.full_like(v, k_sat[0])
        lam = jnp.full_like(v, heat_cond[0])
        for c in range(1, k_sat.shape[0]):
            here = v >= c
            k = jnp.where(here, k_sat[c], k)
            lam = jnp.where(here, heat_cond[c], lam)
        s, f = sigmoid(h), sigmoid(2.0 * t)
        m = 0.05 + 0.4 * s
        head[j], warm[j], perm[j], conduct[j] = h, t, k, lam
        wet[j] = s
        melt[j] = f
        cond[j] = k * (f * s * s + 0.02)
        energy[j] = (1.0 + 2.0 * m) * t + 2.0 * m * f


def team_kernel(masks, head, warm, cond, water, heat):
    steps = head.shape[0]
    upper = [masks[s - 1] > 0.5 for s in DISTANCES]
    lower = [masks[PAIR_DEV + s - 1] > 0.5 for s in DISTANCES]

    def step(j, _):
        for g in range(GROUPS):
            l0, l1 = lanes_of(g, 0), lanes_of(g, 1)
            h0, h1 = head[j, :, l0], head[j, :, l1]
            t0, t1 = warm[j, :, l0], warm[j, :, l1]
            c0, c1 = cond[j, :, l0], cond[j, :, l1]
            total = None
            for s in DISTANCES:
                up, low = upper[s - 1], lower[s - 1]
                back = LANES - s * OWN
                h_low = pltpu.roll(jnp.where(low, h1, h0), back, axis=1)
                t_low = pltpu.roll(jnp.where(low, t1, t0), back, axis=1)
                c_low = pltpu.roll(jnp.where(low, c1, c0), back, axis=1)
                flow = (
                    masks[2 * PAIR_DEV + s - 1]
                    * (jnp.where(up, c1, c0) + c_low)
                    * (jnp.where(up, h1, h0) - h_low + 0.5)
                )
                carried = flow * jnp.where(flow > 0.0, jnp.where(up, t1, t0), t_low)
                flow_in = pltpu.roll(flow, s * OWN, axis=1)
                carried_in = pltpu.roll(carried, s * OWN, axis=1)
                part = (
                    flow_in - flow,
                    jnp.where(low, flow_in, 0.0) - jnp.where(up, flow, 0.0),
                    carried_in - carried,
                    jnp.where(low, carried_in, 0.0) - jnp.where(up, carried, 0.0),
                )
                total = part if total is None else [a + b for a, b in zip(total, part)]
            water[j, :, l0] = total[0] - total[1]
            water[j, :, l1] = total[1]
            heat[j, :, l0] = 2.0 * (total[2] - total[3])
            heat[j, :, l1] = 2.0 * total[3]

    lax.fori_loop(0, steps, step, None)


def cross_flows(cut, masks, mine, theirs):
    row = cut_row(cut)
    sign = sign_of(cut)
    above = place(cut)[1]
    lane = lax.broadcasted_iota(jnp.int32, (SUB, LANES), 1)
    first_block = lax.rem(lane, 2 * EDGE) < EDGE
    h, t, k = mine
    c = passage(h, t, k)
    far = [theirs[0], theirs[1], passage(*theirs)]
    other = [
        jnp.where(first_block, pltpu.roll(v, LANES - EDGE, axis=1), pltpu.roll(v, EDGE, axis=1)) for v in far
    ]
    water = heat = jnp.zeros((SUB, LANES), F32)
    for s in DISTANCES:
        same = masks[row + PAIR_DEV + s - 1] > 0.5
        picked = [jnp.where(same, a, b) for a, b in zip(far, other)]
        apart = (PAIR_DEV - s) * OWN
        if apart:
            shift = jnp.where(above, apart, LANES - apart)
            picked = [pltpu.roll(v, shift, axis=1) for v in picked]
        h_far, t_far, c_far = picked
        flow = masks[row + s - 1] * (c + c_far) * (sign * (h - h_far) + 0.5)
        water = water - flow
        heat = heat - flow * jnp.where(flow > 0.0, t, t_far)
    return water, heat


def advance(steps, cuts, masks, head, warm, conduct, stored, energy, wet, melt, cond, water, heat, top,
            mine, theirs, new_head, new_warm, new_wet, inflow, warm_inflow, ratio, lead, value, finish):
    for j in range(steps):
        w_parts = [water[j, :, m * LANES : (m + 1) * LANES] for m in range(2 * GROUPS)]
        q_parts = [heat[j, :, m * LANES : (m + 1) * LANES] for m in range(2 * GROUPS)]
        for cut in range(cuts):
            beside = masks[cut_row(cut) + 2 * PAIR_DEV]
            w_far, q_far = cross_flows(cut, masks, mine(cut, j), theirs(cut, j))
            for m in range(2 * GROUPS):
                shift = lax.rem(LANES - edge_shift(cut, m), LANES)
                w_parts[m] = w_parts[m] + beside * pltpu.roll(w_far, shift, axis=1)
                q_parts[m] = q_parts[m] + 2.0 * beside * pltpu.roll(q_far, shift, axis=1)
        for m in range(2 * GROUPS):
            inflow[j, :, m * LANES : (m + 1) * LANES] = w_parts[m]
            warm_inflow[j, :, m * LANES : (m + 1) * LANES] = q_parts[m]

    part = lax.broadcasted_iota(jnp.int32, (SUB, ALL), 0)
    group = lax.broadcasted_iota(jnp.int32, (SUB, ALL), 1) // WIDTH
    first_part = jnp.logical_and(part == 0, group == 0)
    last_part = jnp.logical_and(part == SUB - 1, group == GROUPS - 1)

    def faces(fields, potential):
        face_of, rise_of = [], []
        for j in range(steps):
            if j + 1 < steps:
                c_next, v_next = fields[j + 1], potential[j + 1]
                face = 0.5 * (fields[j] + c_next)
            else:
                c_next, v_next = following(fields[0]), following(potential[0])
                face = jnp.where(last_part, 0.0, 0.5 * (fields[j] + c_next))
            face_of.append(face)
            rise_of.append(v_next - potential[j])
        return face_of, rise_of

    k_face, rise = faces([cond[j] for j in range(steps)], head)
    k_top = jnp.where(first_part, 0.0, preceding(k_face[-1]))
    q_face = [k * (1.0 - d) for k, d in zip(k_face, rise)]
    q_top = jnp.where(first_part, 0.0, preceding(q_face[-1]))

    def water_matrix(j):
        above = k_top if j == 0 else k_face[j - 1]
        into = q_top if j == 0 else q_face[j - 1]
        s = wet[j]
        main = 0.8 * s * (1.0 - s) + 0.02 + above + k_face[j]
        source = inflow[j] + into - q_face[j] - 0.8 * (s - stored[j])
        return above, main, k_face[j], source

    def water_done(j, x):
        h = head[j] + x
        new_head[j] = h
        new_wet[j] = sigmoid(h)

    solve(steps, water_matrix, ratio, lead, value, water_done)

    l_cell = [conduct[j] * (1.5 - 0.5 * melt[j]) for j in range(steps)]
    l_face, rise = faces(l_cell, warm)
    l_top = jnp.where(first_part, 0.0, preceding(l_face[-1]))
    g_face = [l * d for l, d in zip(l_face, rise)]
    g_top = jnp.where(first_part, 0.0, preceding(g_face[-1]))
    surface_lam = jnp.where(first_part, 2.0 * l_cell[0], 0.0)

    def heat_matrix(j):
        above = l_top if j == 0 else l_face[j - 1]
        out_of = g_top if j == 0 else g_face[j - 1]
        t, f = warm[j], melt[j]
        m2 = 0.1 + 0.8 * new_wet[j]
        now = (1.0 + m2) * t + m2 * f
        main = 2.0 + 2.0 * m2 * (1.0 + 2.0 * f * (1.0 - f)) + above + l_face[j]
        source = warm_inflow[j] - out_of + g_face[j] - 2.0 * (now - energy[j])
        if j == 0:
            main = main + surface_lam
            source = source + surface_lam * (top[...] - t)
        return above, main, l_face[j], source

    def heat_done(j, x):
        t = warm[j] + x
        new_warm[j] = t
        finish(j, t)

    solve(steps, heat_matrix, ratio, lead, value, heat_done)


def middle_kernel(cuts, *refs):
    masks, head, warm, perm, conduct, wet, melt, cond, energy, top, water, heat, couplings = refs[:13]
    own, far = refs[13 : 13 + cuts], refs[13 + cuts : 13 + 2 * cuts]
    new_head, new_warm, new_wet, new_melt, new_cond = refs[13 + 2 * cuts : 18 + 2 * cuts]
    halos, sent = refs[18 + 2 * cuts : 18 + 3 * cuts], refs[18 + 3 * cuts : 18 + 4 * cuts]
    inflow, warm_inflow, ratio, lead, value = refs[18 + 4 * cuts :]
    steps = head.shape[0]
    packed = {}

    def finish(j, t):
        s, f = new_wet[j], sigmoid(2.0 * t)
        new_melt[j] = f
        new_cond[j] = perm[j] * (f * s * s + 0.02)
        for cut in range(cuts):
            for i, v in enumerate((new_head[j], t)):
                packed[cut, i, j] = halo_of(cut, v)
                halos[cut][i, j] = packed[cut, i, j]

    theirs = [[unsqueeze(cut, [far[cut][i, j] for j in range(steps - 1)]) for i in range(3)] for cut in range(cuts)]
    advance(
        steps, cuts, masks, head, warm, conduct, wet, energy, wet, melt, cond, water, heat, top,
        lambda cut, j: [own[cut][i, j] for i in range(3)],
        lambda cut, j: [theirs[cut][i][j] for i in range(3)],
        new_head, new_warm, new_wet, inflow, warm_inflow, ratio, lead, value, finish,
    )
    for cut in range(cuts):
        for i in range(2):
            values = squeeze(cut, needed_block(cut, couplings), [packed[cut, i, j] for j in range(steps)])
            for j, v in enumerate(values):
                sent[cut][i, j] = v


def last_kernel(chunk, cuts, *refs):
    masks, head, warm, conduct, stored, wet, melt, cond, energy, top, water, heat = refs[:12]
    own, far = refs[12 : 12 + cuts], refs[12 + cuts : 12 + 2 * cuts]
    own_k, far_k = refs[12 + 2 * cuts : 12 + 3 * cuts], refs[12 + 3 * cuts : 12 + 4 * cuts]
    others = refs[12 + 4 * cuts : -10]
    out, new_head, new_warm, new_wet, inflow, warm_inflow, ratio, lead, value, load = refs[-10:]
    steps = head.shape[0]
    cells = steps * GROUPS * SUB
    stride = steps * GROUPS
    theirs = [
        [unsqueeze(cut, [source[i, j] for j in range(steps - 1)]) for source, i in ((far[cut], 0), (far[cut], 1), (far_k[cut], 2))]
        for cut in range(cuts)
    ]
    advance(
        steps, cuts, masks, head, warm, conduct, stored, energy, wet, melt, cond, water, heat, top,
        lambda cut, j: [own[cut][0, j], own[cut][1, j], own_k[cut][2, j]],
        lambda cut, j: [theirs[cut][i][j] for i in range(3)],
        new_head, new_warm, new_wet, inflow, warm_inflow, ratio, lead, value, lambda j, t: None,
    )
    final = chunk == CHUNKS - 1
    for f, field in enumerate((new_head, new_warm)):
        for b in range(2):
            slot = f * 2 + b
            for j in range(steps):
                for g in range(GROUPS):
                    load[slot, pl.ds(g * steps + j, SUB, stride=stride), :] = field[j, :, lanes_of(g, b)]
            turned = load[slot].T.reshape(TEAM, OWN, cells)
            if final:
                out[:, slot * CHUNKS + chunk] = turned
                for c, other in enumerate(others):
                    out[:, slot * CHUNKS + c] = other[:, slot]
            else:
                out[:, slot] = turned


def whole(memory=pltpu.VMEM):
    return pl.BlockSpec(memory_space=memory)


def call(kernel, name, args, outs, scratch=(), specs=None, out_specs=None, limit=VMEM_LIMIT, work=2_000_000):
    return pl.pallas_call(
        kernel,
        out_shape=[jax.ShapeDtypeStruct(shape, F32) for shape in outs],
        in_specs=specs or [whole()] * len(args),
        out_specs=out_specs or [whole()] * len(outs),
        scratch_shapes=scratch,
        compiler_params=pltpu.CompilerParams(vmem_limit_bytes=limit),
        cost_estimate=pl.CostEstimate(flops=work, bytes_accessed=work, transcendentals=0),
        name=name,
    )(*args)


def exchange(tiles, n):
    teams = [list(range(start, start + TEAM)) for start in range(0, n, TEAM)]
    return lax.all_to_all(
        tiles, "cols", split_axis=0, concat_axis=0, tiled=True, axis_index_groups=teams
    )


def swap(cut, n, value):
    pairs = []
    for team in range(cut, n // TEAM - 1, 2):
        for i in range(team * TEAM, (team + 1) * TEAM):
            pairs += [(i, i + TEAM), (i + TEAM, i)]
    return lax.ppermute(value, "cols", pairs)


def on_device(suction, warmth, classes, top, couplings, k_sat, heat_cond):
    n = lax.axis_size("cols")
    cells, width = suction.shape
    steps = cells // (SUB * GROUPS)
    quarters = width // LANES
    cuts = cut_count(n)
    column = (steps, SUB, ALL)
    halo = (steps, SUB, LANES)
    squeezed = (steps - 1, SUB, LANES)
    room = pltpu.VMEM(column, F32)
    smem = whole(pltpu.SMEM)
    hbm = whole(pltpu.HBM)

    masks = call(
        functools.partial(mask_kernel, n), "masks", (couplings,), [(mask_rows(cuts), SUB, LANES)]
    )[0]
    packed = call(
        pack_kernel,
        "pack",
        [pltpu.with_memory_space_constraint(v, pltpu.HBM) for v in (suction, warmth, classes, top.reshape(1, width))],
        [(TEAM, 3 * quarters + 1, OWN, cells)],
        scratch=[
            pltpu.VMEM((2, cells, width), F32),
            pltpu.VMEM((cells, width), classes.dtype),
            pltpu.VMEM((1, width), F32),
            pltpu.SemaphoreType.DMA((4,)),
        ],
        specs=[hbm] * 4,
    )[0]
    got = exchange(packed, n)

    edges = call(
        functools.partial(edge_kernel, cuts),
        "edges",
        (got, couplings, k_sat),
        [(3,) + halo] * (CHUNKS * cuts) + [(3,) + squeezed] * (CHUNKS * cuts),
        scratch=[pltpu.VMEM((3 * CHUNKS * cuts, cells, LANES), F32)],
        specs=[whole(), smem, smem],
    )
    first = [
        call(
            functools.partial(first_kernel, c),
            "first",
            (got, k_sat, heat_cond),
            [column] * 8 + [(1, ALL)],
            scratch=[pltpu.VMEM((6, cells, LANES), F32)],
            specs=[whole(), smem, smem],
        )
        for c in range(CHUNKS)
    ]
    flows, sides = [], []
    for c in range(CHUNKS):
        mine = edges[c * cuts : (c + 1) * cuts]
        sent = edges[(CHUNKS + c) * cuts : (CHUNKS + c + 1) * cuts]
        sides.append((mine, [swap(cut, n, v) for cut, v in enumerate(sent)]))
        flows.append(tuple(call(team_kernel, "team", (masks, first[c][0], first[c][1], first[c][6]), [column] * 2)))

    second, later = [], []
    for c in range(CHUNKS):
        head, warm, perm, conduct, wet, melt, cond, energy, surface = first[c]
        water, heat = flows[c]
        mine, theirs = sides[c]
        values = call(
            functools.partial(middle_kernel, cuts),
            "middle",
            (masks, head, warm, perm, conduct, wet, melt, cond, energy, surface, water, heat, couplings, *mine, *theirs),
            [column] * 5 + [(2,) + halo] * cuts + [(2,) + squeezed] * cuts,
            scratch=[room] * 5,
            specs=[whole()] * 12 + [smem] + [whole()] * (2 * cuts),
        )
        second.append(values[:5])
        mine, sent = values[5 : 5 + cuts], values[5 + cuts :]
        later.append((mine, [swap(cut, n, v) for cut, v in enumerate(sent)]))

    done = []
    for c in range(CHUNKS):
        conduct, stored, energy, surface = first[c][3], first[c][4], first[c][7], first[c][8]
        head, warm, wet, melt, cond = second[c]
        water, heat = call(team_kernel, "team", (masks, head, warm, cond), [column] * 2)
        mine, theirs = later[c]
        mine_k, theirs_k = sides[c]
        final = c == CHUNKS - 1
        done += call(
            functools.partial(last_kernel, c, cuts),
            "last",
            (
                masks, head, warm, conduct, stored, wet, melt, cond, energy, surface, water, heat,
                *mine, *theirs, *mine_k, *theirs_k, *(done if final else ()),
            ),
            [(TEAM, 2 * quarters if final else 4, OWN, cells)],
            scratch=[room] * 8 + [pltpu.VMEM((4, cells, LANES), F32)],
        )
    back = exchange(done[-1], n)
    return tuple(
        call(
            unpack_kernel,
            "unpack",
            (back,),
            [(cells, width)] * 2,
            scratch=[
                pltpu.VMEM((2, cells, width), F32),
                pltpu.SemaphoreType.DMA((2,)),
            ],
            out_specs=[hbm, hbm],
        )
    )


def solution(mesh):
    placed = (P(None, "cols"), P(None, "cols"), P(None, "cols"), P("cols"), P(), P(), P())
    return jax.shard_map(
        on_device,
        mesh=mesh,
        in_specs=placed,
        out_specs=(P(None, "cols"), P(None, "cols")),
        check_vma=False,
    )
```

```python
import functools

import jax
import jax.numpy as jnp
from jax import lax
from jax.experimental import pallas as pl
from jax.experimental.pallas import tpu as pltpu
from jax.sharding import PartitionSpec as P

SPAN = 256
PAIR_DEV = 4
LANES = 128
CHUNKS = SPAN // LANES
TEAM = 16
OWN = LANES // TEAM
SUB = 8
GROUPS = 2
WIDTH = 2 * LANES
ALL = GROUPS * WIDTH
EDGE = PAIR_DEV * OWN
VMEM_LIMIT = 32 * 1024 * 1024
DISTANCES = range(1, PAIR_DEV + 1)
F32 = jnp.float32


def cut_count(n):
    return min(n // TEAM - 1, 2)


def place(cut):
    team = lax.axis_index("cols") // TEAM
    return team, lax.rem(team, 2) == cut


def far_edge(above):
    return jnp.where(above, 0, PAIR_DEV - 1)


def sign_of(cut):
    return jnp.where(place(cut)[1], 1.0, -1.0).astype(F32)


def reciprocal(x):
    return pltpu.reciprocal(x, approx=True)


def sigmoid(x):
    return 0.5 + 0.5 * jnp.tanh(0.5 * x)


def passage(h, t, k):
    s = sigmoid(h)
    return k * (sigmoid(2.0 * t) * s * s + 0.02)


def lanes_of(g, b):
    return slice((g * 2 + b) * LANES, (g * 2 + b + 1) * LANES)


def following(value):
    first, second = value[:, :WIDTH], value[:, WIDTH:]
    return jnp.concatenate([second, pltpu.roll(first, SUB - 1, axis=0)], axis=1)


def preceding(value):
    first, second = value[:, :WIDTH], value[:, WIDTH:]
    return jnp.concatenate([pltpu.roll(second, 1, axis=0), first], axis=1)


def solve(steps, matrix, ratio, lead, value, update):
    c_prev = a_prev = d_prev = None
    for j in range(steps):
        above, main, below, source = matrix(j)
        if j == 0:
            r = reciprocal(main)
            a_prev = above * r
            d_prev = source * r
        else:
            r = reciprocal(main - above * c_prev)
            over = above * r
            a_prev = a_prev * over
            d_prev = source * r + d_prev * over
        c_prev = below * r
        ratio[j] = c_prev
        lead[j] = a_prev
        value[j] = d_prev
    last_c, last_a, last_d = c_prev, a_prev, d_prev
    p_first, a_first, d_first = ratio[steps - 2], lead[steps - 2], value[steps - 2]
    for j in range(steps - 3, -1, -1):
        c = ratio[j]
        p_first = c * p_first
        a_first = lead[j] + c * a_first
        d_first = value[j] + c * d_first
    g = reciprocal(1.0 - last_c * following(a_first))
    up = last_c * following(p_first) * g
    down = last_a * g
    own = (last_d + last_c * following(d_first)) * g
    step = 0
    while step < SUB:
        if step == 0:
            after, before = following, preceding
        else:
            after = functools.partial(pltpu.roll, shift=SUB - step, axis=0)
            before = functools.partial(pltpu.roll, shift=step, axis=0)
        g = reciprocal(1.0 - up * after(down) - down * before(up))
        own = (own + up * after(own) + down * before(own)) * g
        up = up * after(up) * g
        down = down * before(down) * g
        step = max(1, 2 * step)
    over = preceding(own)
    x = own
    update(steps - 1, x)
    for j in range(steps - 2, -1, -1):
        x = ratio[j] * x + (lead[j] * over + value[j])
        update(j, x)


def mask_rows(cuts):
    return 3 * PAIR_DEV + cuts * (2 * PAIR_DEV + 2)


def cut_row(cut):
    return 3 * PAIR_DEV + cut * (2 * PAIR_DEV + 2)


def mask_kernel(n, couplings, out):
    pair_rows = couplings[...].astype(F32)
    pairs = couplings.shape[1]
    pair_id = lax.broadcasted_iota(jnp.int32, (pairs, LANES), 0)
    lane = lax.broadcasted_iota(jnp.int32, (pairs, LANES), 1)
    lane_1 = lax.broadcasted_iota(jnp.int32, (SUB, LANES), 1)

    def chosen(dev, s):
        at = (pair_id == dev * PAIR_DEV + s - 1).astype(F32)
        found = jnp.dot(pair_rows, at, preferred_element_type=F32)
        return found[0:1], found[1:2]

    def put(row, value):
        out[row] = jnp.broadcast_to(value, (SUB, LANES))

    team = lax.axis_index("cols") // TEAM
    dev = team * TEAM + lane // OWN
    for s in DISTANCES:
        put(s - 1, chosen(dev, s)[0])
        put(PAIR_DEV + s - 1, chosen(dev - s, s)[1])
        put(2 * PAIR_DEV + s - 1, jnp.where(lane_1 // OWN + s < TEAM, 0.25, 0.0))
    block = lax.rem(lane_1 // EDGE, 2)
    edge = lax.rem(lane, EDGE) // OWN
    edge_1 = lax.rem(lane_1, EDGE) // OWN
    for cut in range(cut_count(n)):
        _, above = place(cut)
        row = cut_row(cut)
        partner = jnp.where(above, team + 1, team - 1)
        there = jnp.logical_and(partner >= 0, partner < n // TEAM)
        factor = jnp.where(there, 0.25, 0.0) * sign_of(cut)
        for s in DISTANCES:
            start = team * TEAM + jnp.where(above, TEAM - PAIR_DEV, -s)
            up, down = chosen(start + edge, s)
            mine = jnp.where(above, up, down)
            inward = jnp.where(above, edge_1, PAIR_DEV - 1 - edge_1)
            active = jnp.logical_and(inward >= PAIR_DEV - s, jnp.abs(mine - block.astype(F32)) < 0.5)
            put(row + s - 1, jnp.where(active, factor, 0.0))
            apart = jnp.where(above, PAIR_DEV - s, s - PAIR_DEV)
            up, down = chosen(start + edge + apart, s)
            theirs = jnp.where(edge_1 == far_edge(jnp.logical_not(above)), 0.0, jnp.where(above, down, up))
            put(row + PAIR_DEV + s - 1, jnp.where(jnp.abs(theirs - block.astype(F32)) < 0.5, 1.0, 0.0))
        outward = jnp.where(above, LANES - 1 - lane_1, lane_1)
        put(row + 2 * PAIR_DEV, jnp.where(outward < EDGE, 1.0, 0.0))
        single = jnp.logical_and(edge_1 == far_edge(above), block == 0)
        put(row + 2 * PAIR_DEV + 1, jnp.where(single, mine, 0.0))


def pack_kernel(suction, warmth, classes, surface, out, room, class_room, top, in_sems):
    cells = out.shape[-1]
    quarters = 2 * CHUNKS
    into = []
    for f, field in enumerate((suction, warmth, classes, surface)):
        target = (room.at[0], room.at[1], class_room, top)[f]
        into.append(pltpu.make_async_copy(field, target, in_sems.at[f]))
        into[-1].start()

    def put(slot, value):
        out[:, slot] = value.T.reshape(TEAM, OWN, cells)

    for f in range(3):
        into[f].wait()
        for q in range(quarters):
            lanes = slice(q * LANES, (q + 1) * LANES)
            put(f * quarters + q, class_room[:, lanes].astype(F32) if f == 2 else room[f, :, lanes])
    into[3].wait()
    rows = [top[0:1, q * LANES : (q + 1) * LANES] for q in range(quarters)]
    put(3 * quarters, jnp.concatenate(rows + [jnp.zeros((cells - quarters, LANES), F32)], axis=0))


def unpack_kernel(got, suction, warmth, room, sems):
    cells = got.shape[-1]
    quarters = 2 * CHUNKS
    sent = []
    for f, out in enumerate((suction, warmth)):
        for q in range(quarters):
            room[f, :, q * LANES : (q + 1) * LANES] = got[:, f * quarters + q].reshape(LANES, cells).T
        sent.append(pltpu.make_async_copy(room.at[f], out, sems.at[f]))
        sent[-1].start()
    for copy in sent:
        copy.wait()


def edge_shift(cut, m):
    return lax.rem(EDGE * m + jnp.where(place(cut)[1], EDGE, 0), LANES)


def halo_of(cut, value):
    part = lax.broadcasted_iota(jnp.int32, (SUB, LANES), 1) // EDGE
    packed = None
    for m in range(2 * GROUPS):
        moved = pltpu.roll(value[:, m * LANES : (m + 1) * LANES], edge_shift(cut, m), axis=1)
        packed = moved if m == 0 else jnp.where(part == m, moved, packed)
    return packed


def needed_block(cut, couplings):
    team, above = place(cut)
    pair = (team * TEAM + jnp.where(above, TEAM - PAIR_DEV, -1)) * PAIR_DEV + PAIR_DEV - 1
    return couplings[jnp.where(above, 0, 1), jnp.maximum(pair, 0)]


def pieces(above):
    spare = PAIR_DEV + far_edge(above)
    parts = [j if j < PAIR_DEV else j + jnp.where(above, 1, 0) for j in range(2 * PAIR_DEV - 1)]
    return [(part, lax.rem((spare - part) * OWN + LANES, LANES)) for part in parts]


def halo_parts():
    return lax.rem(lax.broadcasted_iota(jnp.int32, (SUB, LANES), 1) // OWN, 2 * PAIR_DEV)


def squeeze(cut, other, values):
    above = place(cut)[1]
    values = [jnp.where(other, pltpu.roll(v, LANES - EDGE, axis=1), v) for v in values]
    spare = halo_parts() == PAIR_DEV + far_edge(above)
    return [
        jnp.where(spare, pltpu.roll(values[-1], shift, axis=1), v)
        for v, (_, shift) in zip(values[:-1], pieces(above))
    ]


def unsqueeze(cut, values):
    part = halo_parts()
    last = values[0]
    for v, (piece, shift) in zip(values, pieces(jnp.logical_not(place(cut)[1]))):
        last = jnp.where(part == piece, pltpu.roll(v, lax.rem(LANES - shift, LANES), axis=1), last)
    return list(values) + [last]


def edge_kernel(cuts, got, couplings, k_sat, *refs):
    halos, sent, load = refs[: CHUNKS * cuts], refs[CHUNKS * cuts : -1], refs[-1]
    cells = got.shape[-1]
    steps = halos[0].shape[1]
    stride = steps * GROUPS
    second = lax.broadcasted_iota(jnp.int32, (SUB, LANES), 1) >= 2 * EDGE
    for chunk in range(CHUNKS):
        for cut in range(cuts):
            start = jnp.where(place(cut)[1], TEAM - PAIR_DEV, 0)
            for f in range(3):
                rows = [
                    got[pl.ds(start, PAIR_DEV), (f * 2 + b) * CHUNKS + chunk].reshape(EDGE, cells)
                    for b in range(2)
                ]
                slot = (chunk * cuts + cut) * 3 + f
                load[slot] = jnp.concatenate(rows * GROUPS, axis=0).T
    for chunk in range(CHUNKS):
        for cut in range(cuts):
            for f in range(3):
                slot = (chunk * cuts + cut) * 3 + f
                values = []
                for j in range(steps):
                    v = jnp.where(
                        second,
                        load[slot, pl.ds(steps + j, SUB, stride=stride), :],
                        load[slot, pl.ds(j, SUB, stride=stride), :],
                    )
                    if f == 2:
                        k = jnp.full_like(v, k_sat[0])
                        for c in range(1, k_sat.shape[0]):
                            k = jnp.where(v >= c, k_sat[c], k)
                        v = k
                    halos[chunk * cuts + cut][f, j] = v
                    values.append(v)
                single = jnp.where(needed_block(cut, couplings) == 1, far_edge(place(cut)[1]), -1)
                for j, v in enumerate(squeeze(cut, halo_parts() == single, values)):
                    sent[chunk * cuts + cut][f, j] = v


def first_kernel(
    chunk, got, k_sat, heat_cond, head, warm, perm, conduct, wet, melt, cond, energy, top, load
):
    cells = got.shape[-1]
    steps = head.shape[0]
    stride = steps * GROUPS

    for field in range(3):
        for b in range(2):
            load[field * 2 + b] = got[:, (field * 2 + b) * CHUNKS + chunk].reshape(LANES, cells).T
    surface = got[:, 6 * CHUNKS].reshape(LANES, cells).T[0:SUB]
    rows = [surface[b * CHUNKS + chunk : b * CHUNKS + chunk + 1] for b in range(2)]
    top[...] = jnp.concatenate(rows * GROUPS, axis=1)

    def fetch(field, j):
        parts = [
            load[field * 2 + b, pl.ds(g * steps + j, SUB, stride=stride), :]
            for g in range(GROUPS)
            for b in range(2)
        ]
        return jnp.concatenate(parts, axis=1)

    for j in range(steps):
        h, t, v = [fetch(field, j) for field in range(3)]
        k = jnp.full_like(v, k_sat[0])
        lam = jnp.full_like(v, heat_cond[0])
        for c in range(1, k_sat.shape[0]):
            here = v >= c
            k = jnp.where(here, k_sat[c], k)
            lam = jnp.where(here, heat_cond[c], lam)
        s, f = sigmoid(h), sigmoid(2.0 * t)
        m = 0.05 + 0.4 * s
        head[j], warm[j], perm[j], conduct[j] = h, t, k, lam
        wet[j] = s
        melt[j] = f
        cond[j] = k * (f * s * s + 0.02)
        energy[j] = (1.0 + 2.0 * m) * t + 2.0 * m * f


def team_kernel(masks, head, warm, cond, water, heat):
    steps = head.shape[0]
    upper = [masks[s - 1] > 0.5 for s in DISTANCES]
    lower = [masks[PAIR_DEV + s - 1] > 0.5 for s in DISTANCES]

    def step(j, _):
        for g in range(GROUPS):
            l0, l1 = lanes_of(g, 0), lanes_of(g, 1)
            h0, h1 = head[j, :, l0], head[j, :, l1]
            t0, t1 = warm[j, :, l0], warm[j, :, l1]
            c0, c1 = cond[j, :, l0], cond[j, :, l1]
            total = None
            for s in DISTANCES:
                up, low = upper[s - 1], lower[s - 1]
                back = LANES - s * OWN
                h_low = pltpu.roll(jnp.where(low, h1, h0), back, axis=1)
                t_low = pltpu.roll(jnp.where(low, t1, t0), back, axis=1)
                c_low = pltpu.roll(jnp.where(low, c1, c0), back, axis=1)
                flow = (
                    masks[2 * PAIR_DEV + s - 1]
                    * (jnp.where(up, c1, c0) + c_low)
                    * (jnp.where(up, h1, h0) - h_low + 0.5)
                )
                carried = flow * jnp.where(flow > 0.0, jnp.where(up, t1, t0), t_low)
                flow_in = pltpu.roll(flow, s * OWN, axis=1)
                carried_in = pltpu.roll(carried, s * OWN, axis=1)
                part = (
                    flow_in - flow,
                    jnp.where(low, flow_in, 0.0) - jnp.where(up, flow, 0.0),
                    carried_in - carried,
                    jnp.where(low, carried_in, 0.0) - jnp.where(up, carried, 0.0),
                )
                total = part if total is None else [a + b for a, b in zip(total, part)]
            water[j, :, l0] = total[0] - total[1]
            water[j, :, l1] = total[1]
            heat[j, :, l0] = 2.0 * (total[2] - total[3])
            heat[j, :, l1] = 2.0 * total[3]

    lax.fori_loop(0, steps, step, None)


def cross_flows(cut, masks, mine, theirs):
    row = cut_row(cut)
    sign = sign_of(cut)
    above = place(cut)[1]
    lane = lax.broadcasted_iota(jnp.int32, (SUB, LANES), 1)
    first_block = lax.rem(lane, 2 * EDGE) < EDGE
    h, t, k = mine
    c = passage(h, t, k)
    far = [theirs[0], theirs[1], passage(*theirs)]
    other = [
        jnp.where(first_block, pltpu.roll(v, LANES - EDGE, axis=1), pltpu.roll(v, EDGE, axis=1)) for v in far
    ]
    water = heat = jnp.zeros((SUB, LANES), F32)
    for s in DISTANCES:
        same = masks[row + PAIR_DEV + s - 1] > 0.5
        picked = [jnp.where(same, a, b) for a, b in zip(far, other)]
        apart = (PAIR_DEV - s) * OWN
        if apart:
            shift = jnp.where(above, apart, LANES - apart)
            picked = [pltpu.roll(v, shift, axis=1) for v in picked]
        h_far, t_far, c_far = picked
        flow = masks[row + s - 1] * (c + c_far) * (sign * (h - h_far) + 0.5)
        water = water - flow
        heat = heat - flow * jnp.where(flow > 0.0, t, t_far)
    return water, heat


def advance(steps, cuts, masks, head, warm, conduct, stored, energy, wet, melt, cond, water, heat, top,
            mine, theirs, new_head, new_warm, new_wet, inflow, warm_inflow, ratio, lead, value, finish):
    for j in range(steps):
        w_parts = [water[j, :, m * LANES : (m + 1) * LANES] for m in range(2 * GROUPS)]
        q_parts = [heat[j, :, m * LANES : (m + 1) * LANES] for m in range(2 * GROUPS)]
        for cut in range(cuts):
            beside = masks[cut_row(cut) + 2 * PAIR_DEV]
            w_far, q_far = cross_flows(cut, masks, mine(cut, j), theirs(cut, j))
            for m in range(2 * GROUPS):
                shift = lax.rem(LANES - edge_shift(cut, m), LANES)
                w_parts[m] = w_parts[m] + beside * pltpu.roll(w_far, shift, axis=1)
                q_parts[m] = q_parts[m] + 2.0 * beside * pltpu.roll(q_far, shift, axis=1)
        for m in range(2 * GROUPS):
            inflow[j, :, m * LANES : (m + 1) * LANES] = w_parts[m]
            warm_inflow[j, :, m * LANES : (m + 1) * LANES] = q_parts[m]

    part = lax.broadcasted_iota(jnp.int32, (SUB, ALL), 0)
    group = lax.broadcasted_iota(jnp.int32, (SUB, ALL), 1) // WIDTH
    first_part = jnp.logical_and(part == 0, group == 0)
    last_part = jnp.logical_and(part == SUB - 1, group == GROUPS - 1)

    def faces(fields, potential):
        face_of, rise_of = [], []
        for j in range(steps):
            if j + 1 < steps:
                c_next, v_next = fields[j + 1], potential[j + 1]
                face = 0.5 * (fields[j] + c_next)
            else:
                c_next, v_next = following(fields[0]), following(potential[0])
                face = jnp.where(last_part, 0.0, 0.5 * (fields[j] + c_next))
            face_of.append(face)
            rise_of.append(v_next - potential[j])
        return face_of, rise_of

    k_face, rise = faces([cond[j] for j in range(steps)], head)
    k_top = jnp.where(first_part, 0.0, preceding(k_face[-1]))
    q_face = [k * (1.0 - d) for k, d in zip(k_face, rise)]
    q_top = jnp.where(first_part, 0.0, preceding(q_face[-1]))

    def water_matrix(j):
        above = k_top if j == 0 else k_face[j - 1]
        into = q_top if j == 0 else q_face[j - 1]
        s = wet[j]
        main = 0.8 * s * (1.0 - s) + 0.02 + above + k_face[j]
        source = inflow[j] + into - q_face[j] - 0.8 * (s - stored[j])
        return above, main, k_face[j], source

    def water_done(j, x):
        h = head[j] + x
        new_head[j] = h
        new_wet[j] = sigmoid(h)

    solve(steps, water_matrix, ratio, lead, value, water_done)

    l_cell = [conduct[j] * (1.5 - 0.5 * melt[j]) for j in range(steps)]
    l_face, rise = faces(l_cell, warm)
    l_top = jnp.where(first_part, 0.0, preceding(l_face[-1]))
    g_face = [l * d for l, d in zip(l_face, rise)]
    g_top = jnp.where(first_part, 0.0, preceding(g_face[-1]))
    surface_lam = jnp.where(first_part, 2.0 * l_cell[0], 0.0)

    def heat_matrix(j):
        above = l_top if j == 0 else l_face[j - 1]
        out_of = g_top if j == 0 else g_face[j - 1]
        t, f = warm[j], melt[j]
        m2 = 0.1 + 0.8 * new_wet[j]
        now = (1.0 + m2) * t + m2 * f
        main = 2.0 + 2.0 * m2 * (1.0 + 2.0 * f * (1.0 - f)) + above + l_face[j]
        source = warm_inflow[j] - out_of + g_face[j] - 2.0 * (now - energy[j])
        if j == 0:
            main = main + surface_lam
            source = source + surface_lam * (top[...] - t)
        return above, main, l_face[j], source

    def heat_done(j, x):
        t = warm[j] + x
        new_warm[j] = t
        finish(j, t)

    solve(steps, heat_matrix, ratio, lead, value, heat_done)


def middle_kernel(cuts, *refs):
    masks, head, warm, perm, conduct, wet, melt, cond, energy, top, water, heat = refs[:12]
    own, far = refs[12 : 12 + cuts], refs[12 + cuts : 12 + 2 * cuts]
    new_head, new_warm, new_wet, new_melt, new_cond = refs[12 + 2 * cuts : 17 + 2 * cuts]
    halos, sent = refs[17 + 2 * cuts : 17 + 3 * cuts], refs[17 + 3 * cuts : 17 + 4 * cuts]
    inflow, warm_inflow, ratio, lead, value = refs[17 + 4 * cuts :]
    steps = head.shape[0]
    packed = {}

    def finish(j, t):
        s, f = new_wet[j], sigmoid(2.0 * t)
        new_melt[j] = f
        new_cond[j] = perm[j] * (f * s * s + 0.02)
        for cut in range(cuts):
            for i, v in enumerate((new_head[j], t)):
                packed[cut, i, j] = halo_of(cut, v)
                halos[cut][i, j] = packed[cut, i, j]

    theirs = [[unsqueeze(cut, [far[cut][i, j] for j in range(steps - 1)]) for i in range(3)] for cut in range(cuts)]
    advance(
        steps, cuts, masks, head, warm, conduct, wet, energy, wet, melt, cond, water, heat, top,
        lambda cut, j: [own[cut][i, j] for i in range(3)],
        lambda cut, j: [theirs[cut][i][j] for i in range(3)],
        new_head, new_warm, new_wet, inflow, warm_inflow, ratio, lead, value, finish,
    )
    for cut in range(cuts):
        for i in range(2):
            other = masks[cut_row(cut) + 2 * PAIR_DEV + 1] > 0.5
            values = squeeze(cut, other, [packed[cut, i, j] for j in range(steps)])
            for j, v in enumerate(values):
                sent[cut][i, j] = v


def last_kernel(chunk, cuts, *refs):
    masks, head, warm, conduct, stored, wet, melt, cond, energy, top, water, heat = refs[:12]
    own, far = refs[12 : 12 + cuts], refs[12 + cuts : 12 + 2 * cuts]
    own_k, far_k = refs[12 + 2 * cuts : 12 + 3 * cuts], refs[12 + 3 * cuts : 12 + 4 * cuts]
    others = refs[12 + 4 * cuts : -10]
    out, new_head, new_warm, new_wet, inflow, warm_inflow, ratio, lead, value, load = refs[-10:]
    steps = head.shape[0]
    cells = steps * GROUPS * SUB
    stride = steps * GROUPS
    theirs = [
        [unsqueeze(cut, [source[i, j] for j in range(steps - 1)]) for source, i in ((far[cut], 0), (far[cut], 1), (far_k[cut], 2))]
        for cut in range(cuts)
    ]
    advance(
        steps, cuts, masks, head, warm, conduct, stored, energy, wet, melt, cond, water, heat, top,
        lambda cut, j: [own[cut][0, j], own[cut][1, j], own_k[cut][2, j]],
        lambda cut, j: [theirs[cut][i][j] for i in range(3)],
        new_head, new_warm, new_wet, inflow, warm_inflow, ratio, lead, value, lambda j, t: None,
    )
    final = chunk == CHUNKS - 1
    for f, field in enumerate((new_head, new_warm)):
        for b in range(2):
            slot = f * 2 + b
            for j in range(steps):
                for g in range(GROUPS):
                    load[slot, pl.ds(g * steps + j, SUB, stride=stride), :] = field[j, :, lanes_of(g, b)]
            turned = load[slot].T.reshape(TEAM, OWN, cells)
            if final:
                out[:, slot * CHUNKS + chunk] = turned
                for c, other in enumerate(others):
                    out[:, slot * CHUNKS + c] = other[:, slot]
            else:
                out[:, slot] = turned


def whole(memory=pltpu.VMEM):
    return pl.BlockSpec(memory_space=memory)


def call(kernel, name, args, outs, scratch=(), specs=None, out_specs=None, limit=VMEM_LIMIT, work=2_000_000):
    return pl.pallas_call(
        kernel,
        out_shape=[jax.ShapeDtypeStruct(shape, F32) for shape in outs],
        in_specs=specs or [whole()] * len(args),
        out_specs=out_specs or [whole()] * len(outs),
        scratch_shapes=scratch,
        compiler_params=pltpu.CompilerParams(vmem_limit_bytes=limit),
        cost_estimate=pl.CostEstimate(flops=work, bytes_accessed=work, transcendentals=0),
        name=name,
    )(*args)


def exchange(tiles, n):
    teams = [list(range(start, start + TEAM)) for start in range(0, n, TEAM)]
    return lax.all_to_all(
        tiles, "cols", split_axis=0, concat_axis=0, tiled=True, axis_index_groups=teams
    )


def swap(cut, n, value):
    pairs = []
    for team in range(cut, n // TEAM - 1, 2):
        for i in range(team * TEAM, (team + 1) * TEAM):
            pairs += [(i, i + TEAM), (i + TEAM, i)]
    return lax.ppermute(value, "cols", pairs)


def on_device(suction, warmth, classes, top, couplings, k_sat, heat_cond):
    n = lax.axis_size("cols")
    cells, width = suction.shape
    steps = cells // (SUB * GROUPS)
    quarters = width // LANES
    cuts = cut_count(n)
    column = (steps, SUB, ALL)
    halo = (steps, SUB, LANES)
    squeezed = (steps - 1, SUB, LANES)
    room = pltpu.VMEM(column, F32)
    smem = whole(pltpu.SMEM)
    hbm = whole(pltpu.HBM)

    masks = call(
        functools.partial(mask_kernel, n), "masks", (couplings,), [(mask_rows(cuts), SUB, LANES)]
    )[0]
    packed = call(
        pack_kernel,
        "pack",
        [pltpu.with_memory_space_constraint(v, pltpu.HBM) for v in (suction, warmth, classes, top.reshape(1, width))],
        [(TEAM, 3 * quarters + 1, OWN, cells)],
        scratch=[
            pltpu.VMEM((2, cells, width), F32),
            pltpu.VMEM((cells, width), classes.dtype),
            pltpu.VMEM((1, width), F32),
            pltpu.SemaphoreType.DMA((4,)),
        ],
        specs=[hbm] * 4,
    )[0]
    got = exchange(packed, n)

    edges = call(
        functools.partial(edge_kernel, cuts),
        "edges",
        (got, couplings, k_sat),
        [(3,) + halo] * (CHUNKS * cuts) + [(3,) + squeezed] * (CHUNKS * cuts),
        scratch=[pltpu.VMEM((3 * CHUNKS * cuts, cells, LANES), F32)],
        specs=[whole(), smem, smem],
    )
    first = [
        call(
            functools.partial(first_kernel, c),
            "first",
            (got, k_sat, heat_cond),
            [column] * 8 + [(1, ALL)],
            scratch=[pltpu.VMEM((6, cells, LANES), F32)],
            specs=[whole(), smem, smem],
        )
        for c in range(CHUNKS)
    ]
    flows, sides = [], []
    for c in range(CHUNKS):
        mine = edges[c * cuts : (c + 1) * cuts]
        sent = edges[(CHUNKS + c) * cuts : (CHUNKS + c + 1) * cuts]
        sides.append((mine, [swap(cut, n, v) for cut, v in enumerate(sent)]))
        flows.append(tuple(call(team_kernel, "team", (masks, first[c][0], first[c][1], first[c][6]), [column] * 2)))

    second, later = [], []
    for c in range(CHUNKS):
        head, warm, perm, conduct, wet, melt, cond, energy, surface = first[c]
        water, heat = flows[c]
        mine, theirs = sides[c]
        values = call(
            functools.partial(middle_kernel, cuts),
            "middle",
            (masks, head, warm, perm, conduct, wet, melt, cond, energy, surface, water, heat, *mine, *theirs),
            [column] * 5 + [(2,) + halo] * cuts + [(2,) + squeezed] * cuts,
            scratch=[room] * 5,
        )
        second.append(values[:5])
        mine, sent = values[5 : 5 + cuts], values[5 + cuts :]
        later.append((mine, [swap(cut, n, v) for cut, v in enumerate(sent)]))

    done = []
    for c in range(CHUNKS):
        conduct, stored, energy, surface = first[c][3], first[c][4], first[c][7], first[c][8]
        head, warm, wet, melt, cond = second[c]
        water, heat = call(team_kernel, "team", (masks, head, warm, cond), [column] * 2)
        mine, theirs = later[c]
        mine_k, theirs_k = sides[c]
        final = c == CHUNKS - 1
        done += call(
            functools.partial(last_kernel, c, cuts),
            "last",
            (
                masks, head, warm, conduct, stored, wet, melt, cond, energy, surface, water, heat,
                *mine, *theirs, *mine_k, *theirs_k, *(done if final else ()),
            ),
            [(TEAM, 2 * quarters if final else 4, OWN, cells)],
            scratch=[room] * 8 + [pltpu.VMEM((4, cells, LANES), F32)],
        )
    back = exchange(done[-1], n)
    return tuple(
        call(
            unpack_kernel,
            "unpack",
            (back,),
            [(cells, width)] * 2,
            scratch=[
                pltpu.VMEM((2, cells, width), F32),
                pltpu.SemaphoreType.DMA((2,)),
            ],
            out_specs=[hbm, hbm],
        )
    )


def solution(mesh):
    placed = (P(None, "cols"), P(None, "cols"), P(None, "cols"), P("cols"), P(), P(), P())
    return jax.shard_map(
        on_device,
        mesh=mesh,
        in_specs=placed,
        out_specs=(P(None, "cols"), P(None, "cols")),
        check_vma=False,
    )
```

```python
import functools

import jax
import jax.numpy as jnp
from jax import lax
from jax.experimental import pallas as pl
from jax.experimental.pallas import tpu as pltpu
from jax.sharding import PartitionSpec as P

SPAN = 256
PAIR_DEV = 4
LANES = 128
CHUNKS = SPAN // LANES
TEAM = 16
OWN = LANES // TEAM
SUB = 8
GROUPS = 2
WIDTH = 2 * LANES
ALL = GROUPS * WIDTH
EDGE = PAIR_DEV * OWN
VMEM_LIMIT = 32 * 1024 * 1024
DISTANCES = range(1, PAIR_DEV + 1)
F32 = jnp.float32


def cut_count(n):
    return min(n // TEAM - 1, 2)


def place(cut):
    team = lax.axis_index("cols") // TEAM
    return team, lax.rem(team, 2) == cut


def far_edge(above):
    return jnp.where(above, 0, PAIR_DEV - 1)


def sign_of(cut):
    return jnp.where(place(cut)[1], 1.0, -1.0).astype(F32)


def reciprocal(x):
    return pltpu.reciprocal(x, approx=True)


def sigmoid(x):
    return 0.5 + 0.5 * jnp.tanh(0.5 * x)


def passage(h, t, k):
    s = sigmoid(h)
    return k * (sigmoid(2.0 * t) * s * s + 0.02)


def lanes_of(g, b):
    return slice((g * 2 + b) * LANES, (g * 2 + b + 1) * LANES)


def following(value):
    first, second = value[:, :WIDTH], value[:, WIDTH:]
    return jnp.concatenate([second, pltpu.roll(first, SUB - 1, axis=0)], axis=1)


def preceding(value):
    first, second = value[:, :WIDTH], value[:, WIDTH:]
    return jnp.concatenate([pltpu.roll(second, 1, axis=0), first], axis=1)


def solve(steps, matrix, ratio, lead, value, update):
    c_prev = a_prev = d_prev = None
    for j in range(steps):
        above, main, below, source = matrix(j)
        if j == 0:
            r = reciprocal(main)
            a_prev = above * r
            d_prev = source * r
        else:
            r = reciprocal(main - above * c_prev)
            over = above * r
            a_prev = a_prev * over
            d_prev = source * r + d_prev * over
        c_prev = below * r
        ratio[j] = c_prev
        lead[j] = a_prev
        value[j] = d_prev
    last_c, last_a, last_d = c_prev, a_prev, d_prev
    p_first, a_first, d_first = ratio[steps - 2], lead[steps - 2], value[steps - 2]
    for j in range(steps - 3, -1, -1):
        c = ratio[j]
        p_first = c * p_first
        a_first = lead[j] + c * a_first
        d_first = value[j] + c * d_first
    g = reciprocal(1.0 - last_c * following(a_first))
    up = last_c * following(p_first) * g
    down = last_a * g
    own = (last_d + last_c * following(d_first)) * g
    step = 0
    while step < SUB:
        if step == 0:
            after, before = following, preceding
        else:
            after = functools.partial(pltpu.roll, shift=SUB - step, axis=0)
            before = functools.partial(pltpu.roll, shift=step, axis=0)
        g = reciprocal(1.0 - up * after(down) - down * before(up))
        own = (own + up * after(own) + down * before(own)) * g
        up = up * after(up) * g
        down = down * before(down) * g
        step = max(1, 2 * step)
    over = preceding(own)
    x = own
    update(steps - 1, x)
    for j in range(steps - 2, -1, -1):
        x = ratio[j] * x + (lead[j] * over + value[j])
        update(j, x)


def mask_rows(cuts):
    return 3 * PAIR_DEV + cuts * (2 * PAIR_DEV + 2)


def cut_row(cut):
    return 3 * PAIR_DEV + cut * (2 * PAIR_DEV + 2)


def mask_kernel(n, couplings, out):
    pair_rows = couplings[...].astype(F32)
    pairs = couplings.shape[1]
    pair_id = lax.broadcasted_iota(jnp.int32, (pairs, LANES), 0)
    lane = lax.broadcasted_iota(jnp.int32, (pairs, LANES), 1)
    lane_1 = lax.broadcasted_iota(jnp.int32, (SUB, LANES), 1)

    def chosen(dev, s):
        at = (pair_id == dev * PAIR_DEV + s - 1).astype(F32)
        found = jnp.dot(pair_rows, at, preferred_element_type=F32)
        return found[0:1], found[1:2]

    def put(row, value):
        out[row] = jnp.broadcast_to(value, (SUB, LANES))

    team = lax.axis_index("cols") // TEAM
    dev = team * TEAM + lane // OWN
    for s in DISTANCES:
        put(s - 1, chosen(dev, s)[0])
        put(PAIR_DEV + s - 1, chosen(dev - s, s)[1])
        put(2 * PAIR_DEV + s - 1, jnp.where(lane_1 // OWN + s < TEAM, 0.25, 0.0))
    block = lax.rem(lane_1 // EDGE, 2)
    edge = lax.rem(lane, EDGE) // OWN
    edge_1 = lax.rem(lane_1, EDGE) // OWN
    for cut in range(cut_count(n)):
        _, above = place(cut)
        row = cut_row(cut)
        partner = jnp.where(above, team + 1, team - 1)
        there = jnp.logical_and(partner >= 0, partner < n // TEAM)
        factor = jnp.where(there, 0.25, 0.0) * sign_of(cut)
        for s in DISTANCES:
            start = team * TEAM + jnp.where(above, TEAM - PAIR_DEV, -s)
            up, down = chosen(start + edge, s)
            mine = jnp.where(above, up, down)
            inward = jnp.where(above, edge_1, PAIR_DEV - 1 - edge_1)
            active = jnp.logical_and(inward >= PAIR_DEV - s, jnp.abs(mine - block.astype(F32)) < 0.5)
            put(row + s - 1, jnp.where(active, factor, 0.0))
            apart = jnp.where(above, PAIR_DEV - s, s - PAIR_DEV)
            up, down = chosen(start + edge + apart, s)
            theirs = jnp.where(edge_1 == far_edge(jnp.logical_not(above)), 0.0, jnp.where(above, down, up))
            put(row + PAIR_DEV + s - 1, jnp.where(jnp.abs(theirs - block.astype(F32)) < 0.5, 1.0, 0.0))
        outward = jnp.where(above, LANES - 1 - lane_1, lane_1)
        put(row + 2 * PAIR_DEV, jnp.where(outward < EDGE, 1.0, 0.0))
        single = jnp.logical_and(edge_1 == far_edge(above), block == 0)
        put(row + 2 * PAIR_DEV + 1, jnp.where(single, mine, 0.0))


def halo_parts():
    return lax.rem(lax.broadcasted_iota(jnp.int32, (SUB, LANES), 1) // OWN, 2 * PAIR_DEV)


def other_block(cut, couplings):
    team, above = place(cut)
    pair = (team * TEAM + jnp.where(above, TEAM - PAIR_DEV, -1)) * PAIR_DEV + PAIR_DEV - 1
    row = jnp.where(above, 0, 1)
    table = couplings[...].astype(F32)
    wanted = jnp.logical_and(
        lax.broadcasted_iota(jnp.int32, table.shape, 0) == row, lax.broadcasted_iota(jnp.int32, table.shape, 1) == pair
    )
    block = jnp.sum(jnp.sum(jnp.where(wanted, table, 0.0), axis=1, keepdims=True), axis=0, keepdims=True)
    single = jnp.where(halo_parts() == far_edge(above), 1.0, 0.0)
    return single * jnp.broadcast_to(block, (SUB, LANES))


def pack_kernel(
    cuts, suction, warmth, classes, surface, couplings, k_sat, out, consts, room, class_room, top, pairs, table, in_sems
):
    cells = out.shape[-1]
    quarters = 2 * CHUNKS
    into = []
    rooms = (room.at[0], room.at[1], class_room, top, pairs, table)
    for f, field in enumerate((suction, warmth, classes, surface, couplings, k_sat)):
        into.append(pltpu.make_async_copy(field, rooms[f], in_sems.at[f]))
        into[-1].start()

    def put(slot, value):
        out[:, slot] = value.T.reshape(TEAM, OWN, cells)

    for f in range(3):
        into[f].wait()
        for q in range(quarters):
            lanes = slice(q * LANES, (q + 1) * LANES)
            put(f * quarters + q, class_room[:, lanes].astype(F32) if f == 2 else room[f, :, lanes])
    for copy in into[3:]:
        copy.wait()
    for c in range(k_sat.shape[1]):
        consts[c] = jnp.broadcast_to(table[0:1, c : c + 1], (SUB, LANES))
    for cut in range(cuts):
        consts[k_sat.shape[1] + cut] = other_block(cut, pairs)
    rows = [top[0:1, q * LANES : (q + 1) * LANES] for q in range(quarters)]
    put(3 * quarters, jnp.concatenate(rows + [jnp.zeros((cells - quarters, LANES), F32)], axis=0))


def unpack_kernel(got, suction, warmth, room, sems):
    cells = got.shape[-1]
    quarters = 2 * CHUNKS
    sent = []
    for f, out in enumerate((suction, warmth)):
        for q in range(quarters):
            room[f, :, q * LANES : (q + 1) * LANES] = got[:, f * quarters + q].reshape(LANES, cells).T
        sent.append(pltpu.make_async_copy(room.at[f], out, sems.at[f]))
        sent[-1].start()
    for copy in sent:
        copy.wait()


def edge_shift(cut, m):
    return lax.rem(EDGE * m + jnp.where(place(cut)[1], EDGE, 0), LANES)


def halo_of(cut, value):
    part = lax.broadcasted_iota(jnp.int32, (SUB, LANES), 1) // EDGE
    packed = None
    for m in range(2 * GROUPS):
        moved = pltpu.roll(value[:, m * LANES : (m + 1) * LANES], edge_shift(cut, m), axis=1)
        packed = moved if m == 0 else jnp.where(part == m, moved, packed)
    return packed


def pieces(above):
    spare = PAIR_DEV + far_edge(above)
    parts = [j if j < PAIR_DEV else j + jnp.where(above, 1, 0) for j in range(2 * PAIR_DEV - 1)]
    return [(part, lax.rem((spare - part) * OWN + LANES, LANES)) for part in parts]


def squeeze(cut, other, values):
    above = place(cut)[1]
    values = [jnp.where(other, pltpu.roll(v, LANES - EDGE, axis=1), v) for v in values]
    spare = halo_parts() == PAIR_DEV + far_edge(above)
    return [
        jnp.where(spare, pltpu.roll(values[-1], shift, axis=1), v)
        for v, (_, shift) in zip(values[:-1], pieces(above))
    ]


def unsqueeze(cut, values):
    part = halo_parts()
    last = values[0]
    for v, (piece, shift) in zip(values, pieces(jnp.logical_not(place(cut)[1]))):
        last = jnp.where(part == piece, pltpu.roll(v, lax.rem(LANES - shift, LANES), axis=1), last)
    return list(values) + [last]


def edge_kernel(chunk, cuts, got, consts, *refs):
    halos, sent, load = refs[:cuts], refs[cuts:-1], refs[-1]
    cells = got.shape[-1]
    steps = halos[0].shape[1]
    stride = steps * GROUPS
    second = lax.broadcasted_iota(jnp.int32, (SUB, LANES), 1) >= 2 * EDGE
    for cut in range(cuts):
        start = jnp.where(place(cut)[1], TEAM - PAIR_DEV, 0)
        for f in range(3):
            rows = [
                got[pl.ds(start, PAIR_DEV), (f * 2 + b) * CHUNKS + chunk].reshape(EDGE, cells) for b in range(2)
            ]
            load[cut * 3 + f] = jnp.concatenate(rows * GROUPS, axis=0).T
    classes = consts.shape[0] - cuts
    table = [consts[c] for c in range(classes)]
    for cut in range(cuts):
        other = consts[classes + cut] > 0.5
        for f in range(3):
            values = []
            for j in range(steps):
                v = jnp.where(
                    second,
                    load[cut * 3 + f, pl.ds(steps + j, SUB, stride=stride), :],
                    load[cut * 3 + f, pl.ds(j, SUB, stride=stride), :],
                )
                if f == 2:
                    k = table[0]
                    for c in range(1, len(table)):
                        k = jnp.where(v >= c, table[c], k)
                    v = k
                halos[cut][f, j] = v
                values.append(v)
            for j, v in enumerate(squeeze(cut, other, values)):
                sent[cut][f, j] = v


def first_kernel(
    chunk, got, k_sat, heat_cond, head, warm, perm, conduct, wet, melt, cond, energy, top, load
):
    cells = got.shape[-1]
    steps = head.shape[0]
    stride = steps * GROUPS

    for field in range(3):
        for b in range(2):
            load[field * 2 + b] = got[:, (field * 2 + b) * CHUNKS + chunk].reshape(LANES, cells).T
    surface = got[:, 6 * CHUNKS].reshape(LANES, cells).T[0:SUB]
    rows = [surface[b * CHUNKS + chunk : b * CHUNKS + chunk + 1] for b in range(2)]
    top[...] = jnp.concatenate(rows * GROUPS, axis=1)

    def fetch(field, j):
        parts = [
            load[field * 2 + b, pl.ds(g * steps + j, SUB, stride=stride), :]
            for g in range(GROUPS)
            for b in range(2)
        ]
        return jnp.concatenate(parts, axis=1)

    for j in range(steps):
        h, t, v = [fetch(field, j) for field in range(3)]
        k = jnp.full_like(v, k_sat[0])
        lam = jnp.full_like(v, heat_cond[0])
        for c in range(1, k_sat.shape[0]):
            here = v >= c
            k = jnp.where(here, k_sat[c], k)
            lam = jnp.where(here, heat_cond[c], lam)
        s, f = sigmoid(h), sigmoid(2.0 * t)
        m = 0.05 + 0.4 * s
        head[j], warm[j], perm[j], conduct[j] = h, t, k, lam
        wet[j] = s
        melt[j] = f
        cond[j] = k * (f * s * s + 0.02)
        energy[j] = (1.0 + 2.0 * m) * t + 2.0 * m * f


def team_kernel(masks, head, warm, cond, water, heat):
    steps = head.shape[0]
    upper = [masks[s - 1] > 0.5 for s in DISTANCES]
    lower = [masks[PAIR_DEV + s - 1] > 0.5 for s in DISTANCES]

    def step(j, _):
        for g in range(GROUPS):
            l0, l1 = lanes_of(g, 0), lanes_of(g, 1)
            h0, h1 = head[j, :, l0], head[j, :, l1]
            t0, t1 = warm[j, :, l0], warm[j, :, l1]
            c0, c1 = cond[j, :, l0], cond[j, :, l1]
            total = None
            for s in DISTANCES:
                up, low = upper[s - 1], lower[s - 1]
                back = LANES - s * OWN
                h_low = pltpu.roll(jnp.where(low, h1, h0), back, axis=1)
                t_low = pltpu.roll(jnp.where(low, t1, t0), back, axis=1)
                c_low = pltpu.roll(jnp.where(low, c1, c0), back, axis=1)
                flow = (
                    masks[2 * PAIR_DEV + s - 1]
                    * (jnp.where(up, c1, c0) + c_low)
                    * (jnp.where(up, h1, h0) - h_low + 0.5)
                )
                carried = flow * jnp.where(flow > 0.0, jnp.where(up, t1, t0), t_low)
                flow_in = pltpu.roll(flow, s * OWN, axis=1)
                carried_in = pltpu.roll(carried, s * OWN, axis=1)
                part = (
                    flow_in - flow,
                    jnp.where(low, flow_in, 0.0) - jnp.where(up, flow, 0.0),
                    carried_in - carried,
                    jnp.where(low, carried_in, 0.0) - jnp.where(up, carried, 0.0),
                )
                total = part if total is None else [a + b for a, b in zip(total, part)]
            water[j, :, l0] = total[0] - total[1]
            water[j, :, l1] = total[1]
            heat[j, :, l0] = 2.0 * (total[2] - total[3])
            heat[j, :, l1] = 2.0 * total[3]

    lax.fori_loop(0, steps, step, None)


def cross_flows(cut, masks, mine, theirs):
    row = cut_row(cut)
    sign = sign_of(cut)
    above = place(cut)[1]
    lane = lax.broadcasted_iota(jnp.int32, (SUB, LANES), 1)
    first_block = lax.rem(lane, 2 * EDGE) < EDGE
    h, t, k = mine
    c = passage(h, t, k)
    far = [theirs[0], theirs[1], passage(*theirs)]
    other = [
        jnp.where(first_block, pltpu.roll(v, LANES - EDGE, axis=1), pltpu.roll(v, EDGE, axis=1)) for v in far
    ]
    water = heat = jnp.zeros((SUB, LANES), F32)
    for s in DISTANCES:
        same = masks[row + PAIR_DEV + s - 1] > 0.5
        picked = [jnp.where(same, a, b) for a, b in zip(far, other)]
        apart = (PAIR_DEV - s) * OWN
        if apart:
            shift = jnp.where(above, apart, LANES - apart)
            picked = [pltpu.roll(v, shift, axis=1) for v in picked]
        h_far, t_far, c_far = picked
        flow = masks[row + s - 1] * (c + c_far) * (sign * (h - h_far) + 0.5)
        water = water - flow
        heat = heat - flow * jnp.where(flow > 0.0, t, t_far)
    return water, heat


def advance(steps, cuts, masks, head, warm, conduct, stored, energy, wet, melt, cond, water, heat, top,
            mine, theirs, new_head, new_warm, new_wet, inflow, warm_inflow, ratio, lead, value, finish):
    for j in range(steps):
        w_parts = [water[j, :, m * LANES : (m + 1) * LANES] for m in range(2 * GROUPS)]
        q_parts = [heat[j, :, m * LANES : (m + 1) * LANES] for m in range(2 * GROUPS)]
        for cut in range(cuts):
            beside = masks[cut_row(cut) + 2 * PAIR_DEV]
            w_far, q_far = cross_flows(cut, masks, mine(cut, j), theirs(cut, j))
            for m in range(2 * GROUPS):
                shift = lax.rem(LANES - edge_shift(cut, m), LANES)
                w_parts[m] = w_parts[m] + beside * pltpu.roll(w_far, shift, axis=1)
                q_parts[m] = q_parts[m] + 2.0 * beside * pltpu.roll(q_far, shift, axis=1)
        for m in range(2 * GROUPS):
            inflow[j, :, m * LANES : (m + 1) * LANES] = w_parts[m]
            warm_inflow[j, :, m * LANES : (m + 1) * LANES] = q_parts[m]

    part = lax.broadcasted_iota(jnp.int32, (SUB, ALL), 0)
    group = lax.broadcasted_iota(jnp.int32, (SUB, ALL), 1) // WIDTH
    first_part = jnp.logical_and(part == 0, group == 0)
    last_part = jnp.logical_and(part == SUB - 1, group == GROUPS - 1)

    def faces(fields, potential):
        face_of, rise_of = [], []
        for j in range(steps):
            if j + 1 < steps:
                c_next, v_next = fields[j + 1], potential[j + 1]
                face = 0.5 * (fields[j] + c_next)
            else:
                c_next, v_next = following(fields[0]), following(potential[0])
                face = jnp.where(last_part, 0.0, 0.5 * (fields[j] + c_next))
            face_of.append(face)
            rise_of.append(v_next - potential[j])
        return face_of, rise_of

    k_face, rise = faces([cond[j] for j in range(steps)], head)
    k_top = jnp.where(first_part, 0.0, preceding(k_face[-1]))
    q_face = [k * (1.0 - d) for k, d in zip(k_face, rise)]
    q_top = jnp.where(first_part, 0.0, preceding(q_face[-1]))

    def water_matrix(j):
        above = k_top if j == 0 else k_face[j - 1]
        into = q_top if j == 0 else q_face[j - 1]
        s = wet[j]
        main = 0.8 * s * (1.0 - s) + 0.02 + above + k_face[j]
        source = inflow[j] + into - q_face[j] - 0.8 * (s - stored[j])
        return above, main, k_face[j], source

    def water_done(j, x):
        h = head[j] + x
        new_head[j] = h
        new_wet[j] = sigmoid(h)

    solve(steps, water_matrix, ratio, lead, value, water_done)

    l_cell = [conduct[j] * (1.5 - 0.5 * melt[j]) for j in range(steps)]
    l_face, rise = faces(l_cell, warm)
    l_top = jnp.where(first_part, 0.0, preceding(l_face[-1]))
    g_face = [l * d for l, d in zip(l_face, rise)]
    g_top = jnp.where(first_part, 0.0, preceding(g_face[-1]))
    surface_lam = jnp.where(first_part, 2.0 * l_cell[0], 0.0)

    def heat_matrix(j):
        above = l_top if j == 0 else l_face[j - 1]
        out_of = g_top if j == 0 else g_face[j - 1]
        t, f = warm[j], melt[j]
        m2 = 0.1 + 0.8 * new_wet[j]
        now = (1.0 + m2) * t + m2 * f
        main = 2.0 + 2.0 * m2 * (1.0 + 2.0 * f * (1.0 - f)) + above + l_face[j]
        source = warm_inflow[j] - out_of + g_face[j] - 2.0 * (now - energy[j])
        if j == 0:
            main = main + surface_lam
            source = source + surface_lam * (top[...] - t)
        return above, main, l_face[j], source

    def heat_done(j, x):
        t = warm[j] + x
        new_warm[j] = t
        finish(j, t)

    solve(steps, heat_matrix, ratio, lead, value, heat_done)


def middle_kernel(cuts, *refs):
    masks, head, warm, perm, conduct, wet, melt, cond, energy, top, water, heat = refs[:12]
    own, far = refs[12 : 12 + cuts], refs[12 + cuts : 12 + 2 * cuts]
    new_head, new_warm, new_wet, new_melt, new_cond = refs[12 + 2 * cuts : 17 + 2 * cuts]
    halos, sent = refs[17 + 2 * cuts : 17 + 3 * cuts], refs[17 + 3 * cuts : 17 + 4 * cuts]
    inflow, warm_inflow, ratio, lead, value = refs[17 + 4 * cuts :]
    steps = head.shape[0]
    packed = {}

    def finish(j, t):
        s, f = new_wet[j], sigmoid(2.0 * t)
        new_melt[j] = f
        new_cond[j] = perm[j] * (f * s * s + 0.02)
        for cut in range(cuts):
            for i, v in enumerate((new_head[j], t)):
                packed[cut, i, j] = halo_of(cut, v)
                halos[cut][i, j] = packed[cut, i, j]

    theirs = [[unsqueeze(cut, [far[cut][i, j] for j in range(steps - 1)]) for i in range(3)] for cut in range(cuts)]
    advance(
        steps, cuts, masks, head, warm, conduct, wet, energy, wet, melt, cond, water, heat, top,
        lambda cut, j: [own[cut][i, j] for i in range(3)],
        lambda cut, j: [theirs[cut][i][j] for i in range(3)],
        new_head, new_warm, new_wet, inflow, warm_inflow, ratio, lead, value, finish,
    )
    for cut in range(cuts):
        for i in range(2):
            other = masks[cut_row(cut) + 2 * PAIR_DEV + 1] > 0.5
            values = squeeze(cut, other, [packed[cut, i, j] for j in range(steps)])
            for j, v in enumerate(values):
                sent[cut][i, j] = v


def last_kernel(chunk, cuts, *refs):
    masks, head, warm, conduct, stored, wet, melt, cond, energy, top, water, heat = refs[:12]
    own, far = refs[12 : 12 + cuts], refs[12 + cuts : 12 + 2 * cuts]
    own_k, far_k = refs[12 + 2 * cuts : 12 + 3 * cuts], refs[12 + 3 * cuts : 12 + 4 * cuts]
    others = refs[12 + 4 * cuts : -10]
    out, new_head, new_warm, new_wet, inflow, warm_inflow, ratio, lead, value, load = refs[-10:]
    steps = head.shape[0]
    cells = steps * GROUPS * SUB
    stride = steps * GROUPS
    theirs = [
        [unsqueeze(cut, [source[i, j] for j in range(steps - 1)]) for source, i in ((far[cut], 0), (far[cut], 1), (far_k[cut], 2))]
        for cut in range(cuts)
    ]
    advance(
        steps, cuts, masks, head, warm, conduct, stored, energy, wet, melt, cond, water, heat, top,
        lambda cut, j: [own[cut][0, j], own[cut][1, j], own_k[cut][2, j]],
        lambda cut, j: [theirs[cut][i][j] for i in range(3)],
        new_head, new_warm, new_wet, inflow, warm_inflow, ratio, lead, value, lambda j, t: None,
    )
    final = chunk == CHUNKS - 1
    for f, field in enumerate((new_head, new_warm)):
        for b in range(2):
            slot = f * 2 + b
            for j in range(steps):
                for g in range(GROUPS):
                    load[slot, pl.ds(g * steps + j, SUB, stride=stride), :] = field[j, :, lanes_of(g, b)]
            turned = load[slot].T.reshape(TEAM, OWN, cells)
            if final:
                out[:, slot * CHUNKS + chunk] = turned
                for c, other in enumerate(others):
                    out[:, slot * CHUNKS + c] = other[:, slot]
            else:
                out[:, slot] = turned


def whole(memory=pltpu.VMEM):
    return pl.BlockSpec(memory_space=memory)


def call(kernel, name, args, outs, scratch=(), specs=None, out_specs=None, limit=VMEM_LIMIT, work=2_000_000):
    return pl.pallas_call(
        kernel,
        out_shape=[jax.ShapeDtypeStruct(shape, F32) for shape in outs],
        in_specs=specs or [whole()] * len(args),
        out_specs=out_specs or [whole()] * len(outs),
        scratch_shapes=scratch,
        compiler_params=pltpu.CompilerParams(vmem_limit_bytes=limit),
        cost_estimate=pl.CostEstimate(flops=work, bytes_accessed=work, transcendentals=0),
        name=name,
    )(*args)


def exchange(tiles, n):
    teams = [list(range(start, start + TEAM)) for start in range(0, n, TEAM)]
    return lax.all_to_all(
        tiles, "cols", split_axis=0, concat_axis=0, tiled=True, axis_index_groups=teams
    )


def swap(cut, n, value):
    pairs = []
    for team in range(cut, n // TEAM - 1, 2):
        for i in range(team * TEAM, (team + 1) * TEAM):
            pairs += [(i, i + TEAM), (i + TEAM, i)]
    return lax.ppermute(value, "cols", pairs)


def on_device(suction, warmth, classes, top, couplings, k_sat, heat_cond):
    n = lax.axis_size("cols")
    cells, width = suction.shape
    steps = cells // (SUB * GROUPS)
    quarters = width // LANES
    cuts = cut_count(n)
    column = (steps, SUB, ALL)
    halo = (steps, SUB, LANES)
    squeezed = (steps - 1, SUB, LANES)
    room = pltpu.VMEM(column, F32)
    smem = whole(pltpu.SMEM)
    hbm = whole(pltpu.HBM)

    masks = call(
        functools.partial(mask_kernel, n), "masks", (couplings,), [(mask_rows(cuts), SUB, LANES)]
    )[0]
    arguments = (suction, warmth, classes, top.reshape(1, width), couplings, k_sat.reshape(1, -1))
    packed, consts = call(
        functools.partial(pack_kernel, cuts),
        "pack",
        [pltpu.with_memory_space_constraint(v, pltpu.HBM) for v in arguments],
        [(TEAM, 3 * quarters + 1, OWN, cells), (k_sat.shape[0] + cuts, SUB, LANES)],
        scratch=[
            pltpu.VMEM((2, cells, width), F32),
            pltpu.VMEM((cells, width), classes.dtype),
            pltpu.VMEM((1, width), F32),
            pltpu.VMEM(couplings.shape, couplings.dtype),
            pltpu.VMEM((1, k_sat.shape[0]), F32),
            pltpu.SemaphoreType.DMA((6,)),
        ],
        specs=[hbm] * 6,
    )
    got = exchange(packed, n)

    edges = [
        call(
            functools.partial(edge_kernel, c, cuts),
            "edges",
            (got, consts),
            [(3,) + halo] * cuts + [(3,) + squeezed] * cuts,
            scratch=[pltpu.VMEM((3 * cuts, cells, LANES), F32)],
        )
        for c in range(CHUNKS)
    ]
    first = [
        call(
            functools.partial(first_kernel, c),
            "first",
            (got, k_sat, heat_cond),
            [column] * 8 + [(1, ALL)],
            scratch=[pltpu.VMEM((6, cells, LANES), F32)],
            specs=[whole(), smem, smem],
        )
        for c in range(CHUNKS)
    ]
    flows, sides = [], []
    for c in range(CHUNKS):
        mine, sent = edges[c][:cuts], edges[c][cuts:]
        sides.append((mine, [swap(cut, n, v) for cut, v in enumerate(sent)]))
        flows.append(tuple(call(team_kernel, "team", (masks, first[c][0], first[c][1], first[c][6]), [column] * 2)))

    second, later = [], []
    for c in range(CHUNKS):
        head, warm, perm, conduct, wet, melt, cond, energy, surface = first[c]
        water, heat = flows[c]
        mine, theirs = sides[c]
        values = call(
            functools.partial(middle_kernel, cuts),
            "middle",
            (masks, head, warm, perm, conduct, wet, melt, cond, energy, surface, water, heat, *mine, *theirs),
            [column] * 5 + [(2,) + halo] * cuts + [(2,) + squeezed] * cuts,
            scratch=[room] * 5,
        )
        second.append(values[:5])
        mine, sent = values[5 : 5 + cuts], values[5 + cuts :]
        later.append((mine, [swap(cut, n, v) for cut, v in enumerate(sent)]))

    done = []
    for c in range(CHUNKS):
        conduct, stored, energy, surface = first[c][3], first[c][4], first[c][7], first[c][8]
        head, warm, wet, melt, cond = second[c]
        water, heat = call(team_kernel, "team", (masks, head, warm, cond), [column] * 2)
        mine, theirs = later[c]
        mine_k, theirs_k = sides[c]
        final = c == CHUNKS - 1
        done += call(
            functools.partial(last_kernel, c, cuts),
            "last",
            (
                masks, head, warm, conduct, stored, wet, melt, cond, energy, surface, water, heat,
                *mine, *theirs, *mine_k, *theirs_k, *(done if final else ()),
            ),
            [(TEAM, 2 * quarters if final else 4, OWN, cells)],
            scratch=[room] * 8 + [pltpu.VMEM((4, cells, LANES), F32)],
        )
    back = exchange(done[-1], n)
    return tuple(
        call(
            unpack_kernel,
            "unpack",
            (back,),
            [(cells, width)] * 2,
            scratch=[
                pltpu.VMEM((2, cells, width), F32),
                pltpu.SemaphoreType.DMA((2,)),
            ],
            out_specs=[hbm, hbm],
        )
    )


def solution(mesh):
    placed = (P(None, "cols"), P(None, "cols"), P(None, "cols"), P("cols"), P(), P(), P())
    return jax.shard_map(
        on_device,
        mesh=mesh,
        in_specs=placed,
        out_specs=(P(None, "cols"), P(None, "cols")),
        check_vma=False,
    )
```

```python
import functools

import jax
import jax.numpy as jnp
from jax import lax
from jax.experimental import pallas as pl
from jax.experimental.pallas import tpu as pltpu
from jax.sharding import PartitionSpec as P

SPAN = 256
PAIR_DEV = 4
LANES = 128
CHUNKS = SPAN // LANES
TEAM = 16
OWN = LANES // TEAM
SUB = 8
GROUPS = 2
WIDTH = 2 * LANES
ALL = GROUPS * WIDTH
EDGE = PAIR_DEV * OWN
VMEM_LIMIT = 32 * 1024 * 1024
DISTANCES = range(1, PAIR_DEV + 1)
F32 = jnp.float32


def cut_count(n):
    return min(n // TEAM - 1, 2)


def place(cut):
    team = lax.axis_index("cols") // TEAM
    return team, lax.rem(team, 2) == cut


def far_edge(above):
    return jnp.where(above, 0, PAIR_DEV - 1)


def sign_of(cut):
    return jnp.where(place(cut)[1], 1.0, -1.0).astype(F32)


def reciprocal(x):
    return pltpu.reciprocal(x, approx=True)


def sigmoid(x):
    return 0.5 + 0.5 * jnp.tanh(0.5 * x)


def passage(h, t, k):
    s = sigmoid(h)
    return k * (sigmoid(2.0 * t) * s * s + 0.02)


def lanes_of(g, b):
    return slice((g * 2 + b) * LANES, (g * 2 + b + 1) * LANES)


def following(value):
    first, second = value[:, :WIDTH], value[:, WIDTH:]
    return jnp.concatenate([second, pltpu.roll(first, SUB - 1, axis=0)], axis=1)


def preceding(value):
    first, second = value[:, :WIDTH], value[:, WIDTH:]
    return jnp.concatenate([pltpu.roll(second, 1, axis=0), first], axis=1)


def solve(steps, matrix, ratio, lead, value, update):
    c_prev = a_prev = d_prev = None
    for j in range(steps):
        above, main, below, source = matrix(j)
        if j == 0:
            r = reciprocal(main)
            a_prev = above * r
            d_prev = source * r
        else:
            r = reciprocal(main - above * c_prev)
            over = above * r
            a_prev = a_prev * over
            d_prev = source * r + d_prev * over
        c_prev = below * r
        ratio[j] = c_prev
        lead[j] = a_prev
        value[j] = d_prev
    last_c, last_a, last_d = c_prev, a_prev, d_prev
    p_first, a_first, d_first = ratio[steps - 2], lead[steps - 2], value[steps - 2]
    for j in range(steps - 3, -1, -1):
        c = ratio[j]
        p_first = c * p_first
        a_first = lead[j] + c * a_first
        d_first = value[j] + c * d_first
    g = reciprocal(1.0 - last_c * following(a_first))
    up = last_c * following(p_first) * g
    down = last_a * g
    own = (last_d + last_c * following(d_first)) * g
    step = 0
    while step < SUB:
        if step == 0:
            after, before = following, preceding
        else:
            after = functools.partial(pltpu.roll, shift=SUB - step, axis=0)
            before = functools.partial(pltpu.roll, shift=step, axis=0)
        g = reciprocal(1.0 - up * after(down) - down * before(up))
        own = (own + up * after(own) + down * before(own)) * g
        up = up * after(up) * g
        down = down * before(down) * g
        step = max(1, 2 * step)
    over = preceding(own)
    x = own
    update(steps - 1, x)
    for j in range(steps - 2, -1, -1):
        x = ratio[j] * x + (lead[j] * over + value[j])
        update(j, x)


def mask_rows(cuts):
    return 3 * PAIR_DEV + cuts * (2 * PAIR_DEV + 2)


def cut_row(cut):
    return 3 * PAIR_DEV + cut * (2 * PAIR_DEV + 2)


def mask_kernel(n, couplings, out):
    pair_rows = couplings[...]
    pairs = couplings.shape[1]
    pair_id = lax.broadcasted_iota(jnp.int32, (pairs, LANES), 0)
    lane = lax.broadcasted_iota(jnp.int32, (pairs, LANES), 1)
    lane_1 = lax.broadcasted_iota(jnp.int32, (SUB, LANES), 1)

    def chosen(dev, s):
        at = (pair_id == dev * PAIR_DEV + s - 1).astype(F32)
        found = jnp.dot(pair_rows, at, preferred_element_type=F32)
        return found[0:1], found[1:2]

    def put(row, value):
        out[row] = jnp.broadcast_to(value, (SUB, LANES))

    team = lax.axis_index("cols") // TEAM
    dev = team * TEAM + lane // OWN
    for s in DISTANCES:
        put(s - 1, chosen(dev, s)[0])
        put(PAIR_DEV + s - 1, chosen(dev - s, s)[1])
        put(2 * PAIR_DEV + s - 1, jnp.where(lane_1 // OWN + s < TEAM, 0.25, 0.0))
    block = lax.rem(lane_1 // EDGE, 2)
    edge = lax.rem(lane, EDGE) // OWN
    edge_1 = lax.rem(lane_1, EDGE) // OWN
    for cut in range(cut_count(n)):
        _, above = place(cut)
        row = cut_row(cut)
        partner = jnp.where(above, team + 1, team - 1)
        there = jnp.logical_and(partner >= 0, partner < n // TEAM)
        factor = jnp.where(there, 0.25, 0.0) * sign_of(cut)
        for s in DISTANCES:
            start = team * TEAM + jnp.where(above, TEAM - PAIR_DEV, -s)
            up, down = chosen(start + edge, s)
            mine = jnp.where(above, up, down)
            inward = jnp.where(above, edge_1, PAIR_DEV - 1 - edge_1)
            active = jnp.logical_and(inward >= PAIR_DEV - s, jnp.abs(mine - block.astype(F32)) < 0.5)
            put(row + s - 1, jnp.where(active, factor, 0.0))
            apart = jnp.where(above, PAIR_DEV - s, s - PAIR_DEV)
            up, down = chosen(start + edge + apart, s)
            theirs = jnp.where(edge_1 == far_edge(jnp.logical_not(above)), 0.0, jnp.where(above, down, up))
            put(row + PAIR_DEV + s - 1, jnp.where(jnp.abs(theirs - block.astype(F32)) < 0.5, 1.0, 0.0))
        outward = jnp.where(above, LANES - 1 - lane_1, lane_1)
        put(row + 2 * PAIR_DEV, jnp.where(outward < EDGE, 1.0, 0.0))
        single = jnp.logical_and(edge_1 == far_edge(above), block == 0)
        put(row + 2 * PAIR_DEV + 1, jnp.where(single, mine, 0.0))


def halo_parts():
    return lax.rem(lax.broadcasted_iota(jnp.int32, (SUB, LANES), 1) // OWN, 2 * PAIR_DEV)


def other_block(cut, couplings):
    team, above = place(cut)
    pair = (team * TEAM + jnp.where(above, TEAM - PAIR_DEV, -1)) * PAIR_DEV + PAIR_DEV - 1
    row = jnp.where(above, 0, 1)
    table = couplings[...].astype(F32)
    wanted = jnp.logical_and(
        lax.broadcasted_iota(jnp.int32, table.shape, 0) == row, lax.broadcasted_iota(jnp.int32, table.shape, 1) == pair
    )
    block = jnp.sum(jnp.sum(jnp.where(wanted, table, 0.0), axis=1, keepdims=True), axis=0, keepdims=True)
    single = jnp.where(halo_parts() == far_edge(above), 1.0, 0.0)
    return single * jnp.broadcast_to(block, (SUB, LANES))


def pack_kernel(
    cuts, suction, warmth, classes, surface, couplings, k_sat, heat_cond, out, consts, pair_rows,
    room, class_room, top, pairs, k_table, heat_table, in_sems,
):
    cells = out.shape[-1]
    quarters = 2 * CHUNKS
    into = []
    rooms = (room.at[0], room.at[1], class_room, top, pairs, k_table, heat_table)
    for f, field in enumerate((suction, warmth, classes, surface, couplings, k_sat, heat_cond)):
        into.append(pltpu.make_async_copy(field, rooms[f], in_sems.at[f]))
        into[-1].start()

    def put(slot, value):
        out[:, slot] = value.T.reshape(TEAM, OWN, cells)

    for f in range(3):
        into[f].wait()
        for q in range(quarters):
            lanes = slice(q * LANES, (q + 1) * LANES)
            put(f * quarters + q, class_room[:, lanes].astype(F32) if f == 2 else room[f, :, lanes])
    for copy in into[3:]:
        copy.wait()
    kinds = k_sat.shape[1]
    for c in range(kinds):
        consts[c] = jnp.broadcast_to(k_table[0:1, c : c + 1], (SUB, LANES))
        consts[kinds + c] = jnp.broadcast_to(heat_table[0:1, c : c + 1], (SUB, LANES))
    for cut in range(cuts):
        consts[2 * kinds + cut] = other_block(cut, pairs)
    pair_rows[...] = pairs[...].astype(F32)
    rows = [top[0:1, q * LANES : (q + 1) * LANES] for q in range(quarters)]
    put(3 * quarters, jnp.concatenate(rows + [jnp.zeros((cells - quarters, LANES), F32)], axis=0))


def unpack_kernel(got, suction, warmth, room, sems):
    cells = got.shape[-1]
    quarters = 2 * CHUNKS
    sent = []
    for f, out in enumerate((suction, warmth)):
        for q in range(quarters):
            room[f, :, q * LANES : (q + 1) * LANES] = got[:, f * quarters + q].reshape(LANES, cells).T
        sent.append(pltpu.make_async_copy(room.at[f], out, sems.at[f]))
        sent[-1].start()
    for copy in sent:
        copy.wait()


def edge_shift(cut, m):
    return lax.rem(EDGE * m + jnp.where(place(cut)[1], EDGE, 0), LANES)


def halo_of(cut, value):
    part = lax.broadcasted_iota(jnp.int32, (SUB, LANES), 1) // EDGE
    packed = None
    for m in range(2 * GROUPS):
        moved = pltpu.roll(value[:, m * LANES : (m + 1) * LANES], edge_shift(cut, m), axis=1)
        packed = moved if m == 0 else jnp.where(part == m, moved, packed)
    return packed


def pieces(above):
    spare = PAIR_DEV + far_edge(above)
    parts = [j if j < PAIR_DEV else j + jnp.where(above, 1, 0) for j in range(2 * PAIR_DEV - 1)]
    return [(part, lax.rem((spare - part) * OWN + LANES, LANES)) for part in parts]


def squeeze(cut, other, values):
    above = place(cut)[1]
    values = [jnp.where(other, pltpu.roll(v, LANES - EDGE, axis=1), v) for v in values]
    spare = halo_parts() == PAIR_DEV + far_edge(above)
    return [
        jnp.where(spare, pltpu.roll(values[-1], shift, axis=1), v)
        for v, (_, shift) in zip(values[:-1], pieces(above))
    ]


def unsqueeze(cut, values):
    part = halo_parts()
    last = values[0]
    for v, (piece, shift) in zip(values, pieces(jnp.logical_not(place(cut)[1]))):
        last = jnp.where(part == piece, pltpu.roll(v, lax.rem(LANES - shift, LANES), axis=1), last)
    return list(values) + [last]


def edge_kernel(chunk, cuts, got, consts, *refs):
    halos, sent, load = refs[:cuts], refs[cuts:-1], refs[-1]
    cells = got.shape[-1]
    steps = halos[0].shape[1]
    stride = steps * GROUPS
    second = lax.broadcasted_iota(jnp.int32, (SUB, LANES), 1) >= 2 * EDGE
    for cut in range(cuts):
        start = jnp.where(place(cut)[1], TEAM - PAIR_DEV, 0)
        for f in range(3):
            rows = [
                got[pl.ds(start, PAIR_DEV), (f * 2 + b) * CHUNKS + chunk].reshape(EDGE, cells) for b in range(2)
            ]
            load[cut * 3 + f] = jnp.concatenate(rows * GROUPS, axis=0).T
    kinds = (consts.shape[0] - cuts) // 2
    table = [consts[c] for c in range(kinds)]
    for cut in range(cuts):
        other = consts[2 * kinds + cut] > 0.5
        for f in range(3):
            values = []
            for j in range(steps):
                v = jnp.where(
                    second,
                    load[cut * 3 + f, pl.ds(steps + j, SUB, stride=stride), :],
                    load[cut * 3 + f, pl.ds(j, SUB, stride=stride), :],
                )
                if f == 2:
                    k = table[0]
                    for c in range(1, len(table)):
                        k = jnp.where(v >= c, table[c], k)
                    v = k
                halos[cut][f, j] = v
                values.append(v)
            for j, v in enumerate(squeeze(cut, other, values)):
                sent[cut][f, j] = v


def first_kernel(
    chunk, kinds, got, consts, head, warm, perm, conduct, wet, melt, cond, energy, top, load
):
    cells = got.shape[-1]
    steps = head.shape[0]
    stride = steps * GROUPS

    for field in range(3):
        for b in range(2):
            load[field * 2 + b] = got[:, (field * 2 + b) * CHUNKS + chunk].reshape(LANES, cells).T
    surface = got[:, 6 * CHUNKS].reshape(LANES, cells).T[0:SUB]
    rows = [surface[b * CHUNKS + chunk : b * CHUNKS + chunk + 1] for b in range(2)]
    top[...] = jnp.concatenate(rows * GROUPS, axis=1)

    def fetch(field, j):
        parts = [
            load[field * 2 + b, pl.ds(g * steps + j, SUB, stride=stride), :]
            for g in range(GROUPS)
            for b in range(2)
        ]
        return jnp.concatenate(parts, axis=1)

    def pick(v):
        parts = []
        for m in range(2 * GROUPS):
            part = v[:, m * LANES : (m + 1) * LANES]
            k, lam = consts[0], consts[kinds]
            for c in range(1, kinds):
                here = part >= c
                k = jnp.where(here, consts[c], k)
                lam = jnp.where(here, consts[kinds + c], lam)
            parts.append((k, lam))
        return [jnp.concatenate(side, axis=1) for side in zip(*parts)]

    for j in range(steps):
        h, t, v = [fetch(field, j) for field in range(3)]
        k, lam = pick(v)
        s, f = sigmoid(h), sigmoid(2.0 * t)
        m = 0.05 + 0.4 * s
        head[j], warm[j], perm[j], conduct[j] = h, t, k, lam
        wet[j] = s
        melt[j] = f
        cond[j] = k * (f * s * s + 0.02)
        energy[j] = (1.0 + 2.0 * m) * t + 2.0 * m * f


def team_kernel(masks, head, warm, cond, water, heat):
    steps = head.shape[0]
    upper = [masks[s - 1] > 0.5 for s in DISTANCES]
    lower = [masks[PAIR_DEV + s - 1] > 0.5 for s in DISTANCES]

    def step(j, _):
        for g in range(GROUPS):
            l0, l1 = lanes_of(g, 0), lanes_of(g, 1)
            h0, h1 = head[j, :, l0], head[j, :, l1]
            t0, t1 = warm[j, :, l0], warm[j, :, l1]
            c0, c1 = cond[j, :, l0], cond[j, :, l1]
            total = None
            for s in DISTANCES:
                up, low = upper[s - 1], lower[s - 1]
                back = LANES - s * OWN
                h_low = pltpu.roll(jnp.where(low, h1, h0), back, axis=1)
                t_low = pltpu.roll(jnp.where(low, t1, t0), back, axis=1)
                c_low = pltpu.roll(jnp.where(low, c1, c0), back, axis=1)
                flow = (
                    masks[2 * PAIR_DEV + s - 1]
                    * (jnp.where(up, c1, c0) + c_low)
                    * (jnp.where(up, h1, h0) - h_low + 0.5)
                )
                carried = flow * jnp.where(flow > 0.0, jnp.where(up, t1, t0), t_low)
                flow_in = pltpu.roll(flow, s * OWN, axis=1)
                carried_in = pltpu.roll(carried, s * OWN, axis=1)
                part = (
                    flow_in - flow,
                    jnp.where(low, flow_in, 0.0) - jnp.where(up, flow, 0.0),
                    carried_in - carried,
                    jnp.where(low, carried_in, 0.0) - jnp.where(up, carried, 0.0),
                )
                total = part if total is None else [a + b for a, b in zip(total, part)]
            water[j, :, l0] = total[0] - total[1]
            water[j, :, l1] = total[1]
            heat[j, :, l0] = 2.0 * (total[2] - total[3])
            heat[j, :, l1] = 2.0 * total[3]

    lax.fori_loop(0, steps, step, None)


def cross_flows(cut, masks, mine, theirs):
    row = cut_row(cut)
    sign = sign_of(cut)
    above = place(cut)[1]
    lane = lax.broadcasted_iota(jnp.int32, (SUB, LANES), 1)
    first_block = lax.rem(lane, 2 * EDGE) < EDGE
    h, t, k = mine
    c = passage(h, t, k)
    far = [theirs[0], theirs[1], passage(*theirs)]
    other = [
        jnp.where(first_block, pltpu.roll(v, LANES - EDGE, axis=1), pltpu.roll(v, EDGE, axis=1)) for v in far
    ]
    water = heat = jnp.zeros((SUB, LANES), F32)
    for s in DISTANCES:
        same = masks[row + PAIR_DEV + s - 1] > 0.5
        picked = [jnp.where(same, a, b) for a, b in zip(far, other)]
        apart = (PAIR_DEV - s) * OWN
        if apart:
            shift = jnp.where(above, apart, LANES - apart)
            picked = [pltpu.roll(v, shift, axis=1) for v in picked]
        h_far, t_far, c_far = picked
        flow = masks[row + s - 1] * (c + c_far) * (sign * (h - h_far) + 0.5)
        water = water - flow
        heat = heat - flow * jnp.where(flow > 0.0, t, t_far)
    return water, heat


def advance(steps, cuts, masks, head, warm, conduct, stored, energy, wet, melt, cond, water, heat, top,
            mine, theirs, new_head, new_warm, new_wet, inflow, warm_inflow, ratio, lead, value, finish):
    for j in range(steps):
        w_parts = [water[j, :, m * LANES : (m + 1) * LANES] for m in range(2 * GROUPS)]
        q_parts = [heat[j, :, m * LANES : (m + 1) * LANES] for m in range(2 * GROUPS)]
        for cut in range(cuts):
            beside = masks[cut_row(cut) + 2 * PAIR_DEV]
            w_far, q_far = cross_flows(cut, masks, mine(cut, j), theirs(cut, j))
            for m in range(2 * GROUPS):
                shift = lax.rem(LANES - edge_shift(cut, m), LANES)
                w_parts[m] = w_parts[m] + beside * pltpu.roll(w_far, shift, axis=1)
                q_parts[m] = q_parts[m] + 2.0 * beside * pltpu.roll(q_far, shift, axis=1)
        for m in range(2 * GROUPS):
            inflow[j, :, m * LANES : (m + 1) * LANES] = w_parts[m]
            warm_inflow[j, :, m * LANES : (m + 1) * LANES] = q_parts[m]

    part = lax.broadcasted_iota(jnp.int32, (SUB, ALL), 0)
    group = lax.broadcasted_iota(jnp.int32, (SUB, ALL), 1) // WIDTH
    first_part = jnp.logical_and(part == 0, group == 0)
    last_part = jnp.logical_and(part == SUB - 1, group == GROUPS - 1)

    def faces(fields, potential):
        face_of, rise_of = [], []
        for j in range(steps):
            if j + 1 < steps:
                c_next, v_next = fields[j + 1], potential[j + 1]
                face = 0.5 * (fields[j] + c_next)
            else:
                c_next, v_next = following(fields[0]), following(potential[0])
                face = jnp.where(last_part, 0.0, 0.5 * (fields[j] + c_next))
            face_of.append(face)
            rise_of.append(v_next - potential[j])
        return face_of, rise_of

    k_face, rise = faces([cond[j] for j in range(steps)], head)
    k_top = jnp.where(first_part, 0.0, preceding(k_face[-1]))
    q_face = [k * (1.0 - d) for k, d in zip(k_face, rise)]
    q_top = jnp.where(first_part, 0.0, preceding(q_face[-1]))

    def water_matrix(j):
        above = k_top if j == 0 else k_face[j - 1]
        into = q_top if j == 0 else q_face[j - 1]
        s = wet[j]
        main = 0.8 * s * (1.0 - s) + 0.02 + above + k_face[j]
        source = inflow[j] + into - q_face[j] - 0.8 * (s - stored[j])
        return above, main, k_face[j], source

    def water_done(j, x):
        h = head[j] + x
        new_head[j] = h
        new_wet[j] = sigmoid(h)

    solve(steps, water_matrix, ratio, lead, value, water_done)

    l_cell = [conduct[j] * (1.5 - 0.5 * melt[j]) for j in range(steps)]
    l_face, rise = faces(l_cell, warm)
    l_top = jnp.where(first_part, 0.0, preceding(l_face[-1]))
    g_face = [l * d for l, d in zip(l_face, rise)]
    g_top = jnp.where(first_part, 0.0, preceding(g_face[-1]))
    surface_lam = jnp.where(first_part, 2.0 * l_cell[0], 0.0)

    def heat_matrix(j):
        above = l_top if j == 0 else l_face[j - 1]
        out_of = g_top if j == 0 else g_face[j - 1]
        t, f = warm[j], melt[j]
        m2 = 0.1 + 0.8 * new_wet[j]
        now = (1.0 + m2) * t + m2 * f
        main = 2.0 + 2.0 * m2 * (1.0 + 2.0 * f * (1.0 - f)) + above + l_face[j]
        source = warm_inflow[j] - out_of + g_face[j] - 2.0 * (now - energy[j])
        if j == 0:
            main = main + surface_lam
            source = source + surface_lam * (top[...] - t)
        return above, main, l_face[j], source

    def heat_done(j, x):
        t = warm[j] + x
        new_warm[j] = t
        finish(j, t)

    solve(steps, heat_matrix, ratio, lead, value, heat_done)


def middle_kernel(cuts, *refs):
    masks, head, warm, perm, conduct, wet, melt, cond, energy, top, water, heat = refs[:12]
    own, far = refs[12 : 12 + cuts], refs[12 + cuts : 12 + 2 * cuts]
    new_head, new_warm, new_wet, new_melt, new_cond = refs[12 + 2 * cuts : 17 + 2 * cuts]
    halos, sent = refs[17 + 2 * cuts : 17 + 3 * cuts], refs[17 + 3 * cuts : 17 + 4 * cuts]
    inflow, warm_inflow, ratio, lead, value = refs[17 + 4 * cuts :]
    steps = head.shape[0]
    packed = {}

    def finish(j, t):
        s, f = new_wet[j], sigmoid(2.0 * t)
        new_melt[j] = f
        new_cond[j] = perm[j] * (f * s * s + 0.02)
        for cut in range(cuts):
            for i, v in enumerate((new_head[j], t)):
                packed[cut, i, j] = halo_of(cut, v)
                halos[cut][i, j] = packed[cut, i, j]

    theirs = [[unsqueeze(cut, [far[cut][i, j] for j in range(steps - 1)]) for i in range(3)] for cut in range(cuts)]
    advance(
        steps, cuts, masks, head, warm, conduct, wet, energy, wet, melt, cond, water, heat, top,
        lambda cut, j: [own[cut][i, j] for i in range(3)],
        lambda cut, j: [theirs[cut][i][j] for i in range(3)],
        new_head, new_warm, new_wet, inflow, warm_inflow, ratio, lead, value, finish,
    )
    for cut in range(cuts):
        for i in range(2):
            other = masks[cut_row(cut) + 2 * PAIR_DEV + 1] > 0.5
            values = squeeze(cut, other, [packed[cut, i, j] for j in range(steps)])
            for j, v in enumerate(values):
                sent[cut][i, j] = v


def last_kernel(chunk, cuts, *refs):
    masks, head, warm, conduct, stored, wet, melt, cond, energy, top, water, heat = refs[:12]
    own, far = refs[12 : 12 + cuts], refs[12 + cuts : 12 + 2 * cuts]
    own_k, far_k = refs[12 + 2 * cuts : 12 + 3 * cuts], refs[12 + 3 * cuts : 12 + 4 * cuts]
    others = refs[12 + 4 * cuts : -10]
    out, new_head, new_warm, new_wet, inflow, warm_inflow, ratio, lead, value, load = refs[-10:]
    steps = head.shape[0]
    cells = steps * GROUPS * SUB
    stride = steps * GROUPS
    theirs = [
        [unsqueeze(cut, [source[i, j] for j in range(steps - 1)]) for source, i in ((far[cut], 0), (far[cut], 1), (far_k[cut], 2))]
        for cut in range(cuts)
    ]
    advance(
        steps, cuts, masks, head, warm, conduct, stored, energy, wet, melt, cond, water, heat, top,
        lambda cut, j: [own[cut][0, j], own[cut][1, j], own_k[cut][2, j]],
        lambda cut, j: [theirs[cut][i][j] for i in range(3)],
        new_head, new_warm, new_wet, inflow, warm_inflow, ratio, lead, value, lambda j, t: None,
    )
    final = chunk == CHUNKS - 1
    for f, field in enumerate((new_head, new_warm)):
        for b in range(2):
            slot = f * 2 + b
            for j in range(steps):
                for g in range(GROUPS):
                    load[slot, pl.ds(g * steps + j, SUB, stride=stride), :] = field[j, :, lanes_of(g, b)]
            turned = load[slot].T.reshape(TEAM, OWN, cells)
            if final:
                out[:, slot * CHUNKS + chunk] = turned
                for c, other in enumerate(others):
                    out[:, slot * CHUNKS + c] = other[:, slot]
            else:
                out[:, slot] = turned


def whole(memory=pltpu.VMEM):
    return pl.BlockSpec(memory_space=memory)


def call(kernel, name, args, outs, scratch=(), specs=None, out_specs=None, limit=VMEM_LIMIT, work=2_000_000):
    return pl.pallas_call(
        kernel,
        out_shape=[jax.ShapeDtypeStruct(shape, F32) for shape in outs],
        in_specs=specs or [whole()] * len(args),
        out_specs=out_specs or [whole()] * len(outs),
        scratch_shapes=scratch,
        compiler_params=pltpu.CompilerParams(vmem_limit_bytes=limit),
        cost_estimate=pl.CostEstimate(flops=work, bytes_accessed=work, transcendentals=0),
        name=name,
    )(*args)


def exchange(tiles, n):
    teams = [list(range(start, start + TEAM)) for start in range(0, n, TEAM)]
    return lax.all_to_all(
        tiles, "cols", split_axis=0, concat_axis=0, tiled=True, axis_index_groups=teams
    )


def swap(cut, n, value):
    pairs = []
    for team in range(cut, n // TEAM - 1, 2):
        for i in range(team * TEAM, (team + 1) * TEAM):
            pairs += [(i, i + TEAM), (i + TEAM, i)]
    return lax.ppermute(value, "cols", pairs)


def on_device(suction, warmth, classes, top, couplings, k_sat, heat_cond):
    n = lax.axis_size("cols")
    cells, width = suction.shape
    steps = cells // (SUB * GROUPS)
    quarters = width // LANES
    cuts = cut_count(n)
    column = (steps, SUB, ALL)
    halo = (steps, SUB, LANES)
    squeezed = (steps - 1, SUB, LANES)
    room = pltpu.VMEM(column, F32)
    hbm = whole(pltpu.HBM)

    arguments = (suction, warmth, classes, top.reshape(1, width), couplings, k_sat.reshape(1, -1), heat_cond.reshape(1, -1))
    kinds = k_sat.shape[0]
    packed, consts, pair_rows = call(
        functools.partial(pack_kernel, cuts),
        "pack",
        [pltpu.with_memory_space_constraint(v, pltpu.HBM) for v in arguments],
        [(TEAM, 3 * quarters + 1, OWN, cells), (2 * kinds + cuts, SUB, LANES), couplings.shape],
        scratch=[
            pltpu.VMEM((2, cells, width), F32),
            pltpu.VMEM((cells, width), classes.dtype),
            pltpu.VMEM((1, width), F32),
            pltpu.VMEM(couplings.shape, couplings.dtype),
            pltpu.VMEM((1, kinds), F32),
            pltpu.VMEM((1, kinds), F32),
            pltpu.SemaphoreType.DMA((7,)),
        ],
        specs=[hbm] * 7,
    )
    masks = call(
        functools.partial(mask_kernel, n), "masks", (pair_rows,), [(mask_rows(cuts), SUB, LANES)]
    )[0]
    got = exchange(packed, n)

    edges = [
        call(
            functools.partial(edge_kernel, c, cuts),
            "edges",
            (got, consts),
            [(3,) + halo] * cuts + [(3,) + squeezed] * cuts,
            scratch=[pltpu.VMEM((3 * cuts, cells, LANES), F32)],
        )
        for c in range(CHUNKS)
    ]
    first = [
        call(
            functools.partial(first_kernel, c, kinds),
            "first",
            (got, consts),
            [column] * 8 + [(1, ALL)],
            scratch=[pltpu.VMEM((6, cells, LANES), F32)],
        )
        for c in range(CHUNKS)
    ]
    flows, sides = [], []
    for c in range(CHUNKS):
        mine, sent = edges[c][:cuts], edges[c][cuts:]
        sides.append((mine, [swap(cut, n, v) for cut, v in enumerate(sent)]))
        flows.append(tuple(call(team_kernel, "team", (masks, first[c][0], first[c][1], first[c][6]), [column] * 2)))

    second, later = [], []
    for c in range(CHUNKS):
        head, warm, perm, conduct, wet, melt, cond, energy, surface = first[c]
        water, heat = flows[c]
        mine, theirs = sides[c]
        values = call(
            functools.partial(middle_kernel, cuts),
            "middle",
            (masks, head, warm, perm, conduct, wet, melt, cond, energy, surface, water, heat, *mine, *theirs),
            [column] * 5 + [(2,) + halo] * cuts + [(2,) + squeezed] * cuts,
            scratch=[room] * 5,
        )
        second.append(values[:5])
        mine, sent = values[5 : 5 + cuts], values[5 + cuts :]
        later.append((mine, [swap(cut, n, v) for cut, v in enumerate(sent)]))

    done = []
    for c in range(CHUNKS):
        conduct, stored, energy, surface = first[c][3], first[c][4], first[c][7], first[c][8]
        head, warm, wet, melt, cond = second[c]
        water, heat = call(team_kernel, "team", (masks, head, warm, cond), [column] * 2)
        mine, theirs = later[c]
        mine_k, theirs_k = sides[c]
        final = c == CHUNKS - 1
        done += call(
            functools.partial(last_kernel, c, cuts),
            "last",
            (
                masks, head, warm, conduct, stored, wet, melt, cond, energy, surface, water, heat,
                *mine, *theirs, *mine_k, *theirs_k, *(done if final else ()),
            ),
            [(TEAM, 2 * quarters if final else 4, OWN, cells)],
            scratch=[room] * 8 + [pltpu.VMEM((4, cells, LANES), F32)],
        )
    back = exchange(done[-1], n)
    return tuple(
        call(
            unpack_kernel,
            "unpack",
            (back,),
            [(cells, width)] * 2,
            scratch=[
                pltpu.VMEM((2, cells, width), F32),
                pltpu.SemaphoreType.DMA((2,)),
            ],
            out_specs=[hbm, hbm],
        )
    )


def solution(mesh):
    placed = (P(None, "cols"), P(None, "cols"), P(None, "cols"), P("cols"), P(), P(), P())
    return jax.shard_map(
        on_device,
        mesh=mesh,
        in_specs=placed,
        out_specs=(P(None, "cols"), P(None, "cols")),
        check_vma=False,
    )
```

```python
import functools

import jax
import jax.numpy as jnp
from jax import lax
from jax.experimental import pallas as pl
from jax.experimental.pallas import tpu as pltpu
from jax.sharding import PartitionSpec as P

SPAN = 256
PAIR_DEV = 4
LANES = 128
CHUNKS = SPAN // LANES
TEAM = 16
ORDER = (0, 14, 2, 12, 4, 10, 6, 8, 1, 15, 3, 13, 5, 11, 7, 9)
OWN = LANES // TEAM
SUB = 8
GROUPS = 2
WIDTH = 2 * LANES
ALL = GROUPS * WIDTH
EDGE = PAIR_DEV * OWN
VMEM_LIMIT = 32 * 1024 * 1024
DISTANCES = range(1, PAIR_DEV + 1)
F32 = jnp.float32


def tiles_of(chunks, slot):
    return jnp.concatenate([chunks[ORDER.index(m), slot] for m in range(TEAM)], axis=0)


def put_tiles(chunks, slot, rows):
    tiles = rows.reshape(TEAM, OWN, rows.shape[1])
    for place_in_order, m in enumerate(ORDER):
        chunks[place_in_order, slot] = tiles[m]


def cut_count(n):
    return min(n // TEAM - 1, 2)


def place(cut):
    team = lax.axis_index("cols") // TEAM
    return team, lax.rem(team, 2) == cut


def far_edge(above):
    return jnp.where(above, 0, PAIR_DEV - 1)


def sign_of(cut):
    return jnp.where(place(cut)[1], 1.0, -1.0).astype(F32)


def reciprocal(x):
    return pltpu.reciprocal(x, approx=True)


def sigmoid(x):
    return 0.5 + 0.5 * jnp.tanh(0.5 * x)


def passage(h, t, k):
    s = sigmoid(h)
    return k * (sigmoid(2.0 * t) * s * s + 0.02)


def lanes_of(g, b):
    return slice((g * 2 + b) * LANES, (g * 2 + b + 1) * LANES)


def following(value):
    first, second = value[:, :WIDTH], value[:, WIDTH:]
    return jnp.concatenate([second, pltpu.roll(first, SUB - 1, axis=0)], axis=1)


def preceding(value):
    first, second = value[:, :WIDTH], value[:, WIDTH:]
    return jnp.concatenate([pltpu.roll(second, 1, axis=0), first], axis=1)


def solve(steps, matrix, ratio, lead, value, update):
    c_prev = a_prev = d_prev = None
    for j in range(steps):
        above, main, below, source = matrix(j)
        if j == 0:
            r = reciprocal(main)
            a_prev = above * r
            d_prev = source * r
        else:
            r = reciprocal(main - above * c_prev)
            over = above * r
            a_prev = a_prev * over
            d_prev = source * r + d_prev * over
        c_prev = below * r
        ratio[j] = c_prev
        lead[j] = a_prev
        value[j] = d_prev
    last_c, last_a, last_d = c_prev, a_prev, d_prev
    p_first, a_first, d_first = ratio[steps - 2], lead[steps - 2], value[steps - 2]
    for j in range(steps - 3, -1, -1):
        c = ratio[j]
        p_first = c * p_first
        a_first = lead[j] + c * a_first
        d_first = value[j] + c * d_first
    g = reciprocal(1.0 - last_c * following(a_first))
    up = last_c * following(p_first) * g
    down = last_a * g
    own = (last_d + last_c * following(d_first)) * g
    step = 0
    while step < SUB:
        if step == 0:
            after, before = following, preceding
        else:
            after = functools.partial(pltpu.roll, shift=SUB - step, axis=0)
            before = functools.partial(pltpu.roll, shift=step, axis=0)
        g = reciprocal(1.0 - up * after(down) - down * before(up))
        own = (own + up * after(own) + down * before(own)) * g
        up = up * after(up) * g
        down = down * before(down) * g
        step = max(1, 2 * step)
    over = preceding(own)
    x = own
    update(steps - 1, x)
    for j in range(steps - 2, -1, -1):
        x = ratio[j] * x + (lead[j] * over + value[j])
        update(j, x)


def mask_rows(cuts):
    return 3 * PAIR_DEV + cuts * (2 * PAIR_DEV + 2)


def cut_row(cut):
    return 3 * PAIR_DEV + cut * (2 * PAIR_DEV + 2)


def mask_kernel(n, couplings, out):
    pair_rows = couplings[...]
    pairs = couplings.shape[1]
    pair_id = lax.broadcasted_iota(jnp.int32, (pairs, LANES), 0)
    lane = lax.broadcasted_iota(jnp.int32, (pairs, LANES), 1)
    lane_1 = lax.broadcasted_iota(jnp.int32, (SUB, LANES), 1)

    def chosen(dev, s):
        at = (pair_id == dev * PAIR_DEV + s - 1).astype(F32)
        found = jnp.dot(pair_rows, at, preferred_element_type=F32)
        return found[0:1], found[1:2]

    def put(row, value):
        out[row] = jnp.broadcast_to(value, (SUB, LANES))

    team = lax.axis_index("cols") // TEAM
    dev = team * TEAM + lane // OWN
    for s in DISTANCES:
        put(s - 1, chosen(dev, s)[0])
        put(PAIR_DEV + s - 1, chosen(dev - s, s)[1])
        put(2 * PAIR_DEV + s - 1, jnp.where(lane_1 // OWN + s < TEAM, 0.25, 0.0))
    block = lax.rem(lane_1 // EDGE, 2)
    edge = lax.rem(lane, EDGE) // OWN
    edge_1 = lax.rem(lane_1, EDGE) // OWN
    for cut in range(cut_count(n)):
        _, above = place(cut)
        row = cut_row(cut)
        partner = jnp.where(above, team + 1, team - 1)
        there = jnp.logical_and(partner >= 0, partner < n // TEAM)
        factor = jnp.where(there, 0.25, 0.0) * sign_of(cut)
        for s in DISTANCES:
            start = team * TEAM + jnp.where(above, TEAM - PAIR_DEV, -s)
            up, down = chosen(start + edge, s)
            mine = jnp.where(above, up, down)
            inward = jnp.where(above, edge_1, PAIR_DEV - 1 - edge_1)
            active = jnp.logical_and(inward >= PAIR_DEV - s, jnp.abs(mine - block.astype(F32)) < 0.5)
            put(row + s - 1, jnp.where(active, factor, 0.0))
            apart = jnp.where(above, PAIR_DEV - s, s - PAIR_DEV)
            up, down = chosen(start + edge + apart, s)
            theirs = jnp.where(edge_1 == far_edge(jnp.logical_not(above)), 0.0, jnp.where(above, down, up))
            put(row + PAIR_DEV + s - 1, jnp.where(jnp.abs(theirs - block.astype(F32)) < 0.5, 1.0, 0.0))
        outward = jnp.where(above, LANES - 1 - lane_1, lane_1)
        put(row + 2 * PAIR_DEV, jnp.where(outward < EDGE, 1.0, 0.0))
        single = jnp.logical_and(edge_1 == far_edge(above), block == 0)
        put(row + 2 * PAIR_DEV + 1, jnp.where(single, mine, 0.0))


def halo_parts():
    return lax.rem(lax.broadcasted_iota(jnp.int32, (SUB, LANES), 1) // OWN, 2 * PAIR_DEV)


def other_block(cut, couplings):
    team, above = place(cut)
    pair = (team * TEAM + jnp.where(above, TEAM - PAIR_DEV, -1)) * PAIR_DEV + PAIR_DEV - 1
    row = jnp.where(above, 0, 1)
    table = couplings[...].astype(F32)
    wanted = jnp.logical_and(
        lax.broadcasted_iota(jnp.int32, table.shape, 0) == row, lax.broadcasted_iota(jnp.int32, table.shape, 1) == pair
    )
    block = jnp.sum(jnp.sum(jnp.where(wanted, table, 0.0), axis=1, keepdims=True), axis=0, keepdims=True)
    single = jnp.where(halo_parts() == far_edge(above), 1.0, 0.0)
    return single * jnp.broadcast_to(block, (SUB, LANES))


def pack_kernel(
    cuts, suction, warmth, classes, surface, couplings, k_sat, heat_cond, out, consts, pair_rows,
    room, class_room, top, pairs, k_table, heat_table, in_sems,
):
    cells = out.shape[-1]
    quarters = 2 * CHUNKS
    into = []
    rooms = (room.at[0], room.at[1], class_room, top, pairs, k_table, heat_table)
    for f, field in enumerate((suction, warmth, classes, surface, couplings, k_sat, heat_cond)):
        into.append(pltpu.make_async_copy(field, rooms[f], in_sems.at[f]))
        into[-1].start()

    def put(slot, value):
        put_tiles(out, slot, value.T)

    for f in range(3):
        into[f].wait()
        for q in range(quarters):
            lanes = slice(q * LANES, (q + 1) * LANES)
            put(f * quarters + q, class_room[:, lanes].astype(F32) if f == 2 else room[f, :, lanes])
    for copy in into[3:]:
        copy.wait()
    kinds = k_sat.shape[1]
    for c in range(kinds):
        consts[c] = jnp.broadcast_to(k_table[0:1, c : c + 1], (SUB, LANES))
        consts[kinds + c] = jnp.broadcast_to(heat_table[0:1, c : c + 1], (SUB, LANES))
    for cut in range(cuts):
        consts[2 * kinds + cut] = other_block(cut, pairs)
    pair_rows[...] = pairs[...].astype(F32)
    rows = [top[0:1, q * LANES : (q + 1) * LANES] for q in range(quarters)]
    put(3 * quarters, jnp.concatenate(rows + [jnp.zeros((cells - quarters, LANES), F32)], axis=0))


def unpack_kernel(got, suction, warmth, room, sems):
    cells = got.shape[-1]
    quarters = 2 * CHUNKS
    sent = []
    for f, out in enumerate((suction, warmth)):
        for q in range(quarters):
            room[f, :, q * LANES : (q + 1) * LANES] = tiles_of(got, f * quarters + q).T
        sent.append(pltpu.make_async_copy(room.at[f], out, sems.at[f]))
        sent[-1].start()
    for copy in sent:
        copy.wait()


def edge_shift(cut, m):
    return lax.rem(EDGE * m + jnp.where(place(cut)[1], EDGE, 0), LANES)


def halo_of(cut, value):
    part = lax.broadcasted_iota(jnp.int32, (SUB, LANES), 1) // EDGE
    packed = None
    for m in range(2 * GROUPS):
        moved = pltpu.roll(value[:, m * LANES : (m + 1) * LANES], edge_shift(cut, m), axis=1)
        packed = moved if m == 0 else jnp.where(part == m, moved, packed)
    return packed


def pieces(above):
    spare = PAIR_DEV + far_edge(above)
    parts = [j if j < PAIR_DEV else j + jnp.where(above, 1, 0) for j in range(2 * PAIR_DEV - 1)]
    return [(part, lax.rem((spare - part) * OWN + LANES, LANES)) for part in parts]


def squeeze(cut, other, values):
    above = place(cut)[1]
    values = [jnp.where(other, pltpu.roll(v, LANES - EDGE, axis=1), v) for v in values]
    spare = halo_parts() == PAIR_DEV + far_edge(above)
    return [
        jnp.where(spare, pltpu.roll(values[-1], shift, axis=1), v)
        for v, (_, shift) in zip(values[:-1], pieces(above))
    ]


def unsqueeze(cut, values):
    part = halo_parts()
    last = values[0]
    for v, (piece, shift) in zip(values, pieces(jnp.logical_not(place(cut)[1]))):
        last = jnp.where(part == piece, pltpu.roll(v, lax.rem(LANES - shift, LANES), axis=1), last)
    return list(values) + [last]


def edge_kernel(chunk, cuts, got, consts, *refs):
    halos, sent, load = refs[:cuts], refs[cuts:-1], refs[-1]
    cells = got.shape[-1]
    steps = halos[0].shape[1]
    stride = steps * GROUPS
    second = lax.broadcasted_iota(jnp.int32, (SUB, LANES), 1) >= 2 * EDGE
    for cut in range(cuts):
        above = place(cut)[1]
        for f in range(3):
            rows = []
            for b in range(2):
                slot = (f * 2 + b) * CHUNKS + chunk
                for m in range(PAIR_DEV):
                    high, low = ORDER.index(TEAM - PAIR_DEV + m), ORDER.index(m)
                    rows.append(jnp.where(above, got[high, slot], got[low, slot]))
            load[cut * 3 + f] = jnp.concatenate(rows * GROUPS, axis=0).T
    kinds = (consts.shape[0] - cuts) // 2
    table = [consts[c] for c in range(kinds)]
    for cut in range(cuts):
        other = consts[2 * kinds + cut] > 0.5
        for f in range(3):
            values = []
            for j in range(steps):
                v = jnp.where(
                    second,
                    load[cut * 3 + f, pl.ds(steps + j, SUB, stride=stride), :],
                    load[cut * 3 + f, pl.ds(j, SUB, stride=stride), :],
                )
                if f == 2:
                    k = table[0]
                    for c in range(1, len(table)):
                        k = jnp.where(v >= c, table[c], k)
                    v = k
                halos[cut][f, j] = v
                values.append(v)
            for j, v in enumerate(squeeze(cut, other, values)):
                sent[cut][f, j] = v


def first_kernel(
    chunk, kinds, got, consts, head, warm, perm, conduct, wet, melt, cond, energy, top, load
):
    cells = got.shape[-1]
    steps = head.shape[0]
    stride = steps * GROUPS

    for field in range(3):
        for b in range(2):
            load[field * 2 + b] = tiles_of(got, (field * 2 + b) * CHUNKS + chunk).T
    surface = tiles_of(got, 6 * CHUNKS).T[0:SUB]
    rows = [surface[b * CHUNKS + chunk : b * CHUNKS + chunk + 1] for b in range(2)]
    top[...] = jnp.concatenate(rows * GROUPS, axis=1)

    def fetch(field, j):
        parts = [
            load[field * 2 + b, pl.ds(g * steps + j, SUB, stride=stride), :]
            for g in range(GROUPS)
            for b in range(2)
        ]
        return jnp.concatenate(parts, axis=1)

    def pick(v):
        parts = []
        for m in range(2 * GROUPS):
            part = v[:, m * LANES : (m + 1) * LANES]
            k, lam = consts[0], consts[kinds]
            for c in range(1, kinds):
                here = part >= c
                k = jnp.where(here, consts[c], k)
                lam = jnp.where(here, consts[kinds + c], lam)
            parts.append((k, lam))
        return [jnp.concatenate(side, axis=1) for side in zip(*parts)]

    for j in range(steps):
        h, t, v = [fetch(field, j) for field in range(3)]
        k, lam = pick(v)
        s, f = sigmoid(h), sigmoid(2.0 * t)
        m = 0.05 + 0.4 * s
        head[j], warm[j], perm[j], conduct[j] = h, t, k, lam
        wet[j] = s
        melt[j] = f
        cond[j] = k * (f * s * s + 0.02)
        energy[j] = (1.0 + 2.0 * m) * t + 2.0 * m * f


def team_kernel(masks, head, warm, cond, water, heat):
    steps = head.shape[0]
    upper = [masks[s - 1] > 0.5 for s in DISTANCES]
    lower = [masks[PAIR_DEV + s - 1] > 0.5 for s in DISTANCES]

    def step(j, _):
        for g in range(GROUPS):
            l0, l1 = lanes_of(g, 0), lanes_of(g, 1)
            h0, h1 = head[j, :, l0], head[j, :, l1]
            t0, t1 = warm[j, :, l0], warm[j, :, l1]
            c0, c1 = cond[j, :, l0], cond[j, :, l1]
            total = None
            for s in DISTANCES:
                up, low = upper[s - 1], lower[s - 1]
                back = LANES - s * OWN
                h_low = pltpu.roll(jnp.where(low, h1, h0), back, axis=1)
                t_low = pltpu.roll(jnp.where(low, t1, t0), back, axis=1)
                c_low = pltpu.roll(jnp.where(low, c1, c0), back, axis=1)
                flow = (
                    masks[2 * PAIR_DEV + s - 1]
                    * (jnp.where(up, c1, c0) + c_low)
                    * (jnp.where(up, h1, h0) - h_low + 0.5)
                )
                carried = flow * jnp.where(flow > 0.0, jnp.where(up, t1, t0), t_low)
                flow_in = pltpu.roll(flow, s * OWN, axis=1)
                carried_in = pltpu.roll(carried, s * OWN, axis=1)
                part = (
                    flow_in - flow,
                    jnp.where(low, flow_in, 0.0) - jnp.where(up, flow, 0.0),
                    carried_in - carried,
                    jnp.where(low, carried_in, 0.0) - jnp.where(up, carried, 0.0),
                )
                total = part if total is None else [a + b for a, b in zip(total, part)]
            water[j, :, l0] = total[0] - total[1]
            water[j, :, l1] = total[1]
            heat[j, :, l0] = 2.0 * (total[2] - total[3])
            heat[j, :, l1] = 2.0 * total[3]

    lax.fori_loop(0, steps, step, None)


def cross_flows(cut, masks, mine, theirs):
    row = cut_row(cut)
    sign = sign_of(cut)
    above = place(cut)[1]
    lane = lax.broadcasted_iota(jnp.int32, (SUB, LANES), 1)
    first_block = lax.rem(lane, 2 * EDGE) < EDGE
    h, t, k = mine
    c = passage(h, t, k)
    far = [theirs[0], theirs[1], passage(*theirs)]
    other = [
        jnp.where(first_block, pltpu.roll(v, LANES - EDGE, axis=1), pltpu.roll(v, EDGE, axis=1)) for v in far
    ]
    water = heat = jnp.zeros((SUB, LANES), F32)
    for s in DISTANCES:
        same = masks[row + PAIR_DEV + s - 1] > 0.5
        picked = [jnp.where(same, a, b) for a, b in zip(far, other)]
        apart = (PAIR_DEV - s) * OWN
        if apart:
            shift = jnp.where(above, apart, LANES - apart)
            picked = [pltpu.roll(v, shift, axis=1) for v in picked]
        h_far, t_far, c_far = picked
        flow = masks[row + s - 1] * (c + c_far) * (sign * (h - h_far) + 0.5)
        water = water - flow
        heat = heat - flow * jnp.where(flow > 0.0, t, t_far)
    return water, heat


def advance(steps, cuts, masks, head, warm, conduct, stored, energy, wet, melt, cond, water, heat, top,
            mine, theirs, new_head, new_warm, new_wet, inflow, warm_inflow, ratio, lead, value, finish):
    for j in range(steps):
        w_parts = [water[j, :, m * LANES : (m + 1) * LANES] for m in range(2 * GROUPS)]
        q_parts = [heat[j, :, m * LANES : (m + 1) * LANES] for m in range(2 * GROUPS)]
        for cut in range(cuts):
            beside = masks[cut_row(cut) + 2 * PAIR_DEV]
            w_far, q_far = cross_flows(cut, masks, mine(cut, j), theirs(cut, j))
            for m in range(2 * GROUPS):
                shift = lax.rem(LANES - edge_shift(cut, m), LANES)
                w_parts[m] = w_parts[m] + beside * pltpu.roll(w_far, shift, axis=1)
                q_parts[m] = q_parts[m] + 2.0 * beside * pltpu.roll(q_far, shift, axis=1)
        for m in range(2 * GROUPS):
            inflow[j, :, m * LANES : (m + 1) * LANES] = w_parts[m]
            warm_inflow[j, :, m * LANES : (m + 1) * LANES] = q_parts[m]

    part = lax.broadcasted_iota(jnp.int32, (SUB, ALL), 0)
    group = lax.broadcasted_iota(jnp.int32, (SUB, ALL), 1) // WIDTH
    first_part = jnp.logical_and(part == 0, group == 0)
    last_part = jnp.logical_and(part == SUB - 1, group == GROUPS - 1)

    def faces(fields, potential):
        face_of, rise_of = [], []
        for j in range(steps):
            if j + 1 < steps:
                c_next, v_next = fields[j + 1], potential[j + 1]
                face = 0.5 * (fields[j] + c_next)
            else:
                c_next, v_next = following(fields[0]), following(potential[0])
                face = jnp.where(last_part, 0.0, 0.5 * (fields[j] + c_next))
            face_of.append(face)
            rise_of.append(v_next - potential[j])
        return face_of, rise_of

    k_face, rise = faces([cond[j] for j in range(steps)], head)
    k_top = jnp.where(first_part, 0.0, preceding(k_face[-1]))
    q_face = [k * (1.0 - d) for k, d in zip(k_face, rise)]
    q_top = jnp.where(first_part, 0.0, preceding(q_face[-1]))

    def water_matrix(j):
        above = k_top if j == 0 else k_face[j - 1]
        into = q_top if j == 0 else q_face[j - 1]
        s = wet[j]
        main = 0.8 * s * (1.0 - s) + 0.02 + above + k_face[j]
        source = inflow[j] + into - q_face[j] - 0.8 * (s - stored[j])
        return above, main, k_face[j], source

    def water_done(j, x):
        h = head[j] + x
        new_head[j] = h
        new_wet[j] = sigmoid(h)

    solve(steps, water_matrix, ratio, lead, value, water_done)

    l_cell = [conduct[j] * (1.5 - 0.5 * melt[j]) for j in range(steps)]
    l_face, rise = faces(l_cell, warm)
    l_top = jnp.where(first_part, 0.0, preceding(l_face[-1]))
    g_face = [l * d for l, d in zip(l_face, rise)]
    g_top = jnp.where(first_part, 0.0, preceding(g_face[-1]))
    surface_lam = jnp.where(first_part, 2.0 * l_cell[0], 0.0)

    def heat_matrix(j):
        above = l_top if j == 0 else l_face[j - 1]
        out_of = g_top if j == 0 else g_face[j - 1]
        t, f = warm[j], melt[j]
        m2 = 0.1 + 0.8 * new_wet[j]
        now = (1.0 + m2) * t + m2 * f
        main = 2.0 + 2.0 * m2 * (1.0 + 2.0 * f * (1.0 - f)) + above + l_face[j]
        source = warm_inflow[j] - out_of + g_face[j] - 2.0 * (now - energy[j])
        if j == 0:
            main = main + surface_lam
            source = source + surface_lam * (top[...] - t)
        return above, main, l_face[j], source

    def heat_done(j, x):
        t = warm[j] + x
        new_warm[j] = t
        finish(j, t)

    solve(steps, heat_matrix, ratio, lead, value, heat_done)


def middle_kernel(cuts, *refs):
    masks, head, warm, perm, conduct, wet, melt, cond, energy, top, water, heat = refs[:12]
    own, far = refs[12 : 12 + cuts], refs[12 + cuts : 12 + 2 * cuts]
    new_head, new_warm, new_wet, new_melt, new_cond = refs[12 + 2 * cuts : 17 + 2 * cuts]
    halos, sent = refs[17 + 2 * cuts : 17 + 3 * cuts], refs[17 + 3 * cuts : 17 + 4 * cuts]
    inflow, warm_inflow, ratio, lead, value = refs[17 + 4 * cuts :]
    steps = head.shape[0]
    packed = {}

    def finish(j, t):
        s, f = new_wet[j], sigmoid(2.0 * t)
        new_melt[j] = f
        new_cond[j] = perm[j] * (f * s * s + 0.02)
        for cut in range(cuts):
            for i, v in enumerate((new_head[j], t)):
                packed[cut, i, j] = halo_of(cut, v)
                halos[cut][i, j] = packed[cut, i, j]

    theirs = [[unsqueeze(cut, [far[cut][i, j] for j in range(steps - 1)]) for i in range(3)] for cut in range(cuts)]
    advance(
        steps, cuts, masks, head, warm, conduct, wet, energy, wet, melt, cond, water, heat, top,
        lambda cut, j: [own[cut][i, j] for i in range(3)],
        lambda cut, j: [theirs[cut][i][j] for i in range(3)],
        new_head, new_warm, new_wet, inflow, warm_inflow, ratio, lead, value, finish,
    )
    for cut in range(cuts):
        for i in range(2):
            other = masks[cut_row(cut) + 2 * PAIR_DEV + 1] > 0.5
            values = squeeze(cut, other, [packed[cut, i, j] for j in range(steps)])
            for j, v in enumerate(values):
                sent[cut][i, j] = v


def last_kernel(chunk, cuts, *refs):
    masks, head, warm, conduct, stored, wet, melt, cond, energy, top, water, heat = refs[:12]
    own, far = refs[12 : 12 + cuts], refs[12 + cuts : 12 + 2 * cuts]
    own_k, far_k = refs[12 + 2 * cuts : 12 + 3 * cuts], refs[12 + 3 * cuts : 12 + 4 * cuts]
    others = refs[12 + 4 * cuts : -10]
    out, new_head, new_warm, new_wet, inflow, warm_inflow, ratio, lead, value, load = refs[-10:]
    steps = head.shape[0]
    cells = steps * GROUPS * SUB
    stride = steps * GROUPS
    theirs = [
        [unsqueeze(cut, [source[i, j] for j in range(steps - 1)]) for source, i in ((far[cut], 0), (far[cut], 1), (far_k[cut], 2))]
        for cut in range(cuts)
    ]
    advance(
        steps, cuts, masks, head, warm, conduct, stored, energy, wet, melt, cond, water, heat, top,
        lambda cut, j: [own[cut][0, j], own[cut][1, j], own_k[cut][2, j]],
        lambda cut, j: [theirs[cut][i][j] for i in range(3)],
        new_head, new_warm, new_wet, inflow, warm_inflow, ratio, lead, value, lambda j, t: None,
    )
    final = chunk == CHUNKS - 1
    for f, field in enumerate((new_head, new_warm)):
        for b in range(2):
            slot = f * 2 + b
            for j in range(steps):
                for g in range(GROUPS):
                    load[slot, pl.ds(g * steps + j, SUB, stride=stride), :] = field[j, :, lanes_of(g, b)]
            put_tiles(out, slot * CHUNKS + chunk if final else slot, load[slot].T)
            if final:
                for c, other in enumerate(others):
                    out[:, slot * CHUNKS + c] = other[:, slot]


def whole(memory=pltpu.VMEM):
    return pl.BlockSpec(memory_space=memory)


def call(kernel, name, args, outs, scratch=(), specs=None, out_specs=None, limit=VMEM_LIMIT, work=2_000_000):
    return pl.pallas_call(
        kernel,
        out_shape=[jax.ShapeDtypeStruct(shape, F32) for shape in outs],
        in_specs=specs or [whole()] * len(args),
        out_specs=out_specs or [whole()] * len(outs),
        scratch_shapes=scratch,
        compiler_params=pltpu.CompilerParams(vmem_limit_bytes=limit),
        cost_estimate=pl.CostEstimate(flops=work, bytes_accessed=work, transcendentals=0),
        name=name,
    )(*args)


def exchange(tiles, n):
    teams = [[start + m for m in ORDER] for start in range(0, n, TEAM)]
    return lax.all_to_all(
        tiles, "cols", split_axis=0, concat_axis=0, tiled=True, axis_index_groups=teams
    )


def swap(cut, n, value):
    pairs = []
    for team in range(cut, n // TEAM - 1, 2):
        for i in range(team * TEAM, (team + 1) * TEAM):
            pairs += [(i, i + TEAM), (i + TEAM, i)]
    return lax.ppermute(value, "cols", pairs)


def on_device(suction, warmth, classes, top, couplings, k_sat, heat_cond):
    n = lax.axis_size("cols")
    cells, width = suction.shape
    steps = cells // (SUB * GROUPS)
    quarters = width // LANES
    cuts = cut_count(n)
    column = (steps, SUB, ALL)
    halo = (steps, SUB, LANES)
    squeezed = (steps - 1, SUB, LANES)
    room = pltpu.VMEM(column, F32)
    hbm = whole(pltpu.HBM)

    arguments = (suction, warmth, classes, top.reshape(1, width), couplings, k_sat.reshape(1, -1), heat_cond.reshape(1, -1))
    kinds = k_sat.shape[0]
    packed, consts, pair_rows = call(
        functools.partial(pack_kernel, cuts),
        "pack",
        [pltpu.with_memory_space_constraint(v, pltpu.HBM) for v in arguments],
        [(TEAM, 3 * quarters + 1, OWN, cells), (2 * kinds + cuts, SUB, LANES), couplings.shape],
        scratch=[
            pltpu.VMEM((2, cells, width), F32),
            pltpu.VMEM((cells, width), classes.dtype),
            pltpu.VMEM((1, width), F32),
            pltpu.VMEM(couplings.shape, couplings.dtype),
            pltpu.VMEM((1, kinds), F32),
            pltpu.VMEM((1, kinds), F32),
            pltpu.SemaphoreType.DMA((7,)),
        ],
        specs=[hbm] * 7,
    )
    masks = call(
        functools.partial(mask_kernel, n), "masks", (pair_rows,), [(mask_rows(cuts), SUB, LANES)]
    )[0]
    got = exchange(packed, n)

    edges = [
        call(
            functools.partial(edge_kernel, c, cuts),
            "edges",
            (got, consts),
            [(3,) + halo] * cuts + [(3,) + squeezed] * cuts,
            scratch=[pltpu.VMEM((3 * cuts, cells, LANES), F32)],
        )
        for c in range(CHUNKS)
    ]
    first = [
        call(
            functools.partial(first_kernel, c, kinds),
            "first",
            (got, consts),
            [column] * 8 + [(1, ALL)],
            scratch=[pltpu.VMEM((6, cells, LANES), F32)],
        )
        for c in range(CHUNKS)
    ]
    flows, sides = [], []
    for c in range(CHUNKS):
        mine, sent = edges[c][:cuts], edges[c][cuts:]
        sides.append((mine, [swap(cut, n, v) for cut, v in enumerate(sent)]))
        flows.append(tuple(call(team_kernel, "team", (masks, first[c][0], first[c][1], first[c][6]), [column] * 2)))

    second, later = [], []
    for c in range(CHUNKS):
        head, warm, perm, conduct, wet, melt, cond, energy, surface = first[c]
        water, heat = flows[c]
        mine, theirs = sides[c]
        values = call(
            functools.partial(middle_kernel, cuts),
            "middle",
            (masks, head, warm, perm, conduct, wet, melt, cond, energy, surface, water, heat, *mine, *theirs),
            [column] * 5 + [(2,) + halo] * cuts + [(2,) + squeezed] * cuts,
            scratch=[room] * 5,
        )
        second.append(values[:5])
        mine, sent = values[5 : 5 + cuts], values[5 + cuts :]
        later.append((mine, [swap(cut, n, v) for cut, v in enumerate(sent)]))

    done = []
    for c in range(CHUNKS):
        conduct, stored, energy, surface = first[c][3], first[c][4], first[c][7], first[c][8]
        head, warm, wet, melt, cond = second[c]
        water, heat = call(team_kernel, "team", (masks, head, warm, cond), [column] * 2)
        mine, theirs = later[c]
        mine_k, theirs_k = sides[c]
        final = c == CHUNKS - 1
        done += call(
            functools.partial(last_kernel, c, cuts),
            "last",
            (
                masks, head, warm, conduct, stored, wet, melt, cond, energy, surface, water, heat,
                *mine, *theirs, *mine_k, *theirs_k, *(done if final else ()),
            ),
            [(TEAM, 2 * quarters if final else 4, OWN, cells)],
            scratch=[room] * 8 + [pltpu.VMEM((4, cells, LANES), F32)],
        )
    back = exchange(done[-1], n)
    return tuple(
        call(
            unpack_kernel,
            "unpack",
            (back,),
            [(cells, width)] * 2,
            scratch=[
                pltpu.VMEM((2, cells, width), F32),
                pltpu.SemaphoreType.DMA((2,)),
            ],
            out_specs=[hbm, hbm],
        )
    )


def solution(mesh):
    placed = (P(None, "cols"), P(None, "cols"), P(None, "cols"), P("cols"), P(), P(), P())
    return jax.shard_map(
        on_device,
        mesh=mesh,
        in_specs=placed,
        out_specs=(P(None, "cols"), P(None, "cols")),
        check_vma=False,
    )
```

```python
import functools

import jax
import jax.numpy as jnp
from jax import lax
from jax.experimental import pallas as pl
from jax.experimental.pallas import tpu as pltpu
from jax.sharding import PartitionSpec as P

SPAN = 256
PAIR_DEV = 4
LANES = 128
CHUNKS = SPAN // LANES
TEAM = 16
OWN = LANES // TEAM
SUB = 8
GROUPS = 2
WIDTH = 2 * LANES
ALL = GROUPS * WIDTH
EDGE = PAIR_DEV * OWN
VMEM_LIMIT = 32 * 1024 * 1024
DISTANCES = range(1, PAIR_DEV + 1)
COPIES = 4
F32 = jnp.float32


def cut_count(n):
    return min(n // TEAM - 1, 2)


def place(cut):
    team = lax.axis_index("cols") // TEAM
    return team, lax.rem(team, 2) == cut


def far_edge(above):
    return jnp.where(above, 0, PAIR_DEV - 1)


def sign_of(cut):
    return jnp.where(place(cut)[1], 1.0, -1.0).astype(F32)


def reciprocal(x):
    return pltpu.reciprocal(x, approx=True)


def sigmoid(x):
    return 0.5 + 0.5 * jnp.tanh(0.5 * x)


def passage(h, t, k):
    s = sigmoid(h)
    return k * (sigmoid(2.0 * t) * s * s + 0.02)


def lanes_of(g, b):
    return slice((g * 2 + b) * LANES, (g * 2 + b + 1) * LANES)


def following(value):
    first, second = value[:, :WIDTH], value[:, WIDTH:]
    return jnp.concatenate([second, pltpu.roll(first, SUB - 1, axis=0)], axis=1)


def preceding(value):
    first, second = value[:, :WIDTH], value[:, WIDTH:]
    return jnp.concatenate([pltpu.roll(second, 1, axis=0), first], axis=1)


def solve(steps, matrix, ratio, lead, value, update):
    c_prev = a_prev = d_prev = None
    for j in range(steps):
        above, main, below, source = matrix(j)
        if j == 0:
            r = reciprocal(main)
            a_prev = above * r
            d_prev = source * r
        else:
            r = reciprocal(main - above * c_prev)
            over = above * r
            a_prev = a_prev * over
            d_prev = source * r + d_prev * over
        c_prev = below * r
        ratio[j] = c_prev
        lead[j] = a_prev
        value[j] = d_prev
    last_c, last_a, last_d = c_prev, a_prev, d_prev
    p_first, a_first, d_first = ratio[steps - 2], lead[steps - 2], value[steps - 2]
    for j in range(steps - 3, -1, -1):
        c = ratio[j]
        p_first = c * p_first
        a_first = lead[j] + c * a_first
        d_first = value[j] + c * d_first
    g = reciprocal(1.0 - last_c * following(a_first))
    up = last_c * following(p_first) * g
    down = last_a * g
    own = (last_d + last_c * following(d_first)) * g
    step = 0
    while step < SUB:
        if step == 0:
            after, before = following, preceding
        else:
            after = functools.partial(pltpu.roll, shift=SUB - step, axis=0)
            before = functools.partial(pltpu.roll, shift=step, axis=0)
        g = reciprocal(1.0 - up * after(down) - down * before(up))
        own = (own + up * after(own) + down * before(own)) * g
        up = up * after(up) * g
        down = down * before(down) * g
        step = max(1, 2 * step)
    over = preceding(own)
    x = own
    update(steps - 1, x)
    for j in range(steps - 2, -1, -1):
        x = ratio[j] * x + (lead[j] * over + value[j])
        update(j, x)


def mask_rows(cuts):
    return 3 * PAIR_DEV + cuts * (2 * PAIR_DEV + 2)


def cut_row(cut):
    return 3 * PAIR_DEV + cut * (2 * PAIR_DEV + 2)


def mask_kernel(n, couplings, out):
    pair_rows = couplings[...]
    pairs = couplings.shape[1]
    pair_id = lax.broadcasted_iota(jnp.int32, (pairs, LANES), 0)
    lane = lax.broadcasted_iota(jnp.int32, (pairs, LANES), 1)
    lane_1 = lax.broadcasted_iota(jnp.int32, (SUB, LANES), 1)

    def chosen(dev, s):
        at = (pair_id == dev * PAIR_DEV + s - 1).astype(F32)
        found = jnp.dot(pair_rows, at, preferred_element_type=F32)
        return found[0:1], found[1:2]

    def put(row, value):
        out[row] = jnp.broadcast_to(value, (SUB, LANES))

    team = lax.axis_index("cols") // TEAM
    dev = team * TEAM + lane // OWN
    for s in DISTANCES:
        put(s - 1, chosen(dev, s)[0])
        put(PAIR_DEV + s - 1, chosen(dev - s, s)[1])
        put(2 * PAIR_DEV + s - 1, jnp.where(lane_1 // OWN + s < TEAM, 0.25, 0.0))
    block = lax.rem(lane_1 // EDGE, 2)
    edge = lax.rem(lane, EDGE) // OWN
    edge_1 = lax.rem(lane_1, EDGE) // OWN
    for cut in range(cut_count(n)):
        _, above = place(cut)
        row = cut_row(cut)
        partner = jnp.where(above, team + 1, team - 1)
        there = jnp.logical_and(partner >= 0, partner < n // TEAM)
        factor = jnp.where(there, 0.25, 0.0) * sign_of(cut)
        for s in DISTANCES:
            start = team * TEAM + jnp.where(above, TEAM - PAIR_DEV, -s)
            up, down = chosen(start + edge, s)
            mine = jnp.where(above, up, down)
            inward = jnp.where(above, edge_1, PAIR_DEV - 1 - edge_1)
            active = jnp.logical_and(inward >= PAIR_DEV - s, jnp.abs(mine - block.astype(F32)) < 0.5)
            put(row + s - 1, jnp.where(active, factor, 0.0))
            apart = jnp.where(above, PAIR_DEV - s, s - PAIR_DEV)
            up, down = chosen(start + edge + apart, s)
            theirs = jnp.where(edge_1 == far_edge(jnp.logical_not(above)), 0.0, jnp.where(above, down, up))
            put(row + PAIR_DEV + s - 1, jnp.where(jnp.abs(theirs - block.astype(F32)) < 0.5, 1.0, 0.0))
        outward = jnp.where(above, LANES - 1 - lane_1, lane_1)
        put(row + 2 * PAIR_DEV, jnp.where(outward < EDGE, 1.0, 0.0))
        single = jnp.logical_and(edge_1 == far_edge(above), block == 0)
        put(row + 2 * PAIR_DEV + 1, jnp.where(single, mine, 0.0))


def halo_parts():
    return lax.rem(lax.broadcasted_iota(jnp.int32, (SUB, LANES), 1) // OWN, 2 * PAIR_DEV)


def other_block(cut, couplings):
    team, above = place(cut)
    pair = (team * TEAM + jnp.where(above, TEAM - PAIR_DEV, -1)) * PAIR_DEV + PAIR_DEV - 1
    row = jnp.where(above, 0, 1)
    table = couplings[...].astype(F32)
    wanted = jnp.logical_and(
        lax.broadcasted_iota(jnp.int32, table.shape, 0) == row, lax.broadcasted_iota(jnp.int32, table.shape, 1) == pair
    )
    block = jnp.sum(jnp.sum(jnp.where(wanted, table, 0.0), axis=1, keepdims=True), axis=0, keepdims=True)
    single = jnp.where(halo_parts() == far_edge(above), 1.0, 0.0)
    return single * jnp.broadcast_to(block, (SUB, LANES))


def pack_kernel(
    cuts, suction, warmth, classes, surface, couplings, k_sat, heat_cond, out, consts, pair_rows,
    room, class_room, top, pairs, k_table, heat_table, in_sems,
):
    cells = out.shape[-1]
    quarters = 2 * CHUNKS
    block = cells // COPIES
    into = []
    for f, field in enumerate((suction, warmth, classes)):
        target = (room.at[0], room.at[1], class_room)[f]
        for i in range(COPIES):
            here = pl.ds(i * block, block)
            into.append(pltpu.make_async_copy(field.at[here], target.at[here], in_sems.at[f, i]))
            into[-1].start()
    for f, (field, target) in enumerate(((surface, top), (couplings, pairs), (k_sat, k_table), (heat_cond, heat_table))):
        into.append(pltpu.make_async_copy(field, target, in_sems.at[3, f]))
        into[-1].start()

    def put(slot, value):
        out[:, slot] = value.T.reshape(TEAM, OWN, cells)

    for f in range(3):
        for copy in into[f * COPIES : (f + 1) * COPIES]:
            copy.wait()
        for q in range(quarters):
            lanes = slice(q * LANES, (q + 1) * LANES)
            put(f * quarters + q, class_room[:, lanes].astype(F32) if f == 2 else room[f, :, lanes])
    for copy in into[3 * COPIES :]:
        copy.wait()
    kinds = k_sat.shape[1]
    for c in range(kinds):
        consts[c] = jnp.broadcast_to(k_table[0:1, c : c + 1], (SUB, LANES))
        consts[kinds + c] = jnp.broadcast_to(heat_table[0:1, c : c + 1], (SUB, LANES))
    for cut in range(cuts):
        consts[2 * kinds + cut] = other_block(cut, pairs)
    pair_rows[...] = pairs[...].astype(F32)
    rows = [top[0:1, q * LANES : (q + 1) * LANES] for q in range(quarters)]
    put(3 * quarters, jnp.concatenate(rows + [jnp.zeros((cells - quarters, LANES), F32)], axis=0))


def unpack_kernel(got, suction, warmth, room, sems):
    cells = got.shape[-1]
    quarters = 2 * CHUNKS
    sent = []
    for f, out in enumerate((suction, warmth)):
        for q in range(quarters):
            room[f, :, q * LANES : (q + 1) * LANES] = got[:, f * quarters + q].reshape(LANES, cells).T
        block = out.shape[0] // COPIES
        for i in range(COPIES):
            here = pl.ds(i * block, block)
            sent.append(pltpu.make_async_copy(room.at[f, here], out.at[here], sems.at[f, i]))
            sent[-1].start()
    for copy in sent:
        copy.wait()


def edge_shift(cut, m):
    return lax.rem(EDGE * m + jnp.where(place(cut)[1], EDGE, 0), LANES)


def halo_of(cut, value):
    part = lax.broadcasted_iota(jnp.int32, (SUB, LANES), 1) // EDGE
    packed = None
    for m in range(2 * GROUPS):
        moved = pltpu.roll(value[:, m * LANES : (m + 1) * LANES], edge_shift(cut, m), axis=1)
        packed = moved if m == 0 else jnp.where(part == m, moved, packed)
    return packed


def pieces(above):
    spare = PAIR_DEV + far_edge(above)
    parts = [j if j < PAIR_DEV else j + jnp.where(above, 1, 0) for j in range(2 * PAIR_DEV - 1)]
    return [(part, lax.rem((spare - part) * OWN + LANES, LANES)) for part in parts]


def squeeze(cut, other, values):
    above = place(cut)[1]
    values = [jnp.where(other, pltpu.roll(v, LANES - EDGE, axis=1), v) for v in values]
    spare = halo_parts() == PAIR_DEV + far_edge(above)
    return [
        jnp.where(spare, pltpu.roll(values[-1], shift, axis=1), v)
        for v, (_, shift) in zip(values[:-1], pieces(above))
    ]


def unsqueeze(cut, values):
    part = halo_parts()
    last = values[0]
    for v, (piece, shift) in zip(values, pieces(jnp.logical_not(place(cut)[1]))):
        last = jnp.where(part == piece, pltpu.roll(v, lax.rem(LANES - shift, LANES), axis=1), last)
    return list(values) + [last]


def edge_kernel(chunk, cuts, got, consts, *refs):
    halos, sent, load = refs[:cuts], refs[cuts:-1], refs[-1]
    cells = got.shape[-1]
    steps = halos[0].shape[1]
    stride = steps * GROUPS
    second = lax.broadcasted_iota(jnp.int32, (SUB, LANES), 1) >= 2 * EDGE
    for cut in range(cuts):
        start = jnp.where(place(cut)[1], TEAM - PAIR_DEV, 0)
        for f in range(3):
            rows = [
                got[pl.ds(start, PAIR_DEV), (f * 2 + b) * CHUNKS + chunk].reshape(EDGE, cells) for b in range(2)
            ]
            load[cut * 3 + f] = jnp.concatenate(rows * GROUPS, axis=0).T
    kinds = (consts.shape[0] - cuts) // 2
    table = [consts[c] for c in range(kinds)]
    for cut in range(cuts):
        other = consts[2 * kinds + cut] > 0.5
        for f in range(3):
            values = []
            for j in range(steps):
                v = jnp.where(
                    second,
                    load[cut * 3 + f, pl.ds(steps + j, SUB, stride=stride), :],
                    load[cut * 3 + f, pl.ds(j, SUB, stride=stride), :],
                )
                if f == 2:
                    k = table[0]
                    for c in range(1, len(table)):
                        k = jnp.where(v >= c, table[c], k)
                    v = k
                halos[cut][f, j] = v
                values.append(v)
            for j, v in enumerate(squeeze(cut, other, values)):
                sent[cut][f, j] = v


def first_kernel(
    chunk, kinds, got, consts, head, warm, perm, conduct, wet, melt, cond, energy, top, load
):
    cells = got.shape[-1]
    steps = head.shape[0]
    stride = steps * GROUPS

    for field in range(3):
        for b in range(2):
            load[field * 2 + b] = got[:, (field * 2 + b) * CHUNKS + chunk].reshape(LANES, cells).T
    surface = got[:, 6 * CHUNKS].reshape(LANES, cells).T[0:SUB]
    rows = [surface[b * CHUNKS + chunk : b * CHUNKS + chunk + 1] for b in range(2)]
    top[...] = jnp.concatenate(rows * GROUPS, axis=1)

    def fetch(field, j):
        parts = [
            load[field * 2 + b, pl.ds(g * steps + j, SUB, stride=stride), :]
            for g in range(GROUPS)
            for b in range(2)
        ]
        return jnp.concatenate(parts, axis=1)

    def pick(v):
        parts = []
        for m in range(2 * GROUPS):
            part = v[:, m * LANES : (m + 1) * LANES]
            k, lam = consts[0], consts[kinds]
            for c in range(1, kinds):
                here = part >= c
                k = jnp.where(here, consts[c], k)
                lam = jnp.where(here, consts[kinds + c], lam)
            parts.append((k, lam))
        return [jnp.concatenate(side, axis=1) for side in zip(*parts)]

    for j in range(steps):
        h, t, v = [fetch(field, j) for field in range(3)]
        k, lam = pick(v)
        s, f = sigmoid(h), sigmoid(2.0 * t)
        m = 0.05 + 0.4 * s
        head[j], warm[j], perm[j], conduct[j] = h, t, k, lam
        wet[j] = s
        melt[j] = f
        cond[j] = k * (f * s * s + 0.02)
        energy[j] = (1.0 + 2.0 * m) * t + 2.0 * m * f


def team_kernel(masks, head, warm, cond, water, heat):
    steps = head.shape[0]
    upper = [masks[s - 1] > 0.5 for s in DISTANCES]
    lower = [masks[PAIR_DEV + s - 1] > 0.5 for s in DISTANCES]

    def step(j, _):
        for g in range(GROUPS):
            l0, l1 = lanes_of(g, 0), lanes_of(g, 1)
            h0, h1 = head[j, :, l0], head[j, :, l1]
            t0, t1 = warm[j, :, l0], warm[j, :, l1]
            c0, c1 = cond[j, :, l0], cond[j, :, l1]
            total = None
            for s in DISTANCES:
                up, low = upper[s - 1], lower[s - 1]
                back = LANES - s * OWN
                h_low = pltpu.roll(jnp.where(low, h1, h0), back, axis=1)
                t_low = pltpu.roll(jnp.where(low, t1, t0), back, axis=1)
                c_low = pltpu.roll(jnp.where(low, c1, c0), back, axis=1)
                flow = (
                    masks[2 * PAIR_DEV + s - 1]
                    * (jnp.where(up, c1, c0) + c_low)
                    * (jnp.where(up, h1, h0) - h_low + 0.5)
                )
                carried = flow * jnp.where(flow > 0.0, jnp.where(up, t1, t0), t_low)
                flow_in = pltpu.roll(flow, s * OWN, axis=1)
                carried_in = pltpu.roll(carried, s * OWN, axis=1)
                part = (
                    flow_in - flow,
                    jnp.where(low, flow_in, 0.0) - jnp.where(up, flow, 0.0),
                    carried_in - carried,
                    jnp.where(low, carried_in, 0.0) - jnp.where(up, carried, 0.0),
                )
                total = part if total is None else [a + b for a, b in zip(total, part)]
            water[j, :, l0] = total[0] - total[1]
            water[j, :, l1] = total[1]
            heat[j, :, l0] = 2.0 * (total[2] - total[3])
            heat[j, :, l1] = 2.0 * total[3]

    lax.fori_loop(0, steps, step, None, unroll=2)


def cross_flows(cut, masks, mine, theirs):
    row = cut_row(cut)
    sign = sign_of(cut)
    above = place(cut)[1]
    lane = lax.broadcasted_iota(jnp.int32, (SUB, LANES), 1)
    first_block = lax.rem(lane, 2 * EDGE) < EDGE
    h, t, k = mine
    c = passage(h, t, k)
    far = [theirs[0], theirs[1], passage(*theirs)]
    other = [
        jnp.where(first_block, pltpu.roll(v, LANES - EDGE, axis=1), pltpu.roll(v, EDGE, axis=1)) for v in far
    ]
    water = heat = jnp.zeros((SUB, LANES), F32)
    for s in DISTANCES:
        same = masks[row + PAIR_DEV + s - 1] > 0.5
        picked = [jnp.where(same, a, b) for a, b in zip(far, other)]
        apart = (PAIR_DEV - s) * OWN
        if apart:
            shift = jnp.where(above, apart, LANES - apart)
            picked = [pltpu.roll(v, shift, axis=1) for v in picked]
        h_far, t_far, c_far = picked
        flow = masks[row + s - 1] * (c + c_far) * (sign * (h - h_far) + 0.5)
        water = water - flow
        heat = heat - flow * jnp.where(flow > 0.0, t, t_far)
    return water, heat


def advance(steps, cuts, masks, head, warm, conduct, stored, energy, wet, melt, cond, water, heat, top,
            mine, theirs, new_head, new_warm, new_wet, inflow, warm_inflow, ratio, lead, value, finish):
    for j in range(steps):
        w_parts = [water[j, :, m * LANES : (m + 1) * LANES] for m in range(2 * GROUPS)]
        q_parts = [heat[j, :, m * LANES : (m + 1) * LANES] for m in range(2 * GROUPS)]
        for cut in range(cuts):
            beside = masks[cut_row(cut) + 2 * PAIR_DEV]
            w_far, q_far = cross_flows(cut, masks, mine(cut, j), theirs(cut, j))
            for m in range(2 * GROUPS):
                shift = lax.rem(LANES - edge_shift(cut, m), LANES)
                w_parts[m] = w_parts[m] + beside * pltpu.roll(w_far, shift, axis=1)
                q_parts[m] = q_parts[m] + 2.0 * beside * pltpu.roll(q_far, shift, axis=1)
        for m in range(2 * GROUPS):
            inflow[j, :, m * LANES : (m + 1) * LANES] = w_parts[m]
            warm_inflow[j, :, m * LANES : (m + 1) * LANES] = q_parts[m]

    part = lax.broadcasted_iota(jnp.int32, (SUB, ALL), 0)
    group = lax.broadcasted_iota(jnp.int32, (SUB, ALL), 1) // WIDTH
    first_part = jnp.logical_and(part == 0, group == 0)
    last_part = jnp.logical_and(part == SUB - 1, group == GROUPS - 1)

    def faces(fields, potential):
        face_of, rise_of = [], []
        for j in range(steps):
            if j + 1 < steps:
                c_next, v_next = fields[j + 1], potential[j + 1]
                face = 0.5 * (fields[j] + c_next)
            else:
                c_next, v_next = following(fields[0]), following(potential[0])
                face = jnp.where(last_part, 0.0, 0.5 * (fields[j] + c_next))
            face_of.append(face)
            rise_of.append(v_next - potential[j])
        return face_of, rise_of

    k_face, rise = faces([cond[j] for j in range(steps)], head)
    k_top = jnp.where(first_part, 0.0, preceding(k_face[-1]))
    q_face = [k * (1.0 - d) for k, d in zip(k_face, rise)]
    q_top = jnp.where(first_part, 0.0, preceding(q_face[-1]))

    def water_matrix(j):
        above = k_top if j == 0 else k_face[j - 1]
        into = q_top if j == 0 else q_face[j - 1]
        s = wet[j]
        main = 0.8 * s * (1.0 - s) + 0.02 + above + k_face[j]
        source = inflow[j] + into - q_face[j] - 0.8 * (s - stored[j])
        return above, main, k_face[j], source

    def water_done(j, x):
        h = head[j] + x
        new_head[j] = h
        new_wet[j] = sigmoid(h)

    solve(steps, water_matrix, ratio, lead, value, water_done)

    l_cell = [conduct[j] * (1.5 - 0.5 * melt[j]) for j in range(steps)]
    l_face, rise = faces(l_cell, warm)
    l_top = jnp.where(first_part, 0.0, preceding(l_face[-1]))
    g_face = [l * d for l, d in zip(l_face, rise)]
    g_top = jnp.where(first_part, 0.0, preceding(g_face[-1]))
    surface_lam = jnp.where(first_part, 2.0 * l_cell[0], 0.0)

    def heat_matrix(j):
        above = l_top if j == 0 else l_face[j - 1]
        out_of = g_top if j == 0 else g_face[j - 1]
        t, f = warm[j], melt[j]
        m2 = 0.1 + 0.8 * new_wet[j]
        now = (1.0 + m2) * t + m2 * f
        main = 2.0 + 2.0 * m2 * (1.0 + 2.0 * f * (1.0 - f)) + above + l_face[j]
        source = warm_inflow[j] - out_of + g_face[j] - 2.0 * (now - energy[j])
        if j == 0:
            main = main + surface_lam
            source = source + surface_lam * (top[...] - t)
        return above, main, l_face[j], source

    def heat_done(j, x):
        t = warm[j] + x
        new_warm[j] = t
        finish(j, t)

    solve(steps, heat_matrix, ratio, lead, value, heat_done)


def middle_kernel(cuts, *refs):
    masks, head, warm, perm, conduct, wet, melt, cond, energy, top, water, heat = refs[:12]
    own, far = refs[12 : 12 + cuts], refs[12 + cuts : 12 + 2 * cuts]
    new_head, new_warm, new_wet, new_melt, new_cond = refs[12 + 2 * cuts : 17 + 2 * cuts]
    halos, sent = refs[17 + 2 * cuts : 17 + 3 * cuts], refs[17 + 3 * cuts : 17 + 4 * cuts]
    inflow, warm_inflow, ratio, lead, value = refs[17 + 4 * cuts :]
    steps = head.shape[0]
    packed = {}

    def finish(j, t):
        s, f = new_wet[j], sigmoid(2.0 * t)
        new_melt[j] = f
        new_cond[j] = perm[j] * (f * s * s + 0.02)
        for cut in range(cuts):
            for i, v in enumerate((new_head[j], t)):
                packed[cut, i, j] = halo_of(cut, v)
                halos[cut][i, j] = packed[cut, i, j]

    theirs = [[unsqueeze(cut, [far[cut][i, j] for j in range(steps - 1)]) for i in range(3)] for cut in range(cuts)]
    advance(
        steps, cuts, masks, head, warm, conduct, wet, energy, wet, melt, cond, water, heat, top,
        lambda cut, j: [own[cut][i, j] for i in range(3)],
        lambda cut, j: [theirs[cut][i][j] for i in range(3)],
        new_head, new_warm, new_wet, inflow, warm_inflow, ratio, lead, value, finish,
    )
    for cut in range(cuts):
        for i in range(2):
            other = masks[cut_row(cut) + 2 * PAIR_DEV + 1] > 0.5
            values = squeeze(cut, other, [packed[cut, i, j] for j in range(steps)])
            for j, v in enumerate(values):
                sent[cut][i, j] = v


def last_kernel(chunk, cuts, *refs):
    masks, head, warm, conduct, stored, wet, melt, cond, energy, top, water, heat = refs[:12]
    own, far = refs[12 : 12 + cuts], refs[12 + cuts : 12 + 2 * cuts]
    own_k, far_k = refs[12 + 2 * cuts : 12 + 3 * cuts], refs[12 + 3 * cuts : 12 + 4 * cuts]
    others = refs[12 + 4 * cuts : -10]
    out, new_head, new_warm, new_wet, inflow, warm_inflow, ratio, lead, value, load = refs[-10:]
    steps = head.shape[0]
    cells = steps * GROUPS * SUB
    stride = steps * GROUPS
    theirs = [
        [unsqueeze(cut, [source[i, j] for j in range(steps - 1)]) for source, i in ((far[cut], 0), (far[cut], 1), (far_k[cut], 2))]
        for cut in range(cuts)
    ]
    advance(
        steps, cuts, masks, head, warm, conduct, stored, energy, wet, melt, cond, water, heat, top,
        lambda cut, j: [own[cut][0, j], own[cut][1, j], own_k[cut][2, j]],
        lambda cut, j: [theirs[cut][i][j] for i in range(3)],
        new_head, new_warm, new_wet, inflow, warm_inflow, ratio, lead, value, lambda j, t: None,
    )
    final = chunk == CHUNKS - 1
    for f, field in enumerate((new_head, new_warm)):
        for b in range(2):
            slot = f * 2 + b
            for j in range(steps):
                for g in range(GROUPS):
                    load[slot, pl.ds(g * steps + j, SUB, stride=stride), :] = field[j, :, lanes_of(g, b)]
            turned = load[slot].T.reshape(TEAM, OWN, cells)
            if final:
                out[:, slot * CHUNKS + chunk] = turned
                for c, other in enumerate(others):
                    out[:, slot * CHUNKS + c] = other[:, slot]
            else:
                out[:, slot] = turned


def whole(memory=pltpu.VMEM):
    return pl.BlockSpec(memory_space=memory)


def call(kernel, name, args, outs, scratch=(), specs=None, out_specs=None, limit=VMEM_LIMIT, work=2_000_000):
    return pl.pallas_call(
        kernel,
        out_shape=[jax.ShapeDtypeStruct(shape, F32) for shape in outs],
        in_specs=specs or [whole()] * len(args),
        out_specs=out_specs or [whole()] * len(outs),
        scratch_shapes=scratch,
        compiler_params=pltpu.CompilerParams(vmem_limit_bytes=limit),
        cost_estimate=pl.CostEstimate(flops=work, bytes_accessed=work, transcendentals=0),
        name=name,
    )(*args)


def exchange(tiles, n):
    teams = [list(range(start, start + TEAM)) for start in range(0, n, TEAM)]
    return lax.all_to_all(
        tiles, "cols", split_axis=0, concat_axis=0, tiled=True, axis_index_groups=teams
    )


def swap(cut, n, value):
    pairs = []
    for team in range(cut, n // TEAM - 1, 2):
        for i in range(team * TEAM, (team + 1) * TEAM):
            pairs += [(i, i + TEAM), (i + TEAM, i)]
    return lax.ppermute(value, "cols", pairs)


def on_device(suction, warmth, classes, top, couplings, k_sat, heat_cond):
    n = lax.axis_size("cols")
    cells, width = suction.shape
    steps = cells // (SUB * GROUPS)
    quarters = width // LANES
    cuts = cut_count(n)
    column = (steps, SUB, ALL)
    halo = (steps, SUB, LANES)
    squeezed = (steps - 1, SUB, LANES)
    room = pltpu.VMEM(column, F32)
    hbm = whole(pltpu.HBM)

    arguments = (suction, warmth, classes, top.reshape(1, width), couplings, k_sat.reshape(1, -1), heat_cond.reshape(1, -1))
    kinds = k_sat.shape[0]
    packed, consts, pair_rows = call(
        functools.partial(pack_kernel, cuts),
        "pack",
        [pltpu.with_memory_space_constraint(v, pltpu.HBM) for v in arguments],
        [(TEAM, 3 * quarters + 1, OWN, cells), (2 * kinds + cuts, SUB, LANES), couplings.shape],
        scratch=[
            pltpu.VMEM((2, cells, width), F32),
            pltpu.VMEM((cells, width), classes.dtype),
            pltpu.VMEM((1, width), F32),
            pltpu.VMEM(couplings.shape, couplings.dtype),
            pltpu.VMEM((1, kinds), F32),
            pltpu.VMEM((1, kinds), F32),
            pltpu.SemaphoreType.DMA((4, COPIES)),
        ],
        specs=[hbm] * 7,
    )
    masks = call(
        functools.partial(mask_kernel, n), "masks", (pair_rows,), [(mask_rows(cuts), SUB, LANES)]
    )[0]
    got = exchange(packed, n)

    edges = [
        call(
            functools.partial(edge_kernel, c, cuts),
            "edges",
            (got, consts),
            [(3,) + halo] * cuts + [(3,) + squeezed] * cuts,
            scratch=[pltpu.VMEM((3 * cuts, cells, LANES), F32)],
        )
        for c in range(CHUNKS)
    ]
    first = [
        call(
            functools.partial(first_kernel, c, kinds),
            "first",
            (got, consts),
            [column] * 8 + [(1, ALL)],
            scratch=[pltpu.VMEM((6, cells, LANES), F32)],
        )
        for c in range(CHUNKS)
    ]
    flows, sides = [], []
    for c in range(CHUNKS):
        mine, sent = edges[c][:cuts], edges[c][cuts:]
        sides.append((mine, [swap(cut, n, v) for cut, v in enumerate(sent)]))
        flows.append(tuple(call(team_kernel, "team", (masks, first[c][0], first[c][1], first[c][6]), [column] * 2)))

    second, later = [], []
    for c in range(CHUNKS):
        head, warm, perm, conduct, wet, melt, cond, energy, surface = first[c]
        water, heat = flows[c]
        mine, theirs = sides[c]
        values = call(
            functools.partial(middle_kernel, cuts),
            "middle",
            (masks, head, warm, perm, conduct, wet, melt, cond, energy, surface, water, heat, *mine, *theirs),
            [column] * 5 + [(2,) + halo] * cuts + [(2,) + squeezed] * cuts,
            scratch=[room] * 5,
        )
        second.append(values[:5])
        mine, sent = values[5 : 5 + cuts], values[5 + cuts :]
        later.append((mine, [swap(cut, n, v) for cut, v in enumerate(sent)]))

    done = []
    for c in range(CHUNKS):
        conduct, stored, energy, surface = first[c][3], first[c][4], first[c][7], first[c][8]
        head, warm, wet, melt, cond = second[c]
        water, heat = call(team_kernel, "team", (masks, head, warm, cond), [column] * 2)
        mine, theirs = later[c]
        mine_k, theirs_k = sides[c]
        final = c == CHUNKS - 1
        done += call(
            functools.partial(last_kernel, c, cuts),
            "last",
            (
                masks, head, warm, conduct, stored, wet, melt, cond, energy, surface, water, heat,
                *mine, *theirs, *mine_k, *theirs_k, *(done if final else ()),
            ),
            [(TEAM, 2 * quarters if final else 4, OWN, cells)],
            scratch=[room] * 8 + [pltpu.VMEM((4, cells, LANES), F32)],
        )
    back = exchange(done[-1], n)
    return tuple(
        call(
            unpack_kernel,
            "unpack",
            (back,),
            [(cells, width)] * 2,
            scratch=[
                pltpu.VMEM((2, cells, width), F32),
                pltpu.SemaphoreType.DMA((2, COPIES)),
            ],
            out_specs=[hbm, hbm],
        )
    )


def solution(mesh):
    placed = (P(None, "cols"), P(None, "cols"), P(None, "cols"), P("cols"), P(), P(), P())
    return jax.shard_map(
        on_device,
        mesh=mesh,
        in_specs=placed,
        out_specs=(P(None, "cols"), P(None, "cols")),
        check_vma=False,
    )
```

```python
import functools

import jax
import jax.numpy as jnp
from jax import lax
from jax.experimental import pallas as pl
from jax.experimental.pallas import tpu as pltpu
from jax.sharding import PartitionSpec as P

SPAN = 256
PAIR_DEV = 4
LANES = 128
CHUNKS = SPAN // LANES
TEAM = 16
OWN = LANES // TEAM
SUB = 8
GROUPS = 2
WIDTH = 2 * LANES
ALL = GROUPS * WIDTH
EDGE = PAIR_DEV * OWN
VMEM_LIMIT = 32 * 1024 * 1024
DISTANCES = range(1, PAIR_DEV + 1)
F32 = jnp.float32


def cut_count(n):
    return min(n // TEAM - 1, 2)


def place(cut):
    team = lax.axis_index("cols") // TEAM
    return team, lax.rem(team, 2) == cut


def far_edge(above):
    return jnp.where(above, 0, PAIR_DEV - 1)


def sign_of(cut):
    return jnp.where(place(cut)[1], 1.0, -1.0).astype(F32)


def reciprocal(x):
    return pltpu.reciprocal(x, approx=True)


def sigmoid(x):
    return 0.5 + 0.5 * jnp.tanh(0.5 * x)


def passage(h, t, k):
    s = sigmoid(h)
    return k * (sigmoid(2.0 * t) * s * s + 0.02)


def lanes_of(g, b):
    return slice((g * 2 + b) * LANES, (g * 2 + b + 1) * LANES)


def following(value):
    first, second = value[:, :WIDTH], value[:, WIDTH:]
    return jnp.concatenate([second, pltpu.roll(first, SUB - 1, axis=0)], axis=1)


def preceding(value):
    first, second = value[:, :WIDTH], value[:, WIDTH:]
    return jnp.concatenate([pltpu.roll(second, 1, axis=0), first], axis=1)


def solve(steps, matrix, ratio, lead, value, update):
    c_prev = a_prev = d_prev = None
    for j in range(steps):
        above, main, below, source = matrix(j)
        if j == 0:
            r = reciprocal(main)
            a_prev = above * r
            d_prev = source * r
        else:
            r = reciprocal(main - above * c_prev)
            over = above * r
            a_prev = a_prev * over
            d_prev = source * r + d_prev * over
        c_prev = below * r
        ratio[j] = c_prev
        lead[j] = a_prev
        value[j] = d_prev
    last_c, last_a, last_d = c_prev, a_prev, d_prev
    p_first, a_first, d_first = ratio[steps - 2], lead[steps - 2], value[steps - 2]
    for j in range(steps - 3, -1, -1):
        c = ratio[j]
        p_first = c * p_first
        a_first = lead[j] + c * a_first
        d_first = value[j] + c * d_first
    g = reciprocal(1.0 - last_c * following(a_first))
    up = last_c * following(p_first) * g
    down = last_a * g
    own = (last_d + last_c * following(d_first)) * g
    step = 0
    while step < SUB:
        if step == 0:
            after, before = following, preceding
        else:
            after = functools.partial(pltpu.roll, shift=SUB - step, axis=0)
            before = functools.partial(pltpu.roll, shift=step, axis=0)
        g = reciprocal(1.0 - up * after(down) - down * before(up))
        own = (own + up * after(own) + down * before(own)) * g
        up = up * after(up) * g
        down = down * before(down) * g
        step = max(1, 2 * step)
    over = preceding(own)
    x = own
    update(steps - 1, x)
    for j in range(steps - 2, -1, -1):
        x = ratio[j] * x + (lead[j] * over + value[j])
        update(j, x)


def mask_rows(cuts):
    return 3 * PAIR_DEV + cuts * (2 * PAIR_DEV + 2)


def cut_row(cut):
    return 3 * PAIR_DEV + cut * (2 * PAIR_DEV + 2)


def mask_kernel(n, couplings, out):
    pair_rows = couplings[...]
    pairs = couplings.shape[1]
    pair_id = lax.broadcasted_iota(jnp.int32, (pairs, LANES), 0)
    lane = lax.broadcasted_iota(jnp.int32, (pairs, LANES), 1)
    lane_1 = lax.broadcasted_iota(jnp.int32, (SUB, LANES), 1)

    def chosen(dev, s):
        at = (pair_id == dev * PAIR_DEV + s - 1).astype(F32)
        found = jnp.dot(pair_rows, at, preferred_element_type=F32)
        return found[0:1], found[1:2]

    def put(row, value):
        out[row] = jnp.broadcast_to(value, (SUB, LANES))

    team = lax.axis_index("cols") // TEAM
    dev = team * TEAM + lane // OWN
    for s in DISTANCES:
        put(s - 1, chosen(dev, s)[0])
        put(PAIR_DEV + s - 1, chosen(dev - s, s)[1])
        put(2 * PAIR_DEV + s - 1, jnp.where(lane_1 // OWN + s < TEAM, 0.25, 0.0))
    block = lax.rem(lane_1 // EDGE, 2)
    edge = lax.rem(lane, EDGE) // OWN
    edge_1 = lax.rem(lane_1, EDGE) // OWN
    for cut in range(cut_count(n)):
        _, above = place(cut)
        row = cut_row(cut)
        partner = jnp.where(above, team + 1, team - 1)
        there = jnp.logical_and(partner >= 0, partner < n // TEAM)
        factor = jnp.where(there, 0.25, 0.0) * sign_of(cut)
        for s in DISTANCES:
            start = team * TEAM + jnp.where(above, TEAM - PAIR_DEV, -s)
            up, down = chosen(start + edge, s)
            mine = jnp.where(above, up, down)
            inward = jnp.where(above, edge_1, PAIR_DEV - 1 - edge_1)
            active = jnp.logical_and(inward >= PAIR_DEV - s, jnp.abs(mine - block.astype(F32)) < 0.5)
            put(row + s - 1, jnp.where(active, factor, 0.0))
            apart = jnp.where(above, PAIR_DEV - s, s - PAIR_DEV)
            up, down = chosen(start + edge + apart, s)
            theirs = jnp.where(edge_1 == far_edge(jnp.logical_not(above)), 0.0, jnp.where(above, down, up))
            put(row + PAIR_DEV + s - 1, jnp.where(jnp.abs(theirs - block.astype(F32)) < 0.5, 1.0, 0.0))
        outward = jnp.where(above, LANES - 1 - lane_1, lane_1)
        put(row + 2 * PAIR_DEV, jnp.where(outward < EDGE, 1.0, 0.0))
        single = jnp.logical_and(edge_1 == far_edge(above), block == 0)
        put(row + 2 * PAIR_DEV + 1, jnp.where(single, mine, 0.0))


def halo_parts():
    return lax.rem(lax.broadcasted_iota(jnp.int32, (SUB, LANES), 1) // OWN, 2 * PAIR_DEV)


def other_block(cut, couplings):
    team, above = place(cut)
    pair = (team * TEAM + jnp.where(above, TEAM - PAIR_DEV, -1)) * PAIR_DEV + PAIR_DEV - 1
    row = jnp.where(above, 0, 1)
    table = couplings[...].astype(F32)
    wanted = jnp.logical_and(
        lax.broadcasted_iota(jnp.int32, table.shape, 0) == row, lax.broadcasted_iota(jnp.int32, table.shape, 1) == pair
    )
    block = jnp.sum(jnp.sum(jnp.where(wanted, table, 0.0), axis=1, keepdims=True), axis=0, keepdims=True)
    single = jnp.where(halo_parts() == far_edge(above), 1.0, 0.0)
    return single * jnp.broadcast_to(block, (SUB, LANES))


def pack_kernel(
    cuts, suction, warmth, classes, surface, couplings, k_sat, heat_cond, out, consts, pair_rows,
    room, class_room, top, pairs, k_table, heat_table, in_sems,
):
    cells = out.shape[-1]
    quarters = 2 * CHUNKS
    into = []
    rooms = (room.at[0], room.at[1], class_room, top, pairs, k_table, heat_table)
    for f, field in enumerate((suction, warmth, classes, surface, couplings, k_sat, heat_cond)):
        into.append(pltpu.make_async_copy(field, rooms[f], in_sems.at[f]))
        into[-1].start()

    def put(slot, value):
        out[:, slot] = value.T.reshape(TEAM, OWN, cells)

    for f in range(3):
        into[f].wait()
        for q in range(quarters):
            lanes = slice(q * LANES, (q + 1) * LANES)
            put(f * quarters + q, class_room[:, lanes].astype(F32) if f == 2 else room[f, :, lanes])
    for copy in into[3:]:
        copy.wait()
    kinds = k_sat.shape[1]
    for c in range(kinds):
        consts[c] = jnp.broadcast_to(k_table[0:1, c : c + 1], (SUB, LANES))
        consts[kinds + c] = jnp.broadcast_to(heat_table[0:1, c : c + 1], (SUB, LANES))
    for cut in range(cuts):
        consts[2 * kinds + cut] = other_block(cut, pairs)
    pair_rows[...] = pairs[...].astype(F32)
    rows = [top[0:1, q * LANES : (q + 1) * LANES] for q in range(quarters)]
    put(3 * quarters, jnp.concatenate(rows + [jnp.zeros((cells - quarters, LANES), F32)], axis=0))


def unpack_kernel(got, suction, warmth, room, sems):
    cells = got.shape[-1]
    quarters = 2 * CHUNKS
    sent = []
    for f, out in enumerate((suction, warmth)):
        for q in range(quarters):
            room[f, :, q * LANES : (q + 1) * LANES] = got[:, f * quarters + q].reshape(LANES, cells).T
        sent.append(pltpu.make_async_copy(room.at[f], out, sems.at[f]))
        sent[-1].start()
    for copy in sent:
        copy.wait()


def edge_shift(cut, m):
    return lax.rem(EDGE * m + jnp.where(place(cut)[1], EDGE, 0), LANES)


def halo_of(cut, value):
    part = lax.broadcasted_iota(jnp.int32, (SUB, LANES), 1) // EDGE
    packed = None
    for m in range(2 * GROUPS):
        moved = pltpu.roll(value[:, m * LANES : (m + 1) * LANES], edge_shift(cut, m), axis=1)
        packed = moved if m == 0 else jnp.where(part == m, moved, packed)
    return packed


def pieces(above):
    spare = PAIR_DEV + far_edge(above)
    parts = [j if j < PAIR_DEV else j + jnp.where(above, 1, 0) for j in range(2 * PAIR_DEV - 1)]
    return [(part, lax.rem((spare - part) * OWN + LANES, LANES)) for part in parts]


def squeeze(cut, other, values):
    above = place(cut)[1]
    values = [jnp.where(other, pltpu.roll(v, LANES - EDGE, axis=1), v) for v in values]
    spare = halo_parts() == PAIR_DEV + far_edge(above)
    return [
        jnp.where(spare, pltpu.roll(values[-1], shift, axis=1), v)
        for v, (_, shift) in zip(values[:-1], pieces(above))
    ]


def unsqueeze(cut, values):
    part = halo_parts()
    last = values[0]
    for v, (piece, shift) in zip(values, pieces(jnp.logical_not(place(cut)[1]))):
        last = jnp.where(part == piece, pltpu.roll(v, lax.rem(LANES - shift, LANES), axis=1), last)
    return list(values) + [last]


def edge_kernel(chunk, cuts, got, consts, *refs):
    halos, sent, load = refs[:cuts], refs[cuts:-1], refs[-1]
    cells = got.shape[-1]
    steps = halos[0].shape[1]
    stride = steps * GROUPS
    second = lax.broadcasted_iota(jnp.int32, (SUB, LANES), 1) >= 2 * EDGE
    for cut in range(cuts):
        start = jnp.where(place(cut)[1], TEAM - PAIR_DEV, 0)
        for f in range(3):
            rows = [
                got[pl.ds(start, PAIR_DEV), (f * 2 + b) * CHUNKS + chunk].reshape(EDGE, cells) for b in range(2)
            ]
            load[cut * 3 + f] = jnp.concatenate(rows * GROUPS, axis=0).T
    kinds = (consts.shape[0] - cuts) // 2
    table = [consts[c] for c in range(kinds)]
    for cut in range(cuts):
        other = consts[2 * kinds + cut] > 0.5
        for f in range(3):
            values = []
            for j in range(steps):
                v = jnp.where(
                    second,
                    load[cut * 3 + f, pl.ds(steps + j, SUB, stride=stride), :],
                    load[cut * 3 + f, pl.ds(j, SUB, stride=stride), :],
                )
                if f == 2:
                    k = table[0]
                    for c in range(1, len(table)):
                        k = jnp.where(v >= c, table[c], k)
                    v = k
                halos[cut][f, j] = v
                values.append(v)
            for j, v in enumerate(squeeze(cut, other, values)):
                sent[cut][f, j] = v


def first_kernel(
    chunk, kinds, got, consts, head, warm, perm, conduct, wet, melt, cond, energy, top, load
):
    cells = got.shape[-1]
    steps = head.shape[0]
    stride = steps * GROUPS

    for field in range(3):
        for b in range(2):
            load[field * 2 + b] = got[:, (field * 2 + b) * CHUNKS + chunk].reshape(LANES, cells).T
    surface = got[:, 6 * CHUNKS].reshape(LANES, cells).T[0:SUB]
    rows = [surface[b * CHUNKS + chunk : b * CHUNKS + chunk + 1] for b in range(2)]
    top[...] = jnp.concatenate(rows * GROUPS, axis=1)

    def fetch(field, j):
        parts = [
            load[field * 2 + b, pl.ds(g * steps + j, SUB, stride=stride), :]
            for g in range(GROUPS)
            for b in range(2)
        ]
        return jnp.concatenate(parts, axis=1)

    def pick(v):
        parts = []
        for m in range(2 * GROUPS):
            part = v[:, m * LANES : (m + 1) * LANES]
            k, lam = consts[0], consts[kinds]
            for c in range(1, kinds):
                here = part >= c
                k = jnp.where(here, consts[c], k)
                lam = jnp.where(here, consts[kinds + c], lam)
            parts.append((k, lam))
        return [jnp.concatenate(side, axis=1) for side in zip(*parts)]

    for j in range(steps):
        h, t, v = [fetch(field, j) for field in range(3)]
        k, lam = pick(v)
        s, f = sigmoid(h), sigmoid(2.0 * t)
        m = 0.05 + 0.4 * s
        head[j], warm[j], perm[j], conduct[j] = h, t, k, lam
        wet[j] = s
        melt[j] = f
        cond[j] = k * (f * s * s + 0.02)
        energy[j] = (1.0 + 2.0 * m) * t + 2.0 * m * f


def team_kernel(masks, head, warm, cond, water, heat):
    steps = head.shape[0]
    upper = [masks[s - 1] > 0.5 for s in DISTANCES]
    lower = [masks[PAIR_DEV + s - 1] > 0.5 for s in DISTANCES]

    def step(j, _):
        for g in range(GROUPS):
            l0, l1 = lanes_of(g, 0), lanes_of(g, 1)
            h0, h1 = head[j, :, l0], head[j, :, l1]
            t0, t1 = warm[j, :, l0], warm[j, :, l1]
            c0, c1 = cond[j, :, l0], cond[j, :, l1]
            total = None
            for s in DISTANCES:
                up, low = upper[s - 1], lower[s - 1]
                back = LANES - s * OWN
                h_low = pltpu.roll(jnp.where(low, h1, h0), back, axis=1)
                t_low = pltpu.roll(jnp.where(low, t1, t0), back, axis=1)
                c_low = pltpu.roll(jnp.where(low, c1, c0), back, axis=1)
                flow = (
                    masks[2 * PAIR_DEV + s - 1]
                    * (jnp.where(up, c1, c0) + c_low)
                    * (jnp.where(up, h1, h0) - h_low + 0.5)
                )
                carried = flow * jnp.where(flow > 0.0, jnp.where(up, t1, t0), t_low)
                flow_in = pltpu.roll(flow, s * OWN, axis=1)
                carried_in = pltpu.roll(carried, s * OWN, axis=1)
                part = (
                    flow_in - flow,
                    jnp.where(low, flow_in, 0.0) - jnp.where(up, flow, 0.0),
                    carried_in - carried,
                    jnp.where(low, carried_in, 0.0) - jnp.where(up, carried, 0.0),
                )
                total = part if total is None else [a + b for a, b in zip(total, part)]
            water[j, :, l0] = total[0] - total[1]
            water[j, :, l1] = total[1]
            heat[j, :, l0] = 2.0 * (total[2] - total[3])
            heat[j, :, l1] = 2.0 * total[3]

    lax.fori_loop(0, steps, step, None, unroll=2)


def cross_flows(cut, masks, mine, theirs):
    row = cut_row(cut)
    sign = sign_of(cut)
    above = place(cut)[1]
    lane = lax.broadcasted_iota(jnp.int32, (SUB, LANES), 1)
    first_block = lax.rem(lane, 2 * EDGE) < EDGE
    h, t, k = mine
    c = passage(h, t, k)
    far = [theirs[0], theirs[1], passage(*theirs)]
    other = [
        jnp.where(first_block, pltpu.roll(v, LANES - EDGE, axis=1), pltpu.roll(v, EDGE, axis=1)) for v in far
    ]
    water = heat = jnp.zeros((SUB, LANES), F32)
    for s in DISTANCES:
        same = masks[row + PAIR_DEV + s - 1] > 0.5
        picked = [jnp.where(same, a, b) for a, b in zip(far, other)]
        apart = (PAIR_DEV - s) * OWN
        if apart:
            shift = jnp.where(above, apart, LANES - apart)
            picked = [pltpu.roll(v, shift, axis=1) for v in picked]
        h_far, t_far, c_far = picked
        flow = masks[row + s - 1] * (c + c_far) * (sign * (h - h_far) + 0.5)
        water = water - flow
        heat = heat - flow * jnp.where(flow > 0.0, t, t_far)
    return water, heat


def advance(steps, cuts, masks, head, warm, conduct, stored, energy, wet, melt, cond, water, heat, top,
            mine, theirs, new_head, new_warm, new_wet, inflow, warm_inflow, ratio, lead, value, finish):
    for j in range(steps):
        w_parts = [water[j, :, m * LANES : (m + 1) * LANES] for m in range(2 * GROUPS)]
        q_parts = [heat[j, :, m * LANES : (m + 1) * LANES] for m in range(2 * GROUPS)]
        for cut in range(cuts):
            beside = masks[cut_row(cut) + 2 * PAIR_DEV]
            w_far, q_far = cross_flows(cut, masks, mine(cut, j), theirs(cut, j))
            for m in range(2 * GROUPS):
                shift = lax.rem(LANES - edge_shift(cut, m), LANES)
                w_parts[m] = w_parts[m] + beside * pltpu.roll(w_far, shift, axis=1)
                q_parts[m] = q_parts[m] + 2.0 * beside * pltpu.roll(q_far, shift, axis=1)
        for m in range(2 * GROUPS):
            inflow[j, :, m * LANES : (m + 1) * LANES] = w_parts[m]
            warm_inflow[j, :, m * LANES : (m + 1) * LANES] = q_parts[m]

    part = lax.broadcasted_iota(jnp.int32, (SUB, ALL), 0)
    group = lax.broadcasted_iota(jnp.int32, (SUB, ALL), 1) // WIDTH
    first_part = jnp.logical_and(part == 0, group == 0)
    last_part = jnp.logical_and(part == SUB - 1, group == GROUPS - 1)

    def faces(fields, potential):
        face_of, rise_of = [], []
        for j in range(steps):
            if j + 1 < steps:
                c_next, v_next = fields[j + 1], potential[j + 1]
                face = 0.5 * (fields[j] + c_next)
            else:
                c_next, v_next = following(fields[0]), following(potential[0])
                face = jnp.where(last_part, 0.0, 0.5 * (fields[j] + c_next))
            face_of.append(face)
            rise_of.append(v_next - potential[j])
        return face_of, rise_of

    k_face, rise = faces([cond[j] for j in range(steps)], head)
    k_top = jnp.where(first_part, 0.0, preceding(k_face[-1]))
    q_face = [k * (1.0 - d) for k, d in zip(k_face, rise)]
    q_top = jnp.where(first_part, 0.0, preceding(q_face[-1]))

    def water_matrix(j):
        above = k_top if j == 0 else k_face[j - 1]
        into = q_top if j == 0 else q_face[j - 1]
        s = wet[j]
        main = 0.8 * s * (1.0 - s) + 0.02 + above + k_face[j]
        source = inflow[j] + into - q_face[j] - 0.8 * (s - stored[j])
        return above, main, k_face[j], source

    def water_done(j, x):
        h = head[j] + x
        new_head[j] = h
        new_wet[j] = sigmoid(h)

    solve(steps, water_matrix, ratio, lead, value, water_done)

    l_cell = [conduct[j] * (1.5 - 0.5 * melt[j]) for j in range(steps)]
    l_face, rise = faces(l_cell, warm)
    l_top = jnp.where(first_part, 0.0, preceding(l_face[-1]))
    g_face = [l * d for l, d in zip(l_face, rise)]
    g_top = jnp.where(first_part, 0.0, preceding(g_face[-1]))
    surface_lam = jnp.where(first_part, 2.0 * l_cell[0], 0.0)

    def heat_matrix(j):
        above = l_top if j == 0 else l_face[j - 1]
        out_of = g_top if j == 0 else g_face[j - 1]
        t, f = warm[j], melt[j]
        m2 = 0.1 + 0.8 * new_wet[j]
        now = (1.0 + m2) * t + m2 * f
        main = 2.0 + 2.0 * m2 * (1.0 + 2.0 * f * (1.0 - f)) + above + l_face[j]
        source = warm_inflow[j] - out_of + g_face[j] - 2.0 * (now - energy[j])
        if j == 0:
            main = main + surface_lam
            source = source + surface_lam * (top[...] - t)
        return above, main, l_face[j], source

    def heat_done(j, x):
        t = warm[j] + x
        new_warm[j] = t
        finish(j, t)

    solve(steps, heat_matrix, ratio, lead, value, heat_done)


def middle_kernel(cuts, *refs):
    masks, head, warm, perm, conduct, wet, melt, cond, energy, top, water, heat = refs[:12]
    own, far = refs[12 : 12 + cuts], refs[12 + cuts : 12 + 2 * cuts]
    new_head, new_warm, new_wet, new_melt, new_cond = refs[12 + 2 * cuts : 17 + 2 * cuts]
    halos, sent = refs[17 + 2 * cuts : 17 + 3 * cuts], refs[17 + 3 * cuts : 17 + 4 * cuts]
    inflow, warm_inflow, ratio, lead, value = refs[17 + 4 * cuts :]
    steps = head.shape[0]
    packed = {}

    def finish(j, t):
        s, f = new_wet[j], sigmoid(2.0 * t)
        new_melt[j] = f
        new_cond[j] = perm[j] * (f * s * s + 0.02)
        for cut in range(cuts):
            for i, v in enumerate((new_head[j], t)):
                packed[cut, i, j] = halo_of(cut, v)
                halos[cut][i, j] = packed[cut, i, j]

    theirs = [[unsqueeze(cut, [far[cut][i, j] for j in range(steps - 1)]) for i in range(3)] for cut in range(cuts)]
    advance(
        steps, cuts, masks, head, warm, conduct, wet, energy, wet, melt, cond, water, heat, top,
        lambda cut, j: [own[cut][i, j] for i in range(3)],
        lambda cut, j: [theirs[cut][i][j] for i in range(3)],
        new_head, new_warm, new_wet, inflow, warm_inflow, ratio, lead, value, finish,
    )
    for cut in range(cuts):
        for i in range(2):
            other = masks[cut_row(cut) + 2 * PAIR_DEV + 1] > 0.5
            values = squeeze(cut, other, [packed[cut, i, j] for j in range(steps)])
            for j, v in enumerate(values):
                sent[cut][i, j] = v


def last_kernel(chunk, cuts, *refs):
    masks, head, warm, conduct, stored, wet, melt, cond, energy, top, water, heat = refs[:12]
    own, far = refs[12 : 12 + cuts], refs[12 + cuts : 12 + 2 * cuts]
    own_k, far_k = refs[12 + 2 * cuts : 12 + 3 * cuts], refs[12 + 3 * cuts : 12 + 4 * cuts]
    others = refs[12 + 4 * cuts : -10]
    out, new_head, new_warm, new_wet, inflow, warm_inflow, ratio, lead, value, load = refs[-10:]
    steps = head.shape[0]
    cells = steps * GROUPS * SUB
    stride = steps * GROUPS
    theirs = [
        [unsqueeze(cut, [source[i, j] for j in range(steps - 1)]) for source, i in ((far[cut], 0), (far[cut], 1), (far_k[cut], 2))]
        for cut in range(cuts)
    ]
    advance(
        steps, cuts, masks, head, warm, conduct, stored, energy, wet, melt, cond, water, heat, top,
        lambda cut, j: [own[cut][0, j], own[cut][1, j], own_k[cut][2, j]],
        lambda cut, j: [theirs[cut][i][j] for i in range(3)],
        new_head, new_warm, new_wet, inflow, warm_inflow, ratio, lead, value, lambda j, t: None,
    )
    final = chunk == CHUNKS - 1
    for f, field in enumerate((new_head, new_warm)):
        for b in range(2):
            slot = f * 2 + b
            for j in range(steps):
                for g in range(GROUPS):
                    load[slot, pl.ds(g * steps + j, SUB, stride=stride), :] = field[j, :, lanes_of(g, b)]
            turned = load[slot].T.reshape(TEAM, OWN, cells)
            if final:
                out[:, slot * CHUNKS + chunk] = turned
                for c, other in enumerate(others):
                    out[:, slot * CHUNKS + c] = other[:, slot]
            else:
                out[:, slot] = turned


def whole(memory=pltpu.VMEM):
    return pl.BlockSpec(memory_space=memory)


def call(kernel, name, args, outs, scratch=(), specs=None, out_specs=None, limit=VMEM_LIMIT, work=2_000_000):
    return pl.pallas_call(
        kernel,
        out_shape=[jax.ShapeDtypeStruct(shape, F32) for shape in outs],
        in_specs=specs or [whole()] * len(args),
        out_specs=out_specs or [whole()] * len(outs),
        scratch_shapes=scratch,
        compiler_params=pltpu.CompilerParams(vmem_limit_bytes=limit),
        cost_estimate=pl.CostEstimate(flops=work, bytes_accessed=work, transcendentals=0),
        name=name,
    )(*args)


def exchange(tiles, n):
    teams = [list(range(start, start + TEAM)) for start in range(0, n, TEAM)]
    return lax.all_to_all(
        tiles, "cols", split_axis=0, concat_axis=0, tiled=True, axis_index_groups=teams
    )


def swap(cut, n, value):
    pairs = []
    for team in range(cut, n // TEAM - 1, 2):
        for i in range(team * TEAM, (team + 1) * TEAM):
            pairs += [(i, i + TEAM), (i + TEAM, i)]
    return lax.ppermute(value, "cols", pairs)


def on_device(suction, warmth, classes, top, couplings, k_sat, heat_cond):
    n = lax.axis_size("cols")
    cells, width = suction.shape
    steps = cells // (SUB * GROUPS)
    quarters = width // LANES
    cuts = cut_count(n)
    column = (steps, SUB, ALL)
    halo = (steps, SUB, LANES)
    squeezed = (steps - 1, SUB, LANES)
    room = pltpu.VMEM(column, F32)
    hbm = whole(pltpu.HBM)

    arguments = (suction, warmth, classes, top.reshape(1, width), couplings, k_sat.reshape(1, -1), heat_cond.reshape(1, -1))
    kinds = k_sat.shape[0]
    packed, consts, pair_rows = call(
        functools.partial(pack_kernel, cuts),
        "pack",
        [pltpu.with_memory_space_constraint(v, pltpu.HBM) for v in arguments],
        [(TEAM, 3 * quarters + 1, OWN, cells), (2 * kinds + cuts, SUB, LANES), couplings.shape],
        scratch=[
            pltpu.VMEM((2, cells, width), F32),
            pltpu.VMEM((cells, width), classes.dtype),
            pltpu.VMEM((1, width), F32),
            pltpu.VMEM(couplings.shape, couplings.dtype),
            pltpu.VMEM((1, kinds), F32),
            pltpu.VMEM((1, kinds), F32),
            pltpu.SemaphoreType.DMA((7,)),
        ],
        specs=[hbm] * 7,
    )
    masks = call(
        functools.partial(mask_kernel, n), "masks", (pair_rows,), [(mask_rows(cuts), SUB, LANES)]
    )[0]
    got = exchange(packed, n)

    edges = [
        call(
            functools.partial(edge_kernel, c, cuts),
            "edges",
            (got, consts),
            [(3,) + halo] * cuts + [(3,) + squeezed] * cuts,
            scratch=[pltpu.VMEM((3 * cuts, cells, LANES), F32)],
        )
        for c in range(CHUNKS)
    ]
    first = [
        call(
            functools.partial(first_kernel, c, kinds),
            "first",
            (got, consts),
            [column] * 8 + [(1, ALL)],
            scratch=[pltpu.VMEM((6, cells, LANES), F32)],
        )
        for c in range(CHUNKS)
    ]
    flows, sides = [], []
    for c in range(CHUNKS):
        mine, sent = edges[c][:cuts], edges[c][cuts:]
        sides.append((mine, [swap(cut, n, v) for cut, v in enumerate(sent)]))
        flows.append(tuple(call(team_kernel, "team", (masks, first[c][0], first[c][1], first[c][6]), [column] * 2)))

    second, later = [], []
    for c in range(CHUNKS):
        head, warm, perm, conduct, wet, melt, cond, energy, surface = first[c]
        water, heat = flows[c]
        mine, theirs = sides[c]
        values = call(
            functools.partial(middle_kernel, cuts),
            "middle",
            (masks, head, warm, perm, conduct, wet, melt, cond, energy, surface, water, heat, *mine, *theirs),
            [column] * 5 + [(2,) + halo] * cuts + [(2,) + squeezed] * cuts,
            scratch=[room] * 5,
        )
        second.append(values[:5])
        later.append((values[5 : 5 + cuts], values[5 + cuts :]))
    leaving = lax.optimization_barrier([sent for _, sent in later])
    later = [(mine, [swap(cut, n, v) for cut, v in enumerate(sent)]) for (mine, _), sent in zip(later, leaving)]

    done = []
    for c in range(CHUNKS):
        conduct, stored, energy, surface = first[c][3], first[c][4], first[c][7], first[c][8]
        head, warm, wet, melt, cond = second[c]
        water, heat = call(team_kernel, "team", (masks, head, warm, cond), [column] * 2)
        mine, theirs = later[c]
        mine_k, theirs_k = sides[c]
        final = c == CHUNKS - 1
        done += call(
            functools.partial(last_kernel, c, cuts),
            "last",
            (
                masks, head, warm, conduct, stored, wet, melt, cond, energy, surface, water, heat,
                *mine, *theirs, *mine_k, *theirs_k, *(done if final else ()),
            ),
            [(TEAM, 2 * quarters if final else 4, OWN, cells)],
            scratch=[room] * 8 + [pltpu.VMEM((4, cells, LANES), F32)],
        )
    back = exchange(done[-1], n)
    return tuple(
        call(
            unpack_kernel,
            "unpack",
            (back,),
            [(cells, width)] * 2,
            scratch=[
                pltpu.VMEM((2, cells, width), F32),
                pltpu.SemaphoreType.DMA((2,)),
            ],
            out_specs=[hbm, hbm],
        )
    )


def solution(mesh):
    placed = (P(None, "cols"), P(None, "cols"), P(None, "cols"), P("cols"), P(), P(), P())
    return jax.shard_map(
        on_device,
        mesh=mesh,
        in_specs=placed,
        out_specs=(P(None, "cols"), P(None, "cols")),
        check_vma=False,
    )
```

```python
import functools

import jax
import jax.numpy as jnp
from jax import lax
from jax.experimental import pallas as pl
from jax.experimental.pallas import tpu as pltpu
from jax.sharding import PartitionSpec as P

SPAN = 256
PAIR_DEV = 4
LANES = 128
CHUNKS = SPAN // LANES
TEAM = 16
OWN = LANES // TEAM
SUB = 8
GROUPS = 2
WIDTH = 2 * LANES
ALL = GROUPS * WIDTH
EDGE = PAIR_DEV * OWN
VMEM_LIMIT = 32 * 1024 * 1024
DISTANCES = range(1, PAIR_DEV + 1)
F32 = jnp.float32


def cut_count(n):
    return min(n // TEAM - 1, 2)


def place(cut):
    team = lax.axis_index("cols") // TEAM
    return team, lax.rem(team, 2) == cut


def far_edge(above):
    return jnp.where(above, 0, PAIR_DEV - 1)


def sign_of(cut):
    return jnp.where(place(cut)[1], 1.0, -1.0).astype(F32)


def reciprocal(x):
    return pltpu.reciprocal(x, approx=True)


def sigmoid(x):
    return 0.5 + 0.5 * jnp.tanh(0.5 * x)


def passage(h, t, k):
    s = sigmoid(h)
    return k * (sigmoid(2.0 * t) * s * s + 0.02)


def lanes_of(g, b):
    return slice((g * 2 + b) * LANES, (g * 2 + b + 1) * LANES)


def following(value):
    first, second = value[:, :WIDTH], value[:, WIDTH:]
    return jnp.concatenate([second, pltpu.roll(first, SUB - 1, axis=0)], axis=1)


def preceding(value):
    first, second = value[:, :WIDTH], value[:, WIDTH:]
    return jnp.concatenate([pltpu.roll(second, 1, axis=0), first], axis=1)


def solve(steps, matrix, ratio, lead, value, update):
    c_prev = a_prev = d_prev = None
    for j in range(steps):
        above, main, below, source = matrix(j)
        if j == 0:
            r = reciprocal(main)
            a_prev = above * r
            d_prev = source * r
        else:
            r = reciprocal(main - above * c_prev)
            over = above * r
            a_prev = a_prev * over
            d_prev = source * r + d_prev * over
        c_prev = below * r
        ratio[j] = c_prev
        lead[j] = a_prev
        value[j] = d_prev
    last_c, last_a, last_d = c_prev, a_prev, d_prev
    p_first, a_first, d_first = ratio[steps - 2], lead[steps - 2], value[steps - 2]
    for j in range(steps - 3, -1, -1):
        c = ratio[j]
        p_first = c * p_first
        a_first = lead[j] + c * a_first
        d_first = value[j] + c * d_first
    g = reciprocal(1.0 - last_c * following(a_first))
    up = last_c * following(p_first) * g
    down = last_a * g
    own = (last_d + last_c * following(d_first)) * g
    step = 0
    while step < SUB:
        if step == 0:
            after, before = following, preceding
        else:
            after = functools.partial(pltpu.roll, shift=SUB - step, axis=0)
            before = functools.partial(pltpu.roll, shift=step, axis=0)
        g = reciprocal(1.0 - up * after(down) - down * before(up))
        own = (own + up * after(own) + down * before(own)) * g
        up = up * after(up) * g
        down = down * before(down) * g
        step = max(1, 2 * step)
    over = preceding(own)
    x = own
    update(steps - 1, x)
    for j in range(steps - 2, -1, -1):
        x = ratio[j] * x + (lead[j] * over + value[j])
        update(j, x)


def mask_rows(cuts):
    return 3 * PAIR_DEV + cuts * (2 * PAIR_DEV + 2)


def cut_row(cut):
    return 3 * PAIR_DEV + cut * (2 * PAIR_DEV + 2)


def mask_kernel(n, couplings, out):
    pair_rows = couplings[...]
    pairs = couplings.shape[1]
    pair_id = lax.broadcasted_iota(jnp.int32, (pairs, LANES), 0)
    lane = lax.broadcasted_iota(jnp.int32, (pairs, LANES), 1)
    lane_1 = lax.broadcasted_iota(jnp.int32, (SUB, LANES), 1)

    def chosen(dev, s):
        at = (pair_id == dev * PAIR_DEV + s - 1).astype(F32)
        found = jnp.dot(pair_rows, at, preferred_element_type=F32)
        return found[0:1], found[1:2]

    def put(row, value):
        out[row] = jnp.broadcast_to(value, (SUB, LANES))

    team = lax.axis_index("cols") // TEAM
    dev = team * TEAM + lane // OWN
    for s in DISTANCES:
        put(s - 1, chosen(dev, s)[0])
        put(PAIR_DEV + s - 1, chosen(dev - s, s)[1])
        put(2 * PAIR_DEV + s - 1, jnp.where(lane_1 // OWN + s < TEAM, 0.25, 0.0))
    block = lax.rem(lane_1 // EDGE, 2)
    edge = lax.rem(lane, EDGE) // OWN
    edge_1 = lax.rem(lane_1, EDGE) // OWN
    for cut in range(cut_count(n)):
        _, above = place(cut)
        row = cut_row(cut)
        partner = jnp.where(above, team + 1, team - 1)
        there = jnp.logical_and(partner >= 0, partner < n // TEAM)
        factor = jnp.where(there, 0.25, 0.0) * sign_of(cut)
        for s in DISTANCES:
            start = team * TEAM + jnp.where(above, TEAM - PAIR_DEV, -s)
            up, down = chosen(start + edge, s)
            mine = jnp.where(above, up, down)
            inward = jnp.where(above, edge_1, PAIR_DEV - 1 - edge_1)
            active = jnp.logical_and(inward >= PAIR_DEV - s, jnp.abs(mine - block.astype(F32)) < 0.5)
            put(row + s - 1, jnp.where(active, factor, 0.0))
            apart = jnp.where(above, PAIR_DEV - s, s - PAIR_DEV)
            up, down = chosen(start + edge + apart, s)
            theirs = jnp.where(edge_1 == far_edge(jnp.logical_not(above)), 0.0, jnp.where(above, down, up))
            put(row + PAIR_DEV + s - 1, jnp.where(jnp.abs(theirs - block.astype(F32)) < 0.5, 1.0, 0.0))
        outward = jnp.where(above, LANES - 1 - lane_1, lane_1)
        put(row + 2 * PAIR_DEV, jnp.where(outward < EDGE, 1.0, 0.0))
        single = jnp.logical_and(edge_1 == far_edge(above), block == 0)
        put(row + 2 * PAIR_DEV + 1, jnp.where(single, mine, 0.0))


def halo_parts():
    return lax.rem(lax.broadcasted_iota(jnp.int32, (SUB, LANES), 1) // OWN, 2 * PAIR_DEV)


def other_block(cut, couplings):
    team, above = place(cut)
    pair = (team * TEAM + jnp.where(above, TEAM - PAIR_DEV, -1)) * PAIR_DEV + PAIR_DEV - 1
    row = jnp.where(above, 0, 1)
    table = couplings[...].astype(F32)
    wanted = jnp.logical_and(
        lax.broadcasted_iota(jnp.int32, table.shape, 0) == row, lax.broadcasted_iota(jnp.int32, table.shape, 1) == pair
    )
    block = jnp.sum(jnp.sum(jnp.where(wanted, table, 0.0), axis=1, keepdims=True), axis=0, keepdims=True)
    single = jnp.where(halo_parts() == far_edge(above), 1.0, 0.0)
    return single * jnp.broadcast_to(block, (SUB, LANES))


def pack_kernel(
    cuts, suction, warmth, classes, surface, couplings, k_sat, heat_cond, out, consts, pair_rows,
    room, class_room, top, pairs, k_table, heat_table, in_sems,
):
    cells = out.shape[-1]
    quarters = 2 * CHUNKS
    into = []
    rooms = (room.at[0], room.at[1], class_room, top, pairs, k_table, heat_table)
    for f, field in enumerate((suction, warmth, classes, surface, couplings, k_sat, heat_cond)):
        into.append(pltpu.make_async_copy(field, rooms[f], in_sems.at[f]))
        into[-1].start()

    def put(slot, value):
        out[:, slot] = value.T.reshape(TEAM, OWN, cells)

    for f in range(3):
        into[f].wait()
        for q in range(quarters):
            lanes = slice(q * LANES, (q + 1) * LANES)
            put(f * quarters + q, class_room[:, lanes].astype(F32) if f == 2 else room[f, :, lanes])
    for copy in into[3:]:
        copy.wait()
    kinds = k_sat.shape[1]
    for c in range(kinds):
        consts[c] = jnp.broadcast_to(k_table[0:1, c : c + 1], (SUB, LANES))
        consts[kinds + c] = jnp.broadcast_to(heat_table[0:1, c : c + 1], (SUB, LANES))
    for cut in range(cuts):
        consts[2 * kinds + cut] = other_block(cut, pairs)
    pair_rows[...] = pairs[...].astype(F32)
    rows = [top[0:1, q * LANES : (q + 1) * LANES] for q in range(quarters)]
    put(3 * quarters, jnp.concatenate(rows + [jnp.zeros((cells - quarters, LANES), F32)], axis=0))


def unpack_kernel(got, suction, warmth, room, sems):
    cells = got.shape[-1]
    quarters = 2 * CHUNKS
    sent = []
    for f, out in enumerate((suction, warmth)):
        for q in range(quarters):
            room[f, :, q * LANES : (q + 1) * LANES] = got[:, f * quarters + q].reshape(LANES, cells).T
        sent.append(pltpu.make_async_copy(room.at[f], out, sems.at[f]))
        sent[-1].start()
    for copy in sent:
        copy.wait()


def edge_shift(cut, m):
    return lax.rem(EDGE * m + jnp.where(place(cut)[1], EDGE, 0), LANES)


def halo_of(cut, value):
    part = lax.broadcasted_iota(jnp.int32, (SUB, LANES), 1) // EDGE
    packed = None
    for m in range(2 * GROUPS):
        moved = pltpu.roll(value[:, m * LANES : (m + 1) * LANES], edge_shift(cut, m), axis=1)
        packed = moved if m == 0 else jnp.where(part == m, moved, packed)
    return packed


def pieces(above):
    spare = PAIR_DEV + far_edge(above)
    parts = [j if j < PAIR_DEV else j + jnp.where(above, 1, 0) for j in range(2 * PAIR_DEV - 1)]
    return [(part, lax.rem((spare - part) * OWN + LANES, LANES)) for part in parts]


def squeeze(cut, other, values):
    above = place(cut)[1]
    values = [jnp.where(other, pltpu.roll(v, LANES - EDGE, axis=1), v) for v in values]
    spare = halo_parts() == PAIR_DEV + far_edge(above)
    return [
        jnp.where(spare, pltpu.roll(values[-1], shift, axis=1), v)
        for v, (_, shift) in zip(values[:-1], pieces(above))
    ]


def unsqueeze(cut, values):
    part = halo_parts()
    last = values[0]
    for v, (piece, shift) in zip(values, pieces(jnp.logical_not(place(cut)[1]))):
        last = jnp.where(part == piece, pltpu.roll(v, lax.rem(LANES - shift, LANES), axis=1), last)
    return list(values) + [last]


def edge_kernel(chunk, cuts, got, consts, *refs):
    halos, sent, load = refs[:cuts], refs[cuts:-1], refs[-1]
    cells = got.shape[-1]
    steps = halos[0].shape[1]
    stride = steps * GROUPS
    second = lax.broadcasted_iota(jnp.int32, (SUB, LANES), 1) >= 2 * EDGE
    for cut in range(cuts):
        start = jnp.where(place(cut)[1], TEAM - PAIR_DEV, 0)
        for f in range(3):
            rows = [
                got[pl.ds(start, PAIR_DEV), (f * 2 + b) * CHUNKS + chunk].reshape(EDGE, cells) for b in range(2)
            ]
            load[cut * 3 + f] = jnp.concatenate(rows * GROUPS, axis=0).T
    kinds = (consts.shape[0] - cuts) // 2
    table = [consts[c] for c in range(kinds)]
    for cut in range(cuts):
        other = consts[2 * kinds + cut] > 0.5
        for f in range(3):
            values = []
            for j in range(steps):
                v = jnp.where(
                    second,
                    load[cut * 3 + f, pl.ds(steps + j, SUB, stride=stride), :],
                    load[cut * 3 + f, pl.ds(j, SUB, stride=stride), :],
                )
                if f == 2:
                    k = table[0]
                    for c in range(1, len(table)):
                        k = jnp.where(v >= c, table[c], k)
                    v = k
                halos[cut][f, j] = v
                values.append(v)
            for j, v in enumerate(squeeze(cut, other, values)):
                sent[cut][f, j] = v


def first_kernel(
    chunk, kinds, got, consts, head, warm, perm, conduct, wet, energy, top, load
):
    cells = got.shape[-1]
    steps = head.shape[0]
    stride = steps * GROUPS

    for field in range(3):
        for b in range(2):
            load[field * 2 + b] = got[:, (field * 2 + b) * CHUNKS + chunk].reshape(LANES, cells).T
    surface = got[:, 6 * CHUNKS].reshape(LANES, cells).T[0:SUB]
    rows = [surface[b * CHUNKS + chunk : b * CHUNKS + chunk + 1] for b in range(2)]
    top[...] = jnp.concatenate(rows * GROUPS, axis=1)

    def fetch(field, j):
        parts = [
            load[field * 2 + b, pl.ds(g * steps + j, SUB, stride=stride), :]
            for g in range(GROUPS)
            for b in range(2)
        ]
        return jnp.concatenate(parts, axis=1)

    def pick(v):
        parts = []
        for m in range(2 * GROUPS):
            part = v[:, m * LANES : (m + 1) * LANES]
            k, lam = consts[0], consts[kinds]
            for c in range(1, kinds):
                here = part >= c
                k = jnp.where(here, consts[c], k)
                lam = jnp.where(here, consts[kinds + c], lam)
            parts.append((k, lam))
        return [jnp.concatenate(side, axis=1) for side in zip(*parts)]

    for j in range(steps):
        h, t, v = [fetch(field, j) for field in range(3)]
        k, lam = pick(v)
        s, f = sigmoid(h), sigmoid(2.0 * t)
        m = 0.05 + 0.4 * s
        head[j], warm[j], perm[j], conduct[j] = h, t, k, lam
        wet[j] = s
        energy[j] = (1.0 + 2.0 * m) * t + 2.0 * m * f


def team_kernel(masks, head, warm, perm, wet, melt, cond, water, heat):
    steps = head.shape[0]
    upper = [masks[s - 1] > 0.5 for s in DISTANCES]
    lower = [masks[PAIR_DEV + s - 1] > 0.5 for s in DISTANCES]

    def step(j, _):
        for g in range(GROUPS):
            l0, l1 = lanes_of(g, 0), lanes_of(g, 1)
            h0, h1 = head[j, :, l0], head[j, :, l1]
            t0, t1 = warm[j, :, l0], warm[j, :, l1]
            conductivity = []
            for t, lanes in ((t0, l0), (t1, l1)):
                s, f = wet[j, :, lanes], sigmoid(2.0 * t)
                melt[j, :, lanes] = f
                conductivity.append(perm[j, :, lanes] * (f * s * s + 0.02))
                cond[j, :, lanes] = conductivity[-1]
            c0, c1 = conductivity
            total = None
            for s in DISTANCES:
                up, low = upper[s - 1], lower[s - 1]
                back = LANES - s * OWN
                h_low = pltpu.roll(jnp.where(low, h1, h0), back, axis=1)
                t_low = pltpu.roll(jnp.where(low, t1, t0), back, axis=1)
                c_low = pltpu.roll(jnp.where(low, c1, c0), back, axis=1)
                flow = (
                    masks[2 * PAIR_DEV + s - 1]
                    * (jnp.where(up, c1, c0) + c_low)
                    * (jnp.where(up, h1, h0) - h_low + 0.5)
                )
                carried = flow * jnp.where(flow > 0.0, jnp.where(up, t1, t0), t_low)
                flow_in = pltpu.roll(flow, s * OWN, axis=1)
                carried_in = pltpu.roll(carried, s * OWN, axis=1)
                part = (
                    flow_in - flow,
                    jnp.where(low, flow_in, 0.0) - jnp.where(up, flow, 0.0),
                    carried_in - carried,
                    jnp.where(low, carried_in, 0.0) - jnp.where(up, carried, 0.0),
                )
                total = part if total is None else [a + b for a, b in zip(total, part)]
            water[j, :, l0] = total[0] - total[1]
            water[j, :, l1] = total[1]
            heat[j, :, l0] = 2.0 * (total[2] - total[3])
            heat[j, :, l1] = 2.0 * total[3]

    lax.fori_loop(0, steps, step, None, unroll=2)


def cross_flows(cut, masks, mine, theirs):
    row = cut_row(cut)
    sign = sign_of(cut)
    above = place(cut)[1]
    lane = lax.broadcasted_iota(jnp.int32, (SUB, LANES), 1)
    first_block = lax.rem(lane, 2 * EDGE) < EDGE
    h, t, k = mine
    c = passage(h, t, k)
    far = [theirs[0], theirs[1], passage(*theirs)]
    other = [
        jnp.where(first_block, pltpu.roll(v, LANES - EDGE, axis=1), pltpu.roll(v, EDGE, axis=1)) for v in far
    ]
    water = heat = jnp.zeros((SUB, LANES), F32)
    for s in DISTANCES:
        same = masks[row + PAIR_DEV + s - 1] > 0.5
        picked = [jnp.where(same, a, b) for a, b in zip(far, other)]
        apart = (PAIR_DEV - s) * OWN
        if apart:
            shift = jnp.where(above, apart, LANES - apart)
            picked = [pltpu.roll(v, shift, axis=1) for v in picked]
        h_far, t_far, c_far = picked
        flow = masks[row + s - 1] * (c + c_far) * (sign * (h - h_far) + 0.5)
        water = water - flow
        heat = heat - flow * jnp.where(flow > 0.0, t, t_far)
    return water, heat


def advance(steps, cuts, masks, head, warm, conduct, stored, energy, wet, melt, cond, water, heat, top,
            mine, theirs, new_head, new_warm, new_wet, inflow, warm_inflow, ratio, lead, value, finish):
    for j in range(steps):
        w_parts = [water[j, :, m * LANES : (m + 1) * LANES] for m in range(2 * GROUPS)]
        q_parts = [heat[j, :, m * LANES : (m + 1) * LANES] for m in range(2 * GROUPS)]
        for cut in range(cuts):
            beside = masks[cut_row(cut) + 2 * PAIR_DEV]
            w_far, q_far = cross_flows(cut, masks, mine(cut, j), theirs(cut, j))
            for m in range(2 * GROUPS):
                shift = lax.rem(LANES - edge_shift(cut, m), LANES)
                w_parts[m] = w_parts[m] + beside * pltpu.roll(w_far, shift, axis=1)
                q_parts[m] = q_parts[m] + 2.0 * beside * pltpu.roll(q_far, shift, axis=1)
        for m in range(2 * GROUPS):
            inflow[j, :, m * LANES : (m + 1) * LANES] = w_parts[m]
            warm_inflow[j, :, m * LANES : (m + 1) * LANES] = q_parts[m]

    part = lax.broadcasted_iota(jnp.int32, (SUB, ALL), 0)
    group = lax.broadcasted_iota(jnp.int32, (SUB, ALL), 1) // WIDTH
    first_part = jnp.logical_and(part == 0, group == 0)
    last_part = jnp.logical_and(part == SUB - 1, group == GROUPS - 1)

    def faces(fields, potential):
        face_of, rise_of = [], []
        for j in range(steps):
            if j + 1 < steps:
                c_next, v_next = fields[j + 1], potential[j + 1]
                face = 0.5 * (fields[j] + c_next)
            else:
                c_next, v_next = following(fields[0]), following(potential[0])
                face = jnp.where(last_part, 0.0, 0.5 * (fields[j] + c_next))
            face_of.append(face)
            rise_of.append(v_next - potential[j])
        return face_of, rise_of

    k_face, rise = faces([cond[j] for j in range(steps)], head)
    k_top = jnp.where(first_part, 0.0, preceding(k_face[-1]))
    q_face = [k * (1.0 - d) for k, d in zip(k_face, rise)]
    q_top = jnp.where(first_part, 0.0, preceding(q_face[-1]))

    def water_matrix(j):
        above = k_top if j == 0 else k_face[j - 1]
        into = q_top if j == 0 else q_face[j - 1]
        s = wet[j]
        main = 0.8 * s * (1.0 - s) + 0.02 + above + k_face[j]
        source = inflow[j] + into - q_face[j] - 0.8 * (s - stored[j])
        return above, main, k_face[j], source

    def water_done(j, x):
        h = head[j] + x
        new_head[j] = h
        new_wet[j] = sigmoid(h)

    solve(steps, water_matrix, ratio, lead, value, water_done)

    l_cell = [conduct[j] * (1.5 - 0.5 * melt[j]) for j in range(steps)]
    l_face, rise = faces(l_cell, warm)
    l_top = jnp.where(first_part, 0.0, preceding(l_face[-1]))
    g_face = [l * d for l, d in zip(l_face, rise)]
    g_top = jnp.where(first_part, 0.0, preceding(g_face[-1]))
    surface_lam = jnp.where(first_part, 2.0 * l_cell[0], 0.0)

    def heat_matrix(j):
        above = l_top if j == 0 else l_face[j - 1]
        out_of = g_top if j == 0 else g_face[j - 1]
        t, f = warm[j], melt[j]
        m2 = 0.1 + 0.8 * new_wet[j]
        now = (1.0 + m2) * t + m2 * f
        main = 2.0 + 2.0 * m2 * (1.0 + 2.0 * f * (1.0 - f)) + above + l_face[j]
        source = warm_inflow[j] - out_of + g_face[j] - 2.0 * (now - energy[j])
        if j == 0:
            main = main + surface_lam
            source = source + surface_lam * (top[...] - t)
        return above, main, l_face[j], source

    def heat_done(j, x):
        t = warm[j] + x
        new_warm[j] = t
        finish(j, t)

    solve(steps, heat_matrix, ratio, lead, value, heat_done)


def middle_kernel(cuts, *refs):
    masks, head, warm, conduct, wet, melt, cond, energy, top, water, heat = refs[:11]
    own, far = refs[11 : 11 + cuts], refs[11 + cuts : 11 + 2 * cuts]
    new_head, new_warm, new_wet = refs[11 + 2 * cuts : 14 + 2 * cuts]
    halos, sent = refs[14 + 2 * cuts : 14 + 3 * cuts], refs[14 + 3 * cuts : 14 + 4 * cuts]
    inflow, warm_inflow, ratio, lead, value = refs[14 + 4 * cuts :]
    steps = head.shape[0]
    packed = {}

    def finish(j, t):
        for cut in range(cuts):
            for i, v in enumerate((new_head[j], t)):
                packed[cut, i, j] = halo_of(cut, v)
                halos[cut][i, j] = packed[cut, i, j]

    theirs = [[unsqueeze(cut, [far[cut][i, j] for j in range(steps - 1)]) for i in range(3)] for cut in range(cuts)]
    advance(
        steps, cuts, masks, head, warm, conduct, wet, energy, wet, melt, cond, water, heat, top,
        lambda cut, j: [own[cut][i, j] for i in range(3)],
        lambda cut, j: [theirs[cut][i][j] for i in range(3)],
        new_head, new_warm, new_wet, inflow, warm_inflow, ratio, lead, value, finish,
    )
    for cut in range(cuts):
        for i in range(2):
            other = masks[cut_row(cut) + 2 * PAIR_DEV + 1] > 0.5
            values = squeeze(cut, other, [packed[cut, i, j] for j in range(steps)])
            for j, v in enumerate(values):
                sent[cut][i, j] = v


def last_kernel(chunk, cuts, *refs):
    masks, head, warm, conduct, stored, wet, melt, cond, energy, top, water, heat = refs[:12]
    own, far = refs[12 : 12 + cuts], refs[12 + cuts : 12 + 2 * cuts]
    own_k, far_k = refs[12 + 2 * cuts : 12 + 3 * cuts], refs[12 + 3 * cuts : 12 + 4 * cuts]
    others = refs[12 + 4 * cuts : -10]
    out, new_head, new_warm, new_wet, inflow, warm_inflow, ratio, lead, value, load = refs[-10:]
    steps = head.shape[0]
    cells = steps * GROUPS * SUB
    stride = steps * GROUPS
    theirs = [
        [unsqueeze(cut, [source[i, j] for j in range(steps - 1)]) for source, i in ((far[cut], 0), (far[cut], 1), (far_k[cut], 2))]
        for cut in range(cuts)
    ]
    advance(
        steps, cuts, masks, head, warm, conduct, stored, energy, wet, melt, cond, water, heat, top,
        lambda cut, j: [own[cut][0, j], own[cut][1, j], own_k[cut][2, j]],
        lambda cut, j: [theirs[cut][i][j] for i in range(3)],
        new_head, new_warm, new_wet, inflow, warm_inflow, ratio, lead, value, lambda j, t: None,
    )
    final = chunk == CHUNKS - 1
    for f, field in enumerate((new_head, new_warm)):
        for b in range(2):
            slot = f * 2 + b
            for j in range(steps):
                for g in range(GROUPS):
                    load[slot, pl.ds(g * steps + j, SUB, stride=stride), :] = field[j, :, lanes_of(g, b)]
            turned = load[slot].T.reshape(TEAM, OWN, cells)
            if final:
                out[:, slot * CHUNKS + chunk] = turned
                for c, other in enumerate(others):
                    out[:, slot * CHUNKS + c] = other[:, slot]
            else:
                out[:, slot] = turned


def whole(memory=pltpu.VMEM):
    return pl.BlockSpec(memory_space=memory)


def call(kernel, name, args, outs, scratch=(), specs=None, out_specs=None, limit=VMEM_LIMIT, work=2_000_000):
    return pl.pallas_call(
        kernel,
        out_shape=[jax.ShapeDtypeStruct(shape, F32) for shape in outs],
        in_specs=specs or [whole()] * len(args),
        out_specs=out_specs or [whole()] * len(outs),
        scratch_shapes=scratch,
        compiler_params=pltpu.CompilerParams(vmem_limit_bytes=limit),
        cost_estimate=pl.CostEstimate(flops=work, bytes_accessed=work, transcendentals=0),
        name=name,
    )(*args)


def exchange(tiles, n):
    teams = [list(range(start, start + TEAM)) for start in range(0, n, TEAM)]
    return lax.all_to_all(
        tiles, "cols", split_axis=0, concat_axis=0, tiled=True, axis_index_groups=teams
    )


def swap(cut, n, value):
    pairs = []
    for team in range(cut, n // TEAM - 1, 2):
        for i in range(team * TEAM, (team + 1) * TEAM):
            pairs += [(i, i + TEAM), (i + TEAM, i)]
    return lax.ppermute(value, "cols", pairs)


def on_device(suction, warmth, classes, top, couplings, k_sat, heat_cond):
    n = lax.axis_size("cols")
    cells, width = suction.shape
    steps = cells // (SUB * GROUPS)
    quarters = width // LANES
    cuts = cut_count(n)
    column = (steps, SUB, ALL)
    halo = (steps, SUB, LANES)
    squeezed = (steps - 1, SUB, LANES)
    room = pltpu.VMEM(column, F32)
    hbm = whole(pltpu.HBM)

    arguments = (suction, warmth, classes, top.reshape(1, width), couplings, k_sat.reshape(1, -1), heat_cond.reshape(1, -1))
    kinds = k_sat.shape[0]
    packed, consts, pair_rows = call(
        functools.partial(pack_kernel, cuts),
        "pack",
        [pltpu.with_memory_space_constraint(v, pltpu.HBM) for v in arguments],
        [(TEAM, 3 * quarters + 1, OWN, cells), (2 * kinds + cuts, SUB, LANES), couplings.shape],
        scratch=[
            pltpu.VMEM((2, cells, width), F32),
            pltpu.VMEM((cells, width), classes.dtype),
            pltpu.VMEM((1, width), F32),
            pltpu.VMEM(couplings.shape, couplings.dtype),
            pltpu.VMEM((1, kinds), F32),
            pltpu.VMEM((1, kinds), F32),
            pltpu.SemaphoreType.DMA((7,)),
        ],
        specs=[hbm] * 7,
    )
    masks = call(
        functools.partial(mask_kernel, n), "masks", (pair_rows,), [(mask_rows(cuts), SUB, LANES)]
    )[0]
    got = exchange(packed, n)

    edges = [
        call(
            functools.partial(edge_kernel, c, cuts),
            "edges",
            (got, consts),
            [(3,) + halo] * cuts + [(3,) + squeezed] * cuts,
            scratch=[pltpu.VMEM((3 * cuts, cells, LANES), F32)],
        )
        for c in range(CHUNKS)
    ]
    first = [
        call(
            functools.partial(first_kernel, c, kinds),
            "first",
            (got, consts),
            [column] * 6 + [(1, ALL)],
            scratch=[pltpu.VMEM((6, cells, LANES), F32)],
        )
        for c in range(CHUNKS)
    ]
    flows, sides = [], []
    for c in range(CHUNKS):
        mine, sent = edges[c][:cuts], edges[c][cuts:]
        sides.append((mine, [swap(cut, n, v) for cut, v in enumerate(sent)]))
        head, warm, perm, conduct, wet, energy, surface = first[c]
        flows.append(call(team_kernel, "team", (masks, head, warm, perm, wet), [column] * 4))

    second, later = [], []
    for c in range(CHUNKS):
        head, warm, perm, conduct, wet, energy, surface = first[c]
        melt, cond, water, heat = flows[c]
        mine, theirs = sides[c]
        values = call(
            functools.partial(middle_kernel, cuts),
            "middle",
            (masks, head, warm, conduct, wet, melt, cond, energy, surface, water, heat, *mine, *theirs),
            [column] * 3 + [(2,) + halo] * cuts + [(2,) + squeezed] * cuts,
            scratch=[room] * 5,
        )
        second.append(values[:3])
        mine, sent = values[3 : 3 + cuts], values[3 + cuts :]
        later.append((mine, [swap(cut, n, v) for cut, v in enumerate(sent)]))

    done = []
    for c in range(CHUNKS):
        _, _, perm, conduct, stored, energy, surface = first[c]
        head, warm, wet = second[c]
        melt, cond, water, heat = call(team_kernel, "team", (masks, head, warm, perm, wet), [column] * 4)
        mine, theirs = later[c]
        mine_k, theirs_k = sides[c]
        final = c == CHUNKS - 1
        done += call(
            functools.partial(last_kernel, c, cuts),
            "last",
            (
                masks, head, warm, conduct, stored, wet, melt, cond, energy, surface, water, heat,
                *mine, *theirs, *mine_k, *theirs_k, *(done if final else ()),
            ),
            [(TEAM, 2 * quarters if final else 4, OWN, cells)],
            scratch=[room] * 8 + [pltpu.VMEM((4, cells, LANES), F32)],
        )
    back = exchange(done[-1], n)
    return tuple(
        call(
            unpack_kernel,
            "unpack",
            (back,),
            [(cells, width)] * 2,
            scratch=[
                pltpu.VMEM((2, cells, width), F32),
                pltpu.SemaphoreType.DMA((2,)),
            ],
            out_specs=[hbm, hbm],
        )
    )


def solution(mesh):
    placed = (P(None, "cols"), P(None, "cols"), P(None, "cols"), P("cols"), P(), P(), P())
    return jax.shard_map(
        on_device,
        mesh=mesh,
        in_specs=placed,
        out_specs=(P(None, "cols"), P(None, "cols")),
        check_vma=False,
    )
```

```python
import functools

import jax
import jax.numpy as jnp
from jax import lax
from jax.experimental import pallas as pl
from jax.experimental.pallas import tpu as pltpu
from jax.sharding import PartitionSpec as P

SPAN = 256
PAIR_DEV = 4
LANES = 128
CHUNKS = SPAN // LANES
TEAM = 16
OWN = LANES // TEAM
SUB = 8
GROUPS = 2
WIDTH = 2 * LANES
ALL = GROUPS * WIDTH
EDGE = PAIR_DEV * OWN
VMEM_LIMIT = 32 * 1024 * 1024
DISTANCES = range(1, PAIR_DEV + 1)
F32 = jnp.float32


def cut_count(n):
    return min(n // TEAM - 1, 2)


def place(cut):
    team = lax.axis_index("cols") // TEAM
    return team, lax.rem(team, 2) == cut


def far_edge(above):
    return jnp.where(above, 0, PAIR_DEV - 1)


def sign_of(cut):
    return jnp.where(place(cut)[1], 1.0, -1.0).astype(F32)


def reciprocal(x):
    return pltpu.reciprocal(x, approx=True)


def sigmoid(x):
    return 0.5 + 0.5 * jnp.tanh(0.5 * x)


def passage(h, t, k):
    s = sigmoid(h)
    return k * (sigmoid(2.0 * t) * s * s + 0.02)


def lanes_of(g, b):
    return slice((g * 2 + b) * LANES, (g * 2 + b + 1) * LANES)


def following(value):
    first, second = value[:, :WIDTH], value[:, WIDTH:]
    return jnp.concatenate([second, pltpu.roll(first, SUB - 1, axis=0)], axis=1)


def preceding(value):
    first, second = value[:, :WIDTH], value[:, WIDTH:]
    return jnp.concatenate([pltpu.roll(second, 1, axis=0), first], axis=1)


def solve(steps, matrix, ratio, lead, value, update):
    c_prev = a_prev = d_prev = None
    for j in range(steps):
        above, main, below, source = matrix(j)
        if j == 0:
            r = reciprocal(main)
            a_prev = above * r
            d_prev = source * r
        else:
            r = reciprocal(main - above * c_prev)
            over = above * r
            a_prev = a_prev * over
            d_prev = source * r + d_prev * over
        c_prev = below * r
        ratio[j] = c_prev
        lead[j] = a_prev
        value[j] = d_prev
    last_c, last_a, last_d = c_prev, a_prev, d_prev
    p_first, a_first, d_first = ratio[steps - 2], lead[steps - 2], value[steps - 2]
    for j in range(steps - 3, -1, -1):
        c = ratio[j]
        p_first = c * p_first
        a_first = lead[j] + c * a_first
        d_first = value[j] + c * d_first
    g = reciprocal(1.0 - last_c * following(a_first))
    up = last_c * following(p_first) * g
    down = last_a * g
    own = (last_d + last_c * following(d_first)) * g
    step = 0
    while step < SUB:
        if step == 0:
            after, before = following, preceding
        else:
            after = functools.partial(pltpu.roll, shift=SUB - step, axis=0)
            before = functools.partial(pltpu.roll, shift=step, axis=0)
        g = reciprocal(1.0 - up * after(down) - down * before(up))
        own = (own + up * after(own) + down * before(own)) * g
        up = up * after(up) * g
        down = down * before(down) * g
        step = max(1, 2 * step)
    over = preceding(own)
    x = own
    update(steps - 1, x)
    for j in range(steps - 2, -1, -1):
        x = ratio[j] * x + (lead[j] * over + value[j])
        update(j, x)


def mask_rows(cuts):
    return 3 * PAIR_DEV + cuts * (2 * PAIR_DEV + 2)


def cut_row(cut):
    return 3 * PAIR_DEV + cut * (2 * PAIR_DEV + 2)


def mask_kernel(n, couplings, out):
    pair_rows = couplings[...].astype(F32)
    pairs = couplings.shape[1]
    pair_id = lax.broadcasted_iota(jnp.int32, (pairs, LANES), 0)
    lane = lax.broadcasted_iota(jnp.int32, (pairs, LANES), 1)
    lane_1 = lax.broadcasted_iota(jnp.int32, (SUB, LANES), 1)

    def chosen(dev, s):
        at = (pair_id == dev * PAIR_DEV + s - 1).astype(F32)
        found = jnp.dot(pair_rows, at, preferred_element_type=F32)
        return found[0:1], found[1:2]

    def put(row, value):
        out[row] = jnp.broadcast_to(value, (SUB, LANES))

    team = lax.axis_index("cols") // TEAM
    dev = team * TEAM + lane // OWN
    for s in DISTANCES:
        put(s - 1, chosen(dev, s)[0])
        put(PAIR_DEV + s - 1, chosen(dev - s, s)[1])
        put(2 * PAIR_DEV + s - 1, jnp.where(lane_1 // OWN + s < TEAM, 0.25, 0.0))
    block = lax.rem(lane_1 // EDGE, 2)
    edge = lax.rem(lane, EDGE) // OWN
    edge_1 = lax.rem(lane_1, EDGE) // OWN
    for cut in range(cut_count(n)):
        _, above = place(cut)
        row = cut_row(cut)
        partner = jnp.where(above, team + 1, team - 1)
        there = jnp.logical_and(partner >= 0, partner < n // TEAM)
        factor = jnp.where(there, 0.25, 0.0) * sign_of(cut)
        for s in DISTANCES:
            start = team * TEAM + jnp.where(above, TEAM - PAIR_DEV, -s)
            up, down = chosen(start + edge, s)
            mine = jnp.where(above, up, down)
            inward = jnp.where(above, edge_1, PAIR_DEV - 1 - edge_1)
            active = jnp.logical_and(inward >= PAIR_DEV - s, jnp.abs(mine - block.astype(F32)) < 0.5)
            put(row + s - 1, jnp.where(active, factor, 0.0))
            apart = jnp.where(above, PAIR_DEV - s, s - PAIR_DEV)
            up, down = chosen(start + edge + apart, s)
            theirs = jnp.where(edge_1 == far_edge(jnp.logical_not(above)), 0.0, jnp.where(above, down, up))
            put(row + PAIR_DEV + s - 1, jnp.where(jnp.abs(theirs - block.astype(F32)) < 0.5, 1.0, 0.0))
        outward = jnp.where(above, LANES - 1 - lane_1, lane_1)
        put(row + 2 * PAIR_DEV, jnp.where(outward < EDGE, 1.0, 0.0))
        single = jnp.logical_and(edge_1 == far_edge(above), block == 0)
        put(row + 2 * PAIR_DEV + 1, jnp.where(single, mine, 0.0))


def halo_parts():
    return lax.rem(lax.broadcasted_iota(jnp.int32, (SUB, LANES), 1) // OWN, 2 * PAIR_DEV)


def other_block(cut, couplings):
    team, above = place(cut)
    pair = (team * TEAM + jnp.where(above, TEAM - PAIR_DEV, -1)) * PAIR_DEV + PAIR_DEV - 1
    row = jnp.where(above, 0, 1)
    table = couplings[...].astype(F32)
    wanted = jnp.logical_and(
        lax.broadcasted_iota(jnp.int32, table.shape, 0) == row, lax.broadcasted_iota(jnp.int32, table.shape, 1) == pair
    )
    block = jnp.sum(jnp.sum(jnp.where(wanted, table, 0.0), axis=1, keepdims=True), axis=0, keepdims=True)
    single = jnp.where(halo_parts() == far_edge(above), 1.0, 0.0)
    return single * jnp.broadcast_to(block, (SUB, LANES))


def pack_kernel(
    cuts, suction, warmth, classes, surface, couplings, k_sat, out, consts, room, class_room, top, pairs, table, in_sems
):
    cells = out.shape[-1]
    quarters = 2 * CHUNKS
    into = []
    rooms = (room.at[0], room.at[1], class_room, top, pairs, table)
    for f, field in enumerate((suction, warmth, classes, surface, couplings, k_sat)):
        into.append(pltpu.make_async_copy(field, rooms[f], in_sems.at[f]))
        into[-1].start()

    def put(slot, value):
        out[:, slot] = value.T.reshape(TEAM, OWN, cells)

    for f in range(3):
        into[f].wait()
        for q in range(quarters):
            lanes = slice(q * LANES, (q + 1) * LANES)
            put(f * quarters + q, class_room[:, lanes].astype(F32) if f == 2 else room[f, :, lanes])
    for copy in into[3:]:
        copy.wait()
    for c in range(k_sat.shape[1]):
        consts[c] = jnp.broadcast_to(table[0:1, c : c + 1], (SUB, LANES))
    for cut in range(cuts):
        consts[k_sat.shape[1] + cut] = other_block(cut, pairs)
    rows = [top[0:1, q * LANES : (q + 1) * LANES] for q in range(quarters)]
    put(3 * quarters, jnp.concatenate(rows + [jnp.zeros((cells - quarters, LANES), F32)], axis=0))


def unpack_kernel(got, suction, warmth, room, sems):
    cells = got.shape[-1]
    quarters = 2 * CHUNKS
    sent = []
    for f, out in enumerate((suction, warmth)):
        for q in range(quarters):
            room[f, :, q * LANES : (q + 1) * LANES] = got[:, f * quarters + q].reshape(LANES, cells).T
        sent.append(pltpu.make_async_copy(room.at[f], out, sems.at[f]))
        sent[-1].start()
    for copy in sent:
        copy.wait()


def edge_shift(cut, m):
    return lax.rem(EDGE * m + jnp.where(place(cut)[1], EDGE, 0), LANES)


def halo_of(cut, value):
    part = lax.broadcasted_iota(jnp.int32, (SUB, LANES), 1) // EDGE
    packed = None
    for m in range(2 * GROUPS):
        moved = pltpu.roll(value[:, m * LANES : (m + 1) * LANES], edge_shift(cut, m), axis=1)
        packed = moved if m == 0 else jnp.where(part == m, moved, packed)
    return packed


def pieces(above):
    spare = PAIR_DEV + far_edge(above)
    parts = [j if j < PAIR_DEV else j + jnp.where(above, 1, 0) for j in range(2 * PAIR_DEV - 1)]
    return [(part, lax.rem((spare - part) * OWN + LANES, LANES)) for part in parts]


def squeeze(cut, other, values):
    above = place(cut)[1]
    values = [jnp.where(other, pltpu.roll(v, LANES - EDGE, axis=1), v) for v in values]
    spare = halo_parts() == PAIR_DEV + far_edge(above)
    return [
        jnp.where(spare, pltpu.roll(values[-1], shift, axis=1), v)
        for v, (_, shift) in zip(values[:-1], pieces(above))
    ]


def unsqueeze(cut, values):
    part = halo_parts()
    last = values[0]
    for v, (piece, shift) in zip(values, pieces(jnp.logical_not(place(cut)[1]))):
        last = jnp.where(part == piece, pltpu.roll(v, lax.rem(LANES - shift, LANES), axis=1), last)
    return list(values) + [last]


def edge_kernel(chunk, cuts, got, consts, *refs):
    halos, sent, load = refs[:cuts], refs[cuts:-1], refs[-1]
    cells = got.shape[-1]
    steps = halos[0].shape[1]
    stride = steps * GROUPS
    second = lax.broadcasted_iota(jnp.int32, (SUB, LANES), 1) >= 2 * EDGE
    for cut in range(cuts):
        start = jnp.where(place(cut)[1], TEAM - PAIR_DEV, 0)
        for f in range(3):
            rows = [
                got[pl.ds(start, PAIR_DEV), (f * 2 + b) * CHUNKS + chunk].reshape(EDGE, cells) for b in range(2)
            ]
            load[cut * 3 + f] = jnp.concatenate(rows * GROUPS, axis=0).T
    classes = consts.shape[0] - cuts
    table = [consts[c] for c in range(classes)]
    for cut in range(cuts):
        other = consts[classes + cut] > 0.5
        for f in range(3):
            values = []
            for j in range(steps):
                v = jnp.where(
                    second,
                    load[cut * 3 + f, pl.ds(steps + j, SUB, stride=stride), :],
                    load[cut * 3 + f, pl.ds(j, SUB, stride=stride), :],
                )
                if f == 2:
                    k = table[0]
                    for c in range(1, len(table)):
                        k = jnp.where(v >= c, table[c], k)
                    v = k
                halos[cut][f, j] = v
                values.append(v)
            for j, v in enumerate(squeeze(cut, other, values)):
                sent[cut][f, j] = v


def first_kernel(
    chunk, got, k_sat, heat_cond, head, warm, perm, conduct, wet, melt, cond, energy, top, load
):
    cells = got.shape[-1]
    steps = head.shape[0]
    stride = steps * GROUPS

    for field in range(3):
        for b in range(2):
            load[field * 2 + b] = got[:, (field * 2 + b) * CHUNKS + chunk].reshape(LANES, cells).T
    surface = got[:, 6 * CHUNKS].reshape(LANES, cells).T[0:SUB]
    rows = [surface[b * CHUNKS + chunk : b * CHUNKS + chunk + 1] for b in range(2)]
    top[...] = jnp.concatenate(rows * GROUPS, axis=1)

    def fetch(field, j):
        parts = [
            load[field * 2 + b, pl.ds(g * steps + j, SUB, stride=stride), :]
            for g in range(GROUPS)
            for b in range(2)
        ]
        return jnp.concatenate(parts, axis=1)

    for j in range(steps):
        h, t, v = [fetch(field, j) for field in range(3)]
        k = jnp.full_like(v, k_sat[0])
        lam = jnp.full_like(v, heat_cond[0])
        for c in range(1, k_sat.shape[0]):
            here = v >= c
            k = jnp.where(here, k_sat[c], k)
            lam = jnp.where(here, heat_cond[c], lam)
        s, f = sigmoid(h), sigmoid(2.0 * t)
        m = 0.05 + 0.4 * s
        head[j], warm[j], perm[j], conduct[j] = h, t, k, lam
        wet[j] = s
        melt[j] = f
        cond[j] = k * (f * s * s + 0.02)
        energy[j] = (1.0 + 2.0 * m) * t + 2.0 * m * f


def team_kernel(masks, head, warm, cond, water, heat):
    steps = head.shape[0]
    upper = [masks[s - 1] > 0.5 for s in DISTANCES]
    lower = [masks[PAIR_DEV + s - 1] > 0.5 for s in DISTANCES]

    def step(j, _):
        for g in range(GROUPS):
            l0, l1 = lanes_of(g, 0), lanes_of(g, 1)
            h0, h1 = head[j, :, l0], head[j, :, l1]
            t0, t1 = warm[j, :, l0], warm[j, :, l1]
            c0, c1 = cond[j, :, l0], cond[j, :, l1]
            total = None
            for s in DISTANCES:
                up, low = upper[s - 1], lower[s - 1]
                back = LANES - s * OWN
                h_low = pltpu.roll(jnp.where(low, h1, h0), back, axis=1)
                t_low = pltpu.roll(jnp.where(low, t1, t0), back, axis=1)
                c_low = pltpu.roll(jnp.where(low, c1, c0), back, axis=1)
                flow = (
                    masks[2 * PAIR_DEV + s - 1]
                    * (jnp.where(up, c1, c0) + c_low)
                    * (jnp.where(up, h1, h0) - h_low + 0.5)
                )
                carried = flow * jnp.where(flow > 0.0, jnp.where(up, t1, t0), t_low)
                flow_in = pltpu.roll(flow, s * OWN, axis=1)
                carried_in = pltpu.roll(carried, s * OWN, axis=1)
                part = (
                    flow_in - flow,
                    jnp.where(low, flow_in, 0.0) - jnp.where(up, flow, 0.0),
                    carried_in - carried,
                    jnp.where(low, carried_in, 0.0) - jnp.where(up, carried, 0.0),
                )
                total = part if total is None else [a + b for a, b in zip(total, part)]
            water[j, :, l0] = total[0] - total[1]
            water[j, :, l1] = total[1]
            heat[j, :, l0] = 2.0 * (total[2] - total[3])
            heat[j, :, l1] = 2.0 * total[3]

    lax.fori_loop(0, steps, step, None)


def cross_flows(cut, masks, mine, theirs):
    row = cut_row(cut)
    sign = sign_of(cut)
    above = place(cut)[1]
    lane = lax.broadcasted_iota(jnp.int32, (SUB, LANES), 1)
    first_block = lax.rem(lane, 2 * EDGE) < EDGE
    h, t, k = mine
    c = passage(h, t, k)
    far = [theirs[0], theirs[1], passage(*theirs)]
    other = [
        jnp.where(first_block, pltpu.roll(v, LANES - EDGE, axis=1), pltpu.roll(v, EDGE, axis=1)) for v in far
    ]
    water = heat = jnp.zeros((SUB, LANES), F32)
    for s in DISTANCES:
        same = masks[row + PAIR_DEV + s - 1] > 0.5
        picked = [jnp.where(same, a, b) for a, b in zip(far, other)]
        apart = (PAIR_DEV - s) * OWN
        if apart:
            shift = jnp.where(above, apart, LANES - apart)
            picked = [pltpu.roll(v, shift, axis=1) for v in picked]
        h_far, t_far, c_far = picked
        flow = masks[row + s - 1] * (c + c_far) * (sign * (h - h_far) + 0.5)
        water = water - flow
        heat = heat - flow * jnp.where(flow > 0.0, t, t_far)
    return water, heat


def ends():
    part = lax.broadcasted_iota(jnp.int32, (SUB, ALL), 0)
    group = lax.broadcasted_iota(jnp.int32, (SUB, ALL), 1) // WIDTH
    return (
        jnp.logical_and(part == 0, group == 0),
        jnp.logical_and(part == SUB - 1, group == GROUPS - 1),
    )


def faces(steps, last_part, fields, potential):
    face_of, rise_of = [], []
    for j in range(steps):
        if j + 1 < steps:
            c_next, v_next = fields[j + 1], potential[j + 1]
            face = 0.5 * (fields[j] + c_next)
        else:
            c_next, v_next = following(fields[0]), following(potential[0])
            face = jnp.where(last_part, 0.0, 0.5 * (fields[j] + c_next))
        face_of.append(face)
        rise_of.append(v_next - potential[j])
    return face_of, rise_of


def levels():
    found = [(following, preceding)]
    step = 1
    while step < SUB:
        found.append(
            (functools.partial(pltpu.roll, shift=SUB - step, axis=0), functools.partial(pltpu.roll, shift=step, axis=0))
        )
        step *= 2
    return found


def factor_kernel(cond, wet, stored, head, water, base, inverse, over, ratio, lead, reduced):
    steps = head.shape[0]
    first_part, last_part = ends()
    k_face, rise = faces(steps, last_part, [cond[j] for j in range(steps)], head)
    k_top = jnp.where(first_part, 0.0, preceding(k_face[-1]))
    q_face = [k * (1.0 - d) for k, d in zip(k_face, rise)]
    q_top = jnp.where(first_part, 0.0, preceding(q_face[-1]))
    c_all, a_all = [], []
    for j in range(steps):
        above = k_top if j == 0 else k_face[j - 1]
        into = q_top if j == 0 else q_face[j - 1]
        s = wet[j]
        base[j] = water[j] + into - q_face[j] - 0.8 * (s - stored[j])
        main = 0.8 * s * (1.0 - s) + 0.02 + above + k_face[j]
        r = reciprocal(main - above * c_all[-1]) if j else reciprocal(main)
        o = above * r
        inverse[j] = r
        over[j] = o
        c_all.append(k_face[j] * r)
        a_all.append(a_all[-1] * o if j else o)
        ratio[j] = c_all[-1]
        lead[j] = a_all[-1]
    p_first, a_first = c_all[-2], a_all[-2]
    for j in range(steps - 3, -1, -1):
        p_first = c_all[j] * p_first
        a_first = a_all[j] + c_all[j] * a_first
    last_c, last_a = c_all[-1], a_all[-1]
    g = reciprocal(1.0 - last_c * following(a_first))
    reduced[0] = g
    reduced[1] = last_c * g
    up = last_c * following(p_first) * g
    down = last_a * g
    for i, (after, before) in enumerate(levels()):
        g = reciprocal(1.0 - up * after(down) - down * before(up))
        reduced[3 * i + 2] = g
        reduced[3 * i + 3] = up * g
        reduced[3 * i + 4] = down * g
        up = up * after(up) * g
        down = down * before(down) * g


def apply_factors(steps, factors, source, value, update):
    inverse, over, ratio, lead, reduced = factors
    d = source(0) * inverse[0]
    value[0] = d
    for j in range(1, steps):
        d = source(j) * inverse[j] + d * over[j]
        value[j] = d
    d_first = value[steps - 2]
    for j in range(steps - 3, -1, -1):
        d_first = value[j] + ratio[j] * d_first
    own = d * reduced[0] + reduced[1] * following(d_first)
    for i, (after, before) in enumerate(levels()):
        own = own * reduced[3 * i + 2] + reduced[3 * i + 3] * after(own) + reduced[3 * i + 4] * before(own)
    above = preceding(own)
    x = own
    update(steps - 1, x)
    for j in range(steps - 2, -1, -1):
        x = ratio[j] * x + (lead[j] * above + value[j])
        update(j, x)


def advance(steps, cuts, masks, head, warm, conduct, energy, melt, factors, water, heat, top,
            mine, theirs, new_head, new_warm, new_wet, inflow, warm_inflow, ratio, lead, value, finish):
    for j in range(steps):
        w_parts = [water[j, :, m * LANES : (m + 1) * LANES] for m in range(2 * GROUPS)]
        q_parts = [heat[j, :, m * LANES : (m + 1) * LANES] for m in range(2 * GROUPS)]
        for cut in range(cuts):
            beside = masks[cut_row(cut) + 2 * PAIR_DEV]
            w_far, q_far = cross_flows(cut, masks, mine(cut, j), theirs(cut, j))
            for m in range(2 * GROUPS):
                shift = lax.rem(LANES - edge_shift(cut, m), LANES)
                w_parts[m] = w_parts[m] + beside * pltpu.roll(w_far, shift, axis=1)
                q_parts[m] = q_parts[m] + 2.0 * beside * pltpu.roll(q_far, shift, axis=1)
        for m in range(2 * GROUPS):
            inflow[j, :, m * LANES : (m + 1) * LANES] = w_parts[m]
            warm_inflow[j, :, m * LANES : (m + 1) * LANES] = q_parts[m]

    first_part, last_part = ends()

    def water_done(j, x):
        h = head[j] + x
        new_head[j] = h
        new_wet[j] = sigmoid(h)

    apply_factors(steps, factors, lambda j: inflow[j], value, water_done)

    l_cell = [conduct[j] * (1.5 - 0.5 * melt[j]) for j in range(steps)]
    l_face, rise = faces(steps, last_part, l_cell, warm)
    l_top = jnp.where(first_part, 0.0, preceding(l_face[-1]))
    g_face = [l * d for l, d in zip(l_face, rise)]
    g_top = jnp.where(first_part, 0.0, preceding(g_face[-1]))
    surface_lam = jnp.where(first_part, 2.0 * l_cell[0], 0.0)

    def heat_matrix(j):
        above = l_top if j == 0 else l_face[j - 1]
        out_of = g_top if j == 0 else g_face[j - 1]
        t, f = warm[j], melt[j]
        m2 = 0.1 + 0.8 * new_wet[j]
        now = (1.0 + m2) * t + m2 * f
        main = 2.0 + 2.0 * m2 * (1.0 + 2.0 * f * (1.0 - f)) + above + l_face[j]
        source = warm_inflow[j] - out_of + g_face[j] - 2.0 * (now - energy[j])
        if j == 0:
            main = main + surface_lam
            source = source + surface_lam * (top[...] - t)
        return above, main, l_face[j], source

    def heat_done(j, x):
        t = warm[j] + x
        new_warm[j] = t
        finish(j, t)

    solve(steps, heat_matrix, ratio, lead, value, heat_done)


def middle_kernel(cuts, *refs):
    masks, head, warm, perm, conduct, melt, energy, top, heat, water = refs[:10]
    factors, refs = refs[10:15], refs[3:]
    own, far = refs[12 : 12 + cuts], refs[12 + cuts : 12 + 2 * cuts]
    new_head, new_warm, new_wet, new_melt, new_cond = refs[12 + 2 * cuts : 17 + 2 * cuts]
    halos, sent = refs[17 + 2 * cuts : 17 + 3 * cuts], refs[17 + 3 * cuts : 17 + 4 * cuts]
    inflow, warm_inflow, ratio, lead, value = refs[17 + 4 * cuts :]
    steps = head.shape[0]
    packed = {}

    def finish(j, t):
        s, f = new_wet[j], sigmoid(2.0 * t)
        new_melt[j] = f
        new_cond[j] = perm[j] * (f * s * s + 0.02)
        for cut in range(cuts):
            for i, v in enumerate((new_head[j], t)):
                packed[cut, i, j] = halo_of(cut, v)
                halos[cut][i, j] = packed[cut, i, j]

    theirs = [[unsqueeze(cut, [far[cut][i, j] for j in range(steps - 1)]) for i in range(3)] for cut in range(cuts)]
    advance(
        steps, cuts, masks, head, warm, conduct, energy, melt, factors, water, heat, top,
        lambda cut, j: [own[cut][i, j] for i in range(3)],
        lambda cut, j: [theirs[cut][i][j] for i in range(3)],
        new_head, new_warm, new_wet, inflow, warm_inflow, ratio, lead, value, finish,
    )
    for cut in range(cuts):
        for i in range(2):
            other = masks[cut_row(cut) + 2 * PAIR_DEV + 1] > 0.5
            values = squeeze(cut, other, [packed[cut, i, j] for j in range(steps)])
            for j, v in enumerate(values):
                sent[cut][i, j] = v


def last_kernel(chunk, cuts, *refs):
    masks, head, warm, conduct, melt, energy, top, heat, water = refs[:9]
    factors, refs = refs[9:14], refs[2:]
    own, far = refs[12 : 12 + cuts], refs[12 + cuts : 12 + 2 * cuts]
    own_k, far_k = refs[12 + 2 * cuts : 12 + 3 * cuts], refs[12 + 3 * cuts : 12 + 4 * cuts]
    others = refs[12 + 4 * cuts : -10]
    out, new_head, new_warm, new_wet, inflow, warm_inflow, ratio, lead, value, load = refs[-10:]
    steps = head.shape[0]
    cells = steps * GROUPS * SUB
    stride = steps * GROUPS
    theirs = [
        [unsqueeze(cut, [source[i, j] for j in range(steps - 1)]) for source, i in ((far[cut], 0), (far[cut], 1), (far_k[cut], 2))]
        for cut in range(cuts)
    ]
    advance(
        steps, cuts, masks, head, warm, conduct, energy, melt, factors, water, heat, top,
        lambda cut, j: [own[cut][0, j], own[cut][1, j], own_k[cut][2, j]],
        lambda cut, j: [theirs[cut][i][j] for i in range(3)],
        new_head, new_warm, new_wet, inflow, warm_inflow, ratio, lead, value, lambda j, t: None,
    )
    final = chunk == CHUNKS - 1
    for f, field in enumerate((new_head, new_warm)):
        for b in range(2):
            slot = f * 2 + b
            for j in range(steps):
                for g in range(GROUPS):
                    load[slot, pl.ds(g * steps + j, SUB, stride=stride), :] = field[j, :, lanes_of(g, b)]
            turned = load[slot].T.reshape(TEAM, OWN, cells)
            if final:
                out[:, slot * CHUNKS + chunk] = turned
                for c, other in enumerate(others):
                    out[:, slot * CHUNKS + c] = other[:, slot]
            else:
                out[:, slot] = turned


def whole(memory=pltpu.VMEM):
    return pl.BlockSpec(memory_space=memory)


def call(kernel, name, args, outs, scratch=(), specs=None, out_specs=None, limit=VMEM_LIMIT, work=2_000_000):
    return pl.pallas_call(
        kernel,
        out_shape=[jax.ShapeDtypeStruct(shape, F32) for shape in outs],
        in_specs=specs or [whole()] * len(args),
        out_specs=out_specs or [whole()] * len(outs),
        scratch_shapes=scratch,
        compiler_params=pltpu.CompilerParams(vmem_limit_bytes=limit),
        cost_estimate=pl.CostEstimate(flops=work, bytes_accessed=work, transcendentals=0),
        name=name,
    )(*args)


def exchange(tiles, n):
    teams = [list(range(start, start + TEAM)) for start in range(0, n, TEAM)]
    return lax.all_to_all(
        tiles, "cols", split_axis=0, concat_axis=0, tiled=True, axis_index_groups=teams
    )


def swap(cut, n, value):
    pairs = []
    for team in range(cut, n // TEAM - 1, 2):
        for i in range(team * TEAM, (team + 1) * TEAM):
            pairs += [(i, i + TEAM), (i + TEAM, i)]
    return lax.ppermute(value, "cols", pairs)


def on_device(suction, warmth, classes, top, couplings, k_sat, heat_cond):
    n = lax.axis_size("cols")
    cells, width = suction.shape
    steps = cells // (SUB * GROUPS)
    quarters = width // LANES
    cuts = cut_count(n)
    column = (steps, SUB, ALL)
    halo = (steps, SUB, LANES)
    squeezed = (steps - 1, SUB, LANES)
    room = pltpu.VMEM(column, F32)
    smem = whole(pltpu.SMEM)
    hbm = whole(pltpu.HBM)

    masks = call(
        functools.partial(mask_kernel, n), "masks", (couplings,), [(mask_rows(cuts), SUB, LANES)]
    )[0]
    arguments = (suction, warmth, classes, top.reshape(1, width), couplings, k_sat.reshape(1, -1))
    packed, consts = call(
        functools.partial(pack_kernel, cuts),
        "pack",
        [pltpu.with_memory_space_constraint(v, pltpu.HBM) for v in arguments],
        [(TEAM, 3 * quarters + 1, OWN, cells), (k_sat.shape[0] + cuts, SUB, LANES)],
        scratch=[
            pltpu.VMEM((2, cells, width), F32),
            pltpu.VMEM((cells, width), classes.dtype),
            pltpu.VMEM((1, width), F32),
            pltpu.VMEM(couplings.shape, couplings.dtype),
            pltpu.VMEM((1, k_sat.shape[0]), F32),
            pltpu.SemaphoreType.DMA((6,)),
        ],
        specs=[hbm] * 6,
    )
    got = exchange(packed, n)

    edges = [
        call(
            functools.partial(edge_kernel, c, cuts),
            "edges",
            (got, consts),
            [(3,) + halo] * cuts + [(3,) + squeezed] * cuts,
            scratch=[pltpu.VMEM((3 * cuts, cells, LANES), F32)],
        )
        for c in range(CHUNKS)
    ]
    first = [
        call(
            functools.partial(first_kernel, c),
            "first",
            (got, k_sat, heat_cond),
            [column] * 8 + [(1, ALL)],
            scratch=[pltpu.VMEM((6, cells, LANES), F32)],
            specs=[whole(), smem, smem],
        )
        for c in range(CHUNKS)
    ]
    def prepare(cond, wet, stored, head, warm):
        water, heat = call(team_kernel, "team", (masks, head, warm, cond), [column] * 2)
        reduced = (2 + 3 * len(levels()), SUB, ALL)
        return (heat, *call(factor_kernel, "factor", (cond, wet, stored, head, water), [column] * 5 + [reduced]))

    flows, sides = [], []
    for c in range(CHUNKS):
        mine, sent = edges[c][:cuts], edges[c][cuts:]
        sides.append((mine, [swap(cut, n, v) for cut, v in enumerate(sent)]))
        flows.append(prepare(first[c][6], first[c][4], first[c][4], first[c][0], first[c][1]))

    second, later = [], []
    for c in range(CHUNKS):
        head, warm, perm, conduct, wet, melt, cond, energy, surface = first[c]
        mine, theirs = sides[c]
        values = call(
            functools.partial(middle_kernel, cuts),
            "middle",
            (masks, head, warm, perm, conduct, melt, energy, surface, *flows[c], *mine, *theirs),
            [column] * 5 + [(2,) + halo] * cuts + [(2,) + squeezed] * cuts,
            scratch=[room] * 5,
        )
        second.append(values[:5])
        mine, sent = values[5 : 5 + cuts], values[5 + cuts :]
        later.append((mine, [swap(cut, n, v) for cut, v in enumerate(sent)]))

    done = []
    for c in range(CHUNKS):
        conduct, stored, energy, surface = first[c][3], first[c][4], first[c][7], first[c][8]
        head, warm, wet, melt, cond = second[c]
        flow = prepare(cond, wet, stored, head, warm)
        mine, theirs = later[c]
        mine_k, theirs_k = sides[c]
        final = c == CHUNKS - 1
        done += call(
            functools.partial(last_kernel, c, cuts),
            "last",
            (
                masks, head, warm, conduct, melt, energy, surface, *flow,
                *mine, *theirs, *mine_k, *theirs_k, *(done if final else ()),
            ),
            [(TEAM, 2 * quarters if final else 4, OWN, cells)],
            scratch=[room] * 8 + [pltpu.VMEM((4, cells, LANES), F32)],
        )
    back = exchange(done[-1], n)
    return tuple(
        call(
            unpack_kernel,
            "unpack",
            (back,),
            [(cells, width)] * 2,
            scratch=[
                pltpu.VMEM((2, cells, width), F32),
                pltpu.SemaphoreType.DMA((2,)),
            ],
            out_specs=[hbm, hbm],
        )
    )


def solution(mesh):
    placed = (P(None, "cols"), P(None, "cols"), P(None, "cols"), P("cols"), P(), P(), P())
    return jax.shard_map(
        on_device,
        mesh=mesh,
        in_specs=placed,
        out_specs=(P(None, "cols"), P(None, "cols")),
        check_vma=False,
    )
```

```python
import functools

import jax
import jax.numpy as jnp
from jax import lax
from jax.experimental import pallas as pl
from jax.experimental.pallas import tpu as pltpu
from jax.sharding import PartitionSpec as P

SPAN = 256
PAIR_DEV = 4
LANES = 128
CHUNKS = SPAN // LANES
TEAM = 16
OWN = LANES // TEAM
SUB = 8
GROUPS = 2
WIDTH = 2 * LANES
ALL = GROUPS * WIDTH
EDGE = PAIR_DEV * OWN
VMEM_LIMIT = 32 * 1024 * 1024
DISTANCES = range(1, PAIR_DEV + 1)
F32 = jnp.float32


def cut_count(n):
    return min(n // TEAM - 1, 2)


def place(cut):
    team = lax.axis_index("cols") // TEAM
    return team, lax.rem(team, 2) == cut


def far_edge(above):
    return jnp.where(above, 0, PAIR_DEV - 1)


def sign_of(cut):
    return jnp.where(place(cut)[1], 1.0, -1.0).astype(F32)


def reciprocal(x):
    return pltpu.reciprocal(x, approx=True)


def sigmoid(x):
    return 0.5 + 0.5 * jnp.tanh(0.5 * x)


def passage(h, t, k):
    s = sigmoid(h)
    return k * (sigmoid(2.0 * t) * s * s + 0.02)


def lanes_of(g, b):
    return slice((g * 2 + b) * LANES, (g * 2 + b + 1) * LANES)


def following(value):
    first, second = value[:, :WIDTH], value[:, WIDTH:]
    return jnp.concatenate([second, pltpu.roll(first, SUB - 1, axis=0)], axis=1)


def preceding(value):
    first, second = value[:, :WIDTH], value[:, WIDTH:]
    return jnp.concatenate([pltpu.roll(second, 1, axis=0), first], axis=1)


def solve(steps, matrix, ratio, lead, value, update):
    c_prev = a_prev = d_prev = None
    for j in range(steps):
        above, main, below, source = matrix(j)
        if j == 0:
            r = reciprocal(main)
            a_prev = above * r
            d_prev = source * r
        else:
            r = reciprocal(main - above * c_prev)
            over = above * r
            a_prev = a_prev * over
            d_prev = source * r + d_prev * over
        c_prev = below * r
        ratio[j] = c_prev
        lead[j] = a_prev
        value[j] = d_prev
    last_c, last_a, last_d = c_prev, a_prev, d_prev
    p_first, a_first, d_first = ratio[steps - 2], lead[steps - 2], value[steps - 2]
    for j in range(steps - 3, -1, -1):
        c = ratio[j]
        p_first = c * p_first
        a_first = lead[j] + c * a_first
        d_first = value[j] + c * d_first
    g = reciprocal(1.0 - last_c * following(a_first))
    up = last_c * following(p_first) * g
    down = last_a * g
    own = (last_d + last_c * following(d_first)) * g
    step = 0
    while step < SUB:
        if step == 0:
            after, before = following, preceding
        else:
            after = functools.partial(pltpu.roll, shift=SUB - step, axis=0)
            before = functools.partial(pltpu.roll, shift=step, axis=0)
        g = reciprocal(1.0 - up * after(down) - down * before(up))
        own = (own + up * after(own) + down * before(own)) * g
        up = up * after(up) * g
        down = down * before(down) * g
        step = max(1, 2 * step)
    over = preceding(own)
    x = own
    update(steps - 1, x)
    for j in range(steps - 2, -1, -1):
        x = ratio[j] * x + (lead[j] * over + value[j])
        update(j, x)


def mask_rows(cuts):
    return 3 * PAIR_DEV + cuts * (2 * PAIR_DEV + 2)


def cut_row(cut):
    return 3 * PAIR_DEV + cut * (2 * PAIR_DEV + 2)


def mask_kernel(n, couplings, out):
    pair_rows = couplings[...]
    pairs = couplings.shape[1]
    pair_id = lax.broadcasted_iota(jnp.int32, (pairs, LANES), 0)
    lane = lax.broadcasted_iota(jnp.int32, (pairs, LANES), 1)
    lane_1 = lax.broadcasted_iota(jnp.int32, (SUB, LANES), 1)

    def chosen(dev, s):
        at = (pair_id == dev * PAIR_DEV + s - 1).astype(F32)
        found = jnp.dot(pair_rows, at, preferred_element_type=F32)
        return found[0:1], found[1:2]

    def put(row, value):
        out[row] = jnp.broadcast_to(value, (SUB, LANES))

    team = lax.axis_index("cols") // TEAM
    dev = team * TEAM + lane // OWN
    for s in DISTANCES:
        put(s - 1, chosen(dev, s)[0])
        put(PAIR_DEV + s - 1, chosen(dev - s, s)[1])
        put(2 * PAIR_DEV + s - 1, jnp.where(lane_1 // OWN + s < TEAM, 0.25, 0.0))
    block = lax.rem(lane_1 // EDGE, 2)
    edge = lax.rem(lane, EDGE) // OWN
    edge_1 = lax.rem(lane_1, EDGE) // OWN
    for cut in range(cut_count(n)):
        _, above = place(cut)
        row = cut_row(cut)
        partner = jnp.where(above, team + 1, team - 1)
        there = jnp.logical_and(partner >= 0, partner < n // TEAM)
        factor = jnp.where(there, 0.25, 0.0) * sign_of(cut)
        for s in DISTANCES:
            start = team * TEAM + jnp.where(above, TEAM - PAIR_DEV, -s)
            up, down = chosen(start + edge, s)
            mine = jnp.where(above, up, down)
            inward = jnp.where(above, edge_1, PAIR_DEV - 1 - edge_1)
            active = jnp.logical_and(inward >= PAIR_DEV - s, jnp.abs(mine - block.astype(F32)) < 0.5)
            put(row + s - 1, jnp.where(active, factor, 0.0))
            apart = jnp.where(above, PAIR_DEV - s, s - PAIR_DEV)
            up, down = chosen(start + edge + apart, s)
            theirs = jnp.where(edge_1 == far_edge(jnp.logical_not(above)), 0.0, jnp.where(above, down, up))
            put(row + PAIR_DEV + s - 1, jnp.where(jnp.abs(theirs - block.astype(F32)) < 0.5, 1.0, 0.0))
        outward = jnp.where(above, LANES - 1 - lane_1, lane_1)
        put(row + 2 * PAIR_DEV, jnp.where(outward < EDGE, 1.0, 0.0))
        single = jnp.logical_and(edge_1 == far_edge(above), block == 0)
        put(row + 2 * PAIR_DEV + 1, jnp.where(single, mine, 0.0))


def halo_parts():
    return lax.rem(lax.broadcasted_iota(jnp.int32, (SUB, LANES), 1) // OWN, 2 * PAIR_DEV)


def other_block(cut, couplings):
    team, above = place(cut)
    pair = (team * TEAM + jnp.where(above, TEAM - PAIR_DEV, -1)) * PAIR_DEV + PAIR_DEV - 1
    row = jnp.where(above, 0, 1)
    table = couplings[...].astype(F32)
    wanted = jnp.logical_and(
        lax.broadcasted_iota(jnp.int32, table.shape, 0) == row, lax.broadcasted_iota(jnp.int32, table.shape, 1) == pair
    )
    block = jnp.sum(jnp.sum(jnp.where(wanted, table, 0.0), axis=1, keepdims=True), axis=0, keepdims=True)
    single = jnp.where(halo_parts() == far_edge(above), 1.0, 0.0)
    return single * jnp.broadcast_to(block, (SUB, LANES))


def pack_kernel(
    cuts, suction, warmth, classes, surface, couplings, k_sat, heat_cond, out, consts, pair_rows,
    room, class_room, top, pairs, k_table, heat_table, in_sems,
):
    cells = out.shape[-1]
    quarters = 2 * CHUNKS
    into = []
    rooms = (room.at[0], room.at[1], class_room, top, pairs, k_table, heat_table)
    for f, field in enumerate((suction, warmth, classes, surface, couplings, k_sat, heat_cond)):
        into.append(pltpu.make_async_copy(field, rooms[f], in_sems.at[f]))
        into[-1].start()

    def put(slot, value):
        out[:, slot] = value.T.reshape(TEAM, OWN, cells)

    for f in range(3):
        into[f].wait()
        for q in range(quarters):
            lanes = slice(q * LANES, (q + 1) * LANES)
            put(f * quarters + q, class_room[:, lanes].astype(F32) if f == 2 else room[f, :, lanes])
    for copy in into[3:]:
        copy.wait()
    kinds = k_sat.shape[1]
    for c in range(kinds):
        consts[c] = jnp.broadcast_to(k_table[0:1, c : c + 1], (SUB, LANES))
        consts[kinds + c] = jnp.broadcast_to(heat_table[0:1, c : c + 1], (SUB, LANES))
    for cut in range(cuts):
        consts[2 * kinds + cut] = other_block(cut, pairs)
    pair_rows[...] = pairs[...].astype(F32)
    rows = [top[0:1, q * LANES : (q + 1) * LANES] for q in range(quarters)]
    put(3 * quarters, jnp.concatenate(rows + [jnp.zeros((cells - quarters, LANES), F32)], axis=0))


def unpack_kernel(got, suction, warmth, room, sems):
    cells = got.shape[-1]
    quarters = 2 * CHUNKS
    sent = []
    for f, out in enumerate((suction, warmth)):
        for q in range(quarters):
            room[f, :, q * LANES : (q + 1) * LANES] = got[:, f * quarters + q].reshape(LANES, cells).T
        sent.append(pltpu.make_async_copy(room.at[f], out, sems.at[f]))
        sent[-1].start()
    for copy in sent:
        copy.wait()


def edge_shift(cut, m):
    return lax.rem(EDGE * m + jnp.where(place(cut)[1], EDGE, 0), LANES)


def halo_of(cut, value):
    part = lax.broadcasted_iota(jnp.int32, (SUB, LANES), 1) // EDGE
    packed = None
    for m in range(2 * GROUPS):
        moved = pltpu.roll(value[:, m * LANES : (m + 1) * LANES], edge_shift(cut, m), axis=1)
        packed = moved if m == 0 else jnp.where(part == m, moved, packed)
    return packed


def pieces(above):
    spare = PAIR_DEV + far_edge(above)
    parts = [j if j < PAIR_DEV else j + jnp.where(above, 1, 0) for j in range(2 * PAIR_DEV - 1)]
    return [(part, lax.rem((spare - part) * OWN + LANES, LANES)) for part in parts]


def squeeze(cut, other, values):
    above = place(cut)[1]
    values = [jnp.where(other, pltpu.roll(v, LANES - EDGE, axis=1), v) for v in values]
    spare = halo_parts() == PAIR_DEV + far_edge(above)
    return [
        jnp.where(spare, pltpu.roll(values[-1], shift, axis=1), v)
        for v, (_, shift) in zip(values[:-1], pieces(above))
    ]


def unsqueeze(cut, values):
    part = halo_parts()
    last = values[0]
    for v, (piece, shift) in zip(values, pieces(jnp.logical_not(place(cut)[1]))):
        last = jnp.where(part == piece, pltpu.roll(v, lax.rem(LANES - shift, LANES), axis=1), last)
    return list(values) + [last]


def edge_kernel(chunk, cuts, got, consts, *refs):
    halos, sent, load = refs[:cuts], refs[cuts:-1], refs[-1]
    cells = got.shape[-1]
    steps = halos[0].shape[1]
    stride = steps * GROUPS
    second = lax.broadcasted_iota(jnp.int32, (SUB, LANES), 1) >= 2 * EDGE
    for cut in range(cuts):
        start = jnp.where(place(cut)[1], TEAM - PAIR_DEV, 0)
        for f in range(3):
            rows = [
                got[pl.ds(start, PAIR_DEV), (f * 2 + b) * CHUNKS + chunk].reshape(EDGE, cells) for b in range(2)
            ]
            load[cut * 3 + f] = jnp.concatenate(rows * GROUPS, axis=0).T
    kinds = (consts.shape[0] - cuts) // 2
    table = [consts[c] for c in range(kinds)]
    for cut in range(cuts):
        other = consts[2 * kinds + cut] > 0.5
        for f in range(3):
            values = []
            for j in range(steps):
                v = jnp.where(
                    second,
                    load[cut * 3 + f, pl.ds(steps + j, SUB, stride=stride), :],
                    load[cut * 3 + f, pl.ds(j, SUB, stride=stride), :],
                )
                if f == 2:
                    k = table[0]
                    for c in range(1, len(table)):
                        k = jnp.where(v >= c, table[c], k)
                    v = k
                halos[cut][f, j] = v
                values.append(v)
            for j, v in enumerate(squeeze(cut, other, values)):
                sent[cut][f, j] = v


def first_kernel(
    chunk, kinds, got, consts, head, warm, perm, conduct, wet, melt, cond, energy, top, load
):
    cells = got.shape[-1]
    steps = head.shape[0]
    stride = steps * GROUPS

    for field in range(3):
        for b in range(2):
            load[field * 2 + b] = got[:, (field * 2 + b) * CHUNKS + chunk].reshape(LANES, cells).T
    surface = got[:, 6 * CHUNKS].reshape(LANES, cells).T[0:SUB]
    rows = [surface[b * CHUNKS + chunk : b * CHUNKS + chunk + 1] for b in range(2)]
    top[...] = jnp.concatenate(rows * GROUPS, axis=1)

    def fetch(field, j):
        parts = [
            load[field * 2 + b, pl.ds(g * steps + j, SUB, stride=stride), :]
            for g in range(GROUPS)
            for b in range(2)
        ]
        return jnp.concatenate(parts, axis=1)

    def pick(v):
        parts = []
        for m in range(2 * GROUPS):
            part = v[:, m * LANES : (m + 1) * LANES]
            k, lam = consts[0], consts[kinds]
            for c in range(1, kinds):
                here = part >= c
                k = jnp.where(here, consts[c], k)
                lam = jnp.where(here, consts[kinds + c], lam)
            parts.append((k, lam))
        return [jnp.concatenate(side, axis=1) for side in zip(*parts)]

    for j in range(steps):
        h, t, v = [fetch(field, j) for field in range(3)]
        k, lam = pick(v)
        s, f = sigmoid(h), sigmoid(2.0 * t)
        m = 0.05 + 0.4 * s
        head[j], warm[j], perm[j], conduct[j] = h, t, k, lam
        wet[j] = s
        melt[j] = f
        cond[j] = k * (f * s * s + 0.02)
        energy[j] = (1.0 + 2.0 * m) * t + 2.0 * m * f


def team_kernel(masks, head, warm, cond, water, heat):
    steps = head.shape[0]
    upper = [masks[s - 1] > 0.5 for s in DISTANCES]
    lower = [masks[PAIR_DEV + s - 1] > 0.5 for s in DISTANCES]

    def step(j, _):
        for g in range(GROUPS):
            l0, l1 = lanes_of(g, 0), lanes_of(g, 1)
            h0, h1 = head[j, :, l0], head[j, :, l1]
            t0, t1 = warm[j, :, l0], warm[j, :, l1]
            c0, c1 = cond[j, :, l0], cond[j, :, l1]
            total = None
            for s in DISTANCES:
                up, low = upper[s - 1], lower[s - 1]
                back = LANES - s * OWN
                h_low = pltpu.roll(jnp.where(low, h1, h0), back, axis=1)
                t_low = pltpu.roll(jnp.where(low, t1, t0), back, axis=1)
                c_low = pltpu.roll(jnp.where(low, c1, c0), back, axis=1)
                flow = (
                    masks[2 * PAIR_DEV + s - 1]
                    * (jnp.where(up, c1, c0) + c_low)
                    * (jnp.where(up, h1, h0) - h_low + 0.5)
                )
                carried = flow * jnp.where(flow > 0.0, jnp.where(up, t1, t0), t_low)
                flow_in = pltpu.roll(flow, s * OWN, axis=1)
                carried_in = pltpu.roll(carried, s * OWN, axis=1)
                part = (
                    flow_in - flow,
                    jnp.where(low, flow_in, 0.0) - jnp.where(up, flow, 0.0),
                    carried_in - carried,
                    jnp.where(low, carried_in, 0.0) - jnp.where(up, carried, 0.0),
                )
                total = part if total is None else [a + b for a, b in zip(total, part)]
            water[j, :, l0] = total[0] - total[1]
            water[j, :, l1] = total[1]
            heat[j, :, l0] = 2.0 * (total[2] - total[3])
            heat[j, :, l1] = 2.0 * total[3]

    lax.fori_loop(0, steps, step, None, unroll=2)


def cross_flows(cut, masks, mine, theirs):
    row = cut_row(cut)
    sign = sign_of(cut)
    above = place(cut)[1]
    lane = lax.broadcasted_iota(jnp.int32, (SUB, LANES), 1)
    first_block = lax.rem(lane, 2 * EDGE) < EDGE
    h, t, k = mine
    c = passage(h, t, k)
    far = [theirs[0], theirs[1], passage(*theirs)]
    other = [
        jnp.where(first_block, pltpu.roll(v, LANES - EDGE, axis=1), pltpu.roll(v, EDGE, axis=1)) for v in far
    ]
    water = heat = jnp.zeros((SUB, LANES), F32)
    for s in DISTANCES:
        same = masks[row + PAIR_DEV + s - 1] > 0.5
        picked = [jnp.where(same, a, b) for a, b in zip(far, other)]
        apart = (PAIR_DEV - s) * OWN
        if apart:
            shift = jnp.where(above, apart, LANES - apart)
            picked = [pltpu.roll(v, shift, axis=1) for v in picked]
        h_far, t_far, c_far = picked
        flow = masks[row + s - 1] * (c + c_far) * (sign * (h - h_far) + 0.5)
        water = water - flow
        heat = heat - flow * jnp.where(flow > 0.0, t, t_far)
    return water, heat


def ends():
    part = lax.broadcasted_iota(jnp.int32, (SUB, ALL), 0)
    group = lax.broadcasted_iota(jnp.int32, (SUB, ALL), 1) // WIDTH
    return (
        jnp.logical_and(part == 0, group == 0),
        jnp.logical_and(part == SUB - 1, group == GROUPS - 1),
    )


def faces(steps, last_part, fields, potential):
    face_of, rise_of = [], []
    for j in range(steps):
        if j + 1 < steps:
            c_next, v_next = fields[j + 1], potential[j + 1]
            face = 0.5 * (fields[j] + c_next)
        else:
            c_next, v_next = following(fields[0]), following(potential[0])
            face = jnp.where(last_part, 0.0, 0.5 * (fields[j] + c_next))
        face_of.append(face)
        rise_of.append(v_next - potential[j])
    return face_of, rise_of


def levels():
    found = [(following, preceding)]
    step = 1
    while step < SUB:
        found.append(
            (functools.partial(pltpu.roll, shift=SUB - step, axis=0), functools.partial(pltpu.roll, shift=step, axis=0))
        )
        step *= 2
    return found


def factor_kernel(cond, wet, stored, head, water, base, inverse, over, ratio, lead, reduced):
    steps = head.shape[0]
    first_part, last_part = ends()
    k_face, rise = faces(steps, last_part, [cond[j] for j in range(steps)], head)
    k_top = jnp.where(first_part, 0.0, preceding(k_face[-1]))
    q_face = [k * (1.0 - d) for k, d in zip(k_face, rise)]
    q_top = jnp.where(first_part, 0.0, preceding(q_face[-1]))
    c_all, a_all = [], []
    for j in range(steps):
        above = k_top if j == 0 else k_face[j - 1]
        into = q_top if j == 0 else q_face[j - 1]
        s = wet[j]
        base[j] = water[j] + into - q_face[j] - 0.8 * (s - stored[j])
        main = 0.8 * s * (1.0 - s) + 0.02 + above + k_face[j]
        r = reciprocal(main - above * c_all[-1]) if j else reciprocal(main)
        o = above * r
        inverse[j] = r
        over[j] = o
        c_all.append(k_face[j] * r)
        a_all.append(a_all[-1] * o if j else o)
        ratio[j] = c_all[-1]
        lead[j] = a_all[-1]
    p_first, a_first = c_all[-2], a_all[-2]
    for j in range(steps - 3, -1, -1):
        p_first = c_all[j] * p_first
        a_first = a_all[j] + c_all[j] * a_first
    last_c, last_a = c_all[-1], a_all[-1]
    g = reciprocal(1.0 - last_c * following(a_first))
    reduced[0] = g
    reduced[1] = last_c * g
    up = last_c * following(p_first) * g
    down = last_a * g
    for i, (after, before) in enumerate(levels()):
        g = reciprocal(1.0 - up * after(down) - down * before(up))
        reduced[3 * i + 2] = g
        reduced[3 * i + 3] = up * g
        reduced[3 * i + 4] = down * g
        up = up * after(up) * g
        down = down * before(down) * g


def apply_factors(steps, factors, source, value, update):
    inverse, over, ratio, lead, reduced = factors
    d = source(0) * inverse[0]
    value[0] = d
    for j in range(1, steps):
        d = source(j) * inverse[j] + d * over[j]
        value[j] = d
    d_first = value[steps - 2]
    for j in range(steps - 3, -1, -1):
        d_first = value[j] + ratio[j] * d_first
    own = d * reduced[0] + reduced[1] * following(d_first)
    for i, (after, before) in enumerate(levels()):
        own = own * reduced[3 * i + 2] + reduced[3 * i + 3] * after(own) + reduced[3 * i + 4] * before(own)
    above = preceding(own)
    x = own
    update(steps - 1, x)
    for j in range(steps - 2, -1, -1):
        x = ratio[j] * x + (lead[j] * above + value[j])
        update(j, x)


def advance(steps, cuts, masks, head, warm, conduct, energy, melt, factors, water, heat, top,
            mine, theirs, new_head, new_warm, new_wet, inflow, warm_inflow, ratio, lead, value, finish):
    for j in range(steps):
        w_parts = [water[j, :, m * LANES : (m + 1) * LANES] for m in range(2 * GROUPS)]
        q_parts = [heat[j, :, m * LANES : (m + 1) * LANES] for m in range(2 * GROUPS)]
        for cut in range(cuts):
            beside = masks[cut_row(cut) + 2 * PAIR_DEV]
            w_far, q_far = cross_flows(cut, masks, mine(cut, j), theirs(cut, j))
            for m in range(2 * GROUPS):
                shift = lax.rem(LANES - edge_shift(cut, m), LANES)
                w_parts[m] = w_parts[m] + beside * pltpu.roll(w_far, shift, axis=1)
                q_parts[m] = q_parts[m] + 2.0 * beside * pltpu.roll(q_far, shift, axis=1)
        for m in range(2 * GROUPS):
            inflow[j, :, m * LANES : (m + 1) * LANES] = w_parts[m]
            warm_inflow[j, :, m * LANES : (m + 1) * LANES] = q_parts[m]

    first_part, last_part = ends()

    def water_done(j, x):
        h = head[j] + x
        new_head[j] = h
        new_wet[j] = sigmoid(h)

    apply_factors(steps, factors, lambda j: inflow[j], value, water_done)

    l_cell = [conduct[j] * (1.5 - 0.5 * melt[j]) for j in range(steps)]
    l_face, rise = faces(steps, last_part, l_cell, warm)
    l_top = jnp.where(first_part, 0.0, preceding(l_face[-1]))
    g_face = [l * d for l, d in zip(l_face, rise)]
    g_top = jnp.where(first_part, 0.0, preceding(g_face[-1]))
    surface_lam = jnp.where(first_part, 2.0 * l_cell[0], 0.0)

    def heat_matrix(j):
        above = l_top if j == 0 else l_face[j - 1]
        out_of = g_top if j == 0 else g_face[j - 1]
        t, f = warm[j], melt[j]
        m2 = 0.1 + 0.8 * new_wet[j]
        now = (1.0 + m2) * t + m2 * f
        main = 2.0 + 2.0 * m2 * (1.0 + 2.0 * f * (1.0 - f)) + above + l_face[j]
        source = warm_inflow[j] - out_of + g_face[j] - 2.0 * (now - energy[j])
        if j == 0:
            main = main + surface_lam
            source = source + surface_lam * (top[...] - t)
        return above, main, l_face[j], source

    def heat_done(j, x):
        t = warm[j] + x
        new_warm[j] = t
        finish(j, t)

    solve(steps, heat_matrix, ratio, lead, value, heat_done)


def middle_kernel(cuts, *refs):
    masks, head, warm, perm, conduct, melt, energy, top, heat, water = refs[:10]
    factors, refs = refs[10:15], refs[3:]
    own, far = refs[12 : 12 + cuts], refs[12 + cuts : 12 + 2 * cuts]
    new_head, new_warm, new_wet, new_melt, new_cond = refs[12 + 2 * cuts : 17 + 2 * cuts]
    halos, sent = refs[17 + 2 * cuts : 17 + 3 * cuts], refs[17 + 3 * cuts : 17 + 4 * cuts]
    inflow, warm_inflow, ratio, lead, value = refs[17 + 4 * cuts :]
    steps = head.shape[0]
    packed = {}

    def finish(j, t):
        s, f = new_wet[j], sigmoid(2.0 * t)
        new_melt[j] = f
        new_cond[j] = perm[j] * (f * s * s + 0.02)
        for cut in range(cuts):
            for i, v in enumerate((new_head[j], t)):
                packed[cut, i, j] = halo_of(cut, v)
                halos[cut][i, j] = packed[cut, i, j]

    theirs = [[unsqueeze(cut, [far[cut][i, j] for j in range(steps - 1)]) for i in range(3)] for cut in range(cuts)]
    advance(
        steps, cuts, masks, head, warm, conduct, energy, melt, factors, water, heat, top,
        lambda cut, j: [own[cut][i, j] for i in range(3)],
        lambda cut, j: [theirs[cut][i][j] for i in range(3)],
        new_head, new_warm, new_wet, inflow, warm_inflow, ratio, lead, value, finish,
    )
    for cut in range(cuts):
        for i in range(2):
            other = masks[cut_row(cut) + 2 * PAIR_DEV + 1] > 0.5
            values = squeeze(cut, other, [packed[cut, i, j] for j in range(steps)])
            for j, v in enumerate(values):
                sent[cut][i, j] = v


def last_kernel(chunk, cuts, *refs):
    masks, head, warm, conduct, melt, energy, top, heat, water = refs[:9]
    factors, refs = refs[9:14], refs[2:]
    own, far = refs[12 : 12 + cuts], refs[12 + cuts : 12 + 2 * cuts]
    own_k, far_k = refs[12 + 2 * cuts : 12 + 3 * cuts], refs[12 + 3 * cuts : 12 + 4 * cuts]
    others = refs[12 + 4 * cuts : -10]
    out, new_head, new_warm, new_wet, inflow, warm_inflow, ratio, lead, value, load = refs[-10:]
    steps = head.shape[0]
    cells = steps * GROUPS * SUB
    stride = steps * GROUPS
    theirs = [
        [unsqueeze(cut, [source[i, j] for j in range(steps - 1)]) for source, i in ((far[cut], 0), (far[cut], 1), (far_k[cut], 2))]
        for cut in range(cuts)
    ]
    advance(
        steps, cuts, masks, head, warm, conduct, energy, melt, factors, water, heat, top,
        lambda cut, j: [own[cut][0, j], own[cut][1, j], own_k[cut][2, j]],
        lambda cut, j: [theirs[cut][i][j] for i in range(3)],
        new_head, new_warm, new_wet, inflow, warm_inflow, ratio, lead, value, lambda j, t: None,
    )
    final = chunk == CHUNKS - 1
    for f, field in enumerate((new_head, new_warm)):
        for b in range(2):
            slot = f * 2 + b
            for j in range(steps):
                for g in range(GROUPS):
                    load[slot, pl.ds(g * steps + j, SUB, stride=stride), :] = field[j, :, lanes_of(g, b)]
            turned = load[slot].T.reshape(TEAM, OWN, cells)
            if final:
                out[:, slot * CHUNKS + chunk] = turned
                for c, other in enumerate(others):
                    out[:, slot * CHUNKS + c] = other[:, slot]
            else:
                out[:, slot] = turned


def whole(memory=pltpu.VMEM):
    return pl.BlockSpec(memory_space=memory)


def call(kernel, name, args, outs, scratch=(), specs=None, out_specs=None, limit=VMEM_LIMIT, work=2_000_000):
    return pl.pallas_call(
        kernel,
        out_shape=[jax.ShapeDtypeStruct(shape, F32) for shape in outs],
        in_specs=specs or [whole()] * len(args),
        out_specs=out_specs or [whole()] * len(outs),
        scratch_shapes=scratch,
        compiler_params=pltpu.CompilerParams(vmem_limit_bytes=limit),
        cost_estimate=pl.CostEstimate(flops=work, bytes_accessed=work, transcendentals=0),
        name=name,
    )(*args)


def exchange(tiles, n):
    teams = [list(range(start, start + TEAM)) for start in range(0, n, TEAM)]
    return lax.all_to_all(
        tiles, "cols", split_axis=0, concat_axis=0, tiled=True, axis_index_groups=teams
    )


def swap(cut, n, value):
    pairs = []
    for team in range(cut, n // TEAM - 1, 2):
        for i in range(team * TEAM, (team + 1) * TEAM):
            pairs += [(i, i + TEAM), (i + TEAM, i)]
    return lax.ppermute(value, "cols", pairs)


def on_device(suction, warmth, classes, top, couplings, k_sat, heat_cond):
    n = lax.axis_size("cols")
    cells, width = suction.shape
    steps = cells // (SUB * GROUPS)
    quarters = width // LANES
    cuts = cut_count(n)
    column = (steps, SUB, ALL)
    halo = (steps, SUB, LANES)
    squeezed = (steps - 1, SUB, LANES)
    room = pltpu.VMEM(column, F32)
    hbm = whole(pltpu.HBM)

    arguments = (suction, warmth, classes, top.reshape(1, width), couplings, k_sat.reshape(1, -1), heat_cond.reshape(1, -1))
    kinds = k_sat.shape[0]
    packed, consts, pair_rows = call(
        functools.partial(pack_kernel, cuts),
        "pack",
        [pltpu.with_memory_space_constraint(v, pltpu.HBM) for v in arguments],
        [(TEAM, 3 * quarters + 1, OWN, cells), (2 * kinds + cuts, SUB, LANES), couplings.shape],
        scratch=[
            pltpu.VMEM((2, cells, width), F32),
            pltpu.VMEM((cells, width), classes.dtype),
            pltpu.VMEM((1, width), F32),
            pltpu.VMEM(couplings.shape, couplings.dtype),
            pltpu.VMEM((1, kinds), F32),
            pltpu.VMEM((1, kinds), F32),
            pltpu.SemaphoreType.DMA((7,)),
        ],
        specs=[hbm] * 7,
    )
    masks = call(
        functools.partial(mask_kernel, n), "masks", (pair_rows,), [(mask_rows(cuts), SUB, LANES)]
    )[0]
    got = exchange(packed, n)

    edges = [
        call(
            functools.partial(edge_kernel, c, cuts),
            "edges",
            (got, consts),
            [(3,) + halo] * cuts + [(3,) + squeezed] * cuts,
            scratch=[pltpu.VMEM((3 * cuts, cells, LANES), F32)],
        )
        for c in range(CHUNKS)
    ]
    first = [
        call(
            functools.partial(first_kernel, c, kinds),
            "first",
            (got, consts),
            [column] * 8 + [(1, ALL)],
            scratch=[pltpu.VMEM((6, cells, LANES), F32)],
        )
        for c in range(CHUNKS)
    ]
    def prepare(cond, wet, stored, head, warm):
        water, heat = call(team_kernel, "team", (masks, head, warm, cond), [column] * 2)
        reduced = (2 + 3 * len(levels()), SUB, ALL)
        return (heat, *call(factor_kernel, "factor", (cond, wet, stored, head, water), [column] * 5 + [reduced]))

    flows, sides = [], []
    for c in range(CHUNKS):
        mine, sent = edges[c][:cuts], edges[c][cuts:]
        sides.append((mine, [swap(cut, n, v) for cut, v in enumerate(sent)]))
        flows.append(prepare(first[c][6], first[c][4], first[c][4], first[c][0], first[c][1]))

    second, later = [], []
    for c in range(CHUNKS):
        head, warm, perm, conduct, wet, melt, cond, energy, surface = first[c]
        mine, theirs = sides[c]
        values = call(
            functools.partial(middle_kernel, cuts),
            "middle",
            (masks, head, warm, perm, conduct, melt, energy, surface, *flows[c], *mine, *theirs),
            [column] * 5 + [(2,) + halo] * cuts + [(2,) + squeezed] * cuts,
            scratch=[room] * 5,
        )
        second.append(values[:5])
        mine, sent = values[5 : 5 + cuts], values[5 + cuts :]
        later.append((mine, [swap(cut, n, v) for cut, v in enumerate(sent)]))

    done = []
    for c in range(CHUNKS):
        conduct, stored, energy, surface = first[c][3], first[c][4], first[c][7], first[c][8]
        head, warm, wet, melt, cond = second[c]
        flow = prepare(cond, wet, stored, head, warm)
        mine, theirs = later[c]
        mine_k, theirs_k = sides[c]
        final = c == CHUNKS - 1
        done += call(
            functools.partial(last_kernel, c, cuts),
            "last",
            (
                masks, head, warm, conduct, melt, energy, surface, *flow,
                *mine, *theirs, *mine_k, *theirs_k, *(done if final else ()),
            ),
            [(TEAM, 2 * quarters if final else 4, OWN, cells)],
            scratch=[room] * 8 + [pltpu.VMEM((4, cells, LANES), F32)],
        )
    back = exchange(done[-1], n)
    return tuple(
        call(
            unpack_kernel,
            "unpack",
            (back,),
            [(cells, width)] * 2,
            scratch=[
                pltpu.VMEM((2, cells, width), F32),
                pltpu.SemaphoreType.DMA((2,)),
            ],
            out_specs=[hbm, hbm],
        )
    )


def solution(mesh):
    placed = (P(None, "cols"), P(None, "cols"), P(None, "cols"), P("cols"), P(), P(), P())
    return jax.shard_map(
        on_device,
        mesh=mesh,
        in_specs=placed,
        out_specs=(P(None, "cols"), P(None, "cols")),
        check_vma=False,
    )
```
